32 devices in a mesh: groups: 2 (over y), ex: 4 (over z), mod: 2 (over x), sub: 2 (over core).
Axes of the slice: x: 2, y: 2, z: 4, core: 2. Of those that a mesh axis runs over, the one named last changes fastest.
Arguments:
- query_grads: bfloat16 [512, 2, 4096], P('ex', 'mod', 'sub'), may hold values from -6 to 6
- train_grads: bfloat16 [4096, 2, 4096], P(('groups', 'ex'), 'mod', 'sub'), parts along dimension 0, may hold values from -0.0625 to 0.0625
- in_inverse: float32 [16, 64, 64], replicated
- out_inverse: float32 [16, 64, 64], replicated
- module_map: int32 [2], P('mod'), may hold values from 0 to 15
Outputs:
- scores: float32 [4096, 3, 128], P(('groups', 'ex', 'mod', 'sub')), parts along dimension 0
The draws below stay inside these ranges and needn't reach their ends.
There are 2 independent parts, one for each index of `groups`. The reference program is written for one: setup_inputs(seed, part) draws one part's arguments, and reference() takes and returns one part's arrays. A program takes and returns all parts, laid end to end along the dimension named above; an argument that names none is the same for every part. Nothing has to cross between parts.
All inputs are finite; a program needn't handle non-finite values.
Results may differ from the reference program's by a relative error of at most 0.0029.
Values may be sent and summed in bfloat16 or wider, within the bound.
No kernel may reach another device: no remote copies, remote signals or barrier semaphores. Data moves between devices by JAX's collectives and lax.ppermute only.
A program may use at most 64 MiB of HBM per device.

```python
import jax
import jax.numpy as jnp
from jax import lax

R_IN = 64
R_OUT = 64
PROJ = 4096
FACTORS = 16
MODULES = 2
TR_DEV = 512
QB = 128
HALF = 1
TRAIN = 2048
QUERIES = 512
N_EX = 4


def factor_table(key, width):
    diag_key, off_key = jax.random.split(key)
    diagonal = jax.random.uniform(diag_key, (FACTORS, width), minval=1.0, maxval=3.0)
    spread = 0.08 * jax.random.normal(off_key, (FACTORS, width, width))
    symmetric = 0.7071 * (spread + jnp.swapaxes(spread, 1, 2))
    eye_mask = jnp.eye(width, dtype=jnp.float32)[None, :, :]
    return (symmetric * (1.0 - eye_mask) + diagonal[:, :, None] * eye_mask).astype(jnp.float32)


def draw_in_inverse(key, part):
    key = jax.random.fold_in(key, 11)
    return factor_table(key, R_IN)


def draw_out_inverse(key, part):
    key = jax.random.fold_in(key, 23)
    return factor_table(key, R_OUT)


def levels(key, dims, pieces, smallest, high):
    loudness, own = 1.0, jax.random.fold_in(key, 6)
    for axis_at, blocks in pieces:
        draws = jnp.exp(jax.random.uniform(jax.random.fold_in(own, axis_at), (blocks,), jnp.float32, smallest / len(pieces), high / len(pieces)))
        loudness = loudness * jnp.repeat(draws, dims[axis_at] // blocks).reshape([-1 if axis == axis_at else 1 for axis in range(len(dims))])
    return loudness


def normal_values(rng, shape, deviation, bound, cuts=(), kind=jnp.bfloat16):
    entries = jax.random.normal(rng, shape, jnp.float32) * deviation
    if len(cuts) > 0:
        entries = levels(rng, shape, cuts, -0.22, 0.18) * entries
    return jnp.clip(entries, min=-bound, max=bound).astype(kind)


def setup_inputs(seed: int = 0, part: int = 0) -> dict:
    key_list = jax.random.split(jax.random.key(seed), 6)
    own_keys = jax.random.split(jax.random.fold_in(key_list[5], part), 6)
    return {
        "query_grads": normal_values(key_list[0], (QUERIES, MODULES, PROJ), 1.0, 6.0, ((0, 4), (1, 2), (2, 2))),
        "train_grads": normal_values(own_keys[1], (TRAIN, MODULES, PROJ), (MODULES * PROJ) ** -0.5, 0.0625, ((0, 4), (1, 2), (2, 2))),
        "in_inverse": draw_in_inverse(jax.random.fold_in(key_list[5], 71), part),
        "out_inverse": draw_out_inverse(jax.random.fold_in(key_list[5], 71), part),
        "module_map": jax.random.randint(key_list[4], (MODULES,), 0, FACTORS).astype(jnp.int32),
    }


precise = lax.Precision.HIGHEST


def precondition(queries, in_used, out_used):
    query_count = queries.shape[0]
    blocks = queries.astype(jnp.float32).reshape(query_count, MODULES, R_OUT, R_IN)
    right_done = jnp.einsum('qmoi,mij->qmoj', blocks, in_used, precision=precise)
    both_done = jnp.einsum('mpo,qmoj->qmpj', out_used, right_done, precision=precise)
    return both_done.astype(jnp.bfloat16).reshape(query_count, MODULES * PROJ)


def reference(query_grads, train_grads, in_inverse, out_inverse, module_map):
    in_used = jnp.take(in_inverse, module_map, axis=0)
    out_used = jnp.take(out_inverse, module_map, axis=0)
    precon = precondition(query_grads, in_used, out_used).reshape(N_EX, QB, MODULES * PROJ)
    train_rows = train_grads.reshape(N_EX, TR_DEV, MODULES * PROJ)

    def score_block(ex_block):
        picked = []
        for offset in range(-HALF, HALF + 1):
            index = ((ex_block + offset + N_EX) % N_EX).astype(jnp.int32)
            picked.append(lax.dynamic_index_in_dim(precon, index, 0, keepdims=False))
        window = jnp.concatenate(picked, axis=0)
        own_train = lax.dynamic_index_in_dim(train_rows, ex_block, 0, keepdims=False)
        return lax.dot_general(own_train, window, (((1,), (1,)), ((), ())), preferred_element_type=jnp.float32)

    results = lax.map(score_block, jnp.arange(N_EX, dtype=jnp.int32))
    return results.reshape(TRAIN, 2 * HALF + 1, QB)
```

```python
import jax
import jax.numpy as jnp
from jax import lax
from jax.sharding import PartitionSpec as P

WINDOW_HALF = 2


precise = lax.Precision.HIGHEST


def shifted(value, axis, steps):
    count = lax.axis_size(axis)
    pairs = [(source, (source + steps) % count) for source in range(count)]
    return lax.ppermute(value, axis, pairs)


def pick(value, index):
    return lax.dynamic_index_in_dim(value, index, 0, keepdims=False)


def reduced(partial):
    mods, subs = lax.axis_size("mod"), lax.axis_size("sub")
    mod, sub = lax.axis_index("mod"), lax.axis_index("sub")
    width = partial.shape[-1]
    cut = partial.reshape(mods, subs, -1, width).swapaxes(0, 1)
    total = pick(cut, sub)
    for step in range(1, subs):
        total = total + shifted(pick(cut, (sub + step) % subs), "sub", step)
    kept = pick(total, mod)
    for step in range(1, mods):
        kept = kept + shifted(pick(total, (mod + step) % mods), "mod", step)
    return kept


def local(query_grads, train_grads, in_inverse, out_inverse, module_map):
    block_rows, mod_count, half_width = query_grads.shape
    rank_in = in_inverse.shape[1]
    rank_out = out_inverse.shape[1]
    own_rows = half_width // rank_in
    subs = lax.axis_size("sub")
    sub = lax.axis_index("sub")

    in_used = pick(in_inverse, module_map[0])
    out_used = pick(out_inverse, module_map[0])
    out_part = lax.dynamic_slice_in_dim(out_used, sub * own_rows, own_rows, 0)

    own = query_grads.reshape(block_rows, own_rows, rank_in)
    left = jnp.zeros((block_rows, own_rows, rank_in), jnp.float32)
    for step in range(subs):
        piece = own if step == 0 else shifted(own, "sub", step)
        source = (sub - step) % subs
        columns = lax.dynamic_slice_in_dim(out_part, source * own_rows, own_rows, 1)
        left = left + jnp.einsum("po,qoi->qpi", columns, piece.astype(jnp.float32), precision=precise)
    precon = jnp.einsum("qpi,ij->qpj", left, in_used, precision=precise)
    precon = precon.astype(jnp.bfloat16).reshape(block_rows, half_width)
    train_rows = train_grads.reshape(train_grads.shape[0], half_width)
    reach = min(WINDOW_HALF, (lax.axis_size("ex") - 1) // 2)

    def block_scores(block):
        return lax.dot_general(
            train_rows, block, (((1,), (1,)), ((), ())), preferred_element_type=jnp.float32
        )

    blocks = {offset: precon if offset == 0 else shifted(precon, "ex", -offset) for offset in range(-reach, reach + 1)}
    done = {0: reduced(block_scores(blocks[0]))}
    far = [offset for offset in range(-reach, reach + 1) if offset != 0]
    both = reduced(jnp.concatenate([block_scores(blocks[offset]) for offset in far], axis=1))
    for place, offset in enumerate(far):
        done[offset] = both[:, place * block_rows : (place + 1) * block_rows]
    return jnp.stack([done[offset] for offset in range(-reach, reach + 1)], axis=1)


def solution(mesh):
    placed = (P("ex", "mod", "sub"), P(("groups", "ex"), "mod", "sub"), P(), P(), P("mod"))
    return jax.shard_map(
        local,
        mesh=mesh,
        in_specs=placed,
        out_specs=P(("groups", "ex", "mod", "sub"), None, None),
        check_vma=False,
    )
```

```python
import jax
import jax.numpy as jnp
from jax import lax
from jax.sharding import PartitionSpec as P

WINDOW_HALF = 2


precise = lax.Precision.HIGHEST


def shifted(value, axis, steps):
    count = lax.axis_size(axis)
    pairs = [(source, (source + steps) % count) for source in range(count)]
    return lax.ppermute(value, axis, pairs)


def to_peer(value, mod_step, sub_step):
    mods, subs = lax.axis_size("mod"), lax.axis_size("sub")
    pairs = []
    for mod in range(mods):
        for sub in range(subs):
            target = ((mod + mod_step) % mods) * subs + (sub + sub_step) % subs
            pairs.append((mod * subs + sub, target))
    return lax.ppermute(value, ("mod", "sub"), pairs)


def rows_of(value, first, count):
    return lax.dynamic_slice_in_dim(value, first, count, 0)


def local(query_grads, train_grads, in_inverse, out_inverse, module_map):
    block_rows, mod_count, half_width = query_grads.shape
    rank_in = in_inverse.shape[1]
    own_rows = half_width // rank_in
    mods, subs = lax.axis_size("mod"), lax.axis_size("sub")
    mod, sub = lax.axis_index("mod"), lax.axis_index("sub")
    parts, part = lax.axis_size("groups"), lax.axis_index("groups")
    reach = min(WINDOW_HALF, (lax.axis_size("ex") - 1) // 2)

    in_used = lax.dynamic_index_in_dim(in_inverse, module_map[0], 0, keepdims=False)
    out_used = lax.dynamic_index_in_dim(out_inverse, module_map[0], 0, keepdims=False)
    out_part = rows_of(out_used, sub * own_rows, own_rows)

    own = query_grads.reshape(block_rows, own_rows, rank_in)
    left = jnp.zeros((own_rows, rank_in, block_rows), jnp.float32)
    for step in range(subs):
        piece = own if step == 0 else shifted(own, "sub", step)
        source = (sub - step) % subs
        columns = lax.dynamic_slice_in_dim(out_part, source * own_rows, own_rows, 1)
        left = left + jnp.einsum("po,qoi->piq", columns, piece.astype(jnp.float32), precision=precise)
    precon = jnp.einsum("piq,ij->pjq", left, in_used, precision=precise)
    precon = precon.astype(jnp.bfloat16).reshape(half_width, block_rows)

    share = 12 * half_width // (32 * parts) * 2 // 128 * 128 if parts > 1 else 0
    shared = share * parts
    train = train_grads.reshape(train_grads.shape[0], half_width)
    dest_rows = train.shape[0] // (mods * subs)

    def scores(block):
        total = None
        for first, rows in block:
            term = lax.dot_general(
                train[:, first : first + rows.shape[0]],
                rows,
                (((1,), (0,)), ((), ())),
                preferred_element_type=jnp.float32,
            )
            total = term if total is None else total + term
        return total

    def reduced(partial):
        kept = None
        for mod_step in range(mods):
            for sub_step in range(subs):
                target = ((mod + mod_step) % mods) * subs + (sub + sub_step) % subs
                rows = rows_of(partial, target * dest_rows, dest_rows)
                if mod_step or sub_step:
                    rows = to_peer(rows, mod_step, sub_step)
                kept = rows if kept is None else kept + rows
        return kept

    offsets = [sign * far for far in range(1, reach + 1) for sign in (-1, 1)]
    mine = rows_of(precon, part * share, share)
    rest = precon[shared:]
    carried = {offset: shifted(mine, "ex", -offset) for offset in offsets}
    common = {offset: shifted(rest, "ex", -offset) for offset in offsets}
    done = {0: reduced(scores([(0, precon)]))}
    for offset in offsets:
        by_group = [carried[offset]]
        for step in range(1, parts):
            by_group.append(shifted(carried[offset], "groups", step))
        block = []
        for place in range(parts):
            rows = by_group[0]
            for step in range(1, parts):
                rows = jnp.where((part - step) % parts == place, by_group[step], rows)
            block.append((place * share, rows))
        block.append((shared, common[offset]))
        done[offset] = reduced(scores(block))
    return jnp.stack([done[offset] for offset in range(-reach, reach + 1)], axis=1)


def solution(mesh):
    placed = (P("ex", "mod", "sub"), P(("groups", "ex"), "mod", "sub"), P(), P(), P("mod"))
    return jax.shard_map(
        local,
        mesh=mesh,
        in_specs=placed,
        out_specs=P(("groups", "ex", "mod", "sub"), None, None),
        check_vma=False,
    )
```

```python
import functools

import jax
import jax.numpy as jnp
from jax import lax
from jax.experimental import pallas as pl
from jax.experimental.pallas import tpu as pltpu
from jax.sharding import PartitionSpec as P

WINDOW_HALF = 2
VMEM_LIMIT = 32 * 1024 * 1024

f32, bf16 = jnp.float32, jnp.bfloat16
in_vmem = pl.BlockSpec(memory_space=pltpu.VMEM)


def keep_near(value):
    return pltpu.with_memory_space_constraint(value, pltpu.VMEM)


def params():
    return pltpu.CompilerParams(vmem_limit_bytes=VMEM_LIMIT)


def shifted(value, axis, steps):
    count = lax.axis_size(axis)
    pairs = [(source, (source + steps) % count) for source in range(count)]
    return lax.ppermute(value, axis, pairs)


def to_peer(value, mod_step, sub_step):
    mods, subs = lax.axis_size("mod"), lax.axis_size("sub")
    pairs = []
    for mod in range(mods):
        for sub in range(subs):
            target = ((mod + mod_step) % mods) * subs + (sub + sub_step) % subs
            pairs.append((mod * subs + sub, target))
    return lax.ppermute(value, ("mod", "sub"), pairs)


def split(value):
    high = value.astype(bf16)
    return high, (value - high.astype(f32)).astype(bf16)


def nt_dot(lhs, rhs):
    return lax.dot_general(lhs, rhs, (((1,), (1,)), ((), ())), preferred_element_type=f32)


def right_rows(pair, raw, right_ref):
    width = pair.shape[0]
    for first in range(0, raw.shape[1], width):
        piece = raw[:, first : first + width]
        right_ref[first : first + width, :] = nt_dot(pair, jnp.concatenate([piece, piece], axis=1))


def first_kernel(place, in_ref, out_ref, raw_ref, right_ref, pair_ref, left_ref):
    turned = in_ref[0].T
    high, low = split(turned)
    high, low = high.astype(f32), low.astype(f32)
    zero = jnp.zeros_like(high)
    pair = jnp.concatenate(
        [
            jnp.concatenate([high, zero, low, zero], axis=1),
            jnp.concatenate([zero, high, zero, low], axis=1),
        ],
        axis=0,
    ).astype(bf16)
    pair_ref[...] = pair
    own_rows = left_ref.shape[0]
    sub = place[1]
    rows = out_ref[0, pl.ds(pl.multiple_of(sub * own_rows, own_rows), own_rows), :]
    swapped = jnp.concatenate([rows[:, own_rows:], rows[:, :own_rows]], axis=1)
    rows = jnp.where(sub == 0, rows, swapped)
    high, low = split(rows)
    high, low = high.astype(f32), low.astype(f32)
    left_ref[...] = jnp.concatenate([high, high, low], axis=1).astype(bf16)
    right_rows(pair, raw_ref, right_ref)


def second_kernel(pair_ref, left_ref, own_ref, raw_ref, result_ref, right_ref, done_ref):
    own_rows = left_ref.shape[0]
    rank_in = result_ref.shape[0] // own_rows
    right_rows(pair_ref[...], raw_ref, right_ref)
    left = left_ref[...]
    for first in range(0, rank_in, 2):
        wide = jnp.concatenate(
            [
                jnp.concatenate(
                    [
                        own_ref[pl.ds(column, own_rows, stride=rank_in), :],
                        right_ref[pl.ds(column, own_rows, stride=rank_in), :],
                    ],
                    axis=0,
                )
                for column in (first, first + 1)
            ],
            axis=1,
        )
        high, low = split(wide)
        both = jnp.dot(left, jnp.concatenate([high, low, high], axis=0), preferred_element_type=f32)
        queries = both.shape[1] // 2
        done_ref[pl.ds(first, own_rows, stride=rank_in), :] = both[:, :queries]
        done_ref[pl.ds(first + 1, own_rows, stride=rank_in), :] = both[:, queries:]
    result_ref[...] = done_ref[...].astype(bf16)


def preconditioned(query_grads, in_inverse, out_inverse, place):
    block_rows, _, half_width = query_grads.shape
    rank_in, rank_out = in_inverse.shape[1], out_inverse.shape[1]
    own_rows = half_width // rank_in
    raw = query_grads.reshape(block_rows, half_width)
    other = shifted(raw, "sub", 1)
    factor = pl.BlockSpec((1, rank_in, rank_in), lambda step, place: (place[0], 0, 0))
    other_factor = pl.BlockSpec((1, rank_out, rank_out), lambda step, place: (place[0], 0, 0))
    right, pair, left = pl.pallas_call(
        first_kernel,
        out_shape=(
            pltpu.VMEM((half_width, block_rows), f32),
            pltpu.VMEM((2 * rank_in, 4 * rank_in), bf16),
            pltpu.VMEM((own_rows, 3 * rank_out), bf16),
        ),
        grid_spec=pltpu.PrefetchScalarGridSpec(
            num_scalar_prefetch=1,
            grid=(1,),
            in_specs=[factor, other_factor, in_vmem],
            out_specs=[in_vmem, in_vmem, in_vmem],
        ),
        compiler_params=params(),
        cost_estimate=pl.CostEstimate(flops=10**9, bytes_accessed=2**21, transcendentals=0),
    )(place, in_inverse, out_inverse, raw)
    return pl.pallas_call(
        second_kernel,
        out_shape=pltpu.VMEM((half_width, block_rows), bf16),
        in_specs=[in_vmem] * 4,
        out_specs=in_vmem,
        scratch_shapes=[pltpu.VMEM((half_width, block_rows), f32)] * 2,
        compiler_params=params(),
        cost_estimate=pl.CostEstimate(flops=10**9, bytes_accessed=2**21, transcendentals=0),
    )(keep_near(pair), keep_near(left), keep_near(right), keep_near(other))


def score_kernel(counts, dests, subs, place, train_ref, *refs):
    outputs = refs[sum(counts) : -1]
    total_ref = refs[-1]
    mods = dests // subs
    sub, mod, part = place[1], place[2], place[3]
    rows = train_ref.shape[0] // dests
    at = 0
    for index, count in enumerate(counts):
        total = None
        for piece in range(count):
            ref = refs[at + piece]
            if count == 1:
                train = train_ref[...]
            elif piece == count - 1:
                train = train_ref[:, train_ref.shape[1] - ref.shape[0] :]
            else:
                share = ref.shape[0]
                source = lax.rem(part - piece + count - 1, count - 1)
                train = train_ref[:, pl.ds(pl.multiple_of(source * share, 128), share)]
            term = jnp.dot(train, ref[...], preferred_element_type=f32)
            total = term if total is None else total + term
        at += count
        total_ref[...] = total
        for dest, output in enumerate(outputs):
            mod_step, sub_step = divmod(dest, subs)
            target = lax.rem(mod + mod_step, mods) * subs + lax.rem(sub + sub_step, subs)
            output[index] = total_ref[pl.ds(pl.multiple_of(target * rows, rows), rows), :]


def scored(place, train, blocks):
    mods, subs = lax.axis_size("mod"), lax.axis_size("sub")
    dests = mods * subs
    queries = blocks[0][0].shape[1]
    counts = tuple(len(block) for block in blocks)
    shape = (len(blocks), train.shape[0] // dests, queries)
    return pl.pallas_call(
        functools.partial(score_kernel, counts, dests, subs),
        out_shape=[pltpu.VMEM(shape, f32)] * dests,
        grid_spec=pltpu.PrefetchScalarGridSpec(
            num_scalar_prefetch=1,
            grid=(1,),
            in_specs=[in_vmem] * (1 + sum(counts)),
            out_specs=[in_vmem] * dests,
            scratch_shapes=[pltpu.VMEM((train.shape[0], queries), f32)],
        ),
        compiler_params=params(),
        cost_estimate=pl.CostEstimate(
            flops=2 * train.size * queries * len(blocks), bytes_accessed=2**22, transcendentals=0
        ),
    )(place, keep_near(train), *[keep_near(part) for block in blocks for part in block])


def sum_kernel(groups, *refs):
    output = refs[-1]
    each = (len(refs) - 1) // len(groups)
    for at, places in enumerate(groups):
        for index, place in enumerate(places):
            total = refs[at * each][index]
            for ref in refs[at * each + 1 : (at + 1) * each]:
                total = total + ref[index]
            output[place] = total


def local(query_grads, train_grads, in_inverse, out_inverse, module_map):
    half_width = query_grads.shape[2]
    mods, subs = lax.axis_size("mod"), lax.axis_size("sub")
    parts, part = lax.axis_size("groups"), lax.axis_index("groups")
    reach = min(WINDOW_HALF, (lax.axis_size("ex") - 1) // 2)
    place = jnp.stack([module_map[0], lax.axis_index("sub"), lax.axis_index("mod"), part]).astype(jnp.int32)
    precon = preconditioned(query_grads, in_inverse, out_inverse, place)

    share = 3 * half_width // (4 * parts) // 128 * 128 if parts > 1 else 0
    shared = share * parts
    train = train_grads.reshape(train_grads.shape[0], half_width)

    offsets = [sign * far for far in range(1, reach + 1) for sign in (1, -1)]
    rest = precon[shared:]
    blocks = {0: [precon]}
    if parts > 1:
        mine = lax.dynamic_slice_in_dim(precon, part * share, share, 0)
        carried = {offset: shifted(mine, "ex", -offset) for offset in offsets}
        common = {offset: shifted(rest, "ex", -offset) for offset in offsets}
        for offset in offsets:
            swapped = [shifted(carried[offset], "groups", step) for step in range(1, parts)]
            blocks[offset] = [carried[offset], *swapped, common[offset]]
    else:
        for offset in offsets:
            blocks[offset] = [shifted(rest, "ex", -offset)]

    groups = [[0, *offsets[:-1]], offsets[-1:]] if offsets else [[0]]
    terms = []
    for members in groups:
        partial = scored(place, train, [blocks[offset] for offset in members])
        for dest, rows in enumerate(partial):
            terms.append(rows if dest == 0 else to_peer(rows, *divmod(dest, subs)))
    rows = train.shape[0] // (mods * subs)
    summed = pl.pallas_call(
        functools.partial(sum_kernel, [[offset + reach for offset in members] for members in groups]),
        out_shape=jax.ShapeDtypeStruct((2 * reach + 1, rows, query_grads.shape[0]), f32),
        in_specs=[in_vmem] * len(terms),
        out_specs=in_vmem,
        compiler_params=params(),
        cost_estimate=pl.CostEstimate(flops=10**6, bytes_accessed=2**20, transcendentals=0),
    )(*[keep_near(term) for term in terms])
    return summed.transpose(1, 0, 2)


def solution(mesh):
    placed = (P("ex", "mod", "sub"), P(("groups", "ex"), "mod", "sub"), P(), P(), P("mod"))
    return jax.shard_map(
        local,
        mesh=mesh,
        in_specs=placed,
        out_specs=P(("groups", "ex", "mod", "sub"), None, None),
        check_vma=False,
    )
```

```python
import functools

import jax
import jax.numpy as jnp
from jax import lax
from jax.experimental import pallas as pl
from jax.experimental.pallas import tpu as pltpu
from jax.sharding import PartitionSpec as P

WINDOW_HALF = 2
VMEM_LIMIT = 32 * 1024 * 1024


f32, bf16 = jnp.float32, jnp.bfloat16
in_vmem = pl.BlockSpec(memory_space=pltpu.VMEM)


def keep_near(value):
    return pltpu.with_memory_space_constraint(value, pltpu.VMEM)


def params():
    return pltpu.CompilerParams(vmem_limit_bytes=VMEM_LIMIT)


def shifted(value, axis, steps):
    count = lax.axis_size(axis)
    pairs = [(source, (source + steps) % count) for source in range(count)]
    return lax.ppermute(value, axis, pairs)


def to_peer(value, mod_step, sub_step):
    mods, subs = lax.axis_size("mod"), lax.axis_size("sub")
    pairs = []
    for mod in range(mods):
        for sub in range(subs):
            target = ((mod + mod_step) % mods) * subs + (sub + sub_step) % subs
            pairs.append((mod * subs + sub, target))
    return lax.ppermute(value, ("mod", "sub"), pairs)


def split(value):
    high = value.astype(bf16)
    return high, (value - high.astype(f32)).astype(bf16)


def nt_dot(lhs, rhs):
    return lax.dot_general(lhs, rhs, (((1,), (1,)), ((), ())), preferred_element_type=f32)


def right_rows(pair, raw, right_ref):
    width = pair.shape[0]
    for first in range(0, raw.shape[1], width):
        piece = raw[:, first : first + width]
        right_ref[first : first + width, :] = nt_dot(pair, jnp.concatenate([piece, piece], axis=1))


def first_kernel(
    map_ref, in_ref, out_ref, raw_ref, right_ref, pair_ref, left_ref, inverse_ref, rows_ref, own_ref, sems
):
    own_rows = left_ref.shape[0]
    sub = lax.axis_index("sub")
    module = map_ref[0]
    mine = out_ref.at[module, pl.ds(pl.multiple_of(sub * own_rows, own_rows), own_rows), :]
    copies = [
        pltpu.make_async_copy(in_ref.at[module], inverse_ref, sems.at[0]),
        pltpu.make_async_copy(mine, rows_ref, sems.at[1]),
        pltpu.make_async_copy(raw_ref, own_ref, sems.at[2]),
    ]
    for copy in copies:
        copy.start()
    copies[0].wait()
    high, low = split(inverse_ref[...].T)
    high, low = high.astype(f32), low.astype(f32)
    zero = jnp.zeros_like(high)
    pair = jnp.concatenate(
        [
            jnp.concatenate([high, zero, low, zero], axis=1),
            jnp.concatenate([zero, high, zero, low], axis=1),
        ],
        axis=0,
    ).astype(bf16)
    pair_ref[...] = pair
    copies[1].wait()
    rows = rows_ref[...]
    swapped = jnp.concatenate([rows[:, own_rows:], rows[:, :own_rows]], axis=1)
    rows = jnp.where(sub == 0, rows, swapped)
    high, low = split(rows)
    high, low = high.astype(f32), low.astype(f32)
    left_ref[...] = jnp.concatenate([high, high, low], axis=1).astype(bf16)
    copies[2].wait()
    right_rows(pair, own_ref, right_ref)


def second_kernel(pair_ref, left_ref, own_ref, raw_ref, result_ref, right_ref, done_ref):
    own_rows = left_ref.shape[0]
    rank_in = result_ref.shape[0] // own_rows
    right_rows(pair_ref[...], raw_ref, right_ref)
    left = left_ref[...]
    for first in range(0, rank_in, 2):
        wide = jnp.concatenate(
            [
                jnp.concatenate(
                    [
                        own_ref[pl.ds(column, own_rows, stride=rank_in), :],
                        right_ref[pl.ds(column, own_rows, stride=rank_in), :],
                    ],
                    axis=0,
                )
                for column in (first, first + 1)
            ],
            axis=1,
        )
        high, low = split(wide)
        both = jnp.dot(left, jnp.concatenate([high, low, high], axis=0), preferred_element_type=f32)
        queries = both.shape[1] // 2
        done_ref[pl.ds(first, own_rows, stride=rank_in), :] = both[:, :queries]
        done_ref[pl.ds(first + 1, own_rows, stride=rank_in), :] = both[:, queries:]
    result_ref[...] = done_ref[...].astype(bf16)


def preconditioned(query_grads, in_inverse, out_inverse, module_map):
    block_rows, _, half_width = query_grads.shape
    rank_in, rank_out = in_inverse.shape[1], out_inverse.shape[1]
    own_rows = half_width // rank_in
    raw = query_grads.reshape(block_rows, half_width)
    other = shifted(raw, "sub", 1)
    anywhere = pl.BlockSpec(memory_space=pl.ANY)
    right, pair, left = pl.pallas_call(
        first_kernel,
        out_shape=(
            pltpu.VMEM((half_width, block_rows), f32),
            pltpu.VMEM((2 * rank_in, 4 * rank_in), bf16),
            pltpu.VMEM((own_rows, 3 * rank_out), bf16),
        ),
        in_specs=[pl.BlockSpec(memory_space=pltpu.SMEM), anywhere, anywhere, anywhere],
        out_specs=[in_vmem, in_vmem, in_vmem],
        scratch_shapes=[
            pltpu.VMEM((rank_in, rank_in), f32),
            pltpu.VMEM((own_rows, rank_out), f32),
            pltpu.VMEM((block_rows, half_width), bf16),
            pltpu.SemaphoreType.DMA((3,)),
        ],
        compiler_params=params(),
        cost_estimate=cost(2),
    )(module_map, *[pltpu.with_memory_space_constraint(x, pltpu.HBM) for x in (in_inverse, out_inverse, raw)])
    return pl.pallas_call(
        second_kernel,
        out_shape=pltpu.VMEM((half_width, block_rows), bf16),
        in_specs=[in_vmem] * 4,
        out_specs=in_vmem,
        scratch_shapes=[pltpu.VMEM((half_width, block_rows), f32)] * 2,
        compiler_params=params(),
        cost_estimate=cost(2),
    )(keep_near(pair), keep_near(left), keep_near(right), keep_near(other))


def part_dot(train_ref, ref, first):
    train = train_ref[:, pl.ds(first, ref.shape[0])]
    return jnp.dot(train, ref[...], preferred_element_type=f32)


def early_kernel(shared, train_ref, mine_ref, rest_ref, total_ref):
    share = mine_ref.shape[0]
    first = pl.multiple_of(lax.axis_index("groups") * share, 128)
    total_ref[...] = part_dot(train_ref, mine_ref, first) + part_dot(train_ref, rest_ref, shared)


def late_kernel(train_ref, *refs):
    total_ref, *swapped, output = refs
    total = total_ref[...]
    parts = len(swapped) + 1
    for step, ref in enumerate(swapped, 1):
        share = ref.shape[0]
        source = lax.rem(lax.axis_index("groups") + parts - step, parts)
        total = total + part_dot(train_ref, ref, pl.multiple_of(source * share, 128))
    output[...] = total


def whole_kernel(train_ref, block_ref, output):
    output[...] = part_dot(train_ref, block_ref, 0)


def cost(micros):
    return pl.CostEstimate(flops=int(micros * 1.15e9), bytes_accessed=0, transcendentals=0)


def dealt(kernel, train, *arrays, micros):
    dests = lax.axis_size("mod") * lax.axis_size("sub")
    queries = arrays[0].shape[1]
    partial = pl.pallas_call(
        kernel,
        out_shape=pltpu.VMEM((train.shape[0], queries), f32),
        in_specs=[in_vmem] * (1 + len(arrays)),
        out_specs=in_vmem,
        compiler_params=params(),
        cost_estimate=cost(micros),
    )(keep_near(train), *map(keep_near, arrays))
    return lax.all_to_all(partial.reshape(dests, -1, queries), ("mod", "sub"), 0, 0)


def early(train, shared, mine, rest, micros):
    return pl.pallas_call(
        functools.partial(early_kernel, shared),
        out_shape=pltpu.VMEM((train.shape[0], mine.shape[1]), f32),
        in_specs=[in_vmem] * 3,
        out_specs=in_vmem,
        compiler_params=params(),
        cost_estimate=cost(micros),
    )(*map(keep_near, (train, mine, rest)))


def sum_kernel(*refs):
    output = refs[-1]
    blocks = output.shape[0]
    each = (len(refs) - 1) // blocks
    for block in range(blocks):
        output[block] = jnp.sum(refs[block][...], axis=0)


def local(query_grads, train_grads, in_inverse, out_inverse, module_map):
    half_width = query_grads.shape[2]
    mods, subs = lax.axis_size("mod"), lax.axis_size("sub")
    parts, part = lax.axis_size("groups"), lax.axis_index("groups")
    reach = min(WINDOW_HALF, (lax.axis_size("ex") - 1) // 2)
    precon = preconditioned(query_grads, in_inverse, out_inverse, module_map)

    share = 3 * half_width // (4 * parts) // 128 * 128
    shared = share * parts
    train = train_grads.reshape(train_grads.shape[0], half_width)

    offsets = [sign * far for far in range(1, reach + 1) for sign in (1, -1)]
    mine = lax.dynamic_slice_in_dim(precon, part * share, share, 0)
    rest = precon[shared:]
    carried = {offset: shifted(mine, "ex", -offset) for offset in offsets}
    common = {offset: shifted(rest, "ex", -offset) for offset in offsets}
    partial = {0: dealt(whole_kernel, train, precon, micros=1)}
    for offset in offsets:
        swapped = [shifted(carried[offset], "groups", step) for step in range(1, parts)]
        total = early(train, shared, carried[offset], common[offset], 1)
        partial[offset] = dealt(late_kernel, train, total, *swapped, micros=1)
    terms = [partial[offset] for offset in range(-reach, reach + 1)]
    rows = train.shape[0] // (mods * subs)
    summed = pl.pallas_call(
        sum_kernel,
        out_shape=jax.ShapeDtypeStruct((2 * reach + 1, rows, query_grads.shape[0]), f32),
        in_specs=[in_vmem] * len(terms),
        out_specs=in_vmem,
        compiler_params=params(),
        cost_estimate=cost(1),
    )(*[keep_near(term) for term in terms])
    return summed.transpose(1, 0, 2)


def solution(mesh):
    placed = (P("ex", "mod", "sub"), P(("groups", "ex"), "mod", "sub"), P(), P(), P("mod"))
    return jax.shard_map(
        local,
        mesh=mesh,
        in_specs=placed,
        out_specs=P(("groups", "ex", "mod", "sub"), None, None),
        check_vma=False,
    )
```

```python
import functools

import jax
import jax.numpy as jnp
from jax import lax
from jax.experimental import pallas as pl
from jax.experimental.pallas import tpu as pltpu
from jax.sharding import PartitionSpec as P

WINDOW_HALF = 2
VMEM_LIMIT = 32 * 1024 * 1024

f32, bf16 = jnp.float32, jnp.bfloat16
in_vmem = pl.BlockSpec(memory_space=pltpu.VMEM)


def keep_near(value):
    return pltpu.with_memory_space_constraint(value, pltpu.VMEM)


def params():
    return pltpu.CompilerParams(vmem_limit_bytes=VMEM_LIMIT)


def shifted(value, axis, steps):
    count = lax.axis_size(axis)
    pairs = [(source, (source + steps) % count) for source in range(count)]
    return lax.ppermute(value, axis, pairs)


def to_peer(value, mod_step, sub_step):
    mods, subs = lax.axis_size("mod"), lax.axis_size("sub")
    pairs = []
    for mod in range(mods):
        for sub in range(subs):
            target = ((mod + mod_step) % mods) * subs + (sub + sub_step) % subs
            pairs.append((mod * subs + sub, target))
    return lax.ppermute(value, ("mod", "sub"), pairs)


def split(value):
    high = value.astype(bf16)
    return high, (value - high.astype(f32)).astype(bf16)


def nt_dot(lhs, rhs):
    return lax.dot_general(lhs, rhs, (((1,), (1,)), ((), ())), preferred_element_type=f32)


def right_rows(pair, raw, right_ref):
    width = pair.shape[0]
    for first in range(0, raw.shape[1], width):
        piece = raw[:, first : first + width]
        right_ref[first : first + width, :] = nt_dot(pair, jnp.concatenate([piece, piece], axis=1))


def first_kernel(
    map_ref, in_ref, out_ref, raw_ref, right_ref, pair_ref, left_ref, inverse_ref, rows_ref, own_ref, sems
):
    own_rows = left_ref.shape[0]
    sub = lax.axis_index("sub")
    module = map_ref[0]
    mine = out_ref.at[module, pl.ds(pl.multiple_of(sub * own_rows, own_rows), own_rows), :]
    copies = [
        pltpu.make_async_copy(in_ref.at[module], inverse_ref, sems.at[0]),
        pltpu.make_async_copy(mine, rows_ref, sems.at[1]),
        pltpu.make_async_copy(raw_ref, own_ref, sems.at[2]),
    ]
    for copy in copies:
        copy.start()
    copies[0].wait()
    high, low = split(inverse_ref[...].T)
    high, low = high.astype(f32), low.astype(f32)
    zero = jnp.zeros_like(high)
    pair = jnp.concatenate(
        [
            jnp.concatenate([high, zero, low, zero], axis=1),
            jnp.concatenate([zero, high, zero, low], axis=1),
        ],
        axis=0,
    ).astype(bf16)
    pair_ref[...] = pair
    copies[1].wait()
    rows = rows_ref[...]
    swapped = jnp.concatenate([rows[:, own_rows:], rows[:, :own_rows]], axis=1)
    rows = jnp.where(sub == 0, rows, swapped)
    high, low = split(rows)
    high, low = high.astype(f32), low.astype(f32)
    left_ref[...] = jnp.concatenate([high, high, low], axis=1).astype(bf16)
    copies[2].wait()
    right_rows(pair, own_ref, right_ref)


def second_kernel(pair_ref, left_ref, own_ref, raw_ref, result_ref, right_ref, done_ref):
    own_rows = left_ref.shape[0]
    rank_in = result_ref.shape[0] // own_rows
    right_rows(pair_ref[...], raw_ref, right_ref)
    left = left_ref[...]
    for first in range(0, rank_in, 2):
        wide = jnp.concatenate(
            [
                jnp.concatenate(
                    [
                        own_ref[pl.ds(column, own_rows, stride=rank_in), :],
                        right_ref[pl.ds(column, own_rows, stride=rank_in), :],
                    ],
                    axis=0,
                )
                for column in (first, first + 1)
            ],
            axis=1,
        )
        high, low = split(wide)
        both = jnp.dot(left, jnp.concatenate([high, low, high], axis=0), preferred_element_type=f32)
        queries = both.shape[1] // 2
        done_ref[pl.ds(first, own_rows, stride=rank_in), :] = both[:, :queries]
        done_ref[pl.ds(first + 1, own_rows, stride=rank_in), :] = both[:, queries:]
    result_ref[...] = done_ref[...].astype(bf16)


def preconditioned(query_grads, in_inverse, out_inverse, module_map):
    block_rows, _, half_width = query_grads.shape
    rank_in, rank_out = in_inverse.shape[1], out_inverse.shape[1]
    own_rows = half_width // rank_in
    raw = query_grads.reshape(block_rows, half_width)
    other = shifted(raw, "sub", 1)
    anywhere = pl.BlockSpec(memory_space=pl.ANY)
    right, pair, left = pl.pallas_call(
        first_kernel,
        out_shape=(
            pltpu.VMEM((half_width, block_rows), f32),
            pltpu.VMEM((2 * rank_in, 4 * rank_in), bf16),
            pltpu.VMEM((own_rows, 3 * rank_out), bf16),
        ),
        in_specs=[pl.BlockSpec(memory_space=pltpu.SMEM), anywhere, anywhere, anywhere],
        out_specs=[in_vmem, in_vmem, in_vmem],
        scratch_shapes=[
            pltpu.VMEM((rank_in, rank_in), f32),
            pltpu.VMEM((own_rows, rank_out), f32),
            pltpu.VMEM((block_rows, half_width), bf16),
            pltpu.SemaphoreType.DMA((3,)),
        ],
        compiler_params=params(),
        cost_estimate=cost(2),
    )(module_map, *[pltpu.with_memory_space_constraint(x, pltpu.HBM) for x in (in_inverse, out_inverse, raw)])
    return pl.pallas_call(
        second_kernel,
        out_shape=pltpu.VMEM((half_width, block_rows), bf16),
        in_specs=[in_vmem] * 4,
        out_specs=in_vmem,
        scratch_shapes=[pltpu.VMEM((half_width, block_rows), f32)] * 2,
        compiler_params=params(),
        cost_estimate=cost(2),
    )(keep_near(pair), keep_near(left), keep_near(right), keep_near(other))


def part_dot(train_ref, ref, first):
    train = train_ref[:, pl.ds(first, ref.shape[0])]
    return jnp.dot(train, ref[...], preferred_element_type=f32)


def early_kernel(shared, train_ref, mine_ref, rest_ref, total_ref):
    share = mine_ref.shape[0]
    first = pl.multiple_of(lax.axis_index("groups") * share, 128)
    total_ref[...] = part_dot(train_ref, mine_ref, first) + part_dot(train_ref, rest_ref, shared)


def late_kernel(dests, subs, train_ref, *refs):
    outputs, sum_ref = refs[-1 - dests : -1], refs[-1]
    total_ref, swapped = refs[0], refs[1 : -1 - dests]
    total = total_ref[...]
    parts = len(swapped) + 1
    for step, ref in enumerate(swapped, 1):
        share = ref.shape[0]
        source = lax.rem(lax.axis_index("groups") + parts - step, parts)
        total = total + part_dot(train_ref, ref, pl.multiple_of(source * share, 128))
    deal(total, subs, sum_ref, outputs)


def whole_kernel(train_ref, block_ref, output):
    output[...] = part_dot(train_ref, block_ref, 0)


def deal(total, subs, sum_ref, outputs):
    sum_ref[...] = total
    mods = len(outputs) // subs
    rows = total.shape[0] // len(outputs)
    for dest, output in enumerate(outputs):
        mod_step, sub_step = divmod(dest, subs)
        target = lax.rem(lax.axis_index("mod") + mod_step, mods) * subs
        target = target + lax.rem(lax.axis_index("sub") + sub_step, subs)
        output[...] = sum_ref[pl.ds(pl.multiple_of(target * rows, rows), rows), :]


def cost(micros):
    return pl.CostEstimate(flops=int(micros * 1.15e9), bytes_accessed=0, transcendentals=0)


def whole(train, block, micros):
    dests = lax.axis_size("mod") * lax.axis_size("sub")
    queries = block.shape[1]
    partial = pl.pallas_call(
        whole_kernel,
        out_shape=pltpu.VMEM((train.shape[0], queries), f32),
        in_specs=[in_vmem] * 2,
        out_specs=in_vmem,
        compiler_params=params(),
        cost_estimate=cost(micros),
    )(keep_near(train), keep_near(block))
    partial = lax.all_to_all(partial.reshape(dests, -1, queries), ("mod", "sub"), 0, 0)
    return [partial]


def late(train, *arrays, micros):
    subs = lax.axis_size("sub")
    dests = lax.axis_size("mod") * subs
    queries = arrays[0].shape[1]
    dealt = pl.pallas_call(
        functools.partial(late_kernel, dests, subs),
        out_shape=[pltpu.VMEM((train.shape[0] // dests, queries), f32)] * dests,
        in_specs=[in_vmem] * (1 + len(arrays)),
        out_specs=[in_vmem] * dests,
        scratch_shapes=[pltpu.VMEM((train.shape[0], queries), f32)],
        compiler_params=params(),
        cost_estimate=cost(micros),
    )(keep_near(train), *map(keep_near, arrays))
    return [rows if dest == 0 else to_peer(rows, *divmod(dest, subs)) for dest, rows in enumerate(dealt)]


def early(train, shared, mine, rest, micros):
    return pl.pallas_call(
        functools.partial(early_kernel, shared),
        out_shape=pltpu.VMEM((train.shape[0], mine.shape[1]), f32),
        in_specs=[in_vmem] * 3,
        out_specs=in_vmem,
        compiler_params=params(),
        cost_estimate=cost(micros),
    )(*map(keep_near, (train, mine, rest)))


def sum_kernel(counts, *refs):
    output = refs[-1]
    at = 0
    for block, count in enumerate(counts):
        total = None
        for ref in refs[at : at + count]:
            pieces = [ref[...]] if len(ref.shape) == 2 else [ref[index] for index in range(ref.shape[0])]
            for piece in pieces:
                total = piece if total is None else total + piece
        output[block] = total
        at += count


def local(query_grads, train_grads, in_inverse, out_inverse, module_map):
    half_width = query_grads.shape[2]
    mods, subs = lax.axis_size("mod"), lax.axis_size("sub")
    parts, part = lax.axis_size("groups"), lax.axis_index("groups")
    reach = min(WINDOW_HALF, (lax.axis_size("ex") - 1) // 2)
    precon = preconditioned(query_grads, in_inverse, out_inverse, module_map)

    share = 3 * half_width // (4 * parts) // 128 * 128
    shared = share * parts
    train = train_grads.reshape(train_grads.shape[0], half_width)

    offsets = [sign * far for far in range(1, reach + 1) for sign in (1, -1)]
    mine = lax.dynamic_slice_in_dim(precon, part * share, share, 0)
    rest = precon[shared:]
    carried = {offset: shifted(mine, "ex", -offset) for offset in offsets}
    common = {offset: shifted(rest, "ex", -offset) for offset in offsets}
    partial = {0: whole(train, precon, 1)}
    for offset in offsets:
        swapped = [shifted(carried[offset], "groups", step) for step in range(1, parts)]
        total = early(train, shared, carried[offset], common[offset], 1)
        partial[offset] = late(train, total, *swapped, micros=1)
    terms = [rows for offset in range(-reach, reach + 1) for rows in partial[offset]]
    rows = train.shape[0] // (mods * subs)
    counts = [len(partial[offset]) for offset in range(-reach, reach + 1)]
    summed = pl.pallas_call(
        functools.partial(sum_kernel, counts),
        out_shape=jax.ShapeDtypeStruct((2 * reach + 1, rows, query_grads.shape[0]), f32),
        in_specs=[in_vmem] * len(terms),
        out_specs=in_vmem,
        compiler_params=params(),
        cost_estimate=cost(1),
    )(*[keep_near(term) for term in terms])
    return summed.transpose(1, 0, 2)


def solution(mesh):
    placed = (P("ex", "mod", "sub"), P(("groups", "ex"), "mod", "sub"), P(), P(), P("mod"))
    return jax.shard_map(
        local,
        mesh=mesh,
        in_specs=placed,
        out_specs=P(("groups", "ex", "mod", "sub"), None, None),
        check_vma=False,
    )
```

```python
import functools

import jax
import jax.numpy as jnp
from jax import lax
from jax.experimental import pallas as pl
from jax.experimental.pallas import tpu as pltpu
from jax.sharding import PartitionSpec as P

WINDOW_HALF = 2
VMEM_LIMIT = 32 * 1024 * 1024

f32, bf16 = jnp.float32, jnp.bfloat16
in_vmem = pl.BlockSpec(memory_space=pltpu.VMEM)


def keep_near(value):
    return pltpu.with_memory_space_constraint(value, pltpu.VMEM)


def params():
    return pltpu.CompilerParams(vmem_limit_bytes=VMEM_LIMIT)


def shifted(value, axis, steps):
    count = lax.axis_size(axis)
    pairs = [(source, (source + steps) % count) for source in range(count)]
    return lax.ppermute(value, axis, pairs)


def to_peer(value, mod_step, sub_step):
    mods, subs = lax.axis_size("mod"), lax.axis_size("sub")
    pairs = []
    for mod in range(mods):
        for sub in range(subs):
            target = ((mod + mod_step) % mods) * subs + (sub + sub_step) % subs
            pairs.append((mod * subs + sub, target))
    return lax.ppermute(value, ("mod", "sub"), pairs)


def split(value):
    high = value.astype(bf16)
    return high, (value - high.astype(f32)).astype(bf16)


def nt_dot(lhs, rhs):
    return lax.dot_general(lhs, rhs, (((1,), (1,)), ((), ())), preferred_element_type=f32)


def right_rows(pair, raw, right_ref):
    width = pair.shape[0]
    for first in range(0, raw.shape[1], width):
        piece = raw[:, first : first + width]
        right_ref[first : first + width, :] = nt_dot(pair, jnp.concatenate([piece, piece], axis=1))


def first_kernel(
    map_ref, in_ref, out_ref, raw_ref, right_ref, pair_ref, left_ref, inverse_ref, rows_ref, own_ref, sems
):
    own_rows = left_ref.shape[0]
    sub = lax.axis_index("sub")
    module = map_ref[0]
    mine = out_ref.at[module, pl.ds(pl.multiple_of(sub * own_rows, own_rows), own_rows), :]
    copies = [
        pltpu.make_async_copy(in_ref.at[module], inverse_ref, sems.at[0]),
        pltpu.make_async_copy(mine, rows_ref, sems.at[1]),
        pltpu.make_async_copy(raw_ref, own_ref, sems.at[2]),
    ]
    for copy in copies:
        copy.start()
    copies[0].wait()
    high, low = split(inverse_ref[...].T)
    high, low = high.astype(f32), low.astype(f32)
    zero = jnp.zeros_like(high)
    pair = jnp.concatenate(
        [
            jnp.concatenate([high, zero, low, zero], axis=1),
            jnp.concatenate([zero, high, zero, low], axis=1),
        ],
        axis=0,
    ).astype(bf16)
    pair_ref[...] = pair
    copies[1].wait()
    rows = rows_ref[...]
    swapped = jnp.concatenate([rows[:, own_rows:], rows[:, :own_rows]], axis=1)
    rows = jnp.where(sub == 0, rows, swapped)
    high, low = split(rows)
    high, low = high.astype(f32), low.astype(f32)
    left_ref[...] = jnp.concatenate([high, high, low], axis=1).astype(bf16)
    copies[2].wait()
    right_rows(pair, own_ref, right_ref)


def second_kernel(pair_ref, left_ref, own_ref, raw_ref, result_ref, right_ref, done_ref):
    own_rows = left_ref.shape[0]
    rank_in = result_ref.shape[0] // own_rows
    right_rows(pair_ref[...], raw_ref, right_ref)
    left = left_ref[...]
    for first in range(0, rank_in, 2):
        wide = jnp.concatenate(
            [
                jnp.concatenate(
                    [
                        own_ref[pl.ds(column, own_rows, stride=rank_in), :],
                        right_ref[pl.ds(column, own_rows, stride=rank_in), :],
                    ],
                    axis=0,
                )
                for column in (first, first + 1)
            ],
            axis=1,
        )
        high, low = split(wide)
        both = jnp.dot(left, jnp.concatenate([high, low, high], axis=0), preferred_element_type=f32)
        queries = both.shape[1] // 2
        done_ref[pl.ds(first, own_rows, stride=rank_in), :] = both[:, :queries]
        done_ref[pl.ds(first + 1, own_rows, stride=rank_in), :] = both[:, queries:]
    result_ref[...] = done_ref[...].astype(bf16)


def preconditioned(query_grads, in_inverse, out_inverse, module_map):
    block_rows, _, half_width = query_grads.shape
    rank_in, rank_out = in_inverse.shape[1], out_inverse.shape[1]
    own_rows = half_width // rank_in
    raw = query_grads.reshape(block_rows, half_width)
    other = shifted(raw, "sub", 1)
    anywhere = pl.BlockSpec(memory_space=pl.ANY)
    right, pair, left = pl.pallas_call(
        first_kernel,
        out_shape=(
            pltpu.VMEM((half_width, block_rows), f32),
            pltpu.VMEM((2 * rank_in, 4 * rank_in), bf16),
            pltpu.VMEM((own_rows, 3 * rank_out), bf16),
        ),
        in_specs=[pl.BlockSpec(memory_space=pltpu.SMEM), anywhere, anywhere, anywhere],
        out_specs=[in_vmem, in_vmem, in_vmem],
        scratch_shapes=[
            pltpu.VMEM((rank_in, rank_in), f32),
            pltpu.VMEM((own_rows, rank_out), f32),
            pltpu.VMEM((block_rows, half_width), bf16),
            pltpu.SemaphoreType.DMA((3,)),
        ],
        compiler_params=params(),
        cost_estimate=cost(2),
    )(module_map, *[pltpu.with_memory_space_constraint(x, pltpu.HBM) for x in (in_inverse, out_inverse, raw)])
    return pl.pallas_call(
        second_kernel,
        out_shape=pltpu.VMEM((half_width, block_rows), bf16),
        in_specs=[in_vmem] * 4,
        out_specs=in_vmem,
        scratch_shapes=[pltpu.VMEM((half_width, block_rows), f32)] * 2,
        compiler_params=params(),
        cost_estimate=cost(2),
    )(keep_near(pair), keep_near(left), keep_near(right), keep_near(other))


def part_dot(train_ref, ref, first):
    train = train_ref[:, pl.ds(first, ref.shape[0])]
    return jnp.dot(train, ref[...], preferred_element_type=f32)


def early_kernel(shared, train_ref, mine_ref, rest_ref, *refs):
    total_ref = refs[-1]
    share = mine_ref.shape[0]
    first = pl.multiple_of(lax.axis_index("groups") * share, 128)
    total_ref[...] = part_dot(train_ref, mine_ref, first) + part_dot(train_ref, rest_ref, shared)


def late_kernel(dests, subs, parts, train_ref, total_ref, *refs):
    outputs, sum_ref = refs[-1 - dests : -1], refs[-1]
    swapped = refs[: parts - 1]
    total = total_ref[...]
    for step, ref in enumerate(swapped, 1):
        share = ref.shape[0]
        source = lax.rem(lax.axis_index("groups") + parts - step, parts)
        total = total + part_dot(train_ref, ref, pl.multiple_of(source * share, 128))
    deal(total, subs, sum_ref, outputs)


def whole_kernel(train_ref, block_ref, output):
    output[...] = part_dot(train_ref, block_ref, 0)


def deal(total, subs, sum_ref, outputs):
    sum_ref[...] = total
    mods = len(outputs) // subs
    rows = total.shape[0] // len(outputs)
    for dest, output in enumerate(outputs):
        mod_step, sub_step = divmod(dest, subs)
        target = lax.rem(lax.axis_index("mod") + mod_step, mods) * subs
        target = target + lax.rem(lax.axis_index("sub") + sub_step, subs)
        output[...] = sum_ref[pl.ds(pl.multiple_of(target * rows, rows), rows), :]


def cost(micros):
    return pl.CostEstimate(flops=int(micros * 1.15e9), bytes_accessed=0, transcendentals=0)


def whole(train, block, micros):
    dests = lax.axis_size("mod") * lax.axis_size("sub")
    queries = block.shape[1]
    partial = pl.pallas_call(
        whole_kernel,
        out_shape=pltpu.VMEM((train.shape[0], queries), f32),
        in_specs=[in_vmem] * 2,
        out_specs=in_vmem,
        compiler_params=params(),
        cost_estimate=cost(micros),
    )(keep_near(train), keep_near(block))
    partial = lax.all_to_all(partial.reshape(dests, -1, queries), ("mod", "sub"), 0, 0)
    return [partial]


def late(train, *arrays, after, micros):
    subs = lax.axis_size("sub")
    dests = lax.axis_size("mod") * subs
    queries = arrays[0].shape[1]
    dealt = pl.pallas_call(
        functools.partial(late_kernel, dests, subs, lax.axis_size("groups")),
        out_shape=[pltpu.VMEM((train.shape[0] // dests, queries), f32)] * dests,
        in_specs=[in_vmem] * (1 + len(arrays)) + [pl.BlockSpec(memory_space=pl.ANY)] * len(after),
        out_specs=[in_vmem] * dests,
        scratch_shapes=[pltpu.VMEM((train.shape[0], queries), f32)],
        compiler_params=params(),
        cost_estimate=cost(micros),
    )(keep_near(train), *map(keep_near, arrays), *after)
    return [rows if dest == 0 else to_peer(rows, *divmod(dest, subs)) for dest, rows in enumerate(dealt)]


def early(train, shared, mine, rest, after, micros):
    return pl.pallas_call(
        functools.partial(early_kernel, shared),
        out_shape=pltpu.VMEM((train.shape[0], mine.shape[1]), f32),
        in_specs=[in_vmem] * 3 + [pl.BlockSpec(memory_space=pl.ANY)] * len(after),
        out_specs=in_vmem,
        compiler_params=params(),
        cost_estimate=cost(micros),
    )(*map(keep_near, (train, mine, rest)), *after)


def summed(refs):
    total = None
    for ref in refs:
        pieces = [ref[...]] if len(ref.shape) == 2 else [ref[index] for index in range(ref.shape[0])]
        for piece in pieces:
            total = piece if total is None else total + piece
    return total


def sum_kernel(places, counts, aliased, *refs):
    inputs, (output, token, held_ref, sems) = refs[:-4], refs[-4:]
    at = 1 if aliased else 0
    copies = []
    for index, (place, count) in enumerate(zip(places, counts)):
        held_ref[index] = summed(inputs[at : at + count])
        copies.append(pltpu.make_async_copy(held_ref.at[index], output.at[place], sems.at[index]))
        copies[-1].start()
        at += count
    token[...] = jnp.zeros_like(token)
    for copy in copies:
        copy.wait()


def settled(places, blocks, earlier, count):
    terms = [term for block in blocks for term in block]
    rows, queries = terms[0].shape[-2:]
    head = [] if earlier is None else [earlier]
    return pl.pallas_call(
        functools.partial(sum_kernel, places, [len(block) for block in blocks], bool(head)),
        out_shape=(
            jax.ShapeDtypeStruct((count, rows, queries), f32),
            pltpu.VMEM((8, 128), f32),
        ),
        in_specs=[pl.BlockSpec(memory_space=pl.ANY)] * len(head) + [in_vmem] * len(terms),
        out_specs=(pl.BlockSpec(memory_space=pl.ANY), in_vmem),
        scratch_shapes=[
            pltpu.VMEM((len(blocks), rows, queries), f32),
            pltpu.SemaphoreType.DMA((len(blocks),)),
        ],
        input_output_aliases={0: 0} if head else {},
        compiler_params=params(),
        cost_estimate=cost(1),
    )(*head, *map(keep_near, terms))


def local(query_grads, train_grads, in_inverse, out_inverse, module_map):
    half_width = query_grads.shape[2]
    mods, subs = lax.axis_size("mod"), lax.axis_size("sub")
    parts, part = lax.axis_size("groups"), lax.axis_index("groups")
    reach = min(WINDOW_HALF, (lax.axis_size("ex") - 1) // 2)
    precon = preconditioned(query_grads, in_inverse, out_inverse, module_map)

    share = 3 * half_width // (4 * parts) // 128 * 128
    shared = share * parts
    train = train_grads.reshape(train_grads.shape[0], half_width)

    offsets = [sign * far for far in range(1, reach + 1) for sign in (1, -1)]
    mine = lax.dynamic_slice_in_dim(precon, part * share, share, 0)
    rest = precon[shared:]
    carried = {offset: shifted(mine, "ex", -offset) for offset in offsets}
    common = {offset: shifted(rest, "ex", -offset) for offset in offsets}
    partial = {0: whole(train, precon, 1)}
    output, after = None, []
    count = 2 * reach + 1
    for offset in offsets:
        swapped = [shifted(carried[offset], "groups", step) for step in range(1, parts)]
        total = early(train, shared, carried[offset], common[offset], after, 1)
        if offset == offsets[-1]:
            places = sorted(partial)
            blocks = [partial[place] for place in places]
            output, token = settled([place + reach for place in places], blocks, None, count)
            after = [token]
        partial[offset] = late(train, total, *swapped, after=after, micros=1)
        after = partial[offset][:1]
    output, _ = settled([offsets[-1] + reach], [partial[offsets[-1]]], output, count)
    return output.transpose(1, 0, 2)


def solution(mesh):
    placed = (P("ex", "mod", "sub"), P(("groups", "ex"), "mod", "sub"), P(), P(), P("mod"))
    return jax.shard_map(
        local,
        mesh=mesh,
        in_specs=placed,
        out_specs=P(("groups", "ex", "mod", "sub"), None, None),
        check_vma=False,
    )
```

```python
import functools

import jax
import jax.numpy as jnp
from jax import lax
from jax.experimental import pallas as pl
from jax.experimental.pallas import tpu as pltpu
from jax.sharding import PartitionSpec as P

WINDOW_HALF = 2
VMEM_LIMIT = 32 * 1024 * 1024

f32, bf16 = jnp.float32, jnp.bfloat16
in_vmem = pl.BlockSpec(memory_space=pltpu.VMEM)
unread = pl.BlockSpec(memory_space=pl.ANY)


def keep_near(value):
    return pltpu.with_memory_space_constraint(value, pltpu.VMEM)


def params():
    return pltpu.CompilerParams(vmem_limit_bytes=VMEM_LIMIT)


def shifted(value, axis, steps):
    count = lax.axis_size(axis)
    pairs = [(source, (source + steps) % count) for source in range(count)]
    return lax.ppermute(value, axis, pairs)


def to_peer(value, mod_step, sub_step):
    mods, subs = lax.axis_size("mod"), lax.axis_size("sub")
    pairs = []
    for mod in range(mods):
        for sub in range(subs):
            target = ((mod + mod_step) % mods) * subs + (sub + sub_step) % subs
            pairs.append((mod * subs + sub, target))
    return lax.ppermute(value, ("mod", "sub"), pairs)


def split(value):
    high = value.astype(bf16)
    return high, (value - high.astype(f32)).astype(bf16)


def nt_dot(lhs, rhs):
    return lax.dot_general(lhs, rhs, (((1,), (1,)), ((), ())), preferred_element_type=f32)


def right_rows(pair, raw, right_ref):
    width = pair.shape[0]
    for first in range(0, raw.shape[1], width):
        piece = raw[:, first : first + width]
        right_ref[first : first + width, :] = nt_dot(pair, jnp.concatenate([piece, piece], axis=1))


def first_kernel(
    map_ref, in_ref, out_ref, raw_ref, right_ref, pair_ref, left_ref, inverse_ref, rows_ref, own_ref, sems
):
    own_rows = left_ref.shape[0]
    sub = lax.axis_index("sub")
    module = map_ref[0]
    mine = out_ref.at[module, pl.ds(pl.multiple_of(sub * own_rows, own_rows), own_rows), :]
    copies = [
        pltpu.make_async_copy(in_ref.at[module], inverse_ref, sems.at[0]),
        pltpu.make_async_copy(mine, rows_ref, sems.at[1]),
        pltpu.make_async_copy(raw_ref, own_ref, sems.at[2]),
    ]
    for copy in copies:
        copy.start()
    copies[0].wait()
    high, low = split(inverse_ref[...].T)
    high, low = high.astype(f32), low.astype(f32)
    zero = jnp.zeros_like(high)
    pair = jnp.concatenate(
        [
            jnp.concatenate([high, zero, low, zero], axis=1),
            jnp.concatenate([zero, high, zero, low], axis=1),
        ],
        axis=0,
    ).astype(bf16)
    pair_ref[...] = pair
    copies[1].wait()
    rows = rows_ref[...]
    swapped = jnp.concatenate([rows[:, own_rows:], rows[:, :own_rows]], axis=1)
    rows = jnp.where(sub == 0, rows, swapped)
    high, low = split(rows)
    high, low = high.astype(f32), low.astype(f32)
    left_ref[...] = jnp.concatenate([high, high, low], axis=1).astype(bf16)
    copies[2].wait()
    right_rows(pair, own_ref, right_ref)


def second_kernel(pair_ref, left_ref, own_ref, raw_ref, result_ref, right_ref, done_ref):
    own_rows = left_ref.shape[0]
    rank_in = done_ref.shape[0] // own_rows
    right_rows(pair_ref[...], raw_ref, right_ref)
    left = left_ref[...]
    for first in range(0, rank_in, 2):
        wide = jnp.concatenate(
            [
                jnp.concatenate(
                    [
                        own_ref[pl.ds(column, own_rows, stride=rank_in), :],
                        right_ref[pl.ds(column, own_rows, stride=rank_in), :],
                    ],
                    axis=0,
                )
                for column in (first, first + 1)
            ],
            axis=1,
        )
        high, low = split(wide)
        both = jnp.dot(left, jnp.concatenate([high, low, high], axis=0), preferred_element_type=f32)
        queries = both.shape[1] // 2
        done_ref[pl.ds(first, own_rows, stride=rank_in), :] = both[:, :queries]
        done_ref[pl.ds(first + 1, own_rows, stride=rank_in), :] = both[:, queries:]
    half = done_ref.shape[0] // 2
    top, bottom = done_ref[:half, :], done_ref[half:, :]
    result_ref[0] = beside(top, swap(bottom)).astype(bf16)
    result_ref[1] = beside(swap(top), bottom).astype(bf16)


def swap(value):
    return pltpu.roll(value, value.shape[1] // 2, 1)


def beside(first, second):
    lane = lax.broadcasted_iota(jnp.int32, first.shape, 1)
    return jnp.where(lane < first.shape[1] // 2, first, second)


def preconditioned(query_grads, in_inverse, out_inverse, module_map):
    block_rows, _, half_width = query_grads.shape
    rank_in, rank_out = in_inverse.shape[1], out_inverse.shape[1]
    own_rows = half_width // rank_in
    raw = query_grads.reshape(block_rows, half_width)
    other = shifted(raw, "sub", 1)
    anywhere = pl.BlockSpec(memory_space=pl.ANY)
    right, pair, left = pl.pallas_call(
        first_kernel,
        out_shape=(
            pltpu.VMEM((half_width, block_rows), f32),
            pltpu.VMEM((2 * rank_in, 4 * rank_in), bf16),
            pltpu.VMEM((own_rows, 3 * rank_out), bf16),
        ),
        in_specs=[pl.BlockSpec(memory_space=pltpu.SMEM), anywhere, anywhere, anywhere],
        out_specs=[in_vmem, in_vmem, in_vmem],
        scratch_shapes=[
            pltpu.VMEM((rank_in, rank_in), f32),
            pltpu.VMEM((own_rows, rank_out), f32),
            pltpu.VMEM((block_rows, half_width), bf16),
            pltpu.SemaphoreType.DMA((3,)),
        ],
        compiler_params=params(),
        cost_estimate=cost(2),
    )(module_map, *[pltpu.with_memory_space_constraint(x, pltpu.HBM) for x in (in_inverse, out_inverse, raw)])
    return pl.pallas_call(
        second_kernel,
        out_shape=pltpu.VMEM((2, half_width // 2, block_rows), bf16),
        in_specs=[in_vmem] * 4,
        out_specs=in_vmem,
        scratch_shapes=[pltpu.VMEM((half_width, block_rows), f32)] * 2,
        compiler_params=params(),
        cost_estimate=cost(2),
    )(keep_near(pair), keep_near(left), keep_near(right), keep_near(other))


def cost(micros):
    return pl.CostEstimate(flops=int(micros * 1.15e9), bytes_accessed=0, transcendentals=0)


def score_kernel(count, train_ref, *refs):
    pieces, output = refs[:count], refs[-1]
    targets, _, lanes = output.shape
    depth = train_ref.shape[1] // 2
    both = jnp.concatenate([piece[...] for piece in pieces], axis=1)
    first = jnp.dot(train_ref[:, :depth], both, preferred_element_type=f32)
    second = jnp.dot(train_ref[:, depth:], both, preferred_element_type=f32)
    half = train_ref.shape[0] // targets // 2
    for index in range(count):
        low = first[:, index * lanes : (index + 1) * lanes]
        high = second[:, index * lanes : (index + 1) * lanes]
        for target in range(targets):
            top = slice(2 * target * half, (2 * target + 1) * half)
            bottom = slice((2 * target + 1) * half, 2 * (target + 1) * half)
            output[target, index * half : (index + 1) * half, :] = beside(
                low[top] + swap(high[top]), swap(low[bottom]) + high[bottom]
            )


def scored(train, pieces, after=()):
    targets = lax.axis_size("mod") * lax.axis_size("sub")
    rows = train.shape[0] // targets // 2 * len(pieces)
    return pl.pallas_call(
        functools.partial(score_kernel, len(pieces)),
        out_shape=pltpu.VMEM((targets, rows, pieces[0].shape[1]), f32),
        in_specs=[in_vmem] * (1 + len(pieces)) + [unread] * len(after),
        out_specs=in_vmem,
        compiler_params=params(),
        cost_estimate=cost(1),
    )(keep_near(train), *map(keep_near, pieces), *after)


def dealt(partial):
    return lax.all_to_all(partial, ("mod", "sub"), 0, 0)


def sent(partial):
    mods, subs = lax.axis_size("mod"), lax.axis_size("sub")
    received = []
    for mod_step in range(mods):
        for sub_step in range(subs):
            target = (lax.axis_index("mod") + mod_step) % mods * subs + (lax.axis_index("sub") + sub_step) % subs
            rows = lax.dynamic_index_in_dim(partial, target, 0, keepdims=False)
            received.append(to_peer(rows, mod_step, sub_step) if mod_step or sub_step else rows)
    return received


def summed(refs):
    total = None
    for ref in refs:
        pieces = [ref[...]] if len(ref.shape) == 2 else [ref[index] for index in range(ref.shape[0])]
        for piece in pieces:
            total = piece if total is None else total + piece
    return total


def unpacked(first, second):
    return jnp.concatenate([beside(first, swap(second)), beside(swap(first), second)], axis=0)


def sum_kernel(count, *refs):
    refs[-1][...] = summed(refs[:count])


def settled(terms, after=()):
    return pl.pallas_call(
        functools.partial(sum_kernel, len(terms)),
        out_shape=pltpu.VMEM(terms[0].shape[-2:], f32),
        in_specs=[in_vmem] * len(terms) + [unread] * len(after),
        out_specs=in_vmem,
        compiler_params=params(),
        cost_estimate=cost(1),
    )(*map(keep_near, terms), *after)


def last_kernel(reach, own_ref, settled_ref, *refs):
    output = refs[-1]
    half = own_ref.shape[0] // 2
    output[reach] = unpacked(own_ref[:half], own_ref[half:])
    late = summed(refs[:-1])
    part = lax.axis_index("groups")
    for far in range(reach):
        mine, first = settled_ref[2 * far * half :][:half], settled_ref[(2 * far + 1) * half :][:half]
        other, second = late[2 * far * half :][:half], late[(2 * far + 1) * half :][:half]
        lower, upper = jnp.where(part == 0, mine, other), jnp.where(part == 0, other, mine)
        output[reach + 1 + far] = unpacked(lower, upper)
        output[reach - 1 - far] = unpacked(first, second)


def finished(reach, own, settled_sums, terms):
    rows, lanes = own.shape
    return pl.pallas_call(
        functools.partial(last_kernel, reach),
        out_shape=jax.ShapeDtypeStruct((2 * reach + 1, rows, lanes), f32),
        in_specs=[in_vmem] * (2 + len(terms)),
        out_specs=in_vmem,
        compiler_params=params(),
        cost_estimate=cost(1),
    )(*map(keep_near, (own, settled_sums, *terms)))


def local(query_grads, train_grads, in_inverse, out_inverse, module_map):
    parts, part = lax.axis_size("groups"), lax.axis_index("groups")
    assert parts == 2
    reach = min(WINDOW_HALF, (lax.axis_size("ex") - 1) // 2)
    precon = preconditioned(query_grads, in_inverse, out_inverse, module_map)
    train = train_grads.reshape(train_grads.shape[0], train_grads.shape[2])

    mine = lax.dynamic_index_in_dim(precon, part, 0, keepdims=False)
    first, second, swaps = [], [], []
    for far in range(1, reach + 1):
        ahead = shifted(mine, "ex", -far)
        first += [ahead, shifted(precon[0], "ex", far)]
        swaps.append(shifted(ahead, "groups", 1))
        second += [swaps[-1], shifted(precon[1], "ex", far)]

    own = settled([dealt(scored(train, [precon[0], precon[1]]))])
    early = settled(sent(scored(train, first)), swaps)
    late = sent(scored(train, second, [early]))
    return finished(reach, own, early, late).transpose(1, 0, 2)


def solution(mesh):
    placed = (P("ex", "mod", "sub"), P(("groups", "ex"), "mod", "sub"), P(), P(), P("mod"))
    return jax.shard_map(
        local,
        mesh=mesh,
        in_specs=placed,
        out_specs=P(("groups", "ex", "mod", "sub"), None, None),
        check_vma=False,
    )
```

```python
import functools

import jax
import jax.numpy as jnp
from jax import lax
from jax.experimental import pallas as pl
from jax.experimental.pallas import tpu as pltpu
from jax.sharding import PartitionSpec as P

WINDOW_HALF = 2
VMEM_LIMIT = 32 * 1024 * 1024

f32, bf16 = jnp.float32, jnp.bfloat16
in_vmem = pl.BlockSpec(memory_space=pltpu.VMEM)


def keep_near(value):
    return pltpu.with_memory_space_constraint(value, pltpu.VMEM)


def params():
    return pltpu.CompilerParams(vmem_limit_bytes=VMEM_LIMIT)


def shifted(value, axis, steps):
    count = lax.axis_size(axis)
    pairs = [(source, (source + steps) % count) for source in range(count)]
    return lax.ppermute(value, axis, pairs)


def to_peer(value, mod_step, sub_step):
    mods, subs = lax.axis_size("mod"), lax.axis_size("sub")
    pairs = []
    for mod in range(mods):
        for sub in range(subs):
            target = ((mod + mod_step) % mods) * subs + (sub + sub_step) % subs
            pairs.append((mod * subs + sub, target))
    return lax.ppermute(value, ("mod", "sub"), pairs)


def split(value):
    high = value.astype(bf16)
    return high, (value - high.astype(f32)).astype(bf16)


def nt_dot(lhs, rhs):
    return lax.dot_general(lhs, rhs, (((1,), (1,)), ((), ())), preferred_element_type=f32)


def right_rows(pair, raw, right_ref):
    width = pair.shape[0]
    for first in range(0, raw.shape[1], width):
        piece = raw[:, first : first + width]
        right_ref[first : first + width, :] = nt_dot(pair, jnp.concatenate([piece, piece], axis=1))


def first_kernel(
    map_ref, in_ref, out_ref, raw_ref, right_ref, pair_ref, left_ref, inverse_ref, rows_ref, own_ref, sems
):
    own_rows = left_ref.shape[0]
    sub = lax.axis_index("sub")
    module = map_ref[0]
    mine = out_ref.at[module, pl.ds(pl.multiple_of(sub * own_rows, own_rows), own_rows), :]
    copies = [
        pltpu.make_async_copy(in_ref.at[module], inverse_ref, sems.at[0]),
        pltpu.make_async_copy(mine, rows_ref, sems.at[1]),
        pltpu.make_async_copy(raw_ref, own_ref, sems.at[2]),
    ]
    for copy in copies:
        copy.start()
    copies[0].wait()
    high, low = split(inverse_ref[...].T)
    high, low = high.astype(f32), low.astype(f32)
    zero = jnp.zeros_like(high)
    pair = jnp.concatenate(
        [
            jnp.concatenate([high, zero, low, zero], axis=1),
            jnp.concatenate([zero, high, zero, low], axis=1),
        ],
        axis=0,
    ).astype(bf16)
    pair_ref[...] = pair
    copies[1].wait()
    rows = rows_ref[...]
    swapped = jnp.concatenate([rows[:, own_rows:], rows[:, :own_rows]], axis=1)
    rows = jnp.where(sub == 0, rows, swapped)
    high, low = split(rows)
    high, low = high.astype(f32), low.astype(f32)
    left_ref[...] = jnp.concatenate([high, high, low], axis=1).astype(bf16)
    copies[2].wait()
    right_rows(pair, own_ref, right_ref)


def second_kernel(pair_ref, left_ref, own_ref, raw_ref, result_ref, right_ref, done_ref):
    own_rows = left_ref.shape[0]
    rank_in = result_ref.shape[0] // own_rows
    right_rows(pair_ref[...], raw_ref, right_ref)
    left = left_ref[...]
    for first in range(0, rank_in, 2):
        wide = jnp.concatenate(
            [
                jnp.concatenate(
                    [
                        own_ref[pl.ds(column, own_rows, stride=rank_in), :],
                        right_ref[pl.ds(column, own_rows, stride=rank_in), :],
                    ],
                    axis=0,
                )
                for column in (first, first + 1)
            ],
            axis=1,
        )
        high, low = split(wide)
        both = jnp.dot(left, jnp.concatenate([high, low, high], axis=0), preferred_element_type=f32)
        queries = both.shape[1] // 2
        done_ref[pl.ds(first, own_rows, stride=rank_in), :] = both[:, :queries]
        done_ref[pl.ds(first + 1, own_rows, stride=rank_in), :] = both[:, queries:]
    result_ref[...] = done_ref[...].astype(bf16)


def preconditioned(query_grads, in_inverse, out_inverse, module_map):
    block_rows, _, half_width = query_grads.shape
    rank_in, rank_out = in_inverse.shape[1], out_inverse.shape[1]
    own_rows = half_width // rank_in
    raw = query_grads.reshape(block_rows, half_width)
    other = shifted(raw, "sub", 1)
    anywhere = pl.BlockSpec(memory_space=pl.ANY)
    right, pair, left = pl.pallas_call(
        first_kernel,
        out_shape=(
            pltpu.VMEM((half_width, block_rows), f32),
            pltpu.VMEM((2 * rank_in, 4 * rank_in), bf16),
            pltpu.VMEM((own_rows, 3 * rank_out), bf16),
        ),
        in_specs=[pl.BlockSpec(memory_space=pltpu.SMEM), anywhere, anywhere, anywhere],
        out_specs=[in_vmem, in_vmem, in_vmem],
        scratch_shapes=[
            pltpu.VMEM((rank_in, rank_in), f32),
            pltpu.VMEM((own_rows, rank_out), f32),
            pltpu.VMEM((block_rows, half_width), bf16),
            pltpu.SemaphoreType.DMA((3,)),
        ],
        compiler_params=params(),
        cost_estimate=cost(2),
    )(module_map, *[pltpu.with_memory_space_constraint(x, pltpu.HBM) for x in (in_inverse, out_inverse, raw)])
    return pl.pallas_call(
        second_kernel,
        out_shape=pltpu.VMEM((half_width, block_rows), bf16),
        in_specs=[in_vmem] * 4,
        out_specs=in_vmem,
        scratch_shapes=[pltpu.VMEM((half_width, block_rows), f32)] * 2,
        compiler_params=params(),
        cost_estimate=cost(2),
    )(keep_near(pair), keep_near(left), keep_near(right), keep_near(other))


def part_dot(train_ref, ref, first):
    train = train_ref[:, pl.ds(first, ref.shape[0])]
    return jnp.dot(train, ref[...], preferred_element_type=f32)


def early_kernel(shared, train_ref, mine_ref, rest_ref, total_ref):
    share = mine_ref.shape[0]
    first = pl.multiple_of(lax.axis_index("groups") * share, 128)
    total_ref[...] = part_dot(train_ref, mine_ref, first) + part_dot(train_ref, rest_ref, shared)


def late_kernel(dests, subs, train_ref, *refs):
    outputs, sum_ref = refs[-1 - dests : -1], refs[-1]
    total_ref, swapped = refs[0], refs[1 : -1 - dests]
    total = total_ref[...]
    parts = len(swapped) + 1
    for step, ref in enumerate(swapped, 1):
        share = ref.shape[0]
        source = lax.rem(lax.axis_index("groups") + parts - step, parts)
        total = total + part_dot(train_ref, ref, pl.multiple_of(source * share, 128))
    deal(total, subs, sum_ref, outputs)


def whole_kernel(train_ref, block_ref, output):
    output[...] = part_dot(train_ref, block_ref, 0)


def deal(total, subs, sum_ref, outputs):
    sum_ref[...] = total
    mods = len(outputs) // subs
    rows = total.shape[0] // len(outputs)
    for dest, output in enumerate(outputs):
        mod_step, sub_step = divmod(dest, subs)
        target = lax.rem(lax.axis_index("mod") + mod_step, mods) * subs
        target = target + lax.rem(lax.axis_index("sub") + sub_step, subs)
        output[...] = sum_ref[pl.ds(pl.multiple_of(target * rows, rows), rows), :].astype(output.dtype)


def cost(micros):
    return pl.CostEstimate(flops=int(micros * 1.15e9), bytes_accessed=0, transcendentals=0)


def whole(train, block, micros):
    dests = lax.axis_size("mod") * lax.axis_size("sub")
    queries = block.shape[1]
    partial = pl.pallas_call(
        whole_kernel,
        out_shape=pltpu.VMEM((train.shape[0], queries), f32),
        in_specs=[in_vmem] * 2,
        out_specs=in_vmem,
        compiler_params=params(),
        cost_estimate=cost(micros),
    )(keep_near(train), keep_near(block))
    partial = lax.all_to_all(partial.reshape(dests, -1, queries), ("mod", "sub"), 0, 0)
    return [partial]


def late(train, *arrays, micros):
    subs = lax.axis_size("sub")
    dests = lax.axis_size("mod") * subs
    queries = arrays[0].shape[1]
    dealt = pl.pallas_call(
        functools.partial(late_kernel, dests, subs),
        out_shape=[pltpu.VMEM((train.shape[0] // dests, queries), bf16 if dest else f32) for dest in range(dests)],
        in_specs=[in_vmem] * (1 + len(arrays)),
        out_specs=[in_vmem] * dests,
        scratch_shapes=[pltpu.VMEM((train.shape[0], queries), f32)],
        compiler_params=params(),
        cost_estimate=cost(micros),
    )(keep_near(train), *map(keep_near, arrays))
    return [rows if dest == 0 else to_peer(rows, *divmod(dest, subs)) for dest, rows in enumerate(dealt)]


def early(train, shared, mine, rest, micros):
    return pl.pallas_call(
        functools.partial(early_kernel, shared),
        out_shape=pltpu.VMEM((train.shape[0], mine.shape[1]), f32),
        in_specs=[in_vmem] * 3,
        out_specs=in_vmem,
        compiler_params=params(),
        cost_estimate=cost(micros),
    )(*map(keep_near, (train, mine, rest)))


def sum_kernel(counts, *refs):
    output = refs[-1]
    at = 0
    for block, count in enumerate(counts):
        total = None
        for ref in refs[at : at + count]:
            pieces = [ref[...]] if len(ref.shape) == 2 else [ref[index] for index in range(ref.shape[0])]
            for piece in pieces:
                piece = piece.astype(f32)
                total = piece if total is None else total + piece
        output[block] = total
        at += count


def local(query_grads, train_grads, in_inverse, out_inverse, module_map):
    half_width = query_grads.shape[2]
    mods, subs = lax.axis_size("mod"), lax.axis_size("sub")
    parts, part = lax.axis_size("groups"), lax.axis_index("groups")
    reach = min(WINDOW_HALF, (lax.axis_size("ex") - 1) // 2)
    precon = preconditioned(query_grads, in_inverse, out_inverse, module_map)

    share = 3 * half_width // (4 * parts) // 128 * 128
    shared = share * parts
    train = train_grads.reshape(train_grads.shape[0], half_width)

    offsets = [sign * far for far in range(1, reach + 1) for sign in (1, -1)]
    mine = lax.dynamic_slice_in_dim(precon, part * share, share, 0)
    rest = precon[shared:]
    carried = {offset: shifted(mine, "ex", -offset) for offset in offsets}
    common = {offset: shifted(rest, "ex", -offset) for offset in offsets}
    partial = {0: whole(train, precon, 1)}
    for offset in offsets:
        swapped = [shifted(carried[offset], "groups", step) for step in range(1, parts)]
        total = early(train, shared, carried[offset], common[offset], 1)
        partial[offset] = late(train, total, *swapped, micros=1)
    terms = [rows for offset in range(-reach, reach + 1) for rows in partial[offset]]
    rows = train.shape[0] // (mods * subs)
    counts = [len(partial[offset]) for offset in range(-reach, reach + 1)]
    summed = pl.pallas_call(
        functools.partial(sum_kernel, counts),
        out_shape=jax.ShapeDtypeStruct((2 * reach + 1, rows, query_grads.shape[0]), f32),
        in_specs=[in_vmem] * len(terms),
        out_specs=in_vmem,
        compiler_params=params(),
        cost_estimate=cost(1),
    )(*[keep_near(term) for term in terms])
    return summed.transpose(1, 0, 2)


def solution(mesh):
    placed = (P("ex", "mod", "sub"), P(("groups", "ex"), "mod", "sub"), P(), P(), P("mod"))
    return jax.shard_map(
        local,
        mesh=mesh,
        in_specs=placed,
        out_specs=P(("groups", "ex", "mod", "sub"), None, None),
        check_vma=False,
    )
```

```python
import functools

import jax
import jax.numpy as jnp
from jax import lax
from jax.experimental import pallas as pl
from jax.experimental.pallas import tpu as pltpu
from jax.sharding import PartitionSpec as P

WINDOW_HALF = 2
VMEM_LIMIT = 32 * 1024 * 1024

f32, bf16 = jnp.float32, jnp.bfloat16
in_vmem = pl.BlockSpec(memory_space=pltpu.VMEM)


def keep_near(value):
    return pltpu.with_memory_space_constraint(value, pltpu.VMEM)


def params():
    return pltpu.CompilerParams(vmem_limit_bytes=VMEM_LIMIT)


def shifted(value, axis, steps):
    count = lax.axis_size(axis)
    pairs = [(source, (source + steps) % count) for source in range(count)]
    return lax.ppermute(value, axis, pairs)


def to_peer(value, mod_step, sub_step):
    mods, subs = lax.axis_size("mod"), lax.axis_size("sub")
    pairs = []
    for mod in range(mods):
        for sub in range(subs):
            target = ((mod + mod_step) % mods) * subs + (sub + sub_step) % subs
            pairs.append((mod * subs + sub, target))
    return lax.ppermute(value, ("mod", "sub"), pairs)


def split(value):
    high = value.astype(bf16)
    return high, (value - high.astype(f32)).astype(bf16)


def nt_dot(lhs, rhs):
    return lax.dot_general(lhs, rhs, (((1,), (1,)), ((), ())), preferred_element_type=f32)


def right_rows(pair, raw, right_ref):
    width = pair.shape[0]
    for first in range(0, raw.shape[1], width):
        piece = raw[:, first : first + width]
        right_ref[first : first + width, :] = nt_dot(pair, jnp.concatenate([piece, piece], axis=1))


def first_kernel(
    map_ref, in_ref, out_ref, raw_ref, right_ref, pair_ref, left_ref, inverse_ref, rows_ref, own_ref, sems
):
    own_rows = left_ref.shape[0]
    sub = lax.axis_index("sub")
    module = map_ref[0]
    mine = out_ref.at[module, pl.ds(pl.multiple_of(sub * own_rows, own_rows), own_rows), :]
    copies = [
        pltpu.make_async_copy(in_ref.at[module], inverse_ref, sems.at[0]),
        pltpu.make_async_copy(mine, rows_ref, sems.at[1]),
        pltpu.make_async_copy(raw_ref, own_ref, sems.at[2]),
    ]
    for copy in copies:
        copy.start()
    copies[0].wait()
    high, low = split(inverse_ref[...].T)
    high, low = high.astype(f32), low.astype(f32)
    zero = jnp.zeros_like(high)
    pair = jnp.concatenate(
        [
            jnp.concatenate([high, zero, low, zero], axis=1),
            jnp.concatenate([zero, high, zero, low], axis=1),
        ],
        axis=0,
    ).astype(bf16)
    pair_ref[...] = pair
    copies[1].wait()
    rows = rows_ref[...]
    swapped = jnp.concatenate([rows[:, own_rows:], rows[:, :own_rows]], axis=1)
    rows = jnp.where(sub == 0, rows, swapped)
    high, low = split(rows)
    high, low = high.astype(f32), low.astype(f32)
    left_ref[...] = jnp.concatenate([high, high, low], axis=1).astype(bf16)
    copies[2].wait()
    right_rows(pair, own_ref, right_ref)


def second_kernel(pair_ref, left_ref, own_ref, raw_ref, result_ref, right_ref, done_ref):
    own_rows = left_ref.shape[0]
    rank_in = result_ref.shape[0] // own_rows
    right_rows(pair_ref[...], raw_ref, right_ref)
    left = left_ref[...]
    for first in range(0, rank_in, 2):
        wide = jnp.concatenate(
            [
                jnp.concatenate(
                    [
                        own_ref[pl.ds(column, own_rows, stride=rank_in), :],
                        right_ref[pl.ds(column, own_rows, stride=rank_in), :],
                    ],
                    axis=0,
                )
                for column in (first, first + 1)
            ],
            axis=1,
        )
        high, low = split(wide)
        both = jnp.dot(left, jnp.concatenate([high, low, high], axis=0), preferred_element_type=f32)
        queries = both.shape[1] // 2
        done_ref[pl.ds(first, own_rows, stride=rank_in), :] = both[:, :queries]
        done_ref[pl.ds(first + 1, own_rows, stride=rank_in), :] = both[:, queries:]
    result_ref[...] = done_ref[...].astype(bf16)


def preconditioned(query_grads, in_inverse, out_inverse, module_map):
    block_rows, _, half_width = query_grads.shape
    rank_in, rank_out = in_inverse.shape[1], out_inverse.shape[1]
    own_rows = half_width // rank_in
    raw = query_grads.reshape(block_rows, half_width)
    other = shifted(raw, "sub", 1)
    anywhere = pl.BlockSpec(memory_space=pl.ANY)
    right, pair, left = pl.pallas_call(
        first_kernel,
        out_shape=(
            pltpu.VMEM((half_width, block_rows), f32),
            pltpu.VMEM((2 * rank_in, 4 * rank_in), bf16),
            pltpu.VMEM((own_rows, 3 * rank_out), bf16),
        ),
        in_specs=[pl.BlockSpec(memory_space=pltpu.SMEM), anywhere, anywhere, anywhere],
        out_specs=[in_vmem, in_vmem, in_vmem],
        scratch_shapes=[
            pltpu.VMEM((rank_in, rank_in), f32),
            pltpu.VMEM((own_rows, rank_out), f32),
            pltpu.VMEM((block_rows, half_width), bf16),
            pltpu.SemaphoreType.DMA((3,)),
        ],
        compiler_params=params(),
        cost_estimate=cost(2),
    )(module_map, *[pltpu.with_memory_space_constraint(x, pltpu.HBM) for x in (in_inverse, out_inverse, raw)])
    return pl.pallas_call(
        second_kernel,
        out_shape=pltpu.VMEM((half_width, block_rows), bf16),
        in_specs=[in_vmem] * 4,
        out_specs=in_vmem,
        scratch_shapes=[pltpu.VMEM((half_width, block_rows), f32)] * 2,
        compiler_params=params(),
        cost_estimate=cost(2),
    )(keep_near(pair), keep_near(left), keep_near(right), keep_near(other))


def part_dot(train_ref, ref, first):
    train = train_ref[:, pl.ds(first, ref.shape[0])]
    return jnp.dot(train, ref[...], preferred_element_type=f32)


def early_kernel(shared, train_ref, mine_ref, rest_ref, total_ref):
    share = mine_ref.shape[0]
    first = pl.multiple_of(lax.axis_index("groups") * share, 128)
    total_ref[...] = part_dot(train_ref, mine_ref, first) + part_dot(train_ref, rest_ref, shared)


def late_kernel(subs, slot, slots, train_ref, *refs):
    own_ref, total_ref, *swapped = refs[: -1 - slots[1]]
    outputs, sum_ref = refs[-1 - slots[1] : -1], refs[-1]
    total = total_ref[...]
    parts = len(swapped) + 1
    for step, ref in enumerate(swapped, 1):
        share = ref.shape[0]
        source = lax.rem(lax.axis_index("groups") + parts - step, parts)
        total = total + part_dot(train_ref, ref, pl.multiple_of(source * share, 128))
    sum_ref[...] = total
    dests = len(outputs)
    mods = dests // subs
    rows = total.shape[0] // dests
    part = rows // slots[0]
    for dest, output in enumerate(outputs):
        mod_step, sub_step = divmod(dest, subs)
        target = lax.rem(lax.axis_index("mod") + mod_step, mods) * subs
        target = target + lax.rem(lax.axis_index("sub") + sub_step, subs)
        first = pl.multiple_of(target * rows, rows)
        output[:rows, :] = sum_ref[pl.ds(first, rows), :].astype(output.dtype)
        output[rows:, :] = own_ref[pl.ds(first + slot * part, part), :].astype(output.dtype)


def whole_kernel(train_ref, block_ref, output):
    output[...] = part_dot(train_ref, block_ref, 0)


def cost(micros):
    return pl.CostEstimate(flops=int(micros * 1.15e9), bytes_accessed=0, transcendentals=0)


def whole(train, block, micros):
    return pl.pallas_call(
        whole_kernel,
        out_shape=pltpu.VMEM((train.shape[0], block.shape[1]), f32),
        in_specs=[in_vmem] * 2,
        out_specs=in_vmem,
        compiler_params=params(),
        cost_estimate=cost(micros),
    )(keep_near(train), keep_near(block))


def late(train, slot, slots, own, total, swapped, micros):
    subs = lax.axis_size("sub")
    dests = lax.axis_size("mod") * subs
    queries = total.shape[1]
    rows = train.shape[0] // dests
    shape = (rows + rows // slots, queries)
    arrays = [own, total, *swapped]
    dealt = pl.pallas_call(
        functools.partial(late_kernel, subs, slot, (slots, dests)),
        out_shape=[pltpu.VMEM(shape, bf16 if dest else f32) for dest in range(dests)],
        in_specs=[in_vmem] * (1 + len(arrays)),
        out_specs=[in_vmem] * dests,
        scratch_shapes=[pltpu.VMEM((train.shape[0], queries), f32)],
        compiler_params=params(),
        cost_estimate=cost(micros),
    )(keep_near(train), *map(keep_near, arrays))
    return [rows if dest == 0 else to_peer(rows, *divmod(dest, subs)) for dest, rows in enumerate(dealt)]


def early(train, shared, mine, rest, micros):
    return pl.pallas_call(
        functools.partial(early_kernel, shared),
        out_shape=pltpu.VMEM((train.shape[0], mine.shape[1]), f32),
        in_specs=[in_vmem] * 3,
        out_specs=in_vmem,
        compiler_params=params(),
        cost_estimate=cost(micros),
    )(*map(keep_near, (train, mine, rest)))


def sum_kernel(places, own_place, *refs):
    output = refs[-1]
    each = (len(refs) - 1) // len(places)
    rows = output.shape[1]
    part = rows // len(places)
    for slot, place in enumerate(places):
        total = None
        for ref in refs[slot * each : (slot + 1) * each]:
            term = ref[...].astype(f32)
            total = term if total is None else total + term
        output[place] = total[:rows]
        output[own_place, slot * part : (slot + 1) * part, :] = total[rows:]


def local(query_grads, train_grads, in_inverse, out_inverse, module_map):
    half_width = query_grads.shape[2]
    mods, subs = lax.axis_size("mod"), lax.axis_size("sub")
    parts, part = lax.axis_size("groups"), lax.axis_index("groups")
    reach = min(WINDOW_HALF, (lax.axis_size("ex") - 1) // 2)
    precon = preconditioned(query_grads, in_inverse, out_inverse, module_map)

    share = 3 * half_width // (4 * parts) // 128 * 128
    shared = share * parts
    train = train_grads.reshape(train_grads.shape[0], half_width)

    offsets = [sign * far for far in range(1, reach + 1) for sign in (1, -1)]
    mine = lax.dynamic_slice_in_dim(precon, part * share, share, 0)
    rest = precon[shared:]
    carried = {offset: shifted(mine, "ex", -offset) for offset in offsets}
    common = {offset: shifted(rest, "ex", -offset) for offset in offsets}
    own = whole(train, precon, 1)
    terms = []
    for slot, offset in enumerate(offsets):
        swapped = [shifted(carried[offset], "groups", step) for step in range(1, parts)]
        total = early(train, shared, carried[offset], common[offset], 1)
        terms += late(train, slot, len(offsets), own, total, swapped, 1)
    rows = train.shape[0] // (mods * subs)
    summed = pl.pallas_call(
        functools.partial(sum_kernel, [offset + reach for offset in offsets], reach),
        out_shape=jax.ShapeDtypeStruct((2 * reach + 1, rows, query_grads.shape[0]), f32),
        in_specs=[in_vmem] * len(terms),
        out_specs=in_vmem,
        compiler_params=params(),
        cost_estimate=cost(1),
    )(*[keep_near(term) for term in terms])
    return summed.transpose(1, 0, 2)


def solution(mesh):
    placed = (P("ex", "mod", "sub"), P(("groups", "ex"), "mod", "sub"), P(), P(), P("mod"))
    return jax.shard_map(
        local,
        mesh=mesh,
        in_specs=placed,
        out_specs=P(("groups", "ex", "mod", "sub"), None, None),
        check_vma=False,
    )
```

```python
import functools

import jax
import jax.numpy as jnp
from jax import lax
from jax.experimental import pallas as pl
from jax.experimental.pallas import tpu as pltpu
from jax.sharding import PartitionSpec as P

WINDOW_HALF = 2
VMEM_LIMIT = 32 * 1024 * 1024

f32, bf16 = jnp.float32, jnp.bfloat16
in_vmem = pl.BlockSpec(memory_space=pltpu.VMEM)


def keep_near(value):
    return pltpu.with_memory_space_constraint(value, pltpu.VMEM)


def params():
    return pltpu.CompilerParams(vmem_limit_bytes=VMEM_LIMIT)


def shifted(value, axis, steps):
    count = lax.axis_size(axis)
    pairs = [(source, (source + steps) % count) for source in range(count)]
    return lax.ppermute(value, axis, pairs)


def to_peer(value, mod_step, sub_step):
    mods, subs = lax.axis_size("mod"), lax.axis_size("sub")
    pairs = []
    for mod in range(mods):
        for sub in range(subs):
            target = ((mod + mod_step) % mods) * subs + (sub + sub_step) % subs
            pairs.append((mod * subs + sub, target))
    return lax.ppermute(value, ("mod", "sub"), pairs)


def split(value):
    high = value.astype(bf16)
    return high, (value - high.astype(f32)).astype(bf16)


def nt_dot(lhs, rhs):
    return lax.dot_general(lhs, rhs, (((1,), (1,)), ((), ())), preferred_element_type=f32)


def right_rows(pair, raw, right_ref):
    width = pair.shape[0]
    for first in range(0, raw.shape[1], width):
        piece = raw[:, first : first + width]
        right_ref[first : first + width, :] = nt_dot(pair, jnp.concatenate([piece, piece], axis=1))


def first_kernel(
    map_ref, in_ref, out_ref, raw_ref, right_ref, pair_ref, left_ref, inverse_ref, rows_ref, own_ref, sems
):
    own_rows = left_ref.shape[0]
    sub = lax.axis_index("sub")
    module = map_ref[0]
    mine = out_ref.at[module, pl.ds(pl.multiple_of(sub * own_rows, own_rows), own_rows), :]
    copies = [
        pltpu.make_async_copy(in_ref.at[module], inverse_ref, sems.at[0]),
        pltpu.make_async_copy(mine, rows_ref, sems.at[1]),
        pltpu.make_async_copy(raw_ref, own_ref, sems.at[2]),
    ]
    for copy in copies:
        copy.start()
    copies[0].wait()
    high, low = split(inverse_ref[...].T)
    high, low = high.astype(f32), low.astype(f32)
    zero = jnp.zeros_like(high)
    pair = jnp.concatenate(
        [
            jnp.concatenate([high, zero, low, zero], axis=1),
            jnp.concatenate([zero, high, zero, low], axis=1),
        ],
        axis=0,
    ).astype(bf16)
    pair_ref[...] = pair
    copies[1].wait()
    rows = rows_ref[...]
    swapped = jnp.concatenate([rows[:, own_rows:], rows[:, :own_rows]], axis=1)
    rows = jnp.where(sub == 0, rows, swapped)
    high, low = split(rows)
    high, low = high.astype(f32), low.astype(f32)
    left_ref[...] = jnp.concatenate([high, high, low], axis=1).astype(bf16)
    copies[2].wait()
    right_rows(pair, own_ref, right_ref)


def second_kernel(pair_ref, left_ref, own_ref, raw_ref, result_ref, right_ref, done_ref):
    own_rows = left_ref.shape[0]
    rank_in = result_ref.shape[0] // own_rows
    right_rows(pair_ref[...], raw_ref, right_ref)
    left = left_ref[...]
    for first in range(0, rank_in, 2):
        wide = jnp.concatenate(
            [
                jnp.concatenate(
                    [
                        own_ref[pl.ds(column, own_rows, stride=rank_in), :],
                        right_ref[pl.ds(column, own_rows, stride=rank_in), :],
                    ],
                    axis=0,
                )
                for column in (first, first + 1)
            ],
            axis=1,
        )
        high, low = split(wide)
        both = jnp.dot(left, jnp.concatenate([high, low, high], axis=0), preferred_element_type=f32)
        queries = both.shape[1] // 2
        done_ref[pl.ds(first, own_rows, stride=rank_in), :] = both[:, :queries]
        done_ref[pl.ds(first + 1, own_rows, stride=rank_in), :] = both[:, queries:]
    result_ref[...] = done_ref[...].astype(bf16)


def preconditioned(query_grads, in_inverse, out_inverse, module_map):
    block_rows, _, half_width = query_grads.shape
    rank_in, rank_out = in_inverse.shape[1], out_inverse.shape[1]
    own_rows = half_width // rank_in
    raw = query_grads.reshape(block_rows, half_width)
    other = shifted(raw, "sub", 1)
    anywhere = pl.BlockSpec(memory_space=pl.ANY)
    right, pair, left = pl.pallas_call(
        first_kernel,
        out_shape=(
            pltpu.VMEM((half_width, block_rows), f32),
            pltpu.VMEM((2 * rank_in, 4 * rank_in), bf16),
            pltpu.VMEM((own_rows, 3 * rank_out), bf16),
        ),
        in_specs=[pl.BlockSpec(memory_space=pltpu.SMEM), anywhere, anywhere, anywhere],
        out_specs=[in_vmem, in_vmem, in_vmem],
        scratch_shapes=[
            pltpu.VMEM((rank_in, rank_in), f32),
            pltpu.VMEM((own_rows, rank_out), f32),
            pltpu.VMEM((block_rows, half_width), bf16),
            pltpu.SemaphoreType.DMA((3,)),
        ],
        compiler_params=params(),
        cost_estimate=cost(2),
    )(module_map, *[pltpu.with_memory_space_constraint(x, pltpu.HBM) for x in (in_inverse, out_inverse, raw)])
    return pl.pallas_call(
        second_kernel,
        out_shape=pltpu.VMEM((half_width, block_rows), bf16),
        in_specs=[in_vmem] * 4,
        out_specs=in_vmem,
        scratch_shapes=[pltpu.VMEM((half_width, block_rows), f32)] * 2,
        compiler_params=params(),
        cost_estimate=cost(2),
    )(keep_near(pair), keep_near(left), keep_near(right), keep_near(other))


def part_dot(train_ref, ref, first):
    train = train_ref[:, pl.ds(first, ref.shape[0])]
    return jnp.dot(train, ref[...], preferred_element_type=f32)


def early_kernel(shared, train_ref, mine_ref, rest_ref, total_ref):
    share = mine_ref.shape[0]
    first = pl.multiple_of(lax.axis_index("groups") * share, 128)
    total_ref[...] = part_dot(train_ref, mine_ref, first) + part_dot(train_ref, rest_ref, shared)


def late_kernel(dests, subs, train_ref, *refs):
    outputs, sum_ref = refs[-1 - dests : -1], refs[-1]
    total_ref, swapped = refs[0], refs[1 : -1 - dests]
    total = total_ref[...]
    parts = len(swapped) + 1
    for step, ref in enumerate(swapped, 1):
        share = ref.shape[0]
        source = lax.rem(lax.axis_index("groups") + parts - step, parts)
        total = total + part_dot(train_ref, ref, pl.multiple_of(source * share, 128))
    deal(total, subs, sum_ref, outputs)


def whole_kernel(mods, subs, train_ref, block_ref, *refs):
    outputs, sum_ref = refs[:-1], refs[-1]
    sum_ref[...] = part_dot(train_ref, block_ref, 0)
    rows = sum_ref.shape[0] // (mods * subs)
    for sub_step, output in enumerate(outputs):
        for mod_step in range(mods):
            output[mod_step * rows : (mod_step + 1) * rows, :] = sum_ref[peer_rows(mod_step, sub_step, mods, subs, rows), :]


def peer_rows(mod_step, sub_step, mods, subs, rows):
    target = lax.rem(lax.axis_index("mod") + mod_step, mods) * subs
    target = target + lax.rem(lax.axis_index("sub") + sub_step, subs)
    return pl.ds(pl.multiple_of(target * rows, rows), rows)


def deal(total, subs, sum_ref, outputs):
    sum_ref[...] = total
    mods = len(outputs) // subs
    rows = total.shape[0] // len(outputs)
    for dest, output in enumerate(outputs):
        place = peer_rows(*divmod(dest, subs), mods, subs, rows)
        output[...] = sum_ref[place, :].astype(output.dtype)


def cost(micros):
    return pl.CostEstimate(flops=int(micros * 1.15e9), bytes_accessed=0, transcendentals=0)


def add_kernel(count, *refs):
    inputs, outputs = refs[:count], refs[count:]
    rows = outputs[0].shape[0]
    for step, output in enumerate(outputs):
        total = None
        for ref in inputs:
            term = ref[step * rows : (step + 1) * rows, :]
            total = term if total is None else total + term
        output[...] = total.astype(output.dtype)


def whole(train, block):
    mods, subs = lax.axis_size("mod"), lax.axis_size("sub")
    rows, queries = train.shape[0] // (mods * subs), block.shape[1]
    dealt = pl.pallas_call(
        functools.partial(whole_kernel, mods, subs),
        out_shape=[pltpu.VMEM((mods * rows, queries), f32)] * subs,
        in_specs=[in_vmem] * 2,
        out_specs=[in_vmem] * subs,
        scratch_shapes=[pltpu.VMEM((train.shape[0], queries), f32)],
        compiler_params=params(),
        cost_estimate=cost(1),
    )(keep_near(train), keep_near(block))
    terms = [to_peer(piece, 0, step) if step else piece for step, piece in enumerate(dealt)]
    added = pl.pallas_call(
        functools.partial(add_kernel, subs),
        out_shape=[pltpu.VMEM((rows, queries), bf16 if step else f32) for step in range(mods)],
        in_specs=[in_vmem] * subs,
        out_specs=[in_vmem] * mods,
        compiler_params=params(),
        cost_estimate=cost(0.1),
    )(*map(keep_near, terms))
    return added, dealt


def held(value, first, after):
    def kernel(value_ref, *refs):
        refs[-1][...] = value_ref[first:, :]

    return pl.pallas_call(
        kernel,
        out_shape=pltpu.VMEM((value.shape[0] - first, value.shape[1]), value.dtype),
        in_specs=[in_vmem] + [pl.BlockSpec(memory_space=pl.ANY)] * len(after),
        out_specs=in_vmem,
        compiler_params=params(),
        cost_estimate=cost(0.1),
    )(keep_near(value), *after)


def late(train, *arrays, micros):
    subs = lax.axis_size("sub")
    dests = lax.axis_size("mod") * subs
    queries = arrays[0].shape[1]
    dealt = pl.pallas_call(
        functools.partial(late_kernel, dests, subs),
        out_shape=[pltpu.VMEM((train.shape[0] // dests, queries), bf16 if dest else f32) for dest in range(dests)],
        in_specs=[in_vmem] * (1 + len(arrays)),
        out_specs=[in_vmem] * dests,
        scratch_shapes=[pltpu.VMEM((train.shape[0], queries), f32)],
        compiler_params=params(),
        cost_estimate=cost(micros),
    )(keep_near(train), *map(keep_near, arrays))
    return [rows if dest == 0 else to_peer(rows, *divmod(dest, subs)) for dest, rows in enumerate(dealt)]


def early(train, shared, mine, rest, micros):
    return pl.pallas_call(
        functools.partial(early_kernel, shared),
        out_shape=pltpu.VMEM((train.shape[0], mine.shape[1]), f32),
        in_specs=[in_vmem] * 3,
        out_specs=in_vmem,
        compiler_params=params(),
        cost_estimate=cost(micros),
    )(*map(keep_near, (train, mine, rest)))


def sum_kernel(counts, *refs):
    output = refs[-1]
    at = 0
    for block, count in enumerate(counts):
        total = None
        for ref in refs[at : at + count]:
            term = ref[...].astype(f32)
            total = term if total is None else total + term
        output[block] = total
        at += count


def local(query_grads, train_grads, in_inverse, out_inverse, module_map):
    half_width = query_grads.shape[2]
    mods, subs = lax.axis_size("mod"), lax.axis_size("sub")
    parts, part = lax.axis_size("groups"), lax.axis_index("groups")
    reach = min(WINDOW_HALF, (lax.axis_size("ex") - 1) // 2)
    precon = preconditioned(query_grads, in_inverse, out_inverse, module_map)

    share = 3 * half_width // (4 * parts) // 128 * 128
    shared = share * parts
    train = train_grads.reshape(train_grads.shape[0], half_width)

    offsets = [sign * far for far in range(1, reach + 1) for sign in (1, -1)]
    mine = lax.dynamic_slice_in_dim(precon, part * share, share, 0)
    added, dealt = whole(train, precon)
    rest = held(precon, shared, dealt[:1])
    carried = {offset: shifted(mine, "ex", -offset) for offset in offsets}
    common = {offset: shifted(rest, "ex", -offset) for offset in offsets}
    partial = {0: [to_peer(piece, step, 0) if step else piece for step, piece in enumerate(added)]}
    for offset in offsets:
        swapped = [shifted(carried[offset], "groups", step) for step in range(1, parts)]
        total = early(train, shared, carried[offset], common[offset], 1)
        partial[offset] = late(train, total, *swapped, micros=1)
    terms = [rows for offset in range(-reach, reach + 1) for rows in partial[offset]]
    rows = train.shape[0] // (mods * subs)
    counts = [len(partial[offset]) for offset in range(-reach, reach + 1)]
    summed = pl.pallas_call(
        functools.partial(sum_kernel, counts),
        out_shape=jax.ShapeDtypeStruct((2 * reach + 1, rows, query_grads.shape[0]), f32),
        in_specs=[in_vmem] * len(terms),
        out_specs=in_vmem,
        compiler_params=params(),
        cost_estimate=cost(1),
    )(*[keep_near(term) for term in terms])
    return summed.transpose(1, 0, 2)


def solution(mesh):
    placed = (P("ex", "mod", "sub"), P(("groups", "ex"), "mod", "sub"), P(), P(), P("mod"))
    return jax.shard_map(
        local,
        mesh=mesh,
        in_specs=placed,
        out_specs=P(("groups", "ex", "mod", "sub"), None, None),
        check_vma=False,
    )
```

```python
import functools

import jax
import jax.numpy as jnp
from jax import lax
from jax.experimental import pallas as pl
from jax.experimental.pallas import tpu as pltpu
from jax.sharding import PartitionSpec as P

WINDOW_HALF = 2
VMEM_LIMIT = 32 * 1024 * 1024

f32, bf16 = jnp.float32, jnp.bfloat16
in_vmem = pl.BlockSpec(memory_space=pltpu.VMEM)


def keep_near(value):
    return pltpu.with_memory_space_constraint(value, pltpu.VMEM)


def params():
    return pltpu.CompilerParams(vmem_limit_bytes=VMEM_LIMIT)


def shifted(value, axis, steps):
    count = lax.axis_size(axis)
    pairs = [(source, (source + steps) % count) for source in range(count)]
    return lax.ppermute(value, axis, pairs)


def to_peer(value, mod_step, sub_step):
    mods, subs = lax.axis_size("mod"), lax.axis_size("sub")
    pairs = []
    for mod in range(mods):
        for sub in range(subs):
            target = ((mod + mod_step) % mods) * subs + (sub + sub_step) % subs
            pairs.append((mod * subs + sub, target))
    return lax.ppermute(value, ("mod", "sub"), pairs)


def split(value):
    high = value.astype(bf16)
    return high, (value - high.astype(f32)).astype(bf16)


def nt_dot(lhs, rhs):
    return lax.dot_general(lhs, rhs, (((1,), (1,)), ((), ())), preferred_element_type=f32)


def right_rows(pair, raw, right_ref):
    width = pair.shape[0]
    for first in range(0, raw.shape[1], width):
        piece = raw[:, first : first + width]
        right_ref[first : first + width, :] = nt_dot(pair, jnp.concatenate([piece, piece], axis=1))


def first_kernel(
    map_ref, in_ref, out_ref, raw_ref, right_ref, pair_ref, left_ref, inverse_ref, rows_ref, own_ref, sems
):
    own_rows = left_ref.shape[0]
    sub = lax.axis_index("sub")
    module = map_ref[0]
    mine = out_ref.at[module, pl.ds(pl.multiple_of(sub * own_rows, own_rows), own_rows), :]
    copies = [
        pltpu.make_async_copy(in_ref.at[module], inverse_ref, sems.at[0]),
        pltpu.make_async_copy(mine, rows_ref, sems.at[1]),
        pltpu.make_async_copy(raw_ref, own_ref, sems.at[2]),
    ]
    for copy in copies:
        copy.start()
    copies[0].wait()
    high, low = split(inverse_ref[...].T)
    high, low = high.astype(f32), low.astype(f32)
    zero = jnp.zeros_like(high)
    pair = jnp.concatenate(
        [
            jnp.concatenate([high, zero, low, zero], axis=1),
            jnp.concatenate([zero, high, zero, low], axis=1),
        ],
        axis=0,
    ).astype(bf16)
    pair_ref[...] = pair
    copies[1].wait()
    rows = rows_ref[...]
    swapped = jnp.concatenate([rows[:, own_rows:], rows[:, :own_rows]], axis=1)
    rows = jnp.where(sub == 0, rows, swapped)
    high, low = split(rows)
    high, low = high.astype(f32), low.astype(f32)
    left_ref[...] = jnp.concatenate([high, high, low], axis=1).astype(bf16)
    copies[2].wait()
    right_rows(pair, own_ref, right_ref)


def second_kernel(pair_ref, left_ref, own_ref, raw_ref, result_ref, right_ref, done_ref):
    own_rows = left_ref.shape[0]
    rank_in = result_ref.shape[0] // own_rows
    right_rows(pair_ref[...], raw_ref, right_ref)
    left = left_ref[...]
    for first in range(0, rank_in, 2):
        wide = jnp.concatenate(
            [
                jnp.concatenate(
                    [
                        own_ref[pl.ds(column, own_rows, stride=rank_in), :],
                        right_ref[pl.ds(column, own_rows, stride=rank_in), :],
                    ],
                    axis=0,
                )
                for column in (first, first + 1)
            ],
            axis=1,
        )
        high, low = split(wide)
        both = jnp.dot(left, jnp.concatenate([high, low, high], axis=0), preferred_element_type=f32)
        queries = both.shape[1] // 2
        done_ref[pl.ds(first, own_rows, stride=rank_in), :] = both[:, :queries]
        done_ref[pl.ds(first + 1, own_rows, stride=rank_in), :] = both[:, queries:]
    result_ref[...] = done_ref[...].astype(bf16)


def preconditioned(query_grads, in_inverse, out_inverse, module_map):
    block_rows, _, half_width = query_grads.shape
    rank_in, rank_out = in_inverse.shape[1], out_inverse.shape[1]
    own_rows = half_width // rank_in
    raw = query_grads.reshape(block_rows, half_width)
    other = shifted(raw, "sub", 1)
    anywhere = pl.BlockSpec(memory_space=pl.ANY)
    right, pair, left = pl.pallas_call(
        first_kernel,
        out_shape=(
            pltpu.VMEM((half_width, block_rows), f32),
            pltpu.VMEM((2 * rank_in, 4 * rank_in), bf16),
            pltpu.VMEM((own_rows, 3 * rank_out), bf16),
        ),
        in_specs=[pl.BlockSpec(memory_space=pltpu.SMEM), anywhere, anywhere, anywhere],
        out_specs=[in_vmem, in_vmem, in_vmem],
        scratch_shapes=[
            pltpu.VMEM((rank_in, rank_in), f32),
            pltpu.VMEM((own_rows, rank_out), f32),
            pltpu.VMEM((block_rows, half_width), bf16),
            pltpu.SemaphoreType.DMA((3,)),
        ],
        compiler_params=params(),
        cost_estimate=cost(2),
    )(module_map, *[pltpu.with_memory_space_constraint(x, pltpu.HBM) for x in (in_inverse, out_inverse, raw)])
    return pl.pallas_call(
        second_kernel,
        out_shape=pltpu.VMEM((half_width, block_rows), bf16),
        in_specs=[in_vmem] * 4,
        out_specs=in_vmem,
        scratch_shapes=[pltpu.VMEM((half_width, block_rows), f32)] * 2,
        compiler_params=params(),
        cost_estimate=cost(2),
    )(keep_near(pair), keep_near(left), keep_near(right), keep_near(other))


def part_dot(train_ref, ref, first):
    train = train_ref[:, pl.ds(first, ref.shape[0])]
    return jnp.dot(train, ref[...], preferred_element_type=f32)


def early_kernel(shared, train_ref, mine_ref, rest_ref, total_ref):
    share = mine_ref.shape[0]
    first = pl.multiple_of(lax.axis_index("groups") * share, 128)
    total_ref[...] = part_dot(train_ref, mine_ref, first) + part_dot(train_ref, rest_ref, shared)


def late_kernel(dests, subs, train_ref, *refs):
    outputs, sum_ref = refs[-1 - dests : -1], refs[-1]
    total_ref, swapped = refs[0], refs[1 : -1 - dests]
    total = total_ref[...]
    parts = len(swapped) + 1
    for step, ref in enumerate(swapped, 1):
        share = ref.shape[0]
        source = lax.rem(lax.axis_index("groups") + parts - step, parts)
        total = total + part_dot(train_ref, ref, pl.multiple_of(source * share, 128))
    deal(total, subs, sum_ref, outputs)


def whole_kernel(mods, subs, train_ref, block_ref, *refs):
    outputs, sum_ref = refs[:-1], refs[-1]
    sum_ref[...] = part_dot(train_ref, block_ref, 0)
    rows = sum_ref.shape[0] // (mods * subs)
    for sub_step, output in enumerate(outputs):
        for mod_step in range(mods):
            output[mod_step * rows : (mod_step + 1) * rows, :] = sum_ref[peer_rows(mod_step, sub_step, mods, subs, rows), :]


def peer_rows(mod_step, sub_step, mods, subs, rows):
    target = lax.rem(lax.axis_index("mod") + mod_step, mods) * subs
    target = target + lax.rem(lax.axis_index("sub") + sub_step, subs)
    return pl.ds(pl.multiple_of(target * rows, rows), rows)


def deal(total, subs, sum_ref, outputs):
    sum_ref[...] = total
    mods = len(outputs) // subs
    rows = total.shape[0] // len(outputs)
    for dest, output in enumerate(outputs):
        place = peer_rows(*divmod(dest, subs), mods, subs, rows)
        output[...] = sum_ref[place, :].astype(output.dtype)


def cost(micros):
    return pl.CostEstimate(flops=int(micros * 1.15e9), bytes_accessed=0, transcendentals=0)


def add_kernel(count, *refs):
    inputs, outputs = refs[:count], refs[count:]
    rows = outputs[0].shape[0]
    for step, output in enumerate(outputs):
        total = None
        for ref in inputs:
            term = ref[step * rows : (step + 1) * rows, :]
            total = term if total is None else total + term
        output[...] = total.astype(output.dtype)


def whole(train, block):
    mods, subs = lax.axis_size("mod"), lax.axis_size("sub")
    rows, queries = train.shape[0] // (mods * subs), block.shape[1]
    dealt = pl.pallas_call(
        functools.partial(whole_kernel, mods, subs),
        out_shape=[pltpu.VMEM((mods * rows, queries), f32)] * subs,
        in_specs=[in_vmem] * 2,
        out_specs=[in_vmem] * subs,
        scratch_shapes=[pltpu.VMEM((train.shape[0], queries), f32)],
        compiler_params=params(),
        cost_estimate=cost(1),
    )(keep_near(train), keep_near(block))
    terms = [to_peer(piece, 0, step) if step else piece for step, piece in enumerate(dealt)]
    added = pl.pallas_call(
        functools.partial(add_kernel, subs),
        out_shape=[pltpu.VMEM((rows, queries), bf16 if step else f32) for step in range(mods)],
        in_specs=[in_vmem] * subs,
        out_specs=[in_vmem] * mods,
        compiler_params=params(),
        cost_estimate=cost(0.1),
    )(*map(keep_near, terms))
    return added, dealt


def held(value, first, after):
    def kernel(value_ref, *refs):
        refs[-1][...] = value_ref[first:, :]

    return pl.pallas_call(
        kernel,
        out_shape=pltpu.VMEM((value.shape[0] - first, value.shape[1]), value.dtype),
        in_specs=[in_vmem] + [pl.BlockSpec(memory_space=pl.ANY)] * len(after),
        out_specs=in_vmem,
        compiler_params=params(),
        cost_estimate=cost(0.1),
    )(keep_near(value), *after)


def late(train, *arrays, micros):
    subs = lax.axis_size("sub")
    dests = lax.axis_size("mod") * subs
    queries = arrays[0].shape[1]
    dealt = pl.pallas_call(
        functools.partial(late_kernel, dests, subs),
        out_shape=[pltpu.VMEM((train.shape[0] // dests, queries), bf16 if dest else f32) for dest in range(dests)],
        in_specs=[in_vmem] * (1 + len(arrays)),
        out_specs=[in_vmem] * dests,
        scratch_shapes=[pltpu.VMEM((train.shape[0], queries), f32)],
        compiler_params=params(),
        cost_estimate=cost(micros),
    )(keep_near(train), *map(keep_near, arrays))
    return [to_peer(rows, *divmod(dest, subs)) if dest else rows for dest, rows in reversed(list(enumerate(dealt)))]


def early(train, shared, mine, rest, micros):
    return pl.pallas_call(
        functools.partial(early_kernel, shared),
        out_shape=pltpu.VMEM((train.shape[0], mine.shape[1]), f32),
        in_specs=[in_vmem] * 3,
        out_specs=in_vmem,
        compiler_params=params(),
        cost_estimate=cost(micros),
    )(*map(keep_near, (train, mine, rest)))


def sum_kernel(places, counts, *refs):
    output = refs[-1]
    at = 0
    for place, count in zip(places, counts):
        total = None
        for ref in refs[at : at + count]:
            term = ref[...].astype(f32)
            total = term if total is None else total + term
        output[place] = total
        at += count


def local(query_grads, train_grads, in_inverse, out_inverse, module_map):
    half_width = query_grads.shape[2]
    mods, subs = lax.axis_size("mod"), lax.axis_size("sub")
    parts, part = lax.axis_size("groups"), lax.axis_index("groups")
    reach = min(WINDOW_HALF, (lax.axis_size("ex") - 1) // 2)
    precon = preconditioned(query_grads, in_inverse, out_inverse, module_map)

    share = 3 * half_width // (4 * parts) // 128 * 128
    shared = share * parts
    train = train_grads.reshape(train_grads.shape[0], half_width)

    offsets = [sign * far for far in range(1, reach + 1) for sign in (1, -1)]
    mine = lax.dynamic_slice_in_dim(precon, part * share, share, 0)
    added, dealt = whole(train, precon)
    rest = held(precon, shared, dealt[:1])
    carried = {offset: shifted(mine, "ex", -offset) for offset in offsets}
    common = {offset: shifted(rest, "ex", -offset) for offset in offsets}
    partial = {0: [to_peer(piece, step, 0) if step else piece for step, piece in enumerate(added)]}
    for offset in offsets:
        swapped = [shifted(carried[offset], "groups", step) for step in range(1, parts)]
        total = early(train, shared, carried[offset], common[offset], 1)
        partial[offset] = late(train, total, *swapped, micros=1)
    order = [*offsets, 0]
    counts = [len(partial[offset]) for offset in order]
    terms = [rows for offset in order for rows in partial[offset]]
    rows = train.shape[0] // (mods * subs)
    summed = pl.pallas_call(
        functools.partial(sum_kernel, [offset + reach for offset in order], counts),
        out_shape=jax.ShapeDtypeStruct((2 * reach + 1, rows, query_grads.shape[0]), f32),
        in_specs=[in_vmem] * len(terms),
        out_specs=in_vmem,
        compiler_params=params(),
        cost_estimate=cost(1),
    )(*[keep_near(term) for term in terms])
    return summed.transpose(1, 0, 2)


def solution(mesh):
    placed = (P("ex", "mod", "sub"), P(("groups", "ex"), "mod", "sub"), P(), P(), P("mod"))
    return jax.shard_map(
        local,
        mesh=mesh,
        in_specs=placed,
        out_specs=P(("groups", "ex", "mod", "sub"), None, None),
        check_vma=False,
    )
```

```python
import functools

import jax
import jax.numpy as jnp
from jax import lax
from jax.experimental import pallas as pl
from jax.experimental.pallas import tpu as pltpu
from jax.sharding import PartitionSpec as P

WINDOW_HALF = 2
VMEM_LIMIT = 32 * 1024 * 1024

f32, bf16 = jnp.float32, jnp.bfloat16
in_vmem = pl.BlockSpec(memory_space=pltpu.VMEM)


def keep_near(value):
    return pltpu.with_memory_space_constraint(value, pltpu.VMEM)


def params():
    return pltpu.CompilerParams(vmem_limit_bytes=VMEM_LIMIT)


def shifted(value, axis, steps):
    count = lax.axis_size(axis)
    pairs = [(source, (source + steps) % count) for source in range(count)]
    return lax.ppermute(value, axis, pairs)


def to_peer(value, mod_step, sub_step):
    mods, subs = lax.axis_size("mod"), lax.axis_size("sub")
    pairs = []
    for mod in range(mods):
        for sub in range(subs):
            target = ((mod + mod_step) % mods) * subs + (sub + sub_step) % subs
            pairs.append((mod * subs + sub, target))
    return lax.ppermute(value, ("mod", "sub"), pairs)


def split(value):
    high = value.astype(bf16)
    return high, (value - high.astype(f32)).astype(bf16)


def nt_dot(lhs, rhs):
    return lax.dot_general(lhs, rhs, (((1,), (1,)), ((), ())), preferred_element_type=f32)


def right_rows(pair, raw, right_ref):
    width = pair.shape[1]
    queries = raw.shape[0]
    for first in range(0, raw.shape[1], 2 * width):
        pieces = [raw[:, at : at + width] for at in (first, first + width)]
        both = nt_dot(pair, jnp.concatenate(pieces, axis=0))
        both = both[:width] + both[width:]
        right_ref[first : first + width, :] = both[:, :queries]
        right_ref[first + width : first + 2 * width, :] = both[:, queries:]


def first_kernel(
    map_ref, in_ref, out_ref, raw_ref, right_ref, pair_ref, left_ref, inverse_ref, rows_ref, own_ref, sems
):
    own_rows = rows_ref.shape[0]
    sub = lax.axis_index("sub")
    module = map_ref[0]
    mine = out_ref.at[module, pl.ds(pl.multiple_of(sub * own_rows, own_rows), own_rows), :]
    copies = [
        pltpu.make_async_copy(in_ref.at[module], inverse_ref, sems.at[0]),
        pltpu.make_async_copy(mine, rows_ref, sems.at[1]),
        pltpu.make_async_copy(raw_ref, own_ref, sems.at[2]),
    ]
    for copy in copies:
        copy.start()
    copies[0].wait()
    high, low = split(inverse_ref[...].T)
    high, low = high.astype(f32), low.astype(f32)
    zero = jnp.zeros_like(high)
    pair = jnp.concatenate(
        [jnp.concatenate(row, axis=1) for row in ([high, zero], [zero, high], [low, zero], [zero, low])], axis=0
    ).astype(bf16)
    pair_ref[...] = pair
    copies[1].wait()
    rows = rows_ref[...]
    swapped = jnp.concatenate([rows[:, own_rows:], rows[:, :own_rows]], axis=1)
    rows = jnp.where(sub == 0, rows, swapped)
    high, low = split(rows)
    high, low = high.astype(f32), low.astype(f32)
    left_ref[...] = jnp.concatenate(
        [jnp.concatenate(row, axis=1) for row in ([high, high], [low, jnp.zeros_like(low)])], axis=0
    ).astype(bf16)
    copies[2].wait()
    right_rows(pair, own_ref, right_ref)


def second_kernel(pair_ref, left_ref, own_ref, raw_ref, result_ref, right_ref, done_ref):
    own_rows = left_ref.shape[0] // 2
    rank_in = result_ref.shape[0] // own_rows
    right_rows(pair_ref[...], raw_ref, right_ref)
    left = left_ref[...]
    for first in range(0, rank_in, 2):
        wide = jnp.concatenate(
            [
                jnp.concatenate(
                    [
                        own_ref[pl.ds(column, own_rows, stride=rank_in), :],
                        right_ref[pl.ds(column, own_rows, stride=rank_in), :],
                    ],
                    axis=0,
                )
                for column in (first, first + 1)
            ],
            axis=1,
        )
        high, low = split(wide)
        both = jnp.dot(left, jnp.concatenate([high, low], axis=0), preferred_element_type=f32)
        both = both[:own_rows] + both[own_rows:]
        queries = both.shape[1] // 2
        done_ref[pl.ds(first, own_rows, stride=rank_in), :] = both[:, :queries]
        done_ref[pl.ds(first + 1, own_rows, stride=rank_in), :] = both[:, queries:]
    result_ref[...] = done_ref[...].astype(bf16)


def preconditioned(query_grads, in_inverse, out_inverse, module_map):
    block_rows, _, half_width = query_grads.shape
    rank_in, rank_out = in_inverse.shape[1], out_inverse.shape[1]
    own_rows = half_width // rank_in
    raw = query_grads.reshape(block_rows, half_width)
    other = shifted(raw, "sub", 1)
    anywhere = pl.BlockSpec(memory_space=pl.ANY)
    right, pair, left = pl.pallas_call(
        first_kernel,
        out_shape=(
            pltpu.VMEM((half_width, block_rows), f32),
            pltpu.VMEM((4 * rank_in, 2 * rank_in), bf16),
            pltpu.VMEM((2 * own_rows, 2 * rank_out), bf16),
        ),
        in_specs=[pl.BlockSpec(memory_space=pltpu.SMEM), anywhere, anywhere, anywhere],
        out_specs=[in_vmem, in_vmem, in_vmem],
        scratch_shapes=[
            pltpu.VMEM((rank_in, rank_in), f32),
            pltpu.VMEM((own_rows, rank_out), f32),
            pltpu.VMEM((block_rows, half_width), bf16),
            pltpu.SemaphoreType.DMA((3,)),
        ],
        compiler_params=params(),
        cost_estimate=cost(2),
    )(module_map, *[pltpu.with_memory_space_constraint(x, pltpu.HBM) for x in (in_inverse, out_inverse, raw)])
    return pl.pallas_call(
        second_kernel,
        out_shape=pltpu.VMEM((half_width, block_rows), bf16),
        in_specs=[in_vmem] * 4,
        out_specs=in_vmem,
        scratch_shapes=[pltpu.VMEM((half_width, block_rows), f32)] * 2,
        compiler_params=params(),
        cost_estimate=cost(2),
    )(keep_near(pair), keep_near(left), keep_near(right), keep_near(other))


def part_dot(train_ref, ref, first):
    train = train_ref[:, pl.ds(first, ref.shape[0])]
    return jnp.dot(train, ref[...], preferred_element_type=f32)


def early_kernel(shared, train_ref, mine_ref, rest_ref, total_ref):
    share = mine_ref.shape[0]
    first = pl.multiple_of(lax.axis_index("groups") * share, 128)
    total_ref[...] = part_dot(train_ref, mine_ref, first) + part_dot(train_ref, rest_ref, shared)


def late_kernel(dests, subs, train_ref, *refs):
    outputs, sum_ref = refs[-1 - dests : -1], refs[-1]
    total_ref, swapped = refs[0], refs[1 : -1 - dests]
    total = total_ref[...]
    parts = len(swapped) + 1
    for step, ref in enumerate(swapped, 1):
        share = ref.shape[0]
        source = lax.rem(lax.axis_index("groups") + parts - step, parts)
        total = total + part_dot(train_ref, ref, pl.multiple_of(source * share, 128))
    deal(total, subs, sum_ref, outputs)


def whole_kernel(mods, subs, train_ref, block_ref, *refs):
    outputs, sum_ref = refs[:-1], refs[-1]
    sum_ref[...] = part_dot(train_ref, block_ref, 0)
    rows = sum_ref.shape[0] // (mods * subs)
    for sub_step, output in enumerate(outputs):
        for mod_step in range(mods):
            output[mod_step * rows : (mod_step + 1) * rows, :] = sum_ref[peer_rows(mod_step, sub_step, mods, subs, rows), :]


def peer_rows(mod_step, sub_step, mods, subs, rows):
    target = lax.rem(lax.axis_index("mod") + mod_step, mods) * subs
    target = target + lax.rem(lax.axis_index("sub") + sub_step, subs)
    return pl.ds(pl.multiple_of(target * rows, rows), rows)


def deal(total, subs, sum_ref, outputs):
    sum_ref[...] = total
    mods = len(outputs) // subs
    rows = total.shape[0] // len(outputs)
    for dest, output in enumerate(outputs):
        place = peer_rows(*divmod(dest, subs), mods, subs, rows)
        output[...] = sum_ref[place, :].astype(output.dtype)


def cost(micros):
    return pl.CostEstimate(flops=int(micros * 1.15e9), bytes_accessed=0, transcendentals=0)


def add_kernel(count, *refs):
    inputs, outputs = refs[:count], refs[count:]
    rows = outputs[0].shape[0]
    for step, output in enumerate(outputs):
        total = None
        for ref in inputs:
            term = ref[step * rows : (step + 1) * rows, :]
            total = term if total is None else total + term
        output[...] = total.astype(output.dtype)


def whole(train, block):
    mods, subs = lax.axis_size("mod"), lax.axis_size("sub")
    rows, queries = train.shape[0] // (mods * subs), block.shape[1]
    dealt = pl.pallas_call(
        functools.partial(whole_kernel, mods, subs),
        out_shape=[pltpu.VMEM((mods * rows, queries), f32)] * subs,
        in_specs=[in_vmem] * 2,
        out_specs=[in_vmem] * subs,
        scratch_shapes=[pltpu.VMEM((train.shape[0], queries), f32)],
        compiler_params=params(),
        cost_estimate=cost(1),
    )(keep_near(train), keep_near(block))
    terms = [to_peer(piece, 0, step) if step else piece for step, piece in enumerate(dealt)]
    added = pl.pallas_call(
        functools.partial(add_kernel, subs),
        out_shape=[pltpu.VMEM((rows, queries), bf16 if step else f32) for step in range(mods)],
        in_specs=[in_vmem] * subs,
        out_specs=[in_vmem] * mods,
        compiler_params=params(),
        cost_estimate=cost(0.1),
    )(*map(keep_near, terms))
    return added, dealt


def held(value, first, after):
    def kernel(value_ref, *refs):
        refs[-1][...] = value_ref[first:, :]

    return pl.pallas_call(
        kernel,
        out_shape=pltpu.VMEM((value.shape[0] - first, value.shape[1]), value.dtype),
        in_specs=[in_vmem] + [pl.BlockSpec(memory_space=pl.ANY)] * len(after),
        out_specs=in_vmem,
        compiler_params=params(),
        cost_estimate=cost(0.1),
    )(keep_near(value), *after)


def late(train, *arrays, micros):
    subs = lax.axis_size("sub")
    dests = lax.axis_size("mod") * subs
    queries = arrays[0].shape[1]
    dealt = pl.pallas_call(
        functools.partial(late_kernel, dests, subs),
        out_shape=[pltpu.VMEM((train.shape[0] // dests, queries), bf16 if dest else f32) for dest in range(dests)],
        in_specs=[in_vmem] * (1 + len(arrays)),
        out_specs=[in_vmem] * dests,
        scratch_shapes=[pltpu.VMEM((train.shape[0], queries), f32)],
        compiler_params=params(),
        cost_estimate=cost(micros),
    )(keep_near(train), *map(keep_near, arrays))
    return [to_peer(rows, *divmod(dest, subs)) if dest else rows for dest, rows in reversed(list(enumerate(dealt)))]


def early(train, shared, mine, rest, micros):
    return pl.pallas_call(
        functools.partial(early_kernel, shared),
        out_shape=pltpu.VMEM((train.shape[0], mine.shape[1]), f32),
        in_specs=[in_vmem] * 3,
        out_specs=in_vmem,
        compiler_params=params(),
        cost_estimate=cost(micros),
    )(*map(keep_near, (train, mine, rest)))


def sum_kernel(places, counts, *refs):
    output = refs[-1]
    at = 0
    for place, count in zip(places, counts):
        total = None
        for ref in refs[at : at + count]:
            term = ref[...].astype(f32)
            total = term if total is None else total + term
        output[place] = total
        at += count


def local(query_grads, train_grads, in_inverse, out_inverse, module_map):
    half_width = query_grads.shape[2]
    mods, subs = lax.axis_size("mod"), lax.axis_size("sub")
    parts, part = lax.axis_size("groups"), lax.axis_index("groups")
    reach = min(WINDOW_HALF, (lax.axis_size("ex") - 1) // 2)
    precon = preconditioned(query_grads, in_inverse, out_inverse, module_map)

    share = 3 * half_width // (4 * parts) // 128 * 128
    shared = share * parts
    train = train_grads.reshape(train_grads.shape[0], half_width)

    offsets = [sign * far for far in range(1, reach + 1) for sign in (1, -1)]
    mine = lax.dynamic_slice_in_dim(precon, part * share, share, 0)
    added, dealt = whole(train, precon)
    rest = held(precon, shared, dealt[:1])
    carried = {offset: shifted(mine, "ex", -offset) for offset in offsets}
    common = {offset: shifted(rest, "ex", -offset) for offset in offsets}
    partial = {0: [to_peer(piece, step, 0) if step else piece for step, piece in enumerate(added)]}
    for offset in offsets:
        swapped = [shifted(carried[offset], "groups", step) for step in range(1, parts)]
        total = early(train, shared, carried[offset], common[offset], 1)
        partial[offset] = late(train, total, *swapped, micros=1)
    order = [*offsets, 0]
    counts = [len(partial[offset]) for offset in order]
    terms = [rows for offset in order for rows in partial[offset]]
    rows = train.shape[0] // (mods * subs)
    summed = pl.pallas_call(
        functools.partial(sum_kernel, [offset + reach for offset in order], counts),
        out_shape=jax.ShapeDtypeStruct((2 * reach + 1, rows, query_grads.shape[0]), f32),
        in_specs=[in_vmem] * len(terms),
        out_specs=in_vmem,
        compiler_params=params(),
        cost_estimate=cost(1),
    )(*[keep_near(term) for term in terms])
    return summed.transpose(1, 0, 2)


def solution(mesh):
    placed = (P("ex", "mod", "sub"), P(("groups", "ex"), "mod", "sub"), P(), P(), P("mod"))
    return jax.shard_map(
        local,
        mesh=mesh,
        in_specs=placed,
        out_specs=P(("groups", "ex", "mod", "sub"), None, None),
        check_vma=False,
    )
```

```python
import functools

import jax
import jax.numpy as jnp
from jax import lax
from jax.experimental import pallas as pl
from jax.experimental.pallas import tpu as pltpu
from jax.sharding import PartitionSpec as P

WINDOW_HALF = 2
PAD = 8
VMEM_LIMIT = 32 * 1024 * 1024

f32, bf16 = jnp.float32, jnp.bfloat16
in_vmem = pl.BlockSpec(memory_space=pltpu.VMEM)


def keep_near(value):
    return pltpu.with_memory_space_constraint(value, pltpu.VMEM)


def params():
    return pltpu.CompilerParams(vmem_limit_bytes=VMEM_LIMIT)


def shifted(value, axis, steps):
    count = lax.axis_size(axis)
    pairs = [(source, (source + steps) % count) for source in range(count)]
    return lax.ppermute(value, axis, pairs)


def to_peer(value, mod_step, sub_step):
    mods, subs = lax.axis_size("mod"), lax.axis_size("sub")
    pairs = []
    for mod in range(mods):
        for sub in range(subs):
            target = ((mod + mod_step) % mods) * subs + (sub + sub_step) % subs
            pairs.append((mod * subs + sub, target))
    return lax.ppermute(value, ("mod", "sub"), pairs)


def split(value):
    high = value.astype(bf16)
    return high, (value - high.astype(f32)).astype(bf16)


def nt_dot(lhs, rhs):
    return lax.dot_general(lhs, rhs, (((1,), (1,)), ((), ())), preferred_element_type=f32)


def right_rows(pair, raw, right_ref):
    width = pair.shape[1]
    queries = raw.shape[0]
    for first in range(0, raw.shape[1], 2 * width):
        pieces = [raw[:, at : at + width] for at in (first, first + width)]
        both = nt_dot(pair, jnp.concatenate(pieces, axis=0))
        both = both[:width] + both[width:]
        half = width // 2
        for index, lanes in enumerate((slice(0, queries), slice(queries, 2 * queries))):
            for row in range(2):
                at = (first // half + 2 * index + row) * (half + PAD)
                right_ref[at : at + half, :] = both[row * half : (row + 1) * half, lanes]


def first_kernel(
    map_ref, in_ref, out_ref, raw_ref, right_ref, pair_ref, left_ref, inverse_ref, rows_ref, own_ref, sems
):
    own_rows = rows_ref.shape[0]
    sub = lax.axis_index("sub")
    module = map_ref[0]
    mine = out_ref.at[module, pl.ds(pl.multiple_of(sub * own_rows, own_rows), own_rows), :]
    copies = [
        pltpu.make_async_copy(in_ref.at[module], inverse_ref, sems.at[0]),
        pltpu.make_async_copy(mine, rows_ref, sems.at[1]),
        pltpu.make_async_copy(raw_ref, own_ref, sems.at[2]),
    ]
    for copy in copies:
        copy.start()
    copies[0].wait()
    high, low = split(inverse_ref[...].T)
    high, low = high.astype(f32), low.astype(f32)
    zero = jnp.zeros_like(high)
    pair = jnp.concatenate(
        [jnp.concatenate(row, axis=1) for row in ([high, zero], [zero, high], [low, zero], [zero, low])], axis=0
    ).astype(bf16)
    pair_ref[...] = pair
    copies[1].wait()
    rows = rows_ref[...]
    swapped = jnp.concatenate([rows[:, own_rows:], rows[:, :own_rows]], axis=1)
    rows = jnp.where(sub == 0, rows, swapped)
    high, low = split(rows)
    high, low = high.astype(f32), low.astype(f32)
    left_ref[...] = jnp.concatenate(
        [jnp.concatenate(row, axis=1) for row in ([high, high], [low, jnp.zeros_like(low)])], axis=0
    ).astype(bf16)
    copies[2].wait()
    right_rows(pair, own_ref, right_ref)


def second_kernel(pair_ref, left_ref, own_ref, raw_ref, result_ref, right_ref, done_ref):
    own_rows = left_ref.shape[0] // 2
    rank_in = result_ref.shape[0] // own_rows
    step = rank_in + PAD
    right_rows(pair_ref[...], raw_ref, right_ref)
    left = left_ref[...]
    for first in range(0, rank_in, 2):
        wide = jnp.concatenate(
            [
                jnp.concatenate(
                    [
                        own_ref[pl.ds(column, own_rows, stride=step), :],
                        right_ref[pl.ds(column, own_rows, stride=step), :],
                    ],
                    axis=0,
                )
                for column in (first, first + 1)
            ],
            axis=1,
        )
        high, low = split(wide)
        both = jnp.dot(left, jnp.concatenate([high, low], axis=0), preferred_element_type=f32)
        both = both[:own_rows] + both[own_rows:]
        queries = both.shape[1] // 2
        done_ref[pl.ds(first, own_rows, stride=step), :] = both[:, :queries]
        done_ref[pl.ds(first + 1, own_rows, stride=step), :] = both[:, queries:]
    for row in range(own_rows):
        result_ref[row * rank_in : (row + 1) * rank_in, :] = done_ref[row * step : row * step + rank_in, :].astype(bf16)


def preconditioned(query_grads, in_inverse, out_inverse, module_map):
    block_rows, _, half_width = query_grads.shape
    rank_in, rank_out = in_inverse.shape[1], out_inverse.shape[1]
    own_rows = half_width // rank_in
    raw = query_grads.reshape(block_rows, half_width)
    other = shifted(raw, "sub", 1)
    anywhere = pl.BlockSpec(memory_space=pl.ANY)
    right, pair, left = pl.pallas_call(
        first_kernel,
        out_shape=(
            pltpu.VMEM((own_rows * (rank_in + PAD), block_rows), f32),
            pltpu.VMEM((4 * rank_in, 2 * rank_in), bf16),
            pltpu.VMEM((2 * own_rows, 2 * rank_out), bf16),
        ),
        in_specs=[pl.BlockSpec(memory_space=pltpu.SMEM), anywhere, anywhere, anywhere],
        out_specs=[in_vmem, in_vmem, in_vmem],
        scratch_shapes=[
            pltpu.VMEM((rank_in, rank_in), f32),
            pltpu.VMEM((own_rows, rank_out), f32),
            pltpu.VMEM((block_rows, half_width), bf16),
            pltpu.SemaphoreType.DMA((3,)),
        ],
        compiler_params=params(),
        cost_estimate=cost(2),
    )(module_map, *[pltpu.with_memory_space_constraint(x, pltpu.HBM) for x in (in_inverse, out_inverse, raw)])
    return pl.pallas_call(
        second_kernel,
        out_shape=pltpu.VMEM((half_width, block_rows), bf16),
        in_specs=[in_vmem] * 4,
        out_specs=in_vmem,
        scratch_shapes=[pltpu.VMEM((own_rows * (rank_in + PAD), block_rows), f32)] * 2,
        compiler_params=params(),
        cost_estimate=cost(2),
    )(keep_near(pair), keep_near(left), keep_near(right), keep_near(other))


def part_dot(train_ref, ref, first):
    train = train_ref[:, pl.ds(first, ref.shape[0])]
    return jnp.dot(train, ref[...], preferred_element_type=f32)


def early_kernel(shared, train_ref, mine_ref, rest_ref, total_ref):
    share = mine_ref.shape[0]
    first = pl.multiple_of(lax.axis_index("groups") * share, 128)
    total_ref[...] = part_dot(train_ref, mine_ref, first) + part_dot(train_ref, rest_ref, shared)


def late_kernel(dests, subs, train_ref, *refs):
    outputs, sum_ref = refs[-1 - dests : -1], refs[-1]
    total_ref, swapped = refs[0], refs[1 : -1 - dests]
    total = total_ref[...]
    parts = len(swapped) + 1
    for step, ref in enumerate(swapped, 1):
        share = ref.shape[0]
        source = lax.rem(lax.axis_index("groups") + parts - step, parts)
        total = total + part_dot(train_ref, ref, pl.multiple_of(source * share, 128))
    deal(total, subs, sum_ref, outputs)


def whole_kernel(mods, subs, train_ref, block_ref, *refs):
    outputs, sum_ref = refs[:-1], refs[-1]
    sum_ref[...] = part_dot(train_ref, block_ref, 0)
    rows = sum_ref.shape[0] // (mods * subs)
    for sub_step, output in enumerate(outputs):
        for mod_step in range(mods):
            output[mod_step * rows : (mod_step + 1) * rows, :] = sum_ref[peer_rows(mod_step, sub_step, mods, subs, rows), :]


def peer_rows(mod_step, sub_step, mods, subs, rows):
    target = lax.rem(lax.axis_index("mod") + mod_step, mods) * subs
    target = target + lax.rem(lax.axis_index("sub") + sub_step, subs)
    return pl.ds(pl.multiple_of(target * rows, rows), rows)


def deal(total, subs, sum_ref, outputs):
    sum_ref[...] = total
    mods = len(outputs) // subs
    rows = total.shape[0] // len(outputs)
    for dest, output in enumerate(outputs):
        place = peer_rows(*divmod(dest, subs), mods, subs, rows)
        output[...] = sum_ref[place, :].astype(output.dtype)


def cost(micros):
    return pl.CostEstimate(flops=int(micros * 1.15e9), bytes_accessed=0, transcendentals=0)


def add_kernel(count, *refs):
    inputs, outputs = refs[:count], refs[count:]
    rows = outputs[0].shape[0]
    for step, output in enumerate(outputs):
        total = None
        for ref in inputs:
            term = ref[step * rows : (step + 1) * rows, :]
            total = term if total is None else total + term
        output[...] = total.astype(output.dtype)


def whole(train, block):
    mods, subs = lax.axis_size("mod"), lax.axis_size("sub")
    rows, queries = train.shape[0] // (mods * subs), block.shape[1]
    dealt = pl.pallas_call(
        functools.partial(whole_kernel, mods, subs),
        out_shape=[pltpu.VMEM((mods * rows, queries), f32)] * subs,
        in_specs=[in_vmem] * 2,
        out_specs=[in_vmem] * subs,
        scratch_shapes=[pltpu.VMEM((train.shape[0], queries), f32)],
        compiler_params=params(),
        cost_estimate=cost(1),
    )(keep_near(train), keep_near(block))
    terms = [to_peer(piece, 0, step) if step else piece for step, piece in enumerate(dealt)]
    added = pl.pallas_call(
        functools.partial(add_kernel, subs),
        out_shape=[pltpu.VMEM((rows, queries), bf16 if step else f32) for step in range(mods)],
        in_specs=[in_vmem] * subs,
        out_specs=[in_vmem] * mods,
        compiler_params=params(),
        cost_estimate=cost(0.1),
    )(*map(keep_near, terms))
    return added, dealt


def held(value, first, after):
    def kernel(value_ref, *refs):
        refs[-1][...] = value_ref[first:, :]

    return pl.pallas_call(
        kernel,
        out_shape=pltpu.VMEM((value.shape[0] - first, value.shape[1]), value.dtype),
        in_specs=[in_vmem] + [pl.BlockSpec(memory_space=pl.ANY)] * len(after),
        out_specs=in_vmem,
        compiler_params=params(),
        cost_estimate=cost(0.1),
    )(keep_near(value), *after)


def late(train, *arrays, micros):
    subs = lax.axis_size("sub")
    dests = lax.axis_size("mod") * subs
    queries = arrays[0].shape[1]
    dealt = pl.pallas_call(
        functools.partial(late_kernel, dests, subs),
        out_shape=[pltpu.VMEM((train.shape[0] // dests, queries), bf16 if dest else f32) for dest in range(dests)],
        in_specs=[in_vmem] * (1 + len(arrays)),
        out_specs=[in_vmem] * dests,
        scratch_shapes=[pltpu.VMEM((train.shape[0], queries), f32)],
        compiler_params=params(),
        cost_estimate=cost(micros),
    )(keep_near(train), *map(keep_near, arrays))
    return [to_peer(rows, *divmod(dest, subs)) if dest else rows for dest, rows in reversed(list(enumerate(dealt)))]


def early(train, shared, mine, rest, micros):
    return pl.pallas_call(
        functools.partial(early_kernel, shared),
        out_shape=pltpu.VMEM((train.shape[0], mine.shape[1]), f32),
        in_specs=[in_vmem] * 3,
        out_specs=in_vmem,
        compiler_params=params(),
        cost_estimate=cost(micros),
    )(*map(keep_near, (train, mine, rest)))


def sum_kernel(places, counts, *refs):
    output = refs[-1]
    at = 0
    for place, count in zip(places, counts):
        total = None
        for ref in refs[at : at + count]:
            term = ref[...].astype(f32)
            total = term if total is None else total + term
        output[place] = total
        at += count


def local(query_grads, train_grads, in_inverse, out_inverse, module_map):
    half_width = query_grads.shape[2]
    mods, subs = lax.axis_size("mod"), lax.axis_size("sub")
    parts, part = lax.axis_size("groups"), lax.axis_index("groups")
    reach = min(WINDOW_HALF, (lax.axis_size("ex") - 1) // 2)
    precon = preconditioned(query_grads, in_inverse, out_inverse, module_map)

    share = 3 * half_width // (4 * parts) // 128 * 128
    shared = share * parts
    train = train_grads.reshape(train_grads.shape[0], half_width)

    offsets = [sign * far for far in range(1, reach + 1) for sign in (1, -1)]
    mine = lax.dynamic_slice_in_dim(precon, part * share, share, 0)
    added, dealt = whole(train, precon)
    rest = held(precon, shared, dealt[:1])
    carried = {offset: shifted(mine, "ex", -offset) for offset in offsets}
    common = {offset: shifted(rest, "ex", -offset) for offset in offsets}
    partial = {0: [to_peer(piece, step, 0) if step else piece for step, piece in enumerate(added)]}
    for offset in offsets:
        swapped = [shifted(carried[offset], "groups", step) for step in range(1, parts)]
        total = early(train, shared, carried[offset], common[offset], 1)
        partial[offset] = late(train, total, *swapped, micros=1)
    order = [*offsets, 0]
    counts = [len(partial[offset]) for offset in order]
    terms = [rows for offset in order for rows in partial[offset]]
    rows = train.shape[0] // (mods * subs)
    summed = pl.pallas_call(
        functools.partial(sum_kernel, [offset + reach for offset in order], counts),
        out_shape=jax.ShapeDtypeStruct((2 * reach + 1, rows, query_grads.shape[0]), f32),
        in_specs=[in_vmem] * len(terms),
        out_specs=in_vmem,
        compiler_params=params(),
        cost_estimate=cost(1),
    )(*[keep_near(term) for term in terms])
    return summed.transpose(1, 0, 2)


def solution(mesh):
    placed = (P("ex", "mod", "sub"), P(("groups", "ex"), "mod", "sub"), P(), P(), P("mod"))
    return jax.shard_map(
        local,
        mesh=mesh,
        in_specs=placed,
        out_specs=P(("groups", "ex", "mod", "sub"), None, None),
        check_vma=False,
    )
```

```python
import functools

import jax
import jax.numpy as jnp
from jax import lax
from jax.experimental import pallas as pl
from jax.experimental.pallas import tpu as pltpu
from jax.sharding import PartitionSpec as P

WINDOW_HALF = 2
PAD = 8
VMEM_LIMIT = 32 * 1024 * 1024

f32, bf16 = jnp.float32, jnp.bfloat16
in_vmem = pl.BlockSpec(memory_space=pltpu.VMEM)


def keep_near(value):
    return pltpu.with_memory_space_constraint(value, pltpu.VMEM)


def params():
    return pltpu.CompilerParams(vmem_limit_bytes=VMEM_LIMIT)


def shifted(value, axis, steps):
    count = lax.axis_size(axis)
    pairs = [(source, (source + steps) % count) for source in range(count)]
    return lax.ppermute(value, axis, pairs)


def to_peer(value, mod_step, sub_step):
    mods, subs = lax.axis_size("mod"), lax.axis_size("sub")
    pairs = []
    for mod in range(mods):
        for sub in range(subs):
            target = ((mod + mod_step) % mods) * subs + (sub + sub_step) % subs
            pairs.append((mod * subs + sub, target))
    return lax.ppermute(value, ("mod", "sub"), pairs)


def split(value):
    high = value.astype(bf16)
    return high, (value - high.astype(f32)).astype(bf16)


def nt_dot(lhs, rhs):
    return lax.dot_general(lhs, rhs, (((1,), (1,)), ((), ())), preferred_element_type=f32)


def right_rows(pair, raw, right_ref):
    width = pair.shape[1]
    queries = raw.shape[0]
    for first in range(0, raw.shape[1], 2 * width):
        pieces = [raw[:, at : at + width] for at in (first, first + width)]
        both = nt_dot(pair, jnp.concatenate(pieces, axis=0))
        both = both[:width] + both[width:]
        half = width // 2
        for index, lanes in enumerate((slice(0, queries), slice(queries, 2 * queries))):
            for row in range(2):
                at = (first // half + 2 * index + row) * (half + PAD)
                right_ref[at : at + half, :] = both[row * half : (row + 1) * half, lanes]


def first_kernel(
    map_ref, in_ref, out_ref, raw_ref, right_ref, pair_ref, left_ref, inverse_ref, rows_ref, own_ref, sems
):
    own_rows = rows_ref.shape[0]
    sub = lax.axis_index("sub")
    module = map_ref[0]
    mine = out_ref.at[module, pl.ds(pl.multiple_of(sub * own_rows, own_rows), own_rows), :]
    copies = [
        pltpu.make_async_copy(in_ref.at[module], inverse_ref, sems.at[0]),
        pltpu.make_async_copy(mine, rows_ref, sems.at[1]),
        pltpu.make_async_copy(raw_ref, own_ref, sems.at[2]),
    ]
    for copy in copies:
        copy.start()
    copies[0].wait()
    high, low = split(inverse_ref[...].T)
    high, low = high.astype(f32), low.astype(f32)
    zero = jnp.zeros_like(high)
    pair = jnp.concatenate(
        [jnp.concatenate(row, axis=1) for row in ([high, zero], [zero, high], [low, zero], [zero, low])], axis=0
    ).astype(bf16)
    pair_ref[...] = pair
    copies[1].wait()
    rows = rows_ref[...]
    swapped = jnp.concatenate([rows[:, own_rows:], rows[:, :own_rows]], axis=1)
    rows = jnp.where(sub == 0, rows, swapped)
    high, low = split(rows)
    high, low = high.astype(f32), low.astype(f32)
    left_ref[...] = jnp.concatenate(
        [jnp.concatenate(row, axis=1) for row in ([high, high], [low, jnp.zeros_like(low)])], axis=0
    ).astype(bf16)
    copies[2].wait()
    right_rows(pair, own_ref, right_ref)


def second_kernel(pair_ref, left_ref, own_ref, raw_ref, result_ref, right_ref, done_ref):
    own_rows = left_ref.shape[0] // 2
    rank_in = result_ref.shape[0] // own_rows
    step = rank_in + PAD
    right_rows(pair_ref[...], raw_ref, right_ref)
    left = left_ref[...]
    for first in range(0, rank_in, 2):
        wide = jnp.concatenate(
            [
                jnp.concatenate(
                    [
                        own_ref[pl.ds(column, own_rows, stride=step), :],
                        right_ref[pl.ds(column, own_rows, stride=step), :],
                    ],
                    axis=0,
                )
                for column in (first, first + 1)
            ],
            axis=1,
        )
        high, low = split(wide)
        both = jnp.dot(left, jnp.concatenate([high, low], axis=0), preferred_element_type=f32)
        both = both[:own_rows] + both[own_rows:]
        queries = both.shape[1] // 2
        done_ref[pl.ds(first, own_rows, stride=step), :] = both[:, :queries]
        done_ref[pl.ds(first + 1, own_rows, stride=step), :] = both[:, queries:]
    for row in range(own_rows):
        result_ref[row * rank_in : (row + 1) * rank_in, :] = done_ref[row * step : row * step + rank_in, :].astype(bf16)


def preconditioned(query_grads, in_inverse, out_inverse, module_map):
    block_rows, _, half_width = query_grads.shape
    rank_in, rank_out = in_inverse.shape[1], out_inverse.shape[1]
    own_rows = half_width // rank_in
    raw = query_grads.reshape(block_rows, half_width)
    other = shifted(raw, "sub", 1)
    anywhere = pl.BlockSpec(memory_space=pl.ANY)
    right, pair, left = pl.pallas_call(
        first_kernel,
        out_shape=(
            pltpu.VMEM((own_rows * (rank_in + PAD), block_rows), f32),
            pltpu.VMEM((4 * rank_in, 2 * rank_in), bf16),
            pltpu.VMEM((2 * own_rows, 2 * rank_out), bf16),
        ),
        in_specs=[pl.BlockSpec(memory_space=pltpu.SMEM), anywhere, anywhere, anywhere],
        out_specs=[in_vmem, in_vmem, in_vmem],
        scratch_shapes=[
            pltpu.VMEM((rank_in, rank_in), f32),
            pltpu.VMEM((own_rows, rank_out), f32),
            pltpu.VMEM((block_rows, half_width), bf16),
            pltpu.SemaphoreType.DMA((3,)),
        ],
        compiler_params=params(),
        cost_estimate=cost(2),
    )(module_map, *[pltpu.with_memory_space_constraint(x, pltpu.HBM) for x in (in_inverse, out_inverse, raw)])
    return pl.pallas_call(
        second_kernel,
        out_shape=pltpu.VMEM((half_width, block_rows), bf16),
        in_specs=[in_vmem] * 4,
        out_specs=in_vmem,
        scratch_shapes=[pltpu.VMEM((own_rows * (rank_in + PAD), block_rows), f32)] * 2,
        compiler_params=params(),
        cost_estimate=cost(2),
    )(keep_near(pair), keep_near(left), keep_near(right), keep_near(other))


def part_dot(train_ref, ref, first):
    train = train_ref[:, pl.ds(first, ref.shape[0])]
    return jnp.dot(train, ref[...], preferred_element_type=f32)


def early_kernel(shared, train_ref, mine_ref, rest_ref, *refs):
    total_ref = refs[-1]
    share = mine_ref.shape[0]
    first = pl.multiple_of(lax.axis_index("groups") * share, 128)
    total_ref[...] = part_dot(train_ref, mine_ref, first) + part_dot(train_ref, rest_ref, shared)


def deal(blocks, outputs):
    mods, subs = lax.axis_size("mod"), len(outputs)
    rows = blocks[0].shape[0] // (mods * subs)
    for sub_step, output in enumerate(outputs):
        at = 0
        for mod_step in range(mods):
            target = lax.rem(lax.axis_index("mod") + mod_step, mods) * subs
            target = target + lax.rem(lax.axis_index("sub") + sub_step, subs)
            for block in blocks:
                output[at : at + rows, :] = block[pl.ds(pl.multiple_of(target * rows, rows), rows), :]
                at += rows


def whole_kernel(train_ref, block_ref, *refs):
    refs[-1][...] = part_dot(train_ref, block_ref, 0)
    deal([refs[-1]], refs[:-1])


def late_kernel(blocks, parts, train_ref, *refs):
    inputs, outputs, sums = refs[: blocks * parts], refs[blocks * parts : -blocks], refs[-blocks:]
    for block, sum_ref in enumerate(sums):
        total_ref, *swapped = inputs[block * parts : (block + 1) * parts]
        total = total_ref[...]
        for step, ref in enumerate(swapped, 1):
            share = ref.shape[0]
            source = lax.rem(lax.axis_index("groups") + parts - step, parts)
            total = total + part_dot(train_ref, ref, pl.multiple_of(source * share, 128))
        sum_ref[...] = total
    deal(sums, outputs)


def cost(micros):
    return pl.CostEstimate(flops=int(micros * 1.15e9), bytes_accessed=0, transcendentals=0)


def add_kernel(count, *refs):
    inputs, outputs = refs[:count], refs[count:]
    rows = outputs[0].shape[0]
    for step, output in enumerate(outputs):
        total = None
        for ref in inputs:
            term = ref[step * rows : (step + 1) * rows, :]
            total = term if total is None else total + term
        output[...] = total.astype(output.dtype)


def dealt(kernel, train, blocks, arrays):
    mods, subs = lax.axis_size("mod"), lax.axis_size("sub")
    queries = arrays[0].shape[1]
    return pl.pallas_call(
        kernel,
        out_shape=[pltpu.VMEM((blocks * train.shape[0] // subs, queries), f32)] * subs,
        in_specs=[in_vmem] * (1 + len(arrays)),
        out_specs=[in_vmem] * subs,
        scratch_shapes=[pltpu.VMEM((train.shape[0], queries), f32)] * blocks,
        compiler_params=params(),
        cost_estimate=cost(1),
    )(keep_near(train), *map(keep_near, arrays))


def add_kernel(count, *refs):
    inputs, outputs = refs[:count], refs[count:]
    rows = outputs[0].shape[0]
    for step, output in enumerate(outputs):
        total = None
        for ref in inputs:
            term = ref[step * rows : (step + 1) * rows, :]
            total = term if total is None else total + term
        output[...] = total.astype(output.dtype)


def reduced(pieces):
    mods, subs = lax.axis_size("mod"), lax.axis_size("sub")
    terms = [to_peer(piece, 0, step) if step else piece for step, piece in enumerate(pieces)]
    shape = (pieces[0].shape[0] // mods, pieces[0].shape[1])
    added = pl.pallas_call(
        functools.partial(add_kernel, subs),
        out_shape=[pltpu.VMEM(shape, bf16 if step else f32) for step in range(mods)],
        in_specs=[in_vmem] * subs,
        out_specs=[in_vmem] * mods,
        compiler_params=params(),
        cost_estimate=cost(0.1),
    )(*map(keep_near, terms))
    return [to_peer(piece, step, 0) if step else piece for step, piece in enumerate(added)]


def held(value, first, after):
    def kernel(value_ref, *refs):
        refs[-1][...] = value_ref[first:, :]

    return pl.pallas_call(
        kernel,
        out_shape=pltpu.VMEM((value.shape[0] - first, value.shape[1]), value.dtype),
        in_specs=[in_vmem] + [pl.BlockSpec(memory_space=pl.ANY)] * len(after),
        out_specs=in_vmem,
        compiler_params=params(),
        cost_estimate=cost(0.1),
    )(keep_near(value), *after)


def late(train, *arrays, micros):
    subs = lax.axis_size("sub")
    dests = lax.axis_size("mod") * subs
    queries = arrays[0].shape[1]
    dealt = pl.pallas_call(
        functools.partial(late_kernel, dests, subs),
        out_shape=[pltpu.VMEM((train.shape[0] // dests, queries), bf16 if dest else f32) for dest in range(dests)],
        in_specs=[in_vmem] * (1 + len(arrays)),
        out_specs=[in_vmem] * dests,
        scratch_shapes=[pltpu.VMEM((train.shape[0], queries), f32)],
        compiler_params=params(),
        cost_estimate=cost(micros),
    )(keep_near(train), *map(keep_near, arrays))
    return [to_peer(rows, *divmod(dest, subs)) if dest else rows for dest, rows in reversed(list(enumerate(dealt)))]


def early(train, shared, mine, rest, after, micros):
    return pl.pallas_call(
        functools.partial(early_kernel, shared),
        out_shape=pltpu.VMEM((train.shape[0], mine.shape[1]), f32),
        in_specs=[in_vmem] * 3 + [pl.BlockSpec(memory_space=pl.ANY)] * len(after),
        out_specs=in_vmem,
        compiler_params=params(),
        cost_estimate=cost(micros),
    )(*map(keep_near, (train, mine, rest)), *after)


def settled(terms):
    def kernel(*refs):
        total = None
        for ref in refs[:-1]:
            term = ref[...].astype(f32)
            total = term if total is None else total + term
        refs[-1][...] = total

    return pl.pallas_call(
        kernel,
        out_shape=pltpu.VMEM(terms[0].shape, f32),
        in_specs=[in_vmem] * len(terms),
        out_specs=in_vmem,
        compiler_params=params(),
        cost_estimate=cost(0.1),
    )(*map(keep_near, terms))


def sum_kernel(places, own_place, *refs):
    output = refs[-1]
    rows = output.shape[1]
    for block, place in enumerate(places):
        total = None
        for ref in refs[:-2]:
            term = ref[block * rows : (block + 1) * rows, :].astype(f32)
            total = term if total is None else total + term
        output[place] = total
    output[own_place] = refs[-2][...]


def local(query_grads, train_grads, in_inverse, out_inverse, module_map):
    half_width = query_grads.shape[2]
    mods, subs = lax.axis_size("mod"), lax.axis_size("sub")
    parts, part = lax.axis_size("groups"), lax.axis_index("groups")
    reach = min(WINDOW_HALF, (lax.axis_size("ex") - 1) // 2)
    precon = preconditioned(query_grads, in_inverse, out_inverse, module_map)

    share = 3 * half_width // (4 * parts) // 128 * 128
    shared = share * parts
    train = train_grads.reshape(train_grads.shape[0], half_width)

    offsets = [sign * far for far in range(1, reach + 1) for sign in (1, -1)]
    mine = lax.dynamic_slice_in_dim(precon, part * share, share, 0)
    own = dealt(whole_kernel, train, 1, [precon])
    rest = held(precon, shared, own[:1])
    carried = {offset: shifted(mine, "ex", -offset) for offset in offsets}
    common = {offset: shifted(rest, "ex", -offset) for offset in offsets}
    own_sum = settled(reduced(own))
    arrays, after = [], [own_sum]
    for offset in offsets:
        arrays.append(early(train, shared, carried[offset], common[offset], after, 1))
        arrays += [shifted(carried[offset], "groups", step) for step in range(1, parts)]
    late = dealt(functools.partial(late_kernel, len(offsets), parts), train, len(offsets), arrays)
    terms = [*reduced(late), own_sum]
    rows = train.shape[0] // (mods * subs)
    summed = pl.pallas_call(
        functools.partial(sum_kernel, [offset + reach for offset in offsets], reach),
        out_shape=jax.ShapeDtypeStruct((2 * reach + 1, rows, query_grads.shape[0]), f32),
        in_specs=[in_vmem] * len(terms),
        out_specs=in_vmem,
        compiler_params=params(),
        cost_estimate=cost(1),
    )(*[keep_near(term) for term in terms])
    return summed.transpose(1, 0, 2)


def solution(mesh):
    placed = (P("ex", "mod", "sub"), P(("groups", "ex"), "mod", "sub"), P(), P(), P("mod"))
    return jax.shard_map(
        local,
        mesh=mesh,
        in_specs=placed,
        out_specs=P(("groups", "ex", "mod", "sub"), None, None),
        check_vma=False,
    )
```

```python
import functools

import jax
import jax.numpy as jnp
from jax import lax
from jax.experimental import pallas as pl
from jax.experimental.pallas import tpu as pltpu
from jax.sharding import PartitionSpec as P

WINDOW_HALF = 2
PAD = 8
VMEM_LIMIT = 32 * 1024 * 1024

f32, bf16 = jnp.float32, jnp.bfloat16
in_vmem = pl.BlockSpec(memory_space=pltpu.VMEM)


def keep_near(value):
    return pltpu.with_memory_space_constraint(value, pltpu.VMEM)


def params():
    return pltpu.CompilerParams(vmem_limit_bytes=VMEM_LIMIT)


def shifted(value, axis, steps):
    count = lax.axis_size(axis)
    pairs = [(source, (source + steps) % count) for source in range(count)]
    return lax.ppermute(value, axis, pairs)


def to_peer(value, mod_step, sub_step):
    mods, subs = lax.axis_size("mod"), lax.axis_size("sub")
    pairs = []
    for mod in range(mods):
        for sub in range(subs):
            target = ((mod + mod_step) % mods) * subs + (sub + sub_step) % subs
            pairs.append((mod * subs + sub, target))
    return lax.ppermute(value, ("mod", "sub"), pairs)


def split(value):
    high = value.astype(bf16)
    return high, (value - high.astype(f32)).astype(bf16)


def nt_dot(lhs, rhs):
    return lax.dot_general(lhs, rhs, (((1,), (1,)), ((), ())), preferred_element_type=f32)


def right_rows(pair, raw, right_ref):
    width = pair.shape[1]
    queries = raw.shape[0]
    for first in range(0, raw.shape[1], 2 * width):
        pieces = [raw[:, at : at + width] for at in (first, first + width)]
        both = nt_dot(pair, jnp.concatenate(pieces, axis=0))
        both = both[:width] + both[width:]
        half = width // 2
        for index, lanes in enumerate((slice(0, queries), slice(queries, 2 * queries))):
            for row in range(2):
                at = (first // half + 2 * index + row) * (half + PAD)
                right_ref[at : at + half, :] = both[row * half : (row + 1) * half, lanes]


def first_kernel(
    map_ref, in_ref, out_ref, raw_ref, right_ref, pair_ref, left_ref, inverse_ref, rows_ref, own_ref, sems
):
    own_rows = rows_ref.shape[0]
    sub = lax.axis_index("sub")
    module = map_ref[0]
    mine = out_ref.at[module, pl.ds(pl.multiple_of(sub * own_rows, own_rows), own_rows), :]
    copies = [
        pltpu.make_async_copy(in_ref.at[module], inverse_ref, sems.at[0]),
        pltpu.make_async_copy(mine, rows_ref, sems.at[1]),
        pltpu.make_async_copy(raw_ref, own_ref, sems.at[2]),
    ]
    for copy in copies:
        copy.start()
    copies[0].wait()
    high, low = split(inverse_ref[...].T)
    high, low = high.astype(f32), low.astype(f32)
    zero = jnp.zeros_like(high)
    pair = jnp.concatenate(
        [jnp.concatenate(row, axis=1) for row in ([high, zero], [zero, high], [low, zero], [zero, low])], axis=0
    ).astype(bf16)
    pair_ref[...] = pair
    copies[1].wait()
    rows = rows_ref[...]
    swapped = jnp.concatenate([rows[:, own_rows:], rows[:, :own_rows]], axis=1)
    rows = jnp.where(sub == 0, rows, swapped)
    high, low = split(rows)
    high, low = high.astype(f32), low.astype(f32)
    left_ref[...] = jnp.concatenate(
        [jnp.concatenate(row, axis=1) for row in ([high, high], [low, jnp.zeros_like(low)])], axis=0
    ).astype(bf16)
    copies[2].wait()
    right_rows(pair, own_ref, right_ref)


def second_kernel(pair_ref, left_ref, own_ref, raw_ref, result_ref, right_ref, done_ref):
    own_rows = left_ref.shape[0] // 2
    rank_in = result_ref.shape[0] // own_rows
    step = rank_in + PAD
    right_rows(pair_ref[...], raw_ref, right_ref)
    left = left_ref[...]
    for first in range(0, rank_in, 2):
        wide = jnp.concatenate(
            [
                jnp.concatenate(
                    [
                        own_ref[pl.ds(column, own_rows, stride=step), :],
                        right_ref[pl.ds(column, own_rows, stride=step), :],
                    ],
                    axis=0,
                )
                for column in (first, first + 1)
            ],
            axis=1,
        )
        high, low = split(wide)
        both = jnp.dot(left, jnp.concatenate([high, low], axis=0), preferred_element_type=f32)
        both = both[:own_rows] + both[own_rows:]
        queries = both.shape[1] // 2
        done_ref[pl.ds(first, own_rows, stride=step), :] = both[:, :queries]
        done_ref[pl.ds(first + 1, own_rows, stride=step), :] = both[:, queries:]
    for row in range(own_rows):
        result_ref[row * rank_in : (row + 1) * rank_in, :] = done_ref[row * step : row * step + rank_in, :].astype(bf16)


def preconditioned(query_grads, in_inverse, out_inverse, module_map):
    block_rows, _, half_width = query_grads.shape
    rank_in, rank_out = in_inverse.shape[1], out_inverse.shape[1]
    own_rows = half_width // rank_in
    raw = query_grads.reshape(block_rows, half_width)
    other = shifted(raw, "sub", 1)
    anywhere = pl.BlockSpec(memory_space=pl.ANY)
    right, pair, left = pl.pallas_call(
        first_kernel,
        out_shape=(
            pltpu.VMEM((own_rows * (rank_in + PAD), block_rows), f32),
            pltpu.VMEM((4 * rank_in, 2 * rank_in), bf16),
            pltpu.VMEM((2 * own_rows, 2 * rank_out), bf16),
        ),
        in_specs=[pl.BlockSpec(memory_space=pltpu.SMEM), anywhere, anywhere, anywhere],
        out_specs=[in_vmem, in_vmem, in_vmem],
        scratch_shapes=[
            pltpu.VMEM((rank_in, rank_in), f32),
            pltpu.VMEM((own_rows, rank_out), f32),
            pltpu.VMEM((block_rows, half_width), bf16),
            pltpu.SemaphoreType.DMA((3,)),
        ],
        compiler_params=params(),
        cost_estimate=cost(2),
    )(module_map, *[pltpu.with_memory_space_constraint(x, pltpu.HBM) for x in (in_inverse, out_inverse, raw)])
    return pl.pallas_call(
        second_kernel,
        out_shape=pltpu.VMEM((half_width, block_rows), bf16),
        in_specs=[in_vmem] * 4,
        out_specs=in_vmem,
        scratch_shapes=[pltpu.VMEM((own_rows * (rank_in + PAD), block_rows), f32)] * 2,
        compiler_params=params(),
        cost_estimate=cost(2),
    )(keep_near(pair), keep_near(left), keep_near(right), keep_near(other))


def part_dot(train_ref, ref, first):
    train = train_ref[:, pl.ds(first, ref.shape[0])]
    return jnp.dot(train, ref[...], preferred_element_type=f32)


def whole_kernel(mods, subs, train_ref, block_ref, *refs):
    outputs, sum_ref = refs[:-1], refs[-1]
    sum_ref[...] = part_dot(train_ref, block_ref, 0)
    rows = sum_ref.shape[0] // (mods * subs)
    for sub_step, output in enumerate(outputs):
        for mod_step in range(mods):
            output[mod_step * rows : (mod_step + 1) * rows, :] = sum_ref[peer_rows(mod_step, sub_step, mods, subs, rows), :]


def peer_rows(mod_step, sub_step, mods, subs, rows):
    target = lax.rem(lax.axis_index("mod") + mod_step, mods) * subs
    target = target + lax.rem(lax.axis_index("sub") + sub_step, subs)
    return pl.ds(pl.multiple_of(target * rows, rows), rows)


def score_kernel(plans, dests, train_ref, *refs):
    count = sum(len(plan) for plan in plans)
    inputs, outputs, sums = list(refs[:count]), (), refs[-len(plans) :]
    if dests:
        outputs = refs[-len(plans) - dests : -len(plans)]
    parts = lax.axis_size("groups")
    for plan, sum_ref in zip(plans, sums):
        total = None
        for kind in plan:
            ref = inputs.pop(0)
            if kind == "total":
                term = ref[...]
            elif kind == "rest":
                term = part_dot(train_ref, ref, train_ref.shape[1] - ref.shape[0])
            else:
                share = ref.shape[0]
                source = lax.rem(lax.axis_index("groups") + parts - kind, parts)
                term = part_dot(train_ref, ref, pl.multiple_of(source * share, 128))
            total = term if total is None else total + term
        sum_ref[...] = total
    mods, subs = lax.axis_size("mod"), lax.axis_size("sub")
    rows = sums[0].shape[0] // (mods * subs)
    for dest, output in enumerate(outputs):
        place = peer_rows(*divmod(dest, subs), mods, subs, rows)
        for block, sum_ref in enumerate(sums):
            output[block * rows : (block + 1) * rows, :] = sum_ref[place, :].astype(output.dtype)


def cost(micros):
    return pl.CostEstimate(flops=int(micros * 1.15e9), bytes_accessed=0, transcendentals=0)


def add_kernel(count, *refs):
    inputs, outputs = refs[:count], refs[count:]
    rows = outputs[0].shape[0]
    for step, output in enumerate(outputs):
        total = None
        for ref in inputs:
            term = ref[step * rows : (step + 1) * rows, :]
            total = term if total is None else total + term
        output[...] = total.astype(output.dtype)


def whole(train, block):
    mods, subs = lax.axis_size("mod"), lax.axis_size("sub")
    rows, queries = train.shape[0] // (mods * subs), block.shape[1]
    dealt = pl.pallas_call(
        functools.partial(whole_kernel, mods, subs),
        out_shape=[pltpu.VMEM((mods * rows, queries), f32)] * subs,
        in_specs=[in_vmem] * 2,
        out_specs=[in_vmem] * subs,
        scratch_shapes=[pltpu.VMEM((train.shape[0], queries), f32)],
        compiler_params=params(),
        cost_estimate=cost(1),
    )(keep_near(train), keep_near(block))
    terms = [to_peer(piece, 0, step) if step else piece for step, piece in enumerate(dealt)]
    added = pl.pallas_call(
        functools.partial(add_kernel, subs),
        out_shape=[pltpu.VMEM((rows, queries), bf16 if step else f32) for step in range(mods)],
        in_specs=[in_vmem] * subs,
        out_specs=[in_vmem] * mods,
        compiler_params=params(),
        cost_estimate=cost(0.1),
    )(*map(keep_near, terms))
    return added, dealt


def held(value, first, after):
    def kernel(value_ref, *refs):
        refs[-1][...] = value_ref[first:, :]

    return pl.pallas_call(
        kernel,
        out_shape=pltpu.VMEM((value.shape[0] - first, value.shape[1]), value.dtype),
        in_specs=[in_vmem] + [pl.BlockSpec(memory_space=pl.ANY)] * len(after),
        out_specs=in_vmem,
        compiler_params=params(),
        cost_estimate=cost(0.1),
    )(keep_near(value), *after)


def scored(train, plans, arrays, dests=0, after=()):
    queries = arrays[0].shape[1]
    whole_shape = (train.shape[0], queries)
    sums = [pltpu.VMEM(whole_shape, f32)] * len(plans)
    part_shape = (len(plans) * train.shape[0] // max(dests, 1), queries)
    outputs = [pltpu.VMEM(part_shape, bf16 if dest else f32) for dest in range(dests)] or sums
    return pl.pallas_call(
        functools.partial(score_kernel, plans, dests),
        out_shape=outputs,
        in_specs=[in_vmem] * (1 + len(arrays)) + [pl.BlockSpec(memory_space=pl.ANY)] * len(after),
        out_specs=[in_vmem] * len(outputs),
        scratch_shapes=sums if dests else [],
        compiler_params=params(),
        cost_estimate=cost(0.1),
    )(*map(keep_near, (train, *arrays)), *after)


def settled(terms):
    def kernel(*refs):
        total = None
        for ref in refs[:-1]:
            term = ref[...].astype(f32)
            total = term if total is None else total + term
        refs[-1][...] = total

    return pl.pallas_call(
        kernel,
        out_shape=pltpu.VMEM(terms[0].shape, f32),
        in_specs=[in_vmem] * len(terms),
        out_specs=in_vmem,
        compiler_params=params(),
        cost_estimate=cost(0.1),
    )(*map(keep_near, terms))


def sum_kernel(places, counts, *refs):
    output = refs[-1]
    rows = output.shape[1]
    at = 0
    for blocks, count in zip(places, counts):
        for block, place in enumerate(blocks):
            total = None
            for ref in refs[at : at + count]:
                term = ref[block * rows : (block + 1) * rows, :].astype(f32)
                total = term if total is None else total + term
            output[place] = total
        at += count


def local(query_grads, train_grads, in_inverse, out_inverse, module_map):
    half_width = query_grads.shape[2]
    mods, subs = lax.axis_size("mod"), lax.axis_size("sub")
    parts, part = lax.axis_size("groups"), lax.axis_index("groups")
    reach = min(WINDOW_HALF, (lax.axis_size("ex") - 1) // 2)
    precon = preconditioned(query_grads, in_inverse, out_inverse, module_map)

    share = 5 * half_width // (8 * parts) // 128 * 128
    shared = share * parts
    train = train_grads.reshape(train_grads.shape[0], half_width)

    offsets = [sign * far for far in range(1, reach + 1) for sign in (-1, 1)]
    mine = lax.dynamic_slice_in_dim(precon, part * share, share, 0)
    added, dealt = whole(train, precon)
    rest = held(precon, shared, dealt[:1])
    carried = {offset: shifted(mine, "ex", -offset) for offset in offsets}
    common = {offset: shifted(rest, "ex", -offset) for offset in offsets}
    *others, last = offsets
    plans = [[0, "rest"] for offset in others] + [[0]]
    arrays = [piece for offset in others for piece in (carried[offset], common[offset])] + [carried[last]]
    own = settled([to_peer(piece, step, 0) if step else piece for step, piece in enumerate(added)])
    totals = scored(train, plans, arrays, after=[own])
    plans = [["total", *range(1, parts)] for offset in offsets]
    arrays = []
    for offset, total in zip(offsets, totals):
        arrays += [total, *[shifted(carried[offset], "groups", step) for step in range(1, parts)]]
    totals = scored(train, plans, arrays)
    plans = [["total"] for offset in others] + [["total", "rest"]]
    partial = scored(train, plans, [*totals, common[last]], mods * subs)
    terms = [to_peer(rows, *divmod(dest, subs)) if dest else rows for dest, rows in reversed(list(enumerate(partial)))]
    terms.append(own)
    rows = train.shape[0] // (mods * subs)
    summed = pl.pallas_call(
        functools.partial(sum_kernel, [[offset + reach for offset in offsets], [reach]], [mods * subs, 1]),
        out_shape=jax.ShapeDtypeStruct((2 * reach + 1, rows, query_grads.shape[0]), f32),
        in_specs=[in_vmem] * len(terms),
        out_specs=in_vmem,
        compiler_params=params(),
        cost_estimate=cost(1),
    )(*[keep_near(term) for term in terms])
    return summed.transpose(1, 0, 2)


def solution(mesh):
    placed = (P("ex", "mod", "sub"), P(("groups", "ex"), "mod", "sub"), P(), P(), P("mod"))
    return jax.shard_map(
        local,
        mesh=mesh,
        in_specs=placed,
        out_specs=P(("groups", "ex", "mod", "sub"), None, None),
        check_vma=False,
    )
```

```python
import functools

import jax
import jax.numpy as jnp
from jax import lax
from jax.experimental import pallas as pl
from jax.experimental.pallas import tpu as pltpu
from jax.sharding import PartitionSpec as P

WINDOW_HALF = 2
PAD = 8
VMEM_LIMIT = 32 * 1024 * 1024

f32, bf16 = jnp.float32, jnp.bfloat16
in_vmem = pl.BlockSpec(memory_space=pltpu.VMEM)


def keep_near(value):
    return pltpu.with_memory_space_constraint(value, pltpu.VMEM)


def params():
    return pltpu.CompilerParams(vmem_limit_bytes=VMEM_LIMIT)


def shifted(value, axis, steps):
    count = lax.axis_size(axis)
    pairs = [(source, (source + steps) % count) for source in range(count)]
    return lax.ppermute(value, axis, pairs)


def to_peer(value, mod_step, sub_step):
    mods, subs = lax.axis_size("mod"), lax.axis_size("sub")
    pairs = []
    for mod in range(mods):
        for sub in range(subs):
            target = ((mod + mod_step) % mods) * subs + (sub + sub_step) % subs
            pairs.append((mod * subs + sub, target))
    return lax.ppermute(value, ("mod", "sub"), pairs)


def split(value):
    high = value.astype(bf16)
    return high, (value - high.astype(f32)).astype(bf16)


def nt_dot(lhs, rhs):
    return lax.dot_general(lhs, rhs, (((1,), (1,)), ((), ())), preferred_element_type=f32)


def right_rows(pair, raw, right_ref):
    width = pair.shape[1]
    queries = raw.shape[0]
    for first in range(0, raw.shape[1], 2 * width):
        pieces = [raw[:, at : at + width] for at in (first, first + width)]
        both = nt_dot(pair, jnp.concatenate(pieces, axis=0))
        both = both[:width] + both[width:]
        half = width // 2
        for index, lanes in enumerate((slice(0, queries), slice(queries, 2 * queries))):
            for row in range(2):
                at = (first // half + 2 * index + row) * (half + PAD)
                right_ref[at : at + half, :] = both[row * half : (row + 1) * half, lanes]


def first_kernel(
    map_ref, in_ref, out_ref, raw_ref, right_ref, pair_ref, left_ref, inverse_ref, rows_ref, own_ref, sems
):
    own_rows = rows_ref.shape[0]
    sub = lax.axis_index("sub")
    module = map_ref[0]
    mine = out_ref.at[module, pl.ds(pl.multiple_of(sub * own_rows, own_rows), own_rows), :]
    copies = [
        pltpu.make_async_copy(in_ref.at[module], inverse_ref, sems.at[0]),
        pltpu.make_async_copy(mine, rows_ref, sems.at[1]),
        pltpu.make_async_copy(raw_ref, own_ref, sems.at[2]),
    ]
    for copy in copies:
        copy.start()
    copies[0].wait()
    high, low = split(inverse_ref[...].T)
    high, low = high.astype(f32), low.astype(f32)
    zero = jnp.zeros_like(high)
    pair = jnp.concatenate(
        [jnp.concatenate(row, axis=1) for row in ([high, zero], [zero, high], [low, zero], [zero, low])], axis=0
    ).astype(bf16)
    pair_ref[...] = pair
    copies[1].wait()
    rows = rows_ref[...]
    swapped = jnp.concatenate([rows[:, own_rows:], rows[:, :own_rows]], axis=1)
    rows = jnp.where(sub == 0, rows, swapped)
    high, low = split(rows)
    high, low = high.astype(f32), low.astype(f32)
    left_ref[...] = jnp.concatenate(
        [jnp.concatenate(row, axis=1) for row in ([high, high], [low, jnp.zeros_like(low)])], axis=0
    ).astype(bf16)
    copies[2].wait()
    right_rows(pair, own_ref, right_ref)


def second_kernel(pair_ref, left_ref, own_ref, raw_ref, result_ref, right_ref, done_ref):
    own_rows = left_ref.shape[0] // 2
    rank_in = result_ref.shape[0] // own_rows
    step = rank_in + PAD
    right_rows(pair_ref[...], raw_ref, right_ref)
    left = left_ref[...]
    for first in range(0, rank_in, 2):
        wide = jnp.concatenate(
            [
                jnp.concatenate(
                    [
                        own_ref[pl.ds(column, own_rows, stride=step), :],
                        right_ref[pl.ds(column, own_rows, stride=step), :],
                    ],
                    axis=0,
                )
                for column in (first, first + 1)
            ],
            axis=1,
        )
        high, low = split(wide)
        both = jnp.dot(left, jnp.concatenate([high, low], axis=0), preferred_element_type=f32)
        both = both[:own_rows] + both[own_rows:]
        queries = both.shape[1] // 2
        done_ref[pl.ds(first, own_rows, stride=step), :] = both[:, :queries]
        done_ref[pl.ds(first + 1, own_rows, stride=step), :] = both[:, queries:]
    for row in range(own_rows):
        result_ref[row * rank_in : (row + 1) * rank_in, :] = done_ref[row * step : row * step + rank_in, :].astype(bf16)


def preconditioned(query_grads, in_inverse, out_inverse, module_map):
    block_rows, _, half_width = query_grads.shape
    rank_in, rank_out = in_inverse.shape[1], out_inverse.shape[1]
    own_rows = half_width // rank_in
    raw = query_grads.reshape(block_rows, half_width)
    other = shifted(raw, "sub", 1)
    anywhere = pl.BlockSpec(memory_space=pl.ANY)
    right, pair, left = pl.pallas_call(
        first_kernel,
        out_shape=(
            pltpu.VMEM((own_rows * (rank_in + PAD), block_rows), f32),
            pltpu.VMEM((4 * rank_in, 2 * rank_in), bf16),
            pltpu.VMEM((2 * own_rows, 2 * rank_out), bf16),
        ),
        in_specs=[pl.BlockSpec(memory_space=pltpu.SMEM), anywhere, anywhere, anywhere],
        out_specs=[in_vmem, in_vmem, in_vmem],
        scratch_shapes=[
            pltpu.VMEM((rank_in, rank_in), f32),
            pltpu.VMEM((own_rows, rank_out), f32),
            pltpu.VMEM((block_rows, half_width), bf16),
            pltpu.SemaphoreType.DMA((3,)),
        ],
        compiler_params=params(),
        cost_estimate=cost(2),
    )(module_map, *[pltpu.with_memory_space_constraint(x, pltpu.HBM) for x in (in_inverse, out_inverse, raw)])
    return pl.pallas_call(
        second_kernel,
        out_shape=pltpu.VMEM((half_width, block_rows), bf16),
        in_specs=[in_vmem] * 4,
        out_specs=in_vmem,
        scratch_shapes=[pltpu.VMEM((own_rows * (rank_in + PAD), block_rows), f32)] * 2,
        compiler_params=params(),
        cost_estimate=cost(2),
    )(keep_near(pair), keep_near(left), keep_near(right), keep_near(other))


def part_dot(train_ref, ref, first):
    train = train_ref[:, pl.ds(first, ref.shape[0])]
    return jnp.dot(train, ref[...], preferred_element_type=f32)


def whole_kernel(mods, subs, train_ref, block_ref, *refs):
    outputs, sum_ref = refs[:-1], refs[-1]
    sum_ref[...] = part_dot(train_ref, block_ref, 0)
    rows = sum_ref.shape[0] // (mods * subs)
    for sub_step, output in enumerate(outputs):
        for mod_step in range(mods):
            output[mod_step * rows : (mod_step + 1) * rows, :] = sum_ref[peer_rows(mod_step, sub_step, mods, subs, rows), :]


def peer_rows(mod_step, sub_step, mods, subs, rows):
    target = lax.rem(lax.axis_index("mod") + mod_step, mods) * subs
    target = target + lax.rem(lax.axis_index("sub") + sub_step, subs)
    return pl.ds(pl.multiple_of(target * rows, rows), rows)


def score_kernel(plans, dests, train_ref, *refs):
    count = sum(len(plan) for plan in plans)
    inputs, outputs, sums = list(refs[:count]), (), refs[-len(plans) :]
    if dests:
        outputs = refs[-len(plans) - dests : -len(plans)]
    parts = lax.axis_size("groups")
    for plan, sum_ref in zip(plans, sums):
        total = None
        for kind in plan:
            ref = inputs.pop(0)
            if kind == "total":
                term = ref[...]
            elif kind == "rest":
                term = part_dot(train_ref, ref, train_ref.shape[1] - ref.shape[0])
            else:
                share = ref.shape[0]
                source = lax.rem(lax.axis_index("groups") + parts - kind, parts)
                term = part_dot(train_ref, ref, pl.multiple_of(source * share, 128))
            total = term if total is None else total + term
        sum_ref[...] = total
    mods, subs = lax.axis_size("mod"), lax.axis_size("sub")
    rows = sums[0].shape[0] // (mods * subs)
    for dest, output in enumerate(outputs):
        place = peer_rows(*divmod(dest, subs), mods, subs, rows)
        for block, sum_ref in enumerate(sums):
            output[block * rows : (block + 1) * rows, :] = sum_ref[place, :].astype(output.dtype)


def cost(micros):
    return pl.CostEstimate(flops=int(micros * 1.15e9), bytes_accessed=0, transcendentals=0)


def add_kernel(count, *refs):
    inputs, outputs = refs[:count], refs[count:]
    rows = outputs[0].shape[0]
    for step, output in enumerate(outputs):
        total = None
        for ref in inputs:
            term = ref[step * rows : (step + 1) * rows, :]
            total = term if total is None else total + term
        output[...] = total.astype(output.dtype)


def whole(train, block):
    mods, subs = lax.axis_size("mod"), lax.axis_size("sub")
    rows, queries = train.shape[0] // (mods * subs), block.shape[1]
    dealt = pl.pallas_call(
        functools.partial(whole_kernel, mods, subs),
        out_shape=[pltpu.VMEM((mods * rows, queries), f32)] * subs,
        in_specs=[in_vmem] * 2,
        out_specs=[in_vmem] * subs,
        scratch_shapes=[pltpu.VMEM((train.shape[0], queries), f32)],
        compiler_params=params(),
        cost_estimate=cost(1),
    )(keep_near(train), keep_near(block))
    terms = [to_peer(piece, 0, step) if step else piece for step, piece in enumerate(dealt)]
    added = pl.pallas_call(
        functools.partial(add_kernel, subs),
        out_shape=[pltpu.VMEM((rows, queries), bf16 if step else f32) for step in range(mods)],
        in_specs=[in_vmem] * subs,
        out_specs=[in_vmem] * mods,
        compiler_params=params(),
        cost_estimate=cost(0.1),
    )(*map(keep_near, terms))
    return added, dealt


def held(value, first, after):
    def kernel(value_ref, *refs):
        refs[-1][...] = value_ref[first:, :]

    return pl.pallas_call(
        kernel,
        out_shape=pltpu.VMEM((value.shape[0] - first, value.shape[1]), value.dtype),
        in_specs=[in_vmem] + [pl.BlockSpec(memory_space=pl.ANY)] * len(after),
        out_specs=in_vmem,
        compiler_params=params(),
        cost_estimate=cost(0.1),
    )(keep_near(value), *after)


def scored(train, plans, arrays, dests=0, after=()):
    queries = arrays[0].shape[1]
    whole_shape = (train.shape[0], queries)
    sums = [pltpu.VMEM(whole_shape, f32)] * len(plans)
    part_shape = (len(plans) * train.shape[0] // max(dests, 1), queries)
    outputs = [pltpu.VMEM(part_shape, bf16 if dest else f32) for dest in range(dests)] or sums
    return pl.pallas_call(
        functools.partial(score_kernel, plans, dests),
        out_shape=outputs,
        in_specs=[in_vmem] * (1 + len(arrays)) + [pl.BlockSpec(memory_space=pl.ANY)] * len(after),
        out_specs=[in_vmem] * len(outputs),
        scratch_shapes=sums if dests else [],
        compiler_params=params(),
        cost_estimate=cost(0.1),
    )(*map(keep_near, (train, *arrays)), *after)


def settled(terms):
    def kernel(*refs):
        total = None
        for ref in refs[:-1]:
            term = ref[...].astype(f32)
            total = term if total is None else total + term
        refs[-1][...] = total

    return pl.pallas_call(
        kernel,
        out_shape=pltpu.VMEM(terms[0].shape, f32),
        in_specs=[in_vmem] * len(terms),
        out_specs=in_vmem,
        compiler_params=params(),
        cost_estimate=cost(0.1),
    )(*map(keep_near, terms))


def sum_kernel(places, counts, *refs):
    output = refs[-1]
    rows = output.shape[1]
    at = 0
    for blocks, count in zip(places, counts):
        for block, place in enumerate(blocks):
            total = None
            for ref in refs[at : at + count]:
                term = ref[block * rows : (block + 1) * rows, :].astype(f32)
                total = term if total is None else total + term
            output[place] = total
        at += count


def local(query_grads, train_grads, in_inverse, out_inverse, module_map):
    half_width = query_grads.shape[2]
    mods, subs = lax.axis_size("mod"), lax.axis_size("sub")
    parts, part = lax.axis_size("groups"), lax.axis_index("groups")
    reach = min(WINDOW_HALF, (lax.axis_size("ex") - 1) // 2)
    precon = preconditioned(query_grads, in_inverse, out_inverse, module_map)

    share = 5 * half_width // (8 * parts) // 128 * 128
    shared = share * parts
    train = train_grads.reshape(train_grads.shape[0], half_width)

    offsets = [sign * far for far in range(1, reach + 1) for sign in (1, -1)]
    mine = lax.dynamic_slice_in_dim(precon, part * share, share, 0)
    added, dealt = whole(train, precon)
    rest = held(precon, shared, dealt[:1])
    carried = {offset: shifted(mine, "ex", -offset) for offset in offsets}
    common = {offset: shifted(rest, "ex", -offset) for offset in offsets}
    own = settled([to_peer(piece, step, 0) if step else piece for step, piece in enumerate(added)])
    terms = []
    for offset in offsets:
        swaps = [shifted(carried[offset], "groups", step) for step in range(1, parts)]
        pieces = [(["rest"], [common[offset]]), (list(range(1, parts)), swaps)]
        if offset == offsets[0]:
            pieces.reverse()
        (kinds, arrays), (late_kinds, late_arrays) = pieces
        (total,) = scored(train, [[0, *kinds]], [carried[offset], *arrays], after=[own])
        partial = scored(train, [["total", *late_kinds]], [total, *late_arrays], mods * subs)
        terms += [to_peer(rows, *divmod(dest, subs)) if dest else rows for dest, rows in reversed(list(enumerate(partial)))]
    terms.append(own)
    rows = train.shape[0] // (mods * subs)
    summed = pl.pallas_call(
        functools.partial(sum_kernel, [[offset + reach] for offset in [*offsets, 0]], [mods * subs] * len(offsets) + [1]),
        out_shape=jax.ShapeDtypeStruct((2 * reach + 1, rows, query_grads.shape[0]), f32),
        in_specs=[in_vmem] * len(terms),
        out_specs=in_vmem,
        compiler_params=params(),
        cost_estimate=cost(1),
    )(*[keep_near(term) for term in terms])
    return summed.transpose(1, 0, 2)


def solution(mesh):
    placed = (P("ex", "mod", "sub"), P(("groups", "ex"), "mod", "sub"), P(), P(), P("mod"))
    return jax.shard_map(
        local,
        mesh=mesh,
        in_specs=placed,
        out_specs=P(("groups", "ex", "mod", "sub"), None, None),
        check_vma=False,
    )
```

```python
import functools

import jax
import jax.numpy as jnp
from jax import lax
from jax.experimental import pallas as pl
from jax.experimental.pallas import tpu as pltpu
from jax.sharding import PartitionSpec as P

WINDOW_HALF = 2
PAD = 8
VMEM_LIMIT = 32 * 1024 * 1024

f32, bf16 = jnp.float32, jnp.bfloat16
in_vmem = pl.BlockSpec(memory_space=pltpu.VMEM)


def keep_near(value):
    return pltpu.with_memory_space_constraint(value, pltpu.VMEM)


def params():
    return pltpu.CompilerParams(vmem_limit_bytes=VMEM_LIMIT)


def shifted(value, axis, steps):
    count = lax.axis_size(axis)
    pairs = [(source, (source + steps) % count) for source in range(count)]
    return lax.ppermute(value, axis, pairs)


def to_peer(value, mod_step, sub_step):
    mods, subs = lax.axis_size("mod"), lax.axis_size("sub")
    pairs = []
    for mod in range(mods):
        for sub in range(subs):
            target = ((mod + mod_step) % mods) * subs + (sub + sub_step) % subs
            pairs.append((mod * subs + sub, target))
    return lax.ppermute(value, ("mod", "sub"), pairs)


def split(value):
    high = value.astype(bf16)
    return high, (value - high.astype(f32)).astype(bf16)


def nt_dot(lhs, rhs):
    return lax.dot_general(lhs, rhs, (((1,), (1,)), ((), ())), preferred_element_type=f32)


def right_rows(pair, raw, right_ref):
    width = pair.shape[1]
    queries = raw.shape[0]
    for first in range(0, raw.shape[1], 2 * width):
        pieces = [raw[:, at : at + width] for at in (first, first + width)]
        both = nt_dot(pair, jnp.concatenate(pieces, axis=0))
        both = both[:width] + both[width:]
        half = width // 2
        for index, lanes in enumerate((slice(0, queries), slice(queries, 2 * queries))):
            for row in range(2):
                at = (first // half + 2 * index + row) * (half + PAD)
                right_ref[at : at + half, :] = both[row * half : (row + 1) * half, lanes]


def first_kernel(
    map_ref, in_ref, out_ref, raw_ref, right_ref, pair_ref, left_ref, inverse_ref, rows_ref, own_ref, sems
):
    own_rows = rows_ref.shape[0]
    sub = lax.axis_index("sub")
    module = map_ref[0]
    mine = out_ref.at[module, pl.ds(pl.multiple_of(sub * own_rows, own_rows), own_rows), :]
    copies = [
        pltpu.make_async_copy(in_ref.at[module], inverse_ref, sems.at[0]),
        pltpu.make_async_copy(mine, rows_ref, sems.at[1]),
        pltpu.make_async_copy(raw_ref, own_ref, sems.at[2]),
    ]
    for copy in copies:
        copy.start()
    copies[0].wait()
    high, low = split(inverse_ref[...].T)
    high, low = high.astype(f32), low.astype(f32)
    zero = jnp.zeros_like(high)
    pair = jnp.concatenate(
        [jnp.concatenate(row, axis=1) for row in ([high, zero], [zero, high], [low, zero], [zero, low])], axis=0
    ).astype(bf16)
    pair_ref[...] = pair
    copies[1].wait()
    rows = rows_ref[...]
    swapped = jnp.concatenate([rows[:, own_rows:], rows[:, :own_rows]], axis=1)
    rows = jnp.where(sub == 0, rows, swapped)
    high, low = split(rows)
    high, low = high.astype(f32), low.astype(f32)
    left_ref[...] = jnp.concatenate(
        [jnp.concatenate(row, axis=1) for row in ([high, high], [low, jnp.zeros_like(low)])], axis=0
    ).astype(bf16)
    copies[2].wait()
    right_rows(pair, own_ref, right_ref)


def second_kernel(pair_ref, left_ref, own_ref, raw_ref, result_ref, right_ref, done_ref):
    own_rows = left_ref.shape[0] // 2
    rank_in = result_ref.shape[0] // own_rows
    step = rank_in + PAD
    right_rows(pair_ref[...], raw_ref, right_ref)
    left = left_ref[...]
    for first in range(0, rank_in, 2):
        wide = jnp.concatenate(
            [
                jnp.concatenate(
                    [
                        own_ref[pl.ds(column, own_rows, stride=step), :],
                        right_ref[pl.ds(column, own_rows, stride=step), :],
                    ],
                    axis=0,
                )
                for column in (first, first + 1)
            ],
            axis=1,
        )
        high, low = split(wide)
        both = jnp.dot(left, jnp.concatenate([high, low], axis=0), preferred_element_type=f32)
        both = both[:own_rows] + both[own_rows:]
        queries = both.shape[1] // 2
        done_ref[pl.ds(first, own_rows, stride=step), :] = both[:, :queries]
        done_ref[pl.ds(first + 1, own_rows, stride=step), :] = both[:, queries:]
    for row in range(own_rows):
        result_ref[row * rank_in : (row + 1) * rank_in, :] = done_ref[row * step : row * step + rank_in, :].astype(bf16)


def preconditioned(query_grads, in_inverse, out_inverse, module_map):
    block_rows, _, half_width = query_grads.shape
    rank_in, rank_out = in_inverse.shape[1], out_inverse.shape[1]
    own_rows = half_width // rank_in
    raw = query_grads.reshape(block_rows, half_width)
    other = shifted(raw, "sub", 1)
    anywhere = pl.BlockSpec(memory_space=pl.ANY)
    right, pair, left = pl.pallas_call(
        first_kernel,
        out_shape=(
            pltpu.VMEM((own_rows * (rank_in + PAD), block_rows), f32),
            pltpu.VMEM((4 * rank_in, 2 * rank_in), bf16),
            pltpu.VMEM((2 * own_rows, 2 * rank_out), bf16),
        ),
        in_specs=[pl.BlockSpec(memory_space=pltpu.SMEM), anywhere, anywhere, anywhere],
        out_specs=[in_vmem, in_vmem, in_vmem],
        scratch_shapes=[
            pltpu.VMEM((rank_in, rank_in), f32),
            pltpu.VMEM((own_rows, rank_out), f32),
            pltpu.VMEM((block_rows, half_width), bf16),
            pltpu.SemaphoreType.DMA((3,)),
        ],
        compiler_params=params(),
        cost_estimate=cost(2),
    )(module_map, *[pltpu.with_memory_space_constraint(x, pltpu.HBM) for x in (in_inverse, out_inverse, raw)])
    return pl.pallas_call(
        second_kernel,
        out_shape=pltpu.VMEM((half_width, block_rows), bf16),
        in_specs=[in_vmem] * 4,
        out_specs=in_vmem,
        scratch_shapes=[pltpu.VMEM((own_rows * (rank_in + PAD), block_rows), f32)] * 2,
        compiler_params=params(),
        cost_estimate=cost(2),
    )(keep_near(pair), keep_near(left), keep_near(right), keep_near(other))


def part_dot(train_ref, ref, first):
    train = train_ref[:, pl.ds(first, ref.shape[0])]
    return jnp.dot(train, ref[...], preferred_element_type=f32)


def whole_kernel(mods, subs, train_ref, block_ref, *refs):
    outputs, sum_ref = refs[:-1], refs[-1]
    sum_ref[...] = part_dot(train_ref, block_ref, 0)
    rows = sum_ref.shape[0] // (mods * subs)
    for sub_step, output in enumerate(outputs):
        for mod_step in range(mods):
            output[mod_step * rows : (mod_step + 1) * rows, :] = sum_ref[peer_rows(mod_step, sub_step, mods, subs, rows), :].astype(output.dtype)


def peer_rows(mod_step, sub_step, mods, subs, rows):
    target = lax.rem(lax.axis_index("mod") + mod_step, mods) * subs
    target = target + lax.rem(lax.axis_index("sub") + sub_step, subs)
    return pl.ds(pl.multiple_of(target * rows, rows), rows)


def score_kernel(plans, dests, train_ref, *refs):
    count = sum(len(plan) for plan in plans)
    inputs, outputs, sums = list(refs[:count]), (), refs[-len(plans) :]
    if dests:
        outputs = refs[-len(plans) - dests : -len(plans)]
    parts = lax.axis_size("groups")
    for plan, sum_ref in zip(plans, sums):
        total = None
        for kind in plan:
            ref = inputs.pop(0)
            if kind == "total":
                term = ref[...]
            elif kind == "rest":
                term = part_dot(train_ref, ref, train_ref.shape[1] - ref.shape[0])
            else:
                share = ref.shape[0]
                source = lax.rem(lax.axis_index("groups") + parts - kind, parts)
                term = part_dot(train_ref, ref, pl.multiple_of(source * share, 128))
            total = term if total is None else total + term
        sum_ref[...] = total
    mods, subs = lax.axis_size("mod"), lax.axis_size("sub")
    rows = sums[0].shape[0] // (mods * subs)
    for dest, output in enumerate(outputs):
        place = peer_rows(*divmod(dest, subs), mods, subs, rows)
        for block, sum_ref in enumerate(sums):
            output[block * rows : (block + 1) * rows, :] = sum_ref[place, :].astype(output.dtype)


def cost(micros):
    return pl.CostEstimate(flops=int(micros * 1.15e9), bytes_accessed=0, transcendentals=0)


def add_kernel(count, *refs):
    inputs, outputs = refs[:count], refs[count:]
    rows = outputs[0].shape[0]
    for step, output in enumerate(outputs):
        total = None
        for ref in inputs:
            term = ref[step * rows : (step + 1) * rows, :].astype(f32)
            total = term if total is None else total + term
        output[...] = total.astype(output.dtype)


def whole(train, block):
    mods, subs = lax.axis_size("mod"), lax.axis_size("sub")
    rows, queries = train.shape[0] // (mods * subs), block.shape[1]
    dealt = pl.pallas_call(
        functools.partial(whole_kernel, mods, subs),
        out_shape=[pltpu.VMEM((mods * rows, queries), bf16 if step else f32) for step in range(subs)],
        in_specs=[in_vmem] * 2,
        out_specs=[in_vmem] * subs,
        scratch_shapes=[pltpu.VMEM((train.shape[0], queries), f32)],
        compiler_params=params(),
        cost_estimate=cost(1),
    )(keep_near(train), keep_near(block))
    terms = [to_peer(piece, 0, step) if step else piece for step, piece in enumerate(dealt)]
    added = pl.pallas_call(
        functools.partial(add_kernel, subs),
        out_shape=[pltpu.VMEM((rows, queries), f32)] * mods,
        in_specs=[in_vmem] * subs,
        out_specs=[in_vmem] * mods,
        compiler_params=params(),
        cost_estimate=cost(0.1),
    )(*map(keep_near, terms))
    return added, dealt


def held(value, first, after):
    def kernel(value_ref, *refs):
        refs[-1][...] = value_ref[first:, :]

    return pl.pallas_call(
        kernel,
        out_shape=pltpu.VMEM((value.shape[0] - first, value.shape[1]), value.dtype),
        in_specs=[in_vmem] + [pl.BlockSpec(memory_space=pl.ANY)] * len(after),
        out_specs=in_vmem,
        compiler_params=params(),
        cost_estimate=cost(0.1),
    )(keep_near(value), *after)


def scored(train, plans, arrays, dests=0, after=()):
    queries = arrays[0].shape[1]
    whole_shape = (train.shape[0], queries)
    sums = [pltpu.VMEM(whole_shape, f32)] * len(plans)
    part_shape = (len(plans) * train.shape[0] // max(dests, 1), queries)
    outputs = [pltpu.VMEM(part_shape, bf16 if dest else f32) for dest in range(dests)] or sums
    return pl.pallas_call(
        functools.partial(score_kernel, plans, dests),
        out_shape=outputs,
        in_specs=[in_vmem] * (1 + len(arrays)) + [pl.BlockSpec(memory_space=pl.ANY)] * len(after),
        out_specs=[in_vmem] * len(outputs),
        scratch_shapes=sums if dests else [],
        compiler_params=params(),
        cost_estimate=cost(0.1),
    )(*map(keep_near, (train, *arrays)), *after)


def settled(terms):
    def kernel(*refs):
        total = None
        for ref in refs[:-1]:
            term = ref[...].astype(f32)
            total = term if total is None else total + term
        refs[-1][...] = total

    return pl.pallas_call(
        kernel,
        out_shape=pltpu.VMEM(terms[0].shape, f32),
        in_specs=[in_vmem] * len(terms),
        out_specs=in_vmem,
        compiler_params=params(),
        cost_estimate=cost(0.1),
    )(*map(keep_near, terms))


def sum_kernel(places, counts, *refs):
    output = refs[-1]
    rows = output.shape[1]
    at = 0
    for blocks, count in zip(places, counts):
        for block, place in enumerate(blocks):
            total = None
            for ref in refs[at : at + count]:
                term = ref[block * rows : (block + 1) * rows, :].astype(f32)
                total = term if total is None else total + term
            output[place] = total
        at += count


def local(query_grads, train_grads, in_inverse, out_inverse, module_map):
    half_width = query_grads.shape[2]
    mods, subs = lax.axis_size("mod"), lax.axis_size("sub")
    parts, part = lax.axis_size("groups"), lax.axis_index("groups")
    reach = min(WINDOW_HALF, (lax.axis_size("ex") - 1) // 2)
    precon = preconditioned(query_grads, in_inverse, out_inverse, module_map)

    share = 5 * half_width // (8 * parts) // 128 * 128
    shared = share * parts
    train = train_grads.reshape(train_grads.shape[0], half_width)

    offsets = [sign * far for far in range(1, reach + 1) for sign in (-1, 1)]
    mine = lax.dynamic_slice_in_dim(precon, part * share, share, 0)
    added, dealt = whole(train, precon)
    rest = held(precon, shared, added[:1])
    carried = {offset: shifted(mine, "ex", -offset) for offset in offsets}
    common = {offset: shifted(rest, "ex", -offset) for offset in offsets}
    *others, last = offsets
    plans = [[0, "rest"] for offset in others] + [[0]]
    arrays = [piece for offset in others for piece in (carried[offset], common[offset])] + [carried[last]]
    own = settled([to_peer(piece, step, 0) if step else piece for step, piece in enumerate(added)])
    totals = scored(train, plans, arrays, after=[own])
    plans = [["total", *range(1, parts)] for offset in offsets]
    arrays = []
    for offset, total in zip(offsets, totals):
        arrays += [total, *[shifted(carried[offset], "groups", step) for step in range(1, parts)]]
    totals = scored(train, plans, arrays)
    plans = [["total"] for offset in others] + [["total", "rest"]]
    partial = scored(train, plans, [*totals, common[last]], mods * subs)
    terms = [to_peer(rows, *divmod(dest, subs)) if dest else rows for dest, rows in reversed(list(enumerate(partial)))]
    terms.append(own)
    rows = train.shape[0] // (mods * subs)
    summed = pl.pallas_call(
        functools.partial(sum_kernel, [[offset + reach for offset in offsets], [reach]], [mods * subs, 1]),
        out_shape=jax.ShapeDtypeStruct((2 * reach + 1, rows, query_grads.shape[0]), f32),
        in_specs=[in_vmem] * len(terms),
        out_specs=in_vmem,
        compiler_params=params(),
        cost_estimate=cost(1),
    )(*[keep_near(term) for term in terms])
    return summed.transpose(1, 0, 2)


def solution(mesh):
    placed = (P("ex", "mod", "sub"), P(("groups", "ex"), "mod", "sub"), P(), P(), P("mod"))
    return jax.shard_map(
        local,
        mesh=mesh,
        in_specs=placed,
        out_specs=P(("groups", "ex", "mod", "sub"), None, None),
        check_vma=False,
    )
```

```python
import functools

import jax
import jax.numpy as jnp
from jax import lax
from jax.experimental import pallas as pl
from jax.experimental.pallas import tpu as pltpu
from jax.sharding import PartitionSpec as P

WINDOW_HALF = 2
PAD = 8
VMEM_LIMIT = 32 * 1024 * 1024

f32, bf16 = jnp.float32, jnp.bfloat16
in_vmem = pl.BlockSpec(memory_space=pltpu.VMEM)


def keep_near(value):
    return pltpu.with_memory_space_constraint(value, pltpu.VMEM)


def params():
    return pltpu.CompilerParams(vmem_limit_bytes=VMEM_LIMIT)


def shifted(value, axis, steps):
    count = lax.axis_size(axis)
    pairs = [(source, (source + steps) % count) for source in range(count)]
    return lax.ppermute(value, axis, pairs)


def to_peer(value, mod_step, sub_step):
    mods, subs = lax.axis_size("mod"), lax.axis_size("sub")
    pairs = []
    for mod in range(mods):
        for sub in range(subs):
            target = ((mod + mod_step) % mods) * subs + (sub + sub_step) % subs
            pairs.append((mod * subs + sub, target))
    return lax.ppermute(value, ("mod", "sub"), pairs)


def split(value):
    high = value.astype(bf16)
    return high, (value - high.astype(f32)).astype(bf16)


def nt_dot(lhs, rhs):
    return lax.dot_general(lhs, rhs, (((1,), (1,)), ((), ())), preferred_element_type=f32)


def right_rows(pair, raw, right_ref):
    width = pair.shape[1]
    queries = raw.shape[0]
    for first in range(0, raw.shape[1], 2 * width):
        pieces = [raw[:, at : at + width] for at in (first, first + width)]
        both = nt_dot(pair, jnp.concatenate(pieces, axis=0))
        both = both[:width] + both[width:]
        half = width // 2
        for index, lanes in enumerate((slice(0, queries), slice(queries, 2 * queries))):
            for row in range(2):
                at = (first // half + 2 * index + row) * (half + PAD)
                right_ref[at : at + half, :] = both[row * half : (row + 1) * half, lanes]


def first_kernel(
    map_ref, in_ref, out_ref, raw_ref, right_ref, pair_ref, left_ref, inverse_ref, rows_ref, own_ref, sems
):
    own_rows = rows_ref.shape[0]
    sub = lax.axis_index("sub")
    module = map_ref[0]
    mine = out_ref.at[module, pl.ds(pl.multiple_of(sub * own_rows, own_rows), own_rows), :]
    copies = [
        pltpu.make_async_copy(in_ref.at[module], inverse_ref, sems.at[0]),
        pltpu.make_async_copy(mine, rows_ref, sems.at[1]),
        pltpu.make_async_copy(raw_ref, own_ref, sems.at[2]),
    ]
    for copy in copies:
        copy.start()
    copies[0].wait()
    high, low = split(inverse_ref[...].T)
    high, low = high.astype(f32), low.astype(f32)
    zero = jnp.zeros_like(high)
    pair = jnp.concatenate(
        [jnp.concatenate(row, axis=1) for row in ([high, zero], [zero, high], [low, zero], [zero, low])], axis=0
    ).astype(bf16)
    pair_ref[...] = pair
    copies[1].wait()
    rows = rows_ref[...]
    swapped = jnp.concatenate([rows[:, own_rows:], rows[:, :own_rows]], axis=1)
    rows = jnp.where(sub == 0, rows, swapped)
    high, low = split(rows)
    high, low = high.astype(f32), low.astype(f32)
    left_ref[...] = jnp.concatenate(
        [jnp.concatenate(row, axis=1) for row in ([high, high], [low, jnp.zeros_like(low)])], axis=0
    ).astype(bf16)
    copies[2].wait()
    right_rows(pair, own_ref, right_ref)


def second_kernel(pair_ref, left_ref, own_ref, raw_ref, result_ref, right_ref, done_ref):
    own_rows = left_ref.shape[0] // 2
    rank_in = result_ref.shape[0] // own_rows
    step = rank_in + PAD
    right_rows(pair_ref[...], raw_ref, right_ref)
    left = left_ref[...]
    for first in range(0, rank_in, 2):
        wide = jnp.concatenate(
            [
                jnp.concatenate(
                    [
                        own_ref[pl.ds(column, own_rows, stride=step), :],
                        right_ref[pl.ds(column, own_rows, stride=step), :],
                    ],
                    axis=0,
                )
                for column in (first, first + 1)
            ],
            axis=1,
        )
        high, low = split(wide)
        both = jnp.dot(left, jnp.concatenate([high, low], axis=0), preferred_element_type=f32)
        both = both[:own_rows] + both[own_rows:]
        queries = both.shape[1] // 2
        done_ref[pl.ds(first, own_rows, stride=step), :] = both[:, :queries]
        done_ref[pl.ds(first + 1, own_rows, stride=step), :] = both[:, queries:]
    for row in range(own_rows):
        result_ref[row * rank_in : (row + 1) * rank_in, :] = done_ref[row * step : row * step + rank_in, :].astype(bf16)


def preconditioned(query_grads, in_inverse, out_inverse, module_map):
    block_rows, _, half_width = query_grads.shape
    rank_in, rank_out = in_inverse.shape[1], out_inverse.shape[1]
    own_rows = half_width // rank_in
    raw = query_grads.reshape(block_rows, half_width)
    other = shifted(raw, "sub", 1)
    anywhere = pl.BlockSpec(memory_space=pl.ANY)
    right, pair, left = pl.pallas_call(
        first_kernel,
        out_shape=(
            pltpu.VMEM((own_rows * (rank_in + PAD), block_rows), f32),
            pltpu.VMEM((4 * rank_in, 2 * rank_in), bf16),
            pltpu.VMEM((2 * own_rows, 2 * rank_out), bf16),
        ),
        in_specs=[pl.BlockSpec(memory_space=pltpu.SMEM), anywhere, anywhere, anywhere],
        out_specs=[in_vmem, in_vmem, in_vmem],
        scratch_shapes=[
            pltpu.VMEM((rank_in, rank_in), f32),
            pltpu.VMEM((own_rows, rank_out), f32),
            pltpu.VMEM((block_rows, half_width), bf16),
            pltpu.SemaphoreType.DMA((3,)),
        ],
        compiler_params=params(),
        cost_estimate=cost(2),
    )(module_map, *[pltpu.with_memory_space_constraint(x, pltpu.HBM) for x in (in_inverse, out_inverse, raw)])
    return pl.pallas_call(
        second_kernel,
        out_shape=pltpu.VMEM((half_width, block_rows), bf16),
        in_specs=[in_vmem] * 4,
        out_specs=in_vmem,
        scratch_shapes=[pltpu.VMEM((own_rows * (rank_in + PAD), block_rows), f32)] * 2,
        compiler_params=params(),
        cost_estimate=cost(2),
    )(keep_near(pair), keep_near(left), keep_near(right), keep_near(other))


def part_dot(train_ref, ref, first):
    train = train_ref[:, pl.ds(first, ref.shape[0])]
    return jnp.dot(train, ref[...], preferred_element_type=f32)


def whole_kernel(mods, subs, train_ref, block_ref, *refs):
    outputs, sum_ref = refs[:-1], refs[-1]
    sum_ref[...] = part_dot(train_ref, block_ref, 0)
    rows = sum_ref.shape[0] // (mods * subs)
    for sub_step, output in enumerate(outputs):
        for mod_step in range(mods):
            output[mod_step * rows : (mod_step + 1) * rows, :] = sum_ref[peer_rows(mod_step, sub_step, mods, subs, rows), :].astype(output.dtype)


def peer_rows(mod_step, sub_step, mods, subs, rows):
    target = lax.rem(lax.axis_index("mod") + mod_step, mods) * subs
    target = target + lax.rem(lax.axis_index("sub") + sub_step, subs)
    return pl.ds(pl.multiple_of(target * rows, rows), rows)


def score_kernel(plans, dests, train_ref, *refs):
    count = sum(len(plan) for plan in plans)
    inputs, outputs, sums = list(refs[:count]), (), refs[-len(plans) :]
    if dests:
        outputs = refs[-len(plans) - dests : -len(plans)]
    parts = lax.axis_size("groups")
    for plan, sum_ref in zip(plans, sums):
        total = None
        for kind in plan:
            ref = inputs.pop(0)
            if kind == "total":
                term = ref[...]
            elif kind == "rest":
                term = part_dot(train_ref, ref, train_ref.shape[1] - ref.shape[0])
            else:
                share = ref.shape[0]
                source = lax.rem(lax.axis_index("groups") + parts - kind, parts)
                term = part_dot(train_ref, ref, pl.multiple_of(source * share, 128))
            total = term if total is None else total + term
        sum_ref[...] = total
    mods, subs = lax.axis_size("mod"), lax.axis_size("sub")
    rows = sums[0].shape[0] // (mods * subs)
    for dest, output in enumerate(outputs):
        place = peer_rows(*divmod(dest, subs), mods, subs, rows)
        for block, sum_ref in enumerate(sums):
            output[block * rows : (block + 1) * rows, :] = sum_ref[place, :].astype(output.dtype)


def cost(micros):
    return pl.CostEstimate(flops=int(micros * 1.15e9), bytes_accessed=0, transcendentals=0)


def add_kernel(count, *refs):
    inputs, outputs = refs[:count], refs[count:]
    rows = outputs[0].shape[0]
    for step, output in enumerate(outputs):
        total = None
        for ref in inputs:
            term = ref[step * rows : (step + 1) * rows, :].astype(f32)
            total = term if total is None else total + term
        output[...] = total.astype(output.dtype)


def whole(train, block):
    mods, subs = lax.axis_size("mod"), lax.axis_size("sub")
    rows, queries = train.shape[0] // (mods * subs), block.shape[1]
    dealt = pl.pallas_call(
        functools.partial(whole_kernel, mods, subs),
        out_shape=[pltpu.VMEM((mods * rows, queries), bf16 if step else f32) for step in range(subs)],
        in_specs=[in_vmem] * 2,
        out_specs=[in_vmem] * subs,
        scratch_shapes=[pltpu.VMEM((train.shape[0], queries), f32)],
        compiler_params=params(),
        cost_estimate=cost(1),
    )(keep_near(train), keep_near(block))
    terms = [to_peer(piece, 0, step) if step else piece for step, piece in enumerate(dealt)]
    added = pl.pallas_call(
        functools.partial(add_kernel, subs),
        out_shape=[pltpu.VMEM((rows, queries), f32)] * mods,
        in_specs=[in_vmem] * subs,
        out_specs=[in_vmem] * mods,
        compiler_params=params(),
        cost_estimate=cost(0.1),
    )(*map(keep_near, terms))
    return added, dealt


def held(value, first, after):
    def kernel(value_ref, *refs):
        refs[-1][...] = value_ref[first:, :]

    return pl.pallas_call(
        kernel,
        out_shape=pltpu.VMEM((value.shape[0] - first, value.shape[1]), value.dtype),
        in_specs=[in_vmem] + [pl.BlockSpec(memory_space=pl.ANY)] * len(after),
        out_specs=in_vmem,
        compiler_params=params(),
        cost_estimate=cost(0.1),
    )(keep_near(value), *after)


def scored(train, plans, arrays, dests=0, after=()):
    queries = arrays[0].shape[1]
    whole_shape = (train.shape[0], queries)
    sums = [pltpu.VMEM(whole_shape, f32)] * len(plans)
    part_shape = (len(plans) * train.shape[0] // max(dests, 1), queries)
    outputs = [pltpu.VMEM(part_shape, bf16 if dest else f32) for dest in range(dests)] or sums
    return pl.pallas_call(
        functools.partial(score_kernel, plans, dests),
        out_shape=outputs,
        in_specs=[in_vmem] * (1 + len(arrays)) + [pl.BlockSpec(memory_space=pl.ANY)] * len(after),
        out_specs=[in_vmem] * len(outputs),
        scratch_shapes=sums if dests else [],
        compiler_params=params(),
        cost_estimate=cost(0.1),
    )(*map(keep_near, (train, *arrays)), *after)


def settled(terms):
    def kernel(*refs):
        total = None
        for ref in refs[:-1]:
            term = ref[...].astype(f32)
            total = term if total is None else total + term
        refs[-1][...] = total

    return pl.pallas_call(
        kernel,
        out_shape=pltpu.VMEM(terms[0].shape, f32),
        in_specs=[in_vmem] * len(terms),
        out_specs=in_vmem,
        compiler_params=params(),
        cost_estimate=cost(0.1),
    )(*map(keep_near, terms))


def sum_kernel(places, counts, *refs):
    output = refs[-1]
    rows = output.shape[1]
    at = 0
    for blocks, count in zip(places, counts):
        for block, place in enumerate(blocks):
            total = None
            for ref in refs[at : at + count]:
                term = ref[block * rows : (block + 1) * rows, :].astype(f32)
                total = term if total is None else total + term
            output[place] = total
        at += count


def local(query_grads, train_grads, in_inverse, out_inverse, module_map):
    half_width = query_grads.shape[2]
    mods, subs = lax.axis_size("mod"), lax.axis_size("sub")
    parts, part = lax.axis_size("groups"), lax.axis_index("groups")
    reach = min(WINDOW_HALF, (lax.axis_size("ex") - 1) // 2)
    precon = preconditioned(query_grads, in_inverse, out_inverse, module_map)

    share = 5 * half_width // (8 * parts) // 128 * 128
    shared = share * parts
    train = train_grads.reshape(train_grads.shape[0], half_width)

    offsets = [sign * far for far in range(1, reach + 1) for sign in (1, -1)]
    mine = lax.dynamic_slice_in_dim(precon, part * share, share, 0)
    added, dealt = whole(train, precon)
    rest = held(precon, shared, added[:1])
    carried = {offset: shifted(mine, "ex", -offset) for offset in offsets}
    common = {offset: shifted(rest, "ex", -offset) for offset in offsets}
    *others, last = offsets
    plans = [[0]] + [[0, "rest"] for offset in others]
    arrays = [carried[last]] + [piece for offset in others for piece in (carried[offset], common[offset])]
    own = settled([to_peer(piece, step, 0) if step else piece for step, piece in enumerate(added)])
    total, *totals = scored(train, plans, arrays, after=[own])
    totals = [*totals, total]
    plans = [["total", *range(1, parts)] for offset in offsets]
    arrays = []
    for offset, total in reversed(list(zip(offsets, totals))):
        arrays += [total, *[shifted(carried[offset], "groups", step) for step in range(1, parts)]]
    totals = reversed(scored(train, plans, arrays))
    plans = [["total"] for offset in others] + [["total", "rest"]]
    partial = scored(train, plans, [*totals, common[last]], mods * subs)
    terms = [to_peer(rows, *divmod(dest, subs)) if dest else rows for dest, rows in reversed(list(enumerate(partial)))]
    terms.append(own)
    rows = train.shape[0] // (mods * subs)
    summed = pl.pallas_call(
        functools.partial(sum_kernel, [[offset + reach for offset in offsets], [reach]], [mods * subs, 1]),
        out_shape=jax.ShapeDtypeStruct((2 * reach + 1, rows, query_grads.shape[0]), f32),
        in_specs=[in_vmem] * len(terms),
        out_specs=in_vmem,
        compiler_params=params(),
        cost_estimate=cost(1),
    )(*[keep_near(term) for term in terms])
    return summed.transpose(1, 0, 2)


def solution(mesh):
    placed = (P("ex", "mod", "sub"), P(("groups", "ex"), "mod", "sub"), P(), P(), P("mod"))
    return jax.shard_map(
        local,
        mesh=mesh,
        in_specs=placed,
        out_specs=P(("groups", "ex", "mod", "sub"), None, None),
        check_vma=False,
    )
```

```python
import functools

import jax
import jax.numpy as jnp
from jax import lax
from jax.experimental import pallas as pl
from jax.experimental.pallas import tpu as pltpu
from jax.sharding import PartitionSpec as P

WINDOW_HALF = 2
PAD = 8
VMEM_LIMIT = 32 * 1024 * 1024

f32, bf16 = jnp.float32, jnp.bfloat16
in_vmem = pl.BlockSpec(memory_space=pltpu.VMEM)


def keep_near(value):
    return pltpu.with_memory_space_constraint(value, pltpu.VMEM)


def params():
    return pltpu.CompilerParams(vmem_limit_bytes=VMEM_LIMIT)


def shifted(value, axis, steps):
    count = lax.axis_size(axis)
    pairs = [(source, (source + steps) % count) for source in range(count)]
    return lax.ppermute(value, axis, pairs)


def to_peer(value, mod_step, sub_step):
    mods, subs = lax.axis_size("mod"), lax.axis_size("sub")
    pairs = []
    for mod in range(mods):
        for sub in range(subs):
            target = ((mod + mod_step) % mods) * subs + (sub + sub_step) % subs
            pairs.append((mod * subs + sub, target))
    return lax.ppermute(value, ("mod", "sub"), pairs)


def split(value):
    high = value.astype(bf16)
    return high, (value - high.astype(f32)).astype(bf16)


def nt_dot(lhs, rhs):
    return lax.dot_general(lhs, rhs, (((1,), (1,)), ((), ())), preferred_element_type=f32)


def right_rows(pair, raw, right_ref):
    width = pair.shape[1]
    queries = raw.shape[0]
    for first in range(0, raw.shape[1], 2 * width):
        pieces = [raw[:, at : at + width] for at in (first, first + width)]
        both = nt_dot(pair, jnp.concatenate(pieces, axis=0))
        both = both[:width] + both[width:]
        half = width // 2
        for index, lanes in enumerate((slice(0, queries), slice(queries, 2 * queries))):
            for row in range(2):
                at = (first // half + 2 * index + row) * (half + PAD)
                right_ref[at : at + half, :] = both[row * half : (row + 1) * half, lanes]


def first_kernel(
    map_ref, in_ref, out_ref, raw_ref, right_ref, pair_ref, left_ref, inverse_ref, rows_ref, own_ref, sems
):
    own_rows = rows_ref.shape[0]
    sub = lax.axis_index("sub")
    module = map_ref[0]
    mine = out_ref.at[module, pl.ds(pl.multiple_of(sub * own_rows, own_rows), own_rows), :]
    copies = [
        pltpu.make_async_copy(in_ref.at[module], inverse_ref, sems.at[0]),
        pltpu.make_async_copy(mine, rows_ref, sems.at[1]),
        pltpu.make_async_copy(raw_ref, own_ref, sems.at[2]),
    ]
    for copy in copies:
        copy.start()
    copies[0].wait()
    high, low = split(inverse_ref[...].T)
    high, low = high.astype(f32), low.astype(f32)
    zero = jnp.zeros_like(high)
    pair = jnp.concatenate(
        [jnp.concatenate(row, axis=1) for row in ([high, zero], [zero, high], [low, zero], [zero, low])], axis=0
    ).astype(bf16)
    pair_ref[...] = pair
    copies[1].wait()
    rows = rows_ref[...]
    swapped = jnp.concatenate([rows[:, own_rows:], rows[:, :own_rows]], axis=1)
    rows = jnp.where(sub == 0, rows, swapped)
    high, low = split(rows)
    high, low = high.astype(f32), low.astype(f32)
    left_ref[...] = jnp.concatenate(
        [jnp.concatenate(row, axis=1) for row in ([high, high], [low, jnp.zeros_like(low)])], axis=0
    ).astype(bf16)
    copies[2].wait()
    right_rows(pair, own_ref, right_ref)


def second_kernel(pair_ref, left_ref, own_ref, raw_ref, result_ref, right_ref, done_ref):
    own_rows = left_ref.shape[0] // 2
    rank_in = result_ref.shape[0] // own_rows
    step = rank_in + PAD
    right_rows(pair_ref[...], raw_ref, right_ref)
    left = left_ref[...]
    for first in range(0, rank_in, 2):
        wide = jnp.concatenate(
            [
                jnp.concatenate(
                    [
                        own_ref[pl.ds(column, own_rows, stride=step), :],
                        right_ref[pl.ds(column, own_rows, stride=step), :],
                    ],
                    axis=0,
                )
                for column in (first, first + 1)
            ],
            axis=1,
        )
        high, low = split(wide)
        both = jnp.dot(left, jnp.concatenate([high, low], axis=0), preferred_element_type=f32)
        both = both[:own_rows] + both[own_rows:]
        queries = both.shape[1] // 2
        done_ref[pl.ds(first, own_rows, stride=step), :] = both[:, :queries]
        done_ref[pl.ds(first + 1, own_rows, stride=step), :] = both[:, queries:]
    for row in range(own_rows):
        result_ref[row * rank_in : (row + 1) * rank_in, :] = done_ref[row * step : row * step + rank_in, :].astype(bf16)


def preconditioned(query_grads, in_inverse, out_inverse, module_map):
    block_rows, _, half_width = query_grads.shape
    rank_in, rank_out = in_inverse.shape[1], out_inverse.shape[1]
    own_rows = half_width // rank_in
    raw = query_grads.reshape(block_rows, half_width)
    other = shifted(raw, "sub", 1)
    anywhere = pl.BlockSpec(memory_space=pl.ANY)
    right, pair, left = pl.pallas_call(
        first_kernel,
        out_shape=(
            pltpu.VMEM((own_rows * (rank_in + PAD), block_rows), f32),
            pltpu.VMEM((4 * rank_in, 2 * rank_in), bf16),
            pltpu.VMEM((2 * own_rows, 2 * rank_out), bf16),
        ),
        in_specs=[pl.BlockSpec(memory_space=pltpu.SMEM), anywhere, anywhere, anywhere],
        out_specs=[in_vmem, in_vmem, in_vmem],
        scratch_shapes=[
            pltpu.VMEM((rank_in, rank_in), f32),
            pltpu.VMEM((own_rows, rank_out), f32),
            pltpu.VMEM((block_rows, half_width), bf16),
            pltpu.SemaphoreType.DMA((3,)),
        ],
        compiler_params=params(),
        cost_estimate=cost(2),
    )(module_map, *[pltpu.with_memory_space_constraint(x, pltpu.HBM) for x in (in_inverse, out_inverse, raw)])
    return pl.pallas_call(
        second_kernel,
        out_shape=pltpu.VMEM((half_width, block_rows), bf16),
        in_specs=[in_vmem] * 4,
        out_specs=in_vmem,
        scratch_shapes=[pltpu.VMEM((own_rows * (rank_in + PAD), block_rows), f32)] * 2,
        compiler_params=params(),
        cost_estimate=cost(2),
    )(keep_near(pair), keep_near(left), keep_near(right), keep_near(other))


def part_dot(train_ref, ref, first):
    train = train_ref[:, pl.ds(first, ref.shape[0])]
    return jnp.dot(train, ref[...], preferred_element_type=f32)


def whole_kernel(mods, subs, train_ref, block_ref, *refs):
    outputs, sum_ref = refs[:-1], refs[-1]
    sum_ref[...] = part_dot(train_ref, block_ref, 0)
    rows = sum_ref.shape[0] // (mods * subs)
    for sub_step, output in enumerate(outputs):
        for mod_step in range(mods):
            output[mod_step * rows : (mod_step + 1) * rows, :] = sum_ref[peer_rows(mod_step, sub_step, mods, subs, rows), :].astype(output.dtype)


def peer_rows(mod_step, sub_step, mods, subs, rows):
    target = lax.rem(lax.axis_index("mod") + mod_step, mods) * subs
    target = target + lax.rem(lax.axis_index("sub") + sub_step, subs)
    return pl.ds(pl.multiple_of(target * rows, rows), rows)


def score_kernel(plans, dests, train_ref, *refs):
    count = sum(len(plan) for plan in plans)
    inputs, outputs, sums = list(refs[:count]), (), refs[-len(plans) :]
    if dests:
        outputs = refs[-len(plans) - dests : -len(plans)]
    parts = lax.axis_size("groups")
    for plan, sum_ref in zip(plans, sums):
        total = None
        for kind in plan:
            ref = inputs.pop(0)
            if kind == "total":
                term = ref[...]
            elif kind == "rest":
                term = part_dot(train_ref, ref, train_ref.shape[1] - ref.shape[0])
            else:
                share = ref.shape[0]
                source = lax.rem(lax.axis_index("groups") + parts - kind, parts)
                term = part_dot(train_ref, ref, pl.multiple_of(source * share, 128))
            total = term if total is None else total + term
        sum_ref[...] = total
    mods, subs = lax.axis_size("mod"), lax.axis_size("sub")
    rows = sums[0].shape[0] // (mods * subs)
    for dest, output in enumerate(outputs):
        place = peer_rows(*divmod(dest, subs), mods, subs, rows)
        for block, sum_ref in enumerate(sums):
            output[block * rows : (block + 1) * rows, :] = sum_ref[place, :].astype(output.dtype)


def cost(micros):
    return pl.CostEstimate(flops=int(micros * 1.15e9), bytes_accessed=0, transcendentals=0)


def add_kernel(count, *refs):
    inputs, outputs = refs[:count], refs[count:]
    rows = outputs[0].shape[0]
    for step, output in enumerate(outputs):
        total = None
        for ref in inputs:
            term = ref[step * rows : (step + 1) * rows, :].astype(f32)
            total = term if total is None else total + term
        output[...] = total.astype(output.dtype)


def whole(train, block):
    mods, subs = lax.axis_size("mod"), lax.axis_size("sub")
    rows, queries = train.shape[0] // (mods * subs), block.shape[1]
    dealt = pl.pallas_call(
        functools.partial(whole_kernel, mods, subs),
        out_shape=[pltpu.VMEM((mods * rows, queries), bf16 if step else f32) for step in range(subs)],
        in_specs=[in_vmem] * 2,
        out_specs=[in_vmem] * subs,
        scratch_shapes=[pltpu.VMEM((train.shape[0], queries), f32)],
        compiler_params=params(),
        cost_estimate=cost(1),
    )(keep_near(train), keep_near(block))
    terms = [to_peer(piece, 0, step) if step else piece for step, piece in enumerate(dealt)]
    added = pl.pallas_call(
        functools.partial(add_kernel, subs),
        out_shape=[pltpu.VMEM((rows, queries), f32)] * mods,
        in_specs=[in_vmem] * subs,
        out_specs=[in_vmem] * mods,
        compiler_params=params(),
        cost_estimate=cost(0.1),
    )(*map(keep_near, terms))
    return added, dealt


def held(value, first, after):
    def kernel(value_ref, *refs):
        refs[-1][...] = value_ref[first:, :]

    return pl.pallas_call(
        kernel,
        out_shape=pltpu.VMEM((value.shape[0] - first, value.shape[1]), value.dtype),
        in_specs=[in_vmem] + [pl.BlockSpec(memory_space=pl.ANY)] * len(after),
        out_specs=in_vmem,
        compiler_params=params(),
        cost_estimate=cost(0.1),
    )(keep_near(value), *after)


def scored(train, plans, arrays, dests=0, after=()):
    queries = arrays[0].shape[1]
    whole_shape = (train.shape[0], queries)
    sums = [pltpu.VMEM(whole_shape, f32)] * len(plans)
    part_shape = (len(plans) * train.shape[0] // max(dests, 1), queries)
    outputs = [pltpu.VMEM(part_shape, bf16 if dest else f32) for dest in range(dests)] or sums
    return pl.pallas_call(
        functools.partial(score_kernel, plans, dests),
        out_shape=outputs,
        in_specs=[in_vmem] * (1 + len(arrays)) + [pl.BlockSpec(memory_space=pl.ANY)] * len(after),
        out_specs=[in_vmem] * len(outputs),
        scratch_shapes=sums if dests else [],
        compiler_params=params(),
        cost_estimate=cost(0.1),
    )(*map(keep_near, (train, *arrays)), *after)


def settled(terms):
    def kernel(*refs):
        total = None
        for ref in refs[:-1]:
            term = ref[...].astype(f32)
            total = term if total is None else total + term
        refs[-1][...] = total

    return pl.pallas_call(
        kernel,
        out_shape=pltpu.VMEM(terms[0].shape, f32),
        in_specs=[in_vmem] * len(terms),
        out_specs=in_vmem,
        compiler_params=params(),
        cost_estimate=cost(0.1),
    )(*map(keep_near, terms))


def sum_kernel(places, counts, *refs):
    output = refs[-1]
    rows = output.shape[1]
    at = 0
    for blocks, count in zip(places, counts):
        for block, place in enumerate(blocks):
            total = None
            for ref in refs[at : at + count]:
                term = ref[block * rows : (block + 1) * rows, :].astype(f32)
                total = term if total is None else total + term
            output[place] = total
        at += count


def local(query_grads, train_grads, in_inverse, out_inverse, module_map):
    half_width = query_grads.shape[2]
    mods, subs = lax.axis_size("mod"), lax.axis_size("sub")
    parts, part = lax.axis_size("groups"), lax.axis_index("groups")
    reach = min(WINDOW_HALF, (lax.axis_size("ex") - 1) // 2)
    precon = preconditioned(query_grads, in_inverse, out_inverse, module_map)

    train = train_grads.reshape(train_grads.shape[0], half_width)
    offsets = [sign * far for far in range(1, reach + 1) for sign in (-1, 1)]
    added, dealt = whole(train, precon)
    carried, common = {}, {}
    for offset in offsets:
        share = half_width // parts if offset < 0 else 8 * half_width // (32 * parts) // 64 * 128
        mine = lax.dynamic_slice_in_dim(precon, part * share, share, 0)
        if offset > 0:
            mine = held(mine, 0, added[:1])
            common[offset] = shifted(held(precon, share * parts, added[:1]), "ex", -offset)
        carried[offset] = shifted(mine, "ex", -offset)
    *others, last = offsets
    plans = [[0, "rest"] if offset in common else [0] for offset in others] + [[0]]
    arrays = []
    for offset in others:
        arrays += [carried[offset], *([common[offset]] if offset in common else [])]
    arrays.append(carried[last])
    own = settled([to_peer(piece, step, 0) if step else piece for step, piece in enumerate(added)])
    totals = scored(train, plans, arrays, after=[own])
    plans = [["total", *range(1, parts)] for offset in offsets]
    arrays = []
    for offset, total in zip(offsets, totals):
        arrays += [total, *[shifted(carried[offset], "groups", step) for step in range(1, parts)]]
    totals = scored(train, plans, arrays)
    plans = [["total"] for offset in others] + [["total", "rest"]]
    partial = scored(train, plans, [*totals, common[last]], mods * subs)
    terms = [to_peer(rows, *divmod(dest, subs)) if dest else rows for dest, rows in reversed(list(enumerate(partial)))]
    terms.append(own)
    rows = train.shape[0] // (mods * subs)
    summed = pl.pallas_call(
        functools.partial(sum_kernel, [[offset + reach for offset in offsets], [reach]], [mods * subs, 1]),
        out_shape=jax.ShapeDtypeStruct((2 * reach + 1, rows, query_grads.shape[0]), f32),
        in_specs=[in_vmem] * len(terms),
        out_specs=in_vmem,
        compiler_params=params(),
        cost_estimate=cost(1),
    )(*[keep_near(term) for term in terms])
    return summed.transpose(1, 0, 2)


def solution(mesh):
    placed = (P("ex", "mod", "sub"), P(("groups", "ex"), "mod", "sub"), P(), P(), P("mod"))
    return jax.shard_map(
        local,
        mesh=mesh,
        in_specs=placed,
        out_specs=P(("groups", "ex", "mod", "sub"), None, None),
        check_vma=False,
    )
```

```python
import functools

import jax
import jax.numpy as jnp
from jax import lax
from jax.experimental import pallas as pl
from jax.experimental.pallas import tpu as pltpu
from jax.sharding import PartitionSpec as P

WINDOW_HALF = 2
PAD = 8
VMEM_LIMIT = 32 * 1024 * 1024

f32, bf16 = jnp.float32, jnp.bfloat16
in_vmem = pl.BlockSpec(memory_space=pltpu.VMEM)


def keep_near(value):
    return pltpu.with_memory_space_constraint(value, pltpu.VMEM)


def params():
    return pltpu.CompilerParams(vmem_limit_bytes=VMEM_LIMIT)


def shifted(value, axis, steps):
    count = lax.axis_size(axis)
    pairs = [(source, (source + steps) % count) for source in range(count)]
    return lax.ppermute(value, axis, pairs)


def to_peer(value, mod_step, sub_step):
    mods, subs = lax.axis_size("mod"), lax.axis_size("sub")
    pairs = []
    for mod in range(mods):
        for sub in range(subs):
            target = ((mod + mod_step) % mods) * subs + (sub + sub_step) % subs
            pairs.append((mod * subs + sub, target))
    return lax.ppermute(value, ("mod", "sub"), pairs)


def split(value):
    high = value.astype(bf16)
    return high, (value - high.astype(f32)).astype(bf16)


def nt_dot(lhs, rhs):
    return lax.dot_general(lhs, rhs, (((1,), (1,)), ((), ())), preferred_element_type=f32)


def right_rows(pair, raw, right_ref):
    width = pair.shape[1]
    queries = raw.shape[0]
    for first in range(0, raw.shape[1], 2 * width):
        pieces = [raw[:, at : at + width] for at in (first, first + width)]
        both = nt_dot(pair, jnp.concatenate(pieces, axis=0))
        both = both[:width] + both[width:]
        half = width // 2
        for index, lanes in enumerate((slice(0, queries), slice(queries, 2 * queries))):
            for row in range(2):
                at = (first // half + 2 * index + row) * (half + PAD)
                right_ref[at : at + half, :] = both[row * half : (row + 1) * half, lanes]


def first_kernel(
    map_ref, in_ref, out_ref, raw_ref, right_ref, pair_ref, left_ref, inverse_ref, rows_ref, own_ref, sems
):
    own_rows = rows_ref.shape[0]
    sub = lax.axis_index("sub")
    module = map_ref[0]
    mine = out_ref.at[module, pl.ds(pl.multiple_of(sub * own_rows, own_rows), own_rows), :]
    copies = [
        pltpu.make_async_copy(in_ref.at[module], inverse_ref, sems.at[0]),
        pltpu.make_async_copy(mine, rows_ref, sems.at[1]),
        pltpu.make_async_copy(raw_ref, own_ref, sems.at[2]),
    ]
    for copy in copies:
        copy.start()
    copies[0].wait()
    high, low = split(inverse_ref[...].T)
    high, low = high.astype(f32), low.astype(f32)
    zero = jnp.zeros_like(high)
    pair = jnp.concatenate(
        [jnp.concatenate(row, axis=1) for row in ([high, zero], [zero, high], [low, zero], [zero, low])], axis=0
    ).astype(bf16)
    pair_ref[...] = pair
    copies[1].wait()
    rows = rows_ref[...]
    swapped = jnp.concatenate([rows[:, own_rows:], rows[:, :own_rows]], axis=1)
    rows = jnp.where(sub == 0, rows, swapped)
    high, low = split(rows)
    high, low = high.astype(f32), low.astype(f32)
    left_ref[...] = jnp.concatenate(
        [jnp.concatenate(row, axis=1) for row in ([high, high], [low, jnp.zeros_like(low)])], axis=0
    ).astype(bf16)
    copies[2].wait()
    right_rows(pair, own_ref, right_ref)


def second_kernel(pair_ref, left_ref, own_ref, raw_ref, result_ref, right_ref, done_ref):
    own_rows = left_ref.shape[0] // 2
    rank_in = result_ref.shape[0] // own_rows
    step = rank_in + PAD
    right_rows(pair_ref[...], raw_ref, right_ref)
    left = left_ref[...]
    for first in range(0, rank_in, 2):
        wide = jnp.concatenate(
            [
                jnp.concatenate(
                    [
                        own_ref[pl.ds(column, own_rows, stride=step), :],
                        right_ref[pl.ds(column, own_rows, stride=step), :],
                    ],
                    axis=0,
                )
                for column in (first, first + 1)
            ],
            axis=1,
        )
        high, low = split(wide)
        both = jnp.dot(left, jnp.concatenate([high, low], axis=0), preferred_element_type=f32)
        both = both[:own_rows] + both[own_rows:]
        queries = both.shape[1] // 2
        done_ref[pl.ds(first, own_rows, stride=step), :] = both[:, :queries]
        done_ref[pl.ds(first + 1, own_rows, stride=step), :] = both[:, queries:]
    for row in range(own_rows):
        result_ref[row * rank_in : (row + 1) * rank_in, :] = done_ref[row * step : row * step + rank_in, :].astype(bf16)


def preconditioned(query_grads, in_inverse, out_inverse, module_map):
    block_rows, _, half_width = query_grads.shape
    rank_in, rank_out = in_inverse.shape[1], out_inverse.shape[1]
    own_rows = half_width // rank_in
    raw = query_grads.reshape(block_rows, half_width)
    other = shifted(raw, "sub", 1)
    anywhere = pl.BlockSpec(memory_space=pl.ANY)
    right, pair, left = pl.pallas_call(
        first_kernel,
        out_shape=(
            pltpu.VMEM((own_rows * (rank_in + PAD), block_rows), f32),
            pltpu.VMEM((4 * rank_in, 2 * rank_in), bf16),
            pltpu.VMEM((2 * own_rows, 2 * rank_out), bf16),
        ),
        in_specs=[pl.BlockSpec(memory_space=pltpu.SMEM), anywhere, anywhere, anywhere],
        out_specs=[in_vmem, in_vmem, in_vmem],
        scratch_shapes=[
            pltpu.VMEM((rank_in, rank_in), f32),
            pltpu.VMEM((own_rows, rank_out), f32),
            pltpu.VMEM((block_rows, half_width), bf16),
            pltpu.SemaphoreType.DMA((3,)),
        ],
        compiler_params=params(),
        cost_estimate=cost(2),
    )(module_map, *[pltpu.with_memory_space_constraint(x, pltpu.HBM) for x in (in_inverse, out_inverse, raw)])
    return pl.pallas_call(
        second_kernel,
        out_shape=pltpu.VMEM((half_width, block_rows), bf16),
        in_specs=[in_vmem] * 4,
        out_specs=in_vmem,
        scratch_shapes=[pltpu.VMEM((own_rows * (rank_in + PAD), block_rows), f32)] * 2,
        compiler_params=params(),
        cost_estimate=cost(2),
    )(keep_near(pair), keep_near(left), keep_near(right), keep_near(other))


def part_dot(train_ref, ref, first):
    train = train_ref[:, pl.ds(first, ref.shape[0])]
    return jnp.dot(train, ref[...], preferred_element_type=f32)


def whole_kernel(mods, subs, train_ref, block_ref, *refs):
    outputs, sum_ref = refs[:-1], refs[-1]
    sum_ref[...] = part_dot(train_ref, block_ref, 0)
    rows = sum_ref.shape[0] // (mods * subs)
    for sub_step, output in enumerate(outputs):
        for mod_step in range(mods):
            output[mod_step * rows : (mod_step + 1) * rows, :] = sum_ref[peer_rows(mod_step, sub_step, mods, subs, rows), :].astype(output.dtype)


def peer_rows(mod_step, sub_step, mods, subs, rows):
    target = lax.rem(lax.axis_index("mod") + mod_step, mods) * subs
    target = target + lax.rem(lax.axis_index("sub") + sub_step, subs)
    return pl.ds(pl.multiple_of(target * rows, rows), rows)


def score_kernel(plans, dests, train_ref, *refs):
    count = sum(len(plan) for plan in plans)
    inputs, outputs, sums = list(refs[:count]), (), refs[-len(plans) :]
    if dests:
        outputs = refs[-len(plans) - dests : -len(plans)]
    parts = lax.axis_size("groups")
    for plan, sum_ref in zip(plans, sums):
        total = None
        for kind in plan:
            ref = inputs.pop(0)
            if kind == "total":
                term = ref[...]
            elif kind == "rest":
                term = part_dot(train_ref, ref, train_ref.shape[1] - ref.shape[0])
            else:
                share = ref.shape[0]
                source = lax.rem(lax.axis_index("groups") + parts - kind, parts)
                term = part_dot(train_ref, ref, pl.multiple_of(source * share, 128))
            total = term if total is None else total + term
        sum_ref[...] = total
    mods, subs = lax.axis_size("mod"), lax.axis_size("sub")
    rows = sums[0].shape[0] // (mods * subs)
    for dest, output in enumerate(outputs):
        place = peer_rows(*divmod(dest, subs), mods, subs, rows)
        for block, sum_ref in enumerate(sums):
            output[block * rows : (block + 1) * rows, :] = sum_ref[place, :].astype(output.dtype)


def cost(micros):
    return pl.CostEstimate(flops=int(micros * 1.15e9), bytes_accessed=0, transcendentals=0)


def add_kernel(count, *refs):
    inputs, outputs = refs[:count], refs[count:]
    rows = outputs[0].shape[0]
    for step, output in enumerate(outputs):
        total = None
        for ref in inputs:
            term = ref[step * rows : (step + 1) * rows, :].astype(f32)
            total = term if total is None else total + term
        output[...] = total.astype(output.dtype)


def whole(train, block):
    mods, subs = lax.axis_size("mod"), lax.axis_size("sub")
    rows, queries = train.shape[0] // (mods * subs), block.shape[1]
    dealt = pl.pallas_call(
        functools.partial(whole_kernel, mods, subs),
        out_shape=[pltpu.VMEM((mods * rows, queries), bf16 if step else f32) for step in range(subs)],
        in_specs=[in_vmem] * 2,
        out_specs=[in_vmem] * subs,
        scratch_shapes=[pltpu.VMEM((train.shape[0], queries), f32)],
        compiler_params=params(),
        cost_estimate=cost(1),
    )(keep_near(train), keep_near(block))
    terms = [to_peer(piece, 0, step) if step else piece for step, piece in enumerate(dealt)]
    added = pl.pallas_call(
        functools.partial(add_kernel, subs),
        out_shape=[pltpu.VMEM((rows, queries), f32)] * mods,
        in_specs=[in_vmem] * subs,
        out_specs=[in_vmem] * mods,
        compiler_params=params(),
        cost_estimate=cost(0.1),
    )(*map(keep_near, terms))
    return added, dealt


def held(value, first, after):
    def kernel(value_ref, *refs):
        refs[-1][...] = value_ref[first:, :]

    return pl.pallas_call(
        kernel,
        out_shape=pltpu.VMEM((value.shape[0] - first, value.shape[1]), value.dtype),
        in_specs=[in_vmem] + [pl.BlockSpec(memory_space=pl.ANY)] * len(after),
        out_specs=in_vmem,
        compiler_params=params(),
        cost_estimate=cost(0.1),
    )(keep_near(value), *after)


def scored(train, plans, arrays, dests=0, after=()):
    queries = arrays[0].shape[1]
    whole_shape = (train.shape[0], queries)
    sums = [pltpu.VMEM(whole_shape, f32)] * len(plans)
    part_shape = (len(plans) * train.shape[0] // max(dests, 1), queries)
    outputs = [pltpu.VMEM(part_shape, bf16 if dest else f32) for dest in range(dests)] or sums
    return pl.pallas_call(
        functools.partial(score_kernel, plans, dests),
        out_shape=outputs,
        in_specs=[in_vmem] * (1 + len(arrays)) + [pl.BlockSpec(memory_space=pl.ANY)] * len(after),
        out_specs=[in_vmem] * len(outputs),
        scratch_shapes=sums if dests else [],
        compiler_params=params(),
        cost_estimate=cost(0.1),
    )(*map(keep_near, (train, *arrays)), *after)


def settled(terms):
    def kernel(*refs):
        total = None
        for ref in refs[:-1]:
            term = ref[...].astype(f32)
            total = term if total is None else total + term
        refs[-1][...] = total

    return pl.pallas_call(
        kernel,
        out_shape=pltpu.VMEM(terms[0].shape, f32),
        in_specs=[in_vmem] * len(terms),
        out_specs=in_vmem,
        compiler_params=params(),
        cost_estimate=cost(0.1),
    )(*map(keep_near, terms))


def sum_kernel(places, counts, *refs):
    output = refs[-1]
    rows = output.shape[1]
    at = 0
    for blocks, count in zip(places, counts):
        for block, place in enumerate(blocks):
            total = None
            for ref in refs[at : at + count]:
                term = ref[block * rows : (block + 1) * rows, :].astype(f32)
                total = term if total is None else total + term
            output[place] = total
        at += count


def local(query_grads, train_grads, in_inverse, out_inverse, module_map):
    half_width = query_grads.shape[2]
    mods, subs = lax.axis_size("mod"), lax.axis_size("sub")
    parts, part = lax.axis_size("groups"), lax.axis_index("groups")
    reach = min(WINDOW_HALF, (lax.axis_size("ex") - 1) // 2)
    precon = preconditioned(query_grads, in_inverse, out_inverse, module_map)

    share = 5 * half_width // (8 * parts) // 128 * 128
    shared = share * parts
    train = train_grads.reshape(train_grads.shape[0], half_width)

    offsets = [sign * far for far in range(1, reach + 1) for sign in (-1, 1)]
    mine = lax.dynamic_slice_in_dim(precon, part * share, share, 0)
    added, dealt = whole(train, precon)
    rest = held(precon, shared, added[:1])
    carried = {offset: shifted(mine, "ex", -offset) for offset in offsets}
    common = {offset: shifted(rest, "ex", -offset) for offset in offsets}
    *others, last = offsets
    plans = [[0, "rest"] for offset in others] + [[0]]
    arrays = [piece for offset in others for piece in (carried[offset], common[offset])] + [carried[last]]
    own = settled([to_peer(piece, step, 0) if step else piece for step, piece in enumerate(added)])
    totals = scored(train, plans, arrays, after=[own])
    plans = [["total", *range(1, parts)] for offset in offsets]
    arrays = []
    for offset, total in zip(offsets, totals):
        arrays += [total, *[shifted(carried[offset], "groups", step) for step in range(1, parts)]]
    totals = scored(train, plans, arrays)
    plans = [["total"] for offset in others] + [["total", "rest"]]
    partial = scored(train, plans, [*totals, common[last]], mods * subs)
    order = [0, 1, *range(mods * subs - 1, 1, -1)]
    terms = [to_peer(partial[dest], *divmod(dest, subs)) if dest else partial[0] for dest in order]
    terms.append(own)
    rows = train.shape[0] // (mods * subs)
    summed = pl.pallas_call(
        functools.partial(sum_kernel, [[offset + reach for offset in offsets], [reach]], [mods * subs, 1]),
        out_shape=jax.ShapeDtypeStruct((2 * reach + 1, rows, query_grads.shape[0]), f32),
        in_specs=[in_vmem] * len(terms),
        out_specs=in_vmem,
        compiler_params=params(),
        cost_estimate=cost(1),
    )(*[keep_near(term) for term in terms])
    return summed.transpose(1, 0, 2)


def solution(mesh):
    placed = (P("ex", "mod", "sub"), P(("groups", "ex"), "mod", "sub"), P(), P(), P("mod"))
    return jax.shard_map(
        local,
        mesh=mesh,
        in_specs=placed,
        out_specs=P(("groups", "ex", "mod", "sub"), None, None),
        check_vma=False,
    )
```

```python
import functools

import jax
import jax.numpy as jnp
from jax import lax
from jax.experimental import pallas as pl
from jax.experimental.pallas import tpu as pltpu
from jax.sharding import PartitionSpec as P

WINDOW_HALF = 2
PAD = 8
VMEM_LIMIT = 32 * 1024 * 1024

f32, bf16 = jnp.float32, jnp.bfloat16
in_vmem = pl.BlockSpec(memory_space=pltpu.VMEM)


def keep_near(value):
    return pltpu.with_memory_space_constraint(value, pltpu.VMEM)


def params():
    return pltpu.CompilerParams(vmem_limit_bytes=VMEM_LIMIT)


def shifted(value, axis, steps):
    count = lax.axis_size(axis)
    pairs = [(source, (source + steps) % count) for source in range(count)]
    return lax.ppermute(value, axis, pairs)


def to_peer(value, mod_step, sub_step):
    mods, subs = lax.axis_size("mod"), lax.axis_size("sub")
    pairs = []
    for mod in range(mods):
        for sub in range(subs):
            target = ((mod + mod_step) % mods) * subs + (sub + sub_step) % subs
            pairs.append((mod * subs + sub, target))
    return lax.ppermute(value, ("mod", "sub"), pairs)


def split(value):
    high = value.astype(bf16)
    return high, (value - high.astype(f32)).astype(bf16)


def nt_dot(lhs, rhs):
    return lax.dot_general(lhs, rhs, (((1,), (1,)), ((), ())), preferred_element_type=f32)


def right_rows(pair, raw, right_ref):
    width = pair.shape[1]
    queries = raw.shape[0]
    for first in range(0, raw.shape[1], 2 * width):
        pieces = [raw[:, at : at + width] for at in (first, first + width)]
        both = nt_dot(pair, jnp.concatenate(pieces, axis=0))
        both = both[:width] + both[width:]
        half = width // 2
        for index, lanes in enumerate((slice(0, queries), slice(queries, 2 * queries))):
            for row in range(2):
                at = (first // half + 2 * index + row) * (half + PAD)
                right_ref[at : at + half, :] = both[row * half : (row + 1) * half, lanes]


def first_kernel(
    share_rows, map_ref, in_ref, out_ref, raw_ref, right_ref, pair_ref, left_ref, mine_ref, inverse_ref, rows_ref, own_ref, sems
):
    own_rows = rows_ref.shape[0]
    sub = lax.axis_index("sub")
    module = map_ref[0]
    mine = out_ref.at[module, pl.ds(pl.multiple_of(sub * own_rows, own_rows), own_rows), :]
    copies = [
        pltpu.make_async_copy(in_ref.at[module], inverse_ref, sems.at[0]),
        pltpu.make_async_copy(mine, rows_ref, sems.at[1]),
        pltpu.make_async_copy(raw_ref, own_ref, sems.at[2]),
    ]
    for copy in copies:
        copy.start()
    copies[0].wait()
    high, low = split(inverse_ref[...].T)
    high, low = high.astype(f32), low.astype(f32)
    zero = jnp.zeros_like(high)
    pair = jnp.concatenate(
        [jnp.concatenate(row, axis=1) for row in ([high, zero], [zero, high], [low, zero], [zero, low])], axis=0
    ).astype(bf16)
    pair_ref[...] = pair
    copies[1].wait()
    rows = rows_ref[...]
    swapped = jnp.concatenate([rows[:, own_rows:], rows[:, :own_rows]], axis=1)
    rows = jnp.where(sub == 0, rows, swapped)
    high, low = split(rows)
    high, low = high.astype(f32), low.astype(f32)
    left = jnp.concatenate(
        [jnp.concatenate(row, axis=1) for row in ([high, high], [low, jnp.zeros_like(low)])], axis=0
    ).astype(bf16)
    left_ref[...] = left
    half = mine_ref.shape[0] // 2
    row = lax.broadcasted_iota(jnp.int32, (2 * half, 2 * own_rows), 0)
    column = lax.broadcasted_iota(jnp.int32, (2 * half, 2 * own_rows), 1)
    within = row - jnp.where(row < half, 0, half)
    wanted = within + lax.axis_index("groups") * share_rows + jnp.where(row < half, 0, own_rows)
    picker = jnp.where((column == wanted) & (within < share_rows), 1.0, 0.0).astype(bf16)
    mine_ref[...] = jnp.dot(picker, left, preferred_element_type=f32).astype(bf16)
    copies[2].wait()
    right_rows(pair, own_ref, right_ref)


def left_rows(left, own_ref, other_ref, done_ref, result_ref):
    rows = left.shape[0] // 2
    own_rows = left.shape[1] // 4
    step = own_ref.shape[0] // own_rows
    rank_in = step - PAD
    for first in range(0, rank_in, 2):
        wide = jnp.concatenate(
            [
                jnp.concatenate(
                    [
                        own_ref[pl.ds(column, own_rows, stride=step), :],
                        other_ref[pl.ds(column, own_rows, stride=step), :],
                    ],
                    axis=0,
                )
                for column in (first, first + 1)
            ],
            axis=1,
        )
        high, low = split(wide)
        both = jnp.dot(left, jnp.concatenate([high, low], axis=0), preferred_element_type=f32)
        both = both[:rows] + both[rows:]
        queries = both.shape[1] // 2
        done_ref[pl.ds(first, rows, stride=step), :] = both[:, :queries]
        done_ref[pl.ds(first + 1, rows, stride=step), :] = both[:, queries:]
    for row in range(result_ref.shape[0] // rank_in):
        result_ref[row * rank_in : (row + 1) * rank_in, :] = done_ref[row * step : row * step + rank_in, :].astype(bf16)


def share_kernel(pair_ref, left_ref, own_ref, raw_ref, result_ref, right_ref, done_ref):
    right_rows(pair_ref[...], raw_ref, right_ref)
    left_rows(left_ref[...], own_ref, right_ref, done_ref, result_ref)


def block_kernel(left_ref, own_ref, other_ref, result_ref, done_ref):
    left_rows(left_ref[...], own_ref, other_ref, done_ref, result_ref)


def preconditioned(query_grads, in_inverse, out_inverse, module_map, share_rows):
    block_rows, _, half_width = query_grads.shape
    rank_in, rank_out = in_inverse.shape[1], out_inverse.shape[1]
    own_rows = half_width // rank_in
    raw = query_grads.reshape(block_rows, half_width)
    other = shifted(raw, "sub", 1)
    anywhere = pl.BlockSpec(memory_space=pl.ANY)
    padded = -(-share_rows // 16) * 16
    right_shape = (own_rows * (rank_in + PAD), block_rows)
    own, pair, left, mine_left = pl.pallas_call(
        functools.partial(first_kernel, share_rows),
        out_shape=(
            pltpu.VMEM(right_shape, f32),
            pltpu.VMEM((4 * rank_in, 2 * rank_in), bf16),
            pltpu.VMEM((2 * own_rows, 2 * rank_out), bf16),
            pltpu.VMEM((2 * padded, 2 * rank_out), bf16),
        ),
        in_specs=[pl.BlockSpec(memory_space=pltpu.SMEM), anywhere, anywhere, anywhere],
        out_specs=[in_vmem] * 4,
        scratch_shapes=[
            pltpu.VMEM((rank_in, rank_in), f32),
            pltpu.VMEM((own_rows, rank_out), f32),
            pltpu.VMEM((block_rows, half_width), bf16),
            pltpu.SemaphoreType.DMA((3,)),
        ],
        compiler_params=params(),
        cost_estimate=cost(2),
    )(module_map, *[pltpu.with_memory_space_constraint(x, pltpu.HBM) for x in (in_inverse, out_inverse, raw)])
    mine, right = pl.pallas_call(
        share_kernel,
        out_shape=(pltpu.VMEM((share_rows * rank_in, block_rows), bf16), pltpu.VMEM(right_shape, f32)),
        in_specs=[in_vmem] * 4,
        out_specs=[in_vmem] * 2,
        scratch_shapes=[pltpu.VMEM((padded * (rank_in + PAD), block_rows), f32)],
        compiler_params=params(),
        cost_estimate=cost(1),
    )(*map(keep_near, (pair, mine_left, own, other)))
    precon = pl.pallas_call(
        block_kernel,
        out_shape=pltpu.VMEM((half_width, block_rows), bf16),
        in_specs=[in_vmem] * 3,
        out_specs=in_vmem,
        scratch_shapes=[pltpu.VMEM(right_shape, f32)],
        compiler_params=params(),
        cost_estimate=cost(0.1),
    )(*map(keep_near, (left, own, right)))
    return precon, mine


def part_dot(train_ref, ref, first):
    train = train_ref[:, pl.ds(first, ref.shape[0])]
    return jnp.dot(train, ref[...], preferred_element_type=f32)


def whole_kernel(mods, subs, train_ref, block_ref, *refs):
    outputs, sum_ref = refs[:-1], refs[-1]
    sum_ref[...] = part_dot(train_ref, block_ref, 0)
    rows = sum_ref.shape[0] // (mods * subs)
    for sub_step, output in enumerate(outputs):
        for mod_step in range(mods):
            output[mod_step * rows : (mod_step + 1) * rows, :] = sum_ref[peer_rows(mod_step, sub_step, mods, subs, rows), :].astype(output.dtype)


def peer_rows(mod_step, sub_step, mods, subs, rows):
    target = lax.rem(lax.axis_index("mod") + mod_step, mods) * subs
    target = target + lax.rem(lax.axis_index("sub") + sub_step, subs)
    return pl.ds(pl.multiple_of(target * rows, rows), rows)


def score_kernel(plans, dests, train_ref, *refs):
    count = sum(len(plan) for plan in plans)
    inputs, outputs, sums = list(refs[:count]), (), refs[-len(plans) :]
    if dests:
        outputs = refs[-len(plans) - dests : -len(plans)]
    parts = lax.axis_size("groups")
    for plan, sum_ref in zip(plans, sums):
        total = None
        for kind in plan:
            ref = inputs.pop(0)
            if kind == "total":
                term = ref[...]
            elif kind == "rest":
                term = part_dot(train_ref, ref, train_ref.shape[1] - ref.shape[0])
            else:
                share = ref.shape[0]
                source = lax.rem(lax.axis_index("groups") + parts - kind, parts)
                term = part_dot(train_ref, ref, pl.multiple_of(source * share, 128))
            total = term if total is None else total + term
        sum_ref[...] = total
    mods, subs = lax.axis_size("mod"), lax.axis_size("sub")
    rows = sums[0].shape[0] // (mods * subs)
    for dest, output in enumerate(outputs):
        place = peer_rows(*divmod(dest, subs), mods, subs, rows)
        for block, sum_ref in enumerate(sums):
            output[block * rows : (block + 1) * rows, :] = sum_ref[place, :].astype(output.dtype)


def cost(micros):
    return pl.CostEstimate(flops=int(micros * 1.15e9), bytes_accessed=0, transcendentals=0)


def add_kernel(count, *refs):
    inputs, outputs = refs[:count], refs[count:]
    rows = outputs[0].shape[0]
    for step, output in enumerate(outputs):
        total = None
        for ref in inputs:
            term = ref[step * rows : (step + 1) * rows, :].astype(f32)
            total = term if total is None else total + term
        output[...] = total.astype(output.dtype)


def whole(train, block):
    mods, subs = lax.axis_size("mod"), lax.axis_size("sub")
    rows, queries = train.shape[0] // (mods * subs), block.shape[1]
    dealt = pl.pallas_call(
        functools.partial(whole_kernel, mods, subs),
        out_shape=[pltpu.VMEM((mods * rows, queries), bf16 if step else f32) for step in range(subs)],
        in_specs=[in_vmem] * 2,
        out_specs=[in_vmem] * subs,
        scratch_shapes=[pltpu.VMEM((train.shape[0], queries), f32)],
        compiler_params=params(),
        cost_estimate=cost(1),
    )(keep_near(train), keep_near(block))
    terms = [to_peer(piece, 0, step) if step else piece for step, piece in enumerate(dealt)]
    added = pl.pallas_call(
        functools.partial(add_kernel, subs),
        out_shape=[pltpu.VMEM((rows, queries), f32)] * mods,
        in_specs=[in_vmem] * subs,
        out_specs=[in_vmem] * mods,
        compiler_params=params(),
        cost_estimate=cost(0.1),
    )(*map(keep_near, terms))
    return added, dealt


def held(value, first, after):
    def kernel(value_ref, *refs):
        refs[-1][...] = value_ref[first:, :]

    return pl.pallas_call(
        kernel,
        out_shape=pltpu.VMEM((value.shape[0] - first, value.shape[1]), value.dtype),
        in_specs=[in_vmem] + [pl.BlockSpec(memory_space=pl.ANY)] * len(after),
        out_specs=in_vmem,
        compiler_params=params(),
        cost_estimate=cost(0.1),
    )(keep_near(value), *after)


def scored(train, plans, arrays, dests=0, after=()):
    queries = arrays[0].shape[1]
    whole_shape = (train.shape[0], queries)
    sums = [pltpu.VMEM(whole_shape, f32)] * len(plans)
    part_shape = (len(plans) * train.shape[0] // max(dests, 1), queries)
    outputs = [pltpu.VMEM(part_shape, bf16 if dest else f32) for dest in range(dests)] or sums
    return pl.pallas_call(
        functools.partial(score_kernel, plans, dests),
        out_shape=outputs,
        in_specs=[in_vmem] * (1 + len(arrays)) + [pl.BlockSpec(memory_space=pl.ANY)] * len(after),
        out_specs=[in_vmem] * len(outputs),
        scratch_shapes=sums if dests else [],
        compiler_params=params(),
        cost_estimate=cost(0.1),
    )(*map(keep_near, (train, *arrays)), *after)


def settled(terms):
    def kernel(*refs):
        total = None
        for ref in refs[:-1]:
            term = ref[...].astype(f32)
            total = term if total is None else total + term
        refs[-1][...] = total

    return pl.pallas_call(
        kernel,
        out_shape=pltpu.VMEM(terms[0].shape, f32),
        in_specs=[in_vmem] * len(terms),
        out_specs=in_vmem,
        compiler_params=params(),
        cost_estimate=cost(0.1),
    )(*map(keep_near, terms))


def sum_kernel(places, counts, *refs):
    output = refs[-1]
    rows = output.shape[1]
    at = 0
    for blocks, count in zip(places, counts):
        for block, place in enumerate(blocks):
            total = None
            for ref in refs[at : at + count]:
                term = ref[block * rows : (block + 1) * rows, :].astype(f32)
                total = term if total is None else total + term
            output[place] = total
        at += count


def local(query_grads, train_grads, in_inverse, out_inverse, module_map):
    half_width = query_grads.shape[2]
    mods, subs = lax.axis_size("mod"), lax.axis_size("sub")
    parts, part = lax.axis_size("groups"), lax.axis_index("groups")
    reach = min(WINDOW_HALF, (lax.axis_size("ex") - 1) // 2)
    share = 5 * half_width // (8 * parts) // 128 * 128
    shared = share * parts
    precon, mine = preconditioned(query_grads, in_inverse, out_inverse, module_map, share // in_inverse.shape[1])
    train = train_grads.reshape(train_grads.shape[0], half_width)

    offsets = [sign * far for far in range(1, reach + 1) for sign in (-1, 1)]
    added, dealt = whole(train, precon)
    rest = held(precon, shared, added[:1])
    carried = {offset: shifted(mine, "ex", -offset) for offset in offsets}
    common = {offset: shifted(rest, "ex", -offset) for offset in offsets}
    *others, last = offsets
    plans = [[0]] + [[0, "rest"] for offset in others]
    arrays = [carried[last]] + [piece for offset in others for piece in (carried[offset], common[offset])]
    own = settled([to_peer(piece, step, 0) if step else piece for step, piece in enumerate(added)])
    total, *totals = scored(train, plans, arrays, after=[own])
    totals.append(total)
    plans = [["total", *range(1, parts)] for offset in offsets]
    arrays = []
    for offset, total in zip(offsets, totals):
        arrays += [total, *[shifted(carried[offset], "groups", step) for step in range(1, parts)]]
    totals = scored(train, plans, arrays)
    plans = [["total"] for offset in others] + [["total", "rest"]]
    partial = scored(train, plans, [*totals, common[last]], mods * subs)
    order = [0, *range(2, mods * subs), 1]
    terms = [to_peer(partial[dest], *divmod(dest, subs)) if dest else partial[0] for dest in order]
    terms.append(own)
    rows = train.shape[0] // (mods * subs)
    summed = pl.pallas_call(
        functools.partial(sum_kernel, [[offset + reach for offset in offsets], [reach]], [mods * subs, 1]),
        out_shape=jax.ShapeDtypeStruct((2 * reach + 1, rows, query_grads.shape[0]), f32),
        in_specs=[in_vmem] * len(terms),
        out_specs=in_vmem,
        compiler_params=params(),
        cost_estimate=cost(1),
    )(*[keep_near(term) for term in terms])
    return summed.transpose(1, 0, 2)


def solution(mesh):
    placed = (P("ex", "mod", "sub"), P(("groups", "ex"), "mod", "sub"), P(), P(), P("mod"))
    return jax.shard_map(
        local,
        mesh=mesh,
        in_specs=placed,
        out_specs=P(("groups", "ex", "mod", "sub"), None, None),
        check_vma=False,
    )
```

```python
import functools

import jax
import jax.numpy as jnp
from jax import lax
from jax.experimental import pallas as pl
from jax.experimental.pallas import tpu as pltpu
from jax.sharding import PartitionSpec as P

WINDOW_HALF = 2
PAD = 8
VMEM_LIMIT = 32 * 1024 * 1024

f32, bf16 = jnp.float32, jnp.bfloat16
in_vmem = pl.BlockSpec(memory_space=pltpu.VMEM)


def keep_near(value):
    return pltpu.with_memory_space_constraint(value, pltpu.VMEM)


def params():
    return pltpu.CompilerParams(vmem_limit_bytes=VMEM_LIMIT)


def shifted(value, axis, steps):
    count = lax.axis_size(axis)
    pairs = [(source, (source + steps) % count) for source in range(count)]
    return lax.ppermute(value, axis, pairs)


def to_peer(value, mod_step, sub_step):
    mods, subs = lax.axis_size("mod"), lax.axis_size("sub")
    pairs = []
    for mod in range(mods):
        for sub in range(subs):
            target = ((mod + mod_step) % mods) * subs + (sub + sub_step) % subs
            pairs.append((mod * subs + sub, target))
    return lax.ppermute(value, ("mod", "sub"), pairs)


def split(value):
    high = value.astype(bf16)
    return high, (value - high.astype(f32)).astype(bf16)


def nt_dot(lhs, rhs):
    return lax.dot_general(lhs, rhs, (((1,), (1,)), ((), ())), preferred_element_type=f32)


def right_rows(pair, raw, right_ref):
    width = pair.shape[1]
    queries = raw.shape[0]
    for first in range(0, raw.shape[1], 2 * width):
        pieces = [raw[:, at : at + width] for at in (first, first + width)]
        both = nt_dot(pair, jnp.concatenate(pieces, axis=0))
        both = both[:width] + both[width:]
        half = width // 2
        for index, lanes in enumerate((slice(0, queries), slice(queries, 2 * queries))):
            for row in range(2):
                at = (first // half + 2 * index + row) * (half + PAD)
                right_ref[at : at + half, :] = both[row * half : (row + 1) * half, lanes]


def first_kernel(
    map_ref, in_ref, out_ref, raw_ref, right_ref, pair_ref, left_ref, inverse_ref, rows_ref, own_ref, sems
):
    own_rows = rows_ref.shape[0]
    sub = lax.axis_index("sub")
    module = map_ref[0]
    mine = out_ref.at[module, pl.ds(pl.multiple_of(sub * own_rows, own_rows), own_rows), :]
    copies = [
        pltpu.make_async_copy(in_ref.at[module], inverse_ref, sems.at[0]),
        pltpu.make_async_copy(mine, rows_ref, sems.at[1]),
        pltpu.make_async_copy(raw_ref, own_ref, sems.at[2]),
    ]
    for copy in copies:
        copy.start()
    copies[0].wait()
    high, low = split(inverse_ref[...].T)
    high, low = high.astype(f32), low.astype(f32)
    zero = jnp.zeros_like(high)
    pair = jnp.concatenate(
        [jnp.concatenate(row, axis=1) for row in ([high, zero], [zero, high], [low, zero], [zero, low])], axis=0
    ).astype(bf16)
    pair_ref[...] = pair
    copies[1].wait()
    copies[2].wait()
    right_rows(pair, own_ref, right_ref)
    rows = rows_ref[...]
    swapped = jnp.concatenate([rows[:, own_rows:], rows[:, :own_rows]], axis=1)
    rows = jnp.where(sub == 0, rows, swapped)
    high, low = split(rows)
    high, low = high.astype(f32), low.astype(f32)
    left_ref[...] = jnp.concatenate(
        [jnp.concatenate(row, axis=1) for row in ([high, high], [low, jnp.zeros_like(low)])], axis=0
    ).astype(bf16)


def second_kernel(pair_ref, left_ref, own_ref, raw_ref, result_ref, right_ref, done_ref):
    own_rows = left_ref.shape[0] // 2
    rank_in = result_ref.shape[0] // own_rows
    step = rank_in + PAD
    right_rows(pair_ref[...], raw_ref, right_ref)
    left = left_ref[...]
    for first in range(0, rank_in, 2):
        wide = jnp.concatenate(
            [
                jnp.concatenate(
                    [
                        own_ref[pl.ds(column, own_rows, stride=step), :],
                        right_ref[pl.ds(column, own_rows, stride=step), :],
                    ],
                    axis=0,
                )
                for column in (first, first + 1)
            ],
            axis=1,
        )
        high, low = split(wide)
        both = jnp.dot(left, jnp.concatenate([high, low], axis=0), preferred_element_type=f32)
        both = both[:own_rows] + both[own_rows:]
        queries = both.shape[1] // 2
        done_ref[pl.ds(first, own_rows, stride=step), :] = both[:, :queries]
        done_ref[pl.ds(first + 1, own_rows, stride=step), :] = both[:, queries:]
    for row in range(own_rows):
        result_ref[row * rank_in : (row + 1) * rank_in, :] = done_ref[row * step : row * step + rank_in, :].astype(bf16)


def preconditioned(query_grads, in_inverse, out_inverse, module_map):
    block_rows, _, half_width = query_grads.shape
    rank_in, rank_out = in_inverse.shape[1], out_inverse.shape[1]
    own_rows = half_width // rank_in
    raw = query_grads.reshape(block_rows, half_width)
    other = shifted(raw, "sub", 1)
    anywhere = pl.BlockSpec(memory_space=pl.ANY)
    right, pair, left = pl.pallas_call(
        first_kernel,
        out_shape=(
            pltpu.VMEM((own_rows * (rank_in + PAD), block_rows), f32),
            pltpu.VMEM((4 * rank_in, 2 * rank_in), bf16),
            pltpu.VMEM((2 * own_rows, 2 * rank_out), bf16),
        ),
        in_specs=[pl.BlockSpec(memory_space=pltpu.SMEM), anywhere, anywhere, anywhere],
        out_specs=[in_vmem, in_vmem, in_vmem],
        scratch_shapes=[
            pltpu.VMEM((rank_in, rank_in), f32),
            pltpu.VMEM((own_rows, rank_out), f32),
            pltpu.VMEM((block_rows, half_width), bf16),
            pltpu.SemaphoreType.DMA((3,)),
        ],
        compiler_params=params(),
        cost_estimate=cost(2),
    )(module_map, *[pltpu.with_memory_space_constraint(x, pltpu.HBM) for x in (in_inverse, out_inverse, raw)])
    return pl.pallas_call(
        second_kernel,
        out_shape=pltpu.VMEM((half_width, block_rows), bf16),
        in_specs=[in_vmem] * 4,
        out_specs=in_vmem,
        scratch_shapes=[pltpu.VMEM((own_rows * (rank_in + PAD), block_rows), f32)] * 2,
        compiler_params=params(),
        cost_estimate=cost(2),
    )(keep_near(pair), keep_near(left), keep_near(right), keep_near(other))


def part_dot(train_ref, ref, first):
    train = train_ref[:, pl.ds(first, ref.shape[0])]
    return jnp.dot(train, ref[...], preferred_element_type=f32)


def whole_kernel(mods, subs, train_ref, block_ref, *refs):
    outputs, sum_ref = refs[:-1], refs[-1]
    sum_ref[...] = part_dot(train_ref, block_ref, 0)
    rows = sum_ref.shape[0] // (mods * subs)
    for sub_step, output in enumerate(outputs):
        for mod_step in range(mods):
            output[mod_step * rows : (mod_step + 1) * rows, :] = sum_ref[peer_rows(mod_step, sub_step, mods, subs, rows), :].astype(output.dtype)


def peer_rows(mod_step, sub_step, mods, subs, rows):
    target = lax.rem(lax.axis_index("mod") + mod_step, mods) * subs
    target = target + lax.rem(lax.axis_index("sub") + sub_step, subs)
    return pl.ds(pl.multiple_of(target * rows, rows), rows)


def score_kernel(plans, dests, train_ref, *refs):
    count = sum(len(plan) for plan in plans)
    inputs, outputs, sums = list(refs[:count]), (), refs[-len(plans) :]
    if dests:
        outputs = refs[-len(plans) - dests : -len(plans)]
    parts = lax.axis_size("groups")
    blocks = []
    for plan, sum_ref in zip(plans, sums):
        if plan == ["total"]:
            blocks.append(inputs.pop(0))
            continue
        blocks.append(sum_ref)
        total = None
        for kind in plan:
            ref = inputs.pop(0)
            if kind == "total":
                term = ref[...]
            elif kind == "rest":
                term = part_dot(train_ref, ref, train_ref.shape[1] - ref.shape[0])
            else:
                share = ref.shape[0]
                source = lax.rem(lax.axis_index("groups") + parts - kind, parts)
                term = part_dot(train_ref, ref, pl.multiple_of(source * share, 128))
            total = term if total is None else total + term
        sum_ref[...] = total
    mods, subs = lax.axis_size("mod"), lax.axis_size("sub")
    rows = sums[0].shape[0] // (mods * subs)
    for dest, output in enumerate(outputs):
        place = peer_rows(*divmod(dest, subs), mods, subs, rows)
        for block, block_ref in enumerate(blocks):
            output[block * rows : (block + 1) * rows, :] = block_ref[place, :].astype(output.dtype)


def cost(micros):
    return pl.CostEstimate(flops=int(micros * 1.15e9), bytes_accessed=0, transcendentals=0)


def add_kernel(count, *refs):
    inputs, outputs = refs[:count], refs[count:]
    rows = outputs[0].shape[0]
    for step, output in enumerate(outputs):
        total = None
        for ref in inputs:
            term = ref[step * rows : (step + 1) * rows, :].astype(f32)
            total = term if total is None else total + term
        output[...] = total.astype(output.dtype)


def whole(train, block):
    mods, subs = lax.axis_size("mod"), lax.axis_size("sub")
    rows, queries = train.shape[0] // (mods * subs), block.shape[1]
    dealt = pl.pallas_call(
        functools.partial(whole_kernel, mods, subs),
        out_shape=[pltpu.VMEM((mods * rows, queries), bf16 if step else f32) for step in range(subs)],
        in_specs=[in_vmem] * 2,
        out_specs=[in_vmem] * subs,
        scratch_shapes=[pltpu.VMEM((train.shape[0], queries), f32)],
        compiler_params=params(),
        cost_estimate=cost(1),
    )(keep_near(train), keep_near(block))
    terms = [to_peer(piece, 0, step) if step else piece for step, piece in enumerate(dealt)]
    added = pl.pallas_call(
        functools.partial(add_kernel, subs),
        out_shape=[pltpu.VMEM((rows, queries), f32)] * mods,
        in_specs=[in_vmem] * subs,
        out_specs=[in_vmem] * mods,
        compiler_params=params(),
        cost_estimate=cost(0.1),
    )(*map(keep_near, terms))
    return added, dealt


def held(value, first, after):
    def kernel(value_ref, *refs):
        refs[-1][...] = value_ref[first:, :]

    return pl.pallas_call(
        kernel,
        out_shape=pltpu.VMEM((value.shape[0] - first, value.shape[1]), value.dtype),
        in_specs=[in_vmem] + [pl.BlockSpec(memory_space=pl.ANY)] * len(after),
        out_specs=in_vmem,
        compiler_params=params(),
        cost_estimate=cost(0.1),
    )(keep_near(value), *after)


def scored(train, plans, arrays, dests=0, after=()):
    queries = arrays[0].shape[1]
    whole_shape = (train.shape[0], queries)
    sums = [pltpu.VMEM(whole_shape, f32)] * len(plans)
    part_shape = (len(plans) * train.shape[0] // max(dests, 1), queries)
    outputs = [pltpu.VMEM(part_shape, bf16 if dest else f32) for dest in range(dests)] or sums
    return pl.pallas_call(
        functools.partial(score_kernel, plans, dests),
        out_shape=outputs,
        in_specs=[in_vmem] * (1 + len(arrays)) + [pl.BlockSpec(memory_space=pl.ANY)] * len(after),
        out_specs=[in_vmem] * len(outputs),
        scratch_shapes=sums if dests else [],
        compiler_params=params(),
        cost_estimate=cost(0.1),
    )(*map(keep_near, (train, *arrays)), *after)


def settled(terms):
    def kernel(*refs):
        total = None
        for ref in refs[:-1]:
            term = ref[...].astype(f32)
            total = term if total is None else total + term
        refs[-1][...] = total

    return pl.pallas_call(
        kernel,
        out_shape=pltpu.VMEM(terms[0].shape, f32),
        in_specs=[in_vmem] * len(terms),
        out_specs=in_vmem,
        compiler_params=params(),
        cost_estimate=cost(0.1),
    )(*map(keep_near, terms))


def sum_kernel(places, counts, *refs):
    output = refs[-1]
    rows = output.shape[1]
    at = 0
    for blocks, count in zip(places, counts):
        for block, place in enumerate(blocks):
            total = None
            for ref in refs[at : at + count]:
                term = ref[block * rows : (block + 1) * rows, :].astype(f32)
                total = term if total is None else total + term
            output[place] = total
        at += count


def local(query_grads, train_grads, in_inverse, out_inverse, module_map):
    half_width = query_grads.shape[2]
    mods, subs = lax.axis_size("mod"), lax.axis_size("sub")
    parts, part = lax.axis_size("groups"), lax.axis_index("groups")
    reach = min(WINDOW_HALF, (lax.axis_size("ex") - 1) // 2)
    precon = preconditioned(query_grads, in_inverse, out_inverse, module_map)

    share = 5 * half_width // (8 * parts) // 128 * 128
    shared = share * parts
    train = train_grads.reshape(train_grads.shape[0], half_width)

    offsets = [sign * far for far in range(1, reach + 1) for sign in (-1, 1)]
    mine = lax.dynamic_slice_in_dim(precon, part * share, share, 0)
    added, dealt = whole(train, precon)
    rest = held(precon, shared, added[:1])
    carried = {offset: shifted(mine, "ex", -offset) for offset in offsets}
    common = {offset: shifted(rest, "ex", -offset) for offset in offsets}
    *others, last = offsets
    plans = [[0, "rest"] for offset in others] + [[0]]
    arrays = [piece for offset in others for piece in (carried[offset], common[offset])] + [carried[last]]
    own = settled([to_peer(piece, step, 0) if step else piece for step, piece in enumerate(added)])
    totals = scored(train, plans, arrays, after=[own])
    plans = [["total", *range(1, parts)] for offset in offsets]
    arrays = []
    for offset, total in zip(offsets, totals):
        arrays += [total, *[shifted(carried[offset], "groups", step) for step in range(1, parts)]]
    swapped = scored(train, plans, arrays)
    plans = [["total"] for offset in others] + [["total", "rest"]]
    partial = scored(train, plans, [*swapped, common[last]], mods * subs)
    terms = [to_peer(rows, *divmod(dest, subs)) if dest else rows for dest, rows in reversed(list(enumerate(partial)))]
    terms.append(own)
    rows = train.shape[0] // (mods * subs)
    summed = pl.pallas_call(
        functools.partial(sum_kernel, [[offset + reach for offset in offsets], [reach]], [mods * subs, 1]),
        out_shape=jax.ShapeDtypeStruct((2 * reach + 1, rows, query_grads.shape[0]), f32),
        in_specs=[in_vmem] * len(terms),
        out_specs=in_vmem,
        compiler_params=params(),
        cost_estimate=cost(1),
    )(*[keep_near(term) for term in terms])
    return summed.transpose(1, 0, 2)


def solution(mesh):
    placed = (P("ex", "mod", "sub"), P(("groups", "ex"), "mod", "sub"), P(), P(), P("mod"))
    return jax.shard_map(
        local,
        mesh=mesh,
        in_specs=placed,
        out_specs=P(("groups", "ex", "mod", "sub"), None, None),
        check_vma=False,
    )
```

```python
import functools

import jax
import jax.numpy as jnp
from jax import lax
from jax.experimental import pallas as pl
from jax.experimental.pallas import tpu as pltpu
from jax.sharding import PartitionSpec as P

WINDOW_HALF = 2
PAD = 8
VMEM_LIMIT = 32 * 1024 * 1024

f32, bf16 = jnp.float32, jnp.bfloat16
in_vmem = pl.BlockSpec(memory_space=pltpu.VMEM)


def keep_near(value):
    return pltpu.with_memory_space_constraint(value, pltpu.VMEM)


def params():
    return pltpu.CompilerParams(vmem_limit_bytes=VMEM_LIMIT)


def shifted(value, axis, steps):
    count = lax.axis_size(axis)
    pairs = [(source, (source + steps) % count) for source in range(count)]
    return lax.ppermute(value, axis, pairs)


def to_peer(value, mod_step, sub_step):
    mods, subs = lax.axis_size("mod"), lax.axis_size("sub")
    pairs = []
    for mod in range(mods):
        for sub in range(subs):
            target = ((mod + mod_step) % mods) * subs + (sub + sub_step) % subs
            pairs.append((mod * subs + sub, target))
    return lax.ppermute(value, ("mod", "sub"), pairs)


def split(value):
    high = value.astype(bf16)
    return high, (value - high.astype(f32)).astype(bf16)


def nt_dot(lhs, rhs):
    return lax.dot_general(lhs, rhs, (((1,), (1,)), ((), ())), preferred_element_type=f32)


def right_rows(pair, raw, right_ref):
    width = pair.shape[1]
    queries = raw.shape[0]
    for first in range(0, raw.shape[1], 2 * width):
        pieces = [raw[:, at : at + width] for at in (first, first + width)]
        both = nt_dot(pair, jnp.concatenate(pieces, axis=0))
        both = both[:width] + both[width:]
        half = width // 2
        for index, lanes in enumerate((slice(0, queries), slice(queries, 2 * queries))):
            for row in range(2):
                at = (first // half + 2 * index + row) * (half + PAD)
                right_ref[at : at + half, :] = both[row * half : (row + 1) * half, lanes]


def first_kernel(
    map_ref, in_ref, out_ref, raw_ref, right_ref, pair_ref, left_ref, inverse_ref, rows_ref, own_ref, sems
):
    own_rows = rows_ref.shape[0]
    sub = lax.axis_index("sub")
    module = map_ref[0]
    mine = out_ref.at[module, pl.ds(pl.multiple_of(sub * own_rows, own_rows), own_rows), :]
    copies = [
        pltpu.make_async_copy(in_ref.at[module], inverse_ref, sems.at[0]),
        pltpu.make_async_copy(mine, rows_ref, sems.at[1]),
        pltpu.make_async_copy(raw_ref, own_ref, sems.at[2]),
    ]
    for copy in copies:
        copy.start()
    copies[0].wait()
    high, low = split(inverse_ref[...].T)
    high, low = high.astype(f32), low.astype(f32)
    zero = jnp.zeros_like(high)
    pair = jnp.concatenate(
        [jnp.concatenate(row, axis=1) for row in ([high, zero], [zero, high], [low, zero], [zero, low])], axis=0
    ).astype(bf16)
    pair_ref[...] = pair
    copies[1].wait()
    rows = rows_ref[...]
    swapped = jnp.concatenate([rows[:, own_rows:], rows[:, :own_rows]], axis=1)
    rows = jnp.where(sub == 0, rows, swapped)
    high, low = split(rows)
    high, low = high.astype(f32), low.astype(f32)
    left_ref[...] = jnp.concatenate(
        [jnp.concatenate(row, axis=1) for row in ([high, high], [low, jnp.zeros_like(low)])], axis=0
    ).astype(bf16)
    copies[2].wait()
    right_rows(pair, own_ref, right_ref)


def second_kernel(pair_ref, left_ref, own_ref, raw_ref, result_ref, right_ref, done_ref):
    own_rows = left_ref.shape[0] // 2
    rank_in = result_ref.shape[0] // own_rows
    step = rank_in + PAD
    right_rows(pair_ref[...], raw_ref, right_ref)
    left = left_ref[...]
    for first in range(0, rank_in, 2):
        wide = jnp.concatenate(
            [
                jnp.concatenate(
                    [
                        own_ref[pl.ds(column, own_rows, stride=step), :],
                        right_ref[pl.ds(column, own_rows, stride=step), :],
                    ],
                    axis=0,
                )
                for column in (first, first + 1)
            ],
            axis=1,
        )
        high, low = split(wide)
        both = jnp.dot(left, jnp.concatenate([high, low], axis=0), preferred_element_type=f32)
        both = both[:own_rows] + both[own_rows:]
        queries = both.shape[1] // 2
        done_ref[pl.ds(first, own_rows, stride=step), :] = both[:, :queries]
        done_ref[pl.ds(first + 1, own_rows, stride=step), :] = both[:, queries:]
    for row in range(own_rows):
        result_ref[row * rank_in : (row + 1) * rank_in, :] = done_ref[row * step : row * step + rank_in, :].astype(bf16)


def preconditioned(query_grads, in_inverse, out_inverse, module_map):
    block_rows, _, half_width = query_grads.shape
    rank_in, rank_out = in_inverse.shape[1], out_inverse.shape[1]
    own_rows = half_width // rank_in
    raw = query_grads.reshape(block_rows, half_width)
    other = shifted(raw, "sub", 1)
    anywhere = pl.BlockSpec(memory_space=pl.ANY)
    right, pair, left = pl.pallas_call(
        first_kernel,
        out_shape=(
            pltpu.VMEM((own_rows * (rank_in + PAD), block_rows), f32),
            pltpu.VMEM((4 * rank_in, 2 * rank_in), bf16),
            pltpu.VMEM((2 * own_rows, 2 * rank_out), bf16),
        ),
        in_specs=[pl.BlockSpec(memory_space=pltpu.SMEM), anywhere, anywhere, anywhere],
        out_specs=[in_vmem, in_vmem, in_vmem],
        scratch_shapes=[
            pltpu.VMEM((rank_in, rank_in), f32),
            pltpu.VMEM((own_rows, rank_out), f32),
            pltpu.VMEM((block_rows, half_width), bf16),
            pltpu.SemaphoreType.DMA((3,)),
        ],
        compiler_params=params(),
        cost_estimate=cost(2),
    )(module_map, *[pltpu.with_memory_space_constraint(x, pltpu.HBM) for x in (in_inverse, out_inverse, raw)])
    return pl.pallas_call(
        second_kernel,
        out_shape=pltpu.VMEM((half_width, block_rows), bf16),
        in_specs=[in_vmem] * 4,
        out_specs=in_vmem,
        scratch_shapes=[pltpu.VMEM((own_rows * (rank_in + PAD), block_rows), f32)] * 2,
        compiler_params=params(),
        cost_estimate=cost(2),
    )(keep_near(pair), keep_near(left), keep_near(right), keep_near(other))


def part_dot(train_ref, ref, first):
    train = train_ref[:, pl.ds(first, ref.shape[0])]
    return jnp.dot(train, ref[...], preferred_element_type=f32)


def whole_kernel(mods, subs, train_ref, block_ref, *refs):
    outputs, sum_ref = refs[:-1], refs[-1]
    sum_ref[...] = part_dot(train_ref, block_ref, 0)
    rows = sum_ref.shape[0] // (mods * subs)
    for sub_step, output in enumerate(outputs):
        for mod_step in range(mods):
            output[mod_step * rows : (mod_step + 1) * rows, :] = sum_ref[peer_rows(mod_step, sub_step, mods, subs, rows), :].astype(output.dtype)


def peer_rows(mod_step, sub_step, mods, subs, rows):
    target = lax.rem(lax.axis_index("mod") + mod_step, mods) * subs
    target = target + lax.rem(lax.axis_index("sub") + sub_step, subs)
    return pl.ds(pl.multiple_of(target * rows, rows), rows)


def score_kernel(plans, dests, train_ref, *refs):
    count = sum(len(plan) for plan in plans)
    inputs, outputs, sums = list(refs[:count]), (), refs[-len(plans) :]
    if dests:
        outputs = refs[-len(plans) - dests : -len(plans)]
    parts = lax.axis_size("groups")
    for plan, sum_ref in zip(plans, sums):
        total = None
        for kind in plan:
            ref = inputs.pop(0)
            if kind == "total":
                term = ref[...]
            elif kind == "rest":
                term = part_dot(train_ref, ref, train_ref.shape[1] - ref.shape[0])
            else:
                share = ref.shape[0]
                source = lax.rem(lax.axis_index("groups") + parts - kind, parts)
                term = part_dot(train_ref, ref, pl.multiple_of(source * share, 128))
            total = term if total is None else total + term
        sum_ref[...] = total
    mods, subs = lax.axis_size("mod"), lax.axis_size("sub")
    rows = sums[0].shape[0] // (mods * subs)
    for dest, output in enumerate(outputs):
        place = peer_rows(*divmod(dest, subs), mods, subs, rows)
        for block, sum_ref in enumerate(sums):
            output[block * rows : (block + 1) * rows, :] = sum_ref[place, :].astype(output.dtype)


def cost(micros):
    return pl.CostEstimate(flops=int(micros * 1.15e9), bytes_accessed=0, transcendentals=0)


def add_kernel(count, *refs):
    inputs, outputs = refs[:count], refs[count:]
    rows = outputs[0].shape[0]
    for step, output in enumerate(outputs):
        total = None
        for ref in inputs:
            term = ref[step * rows : (step + 1) * rows, :].astype(f32)
            total = term if total is None else total + term
        output[...] = total.astype(output.dtype)


def whole(train, block):
    mods, subs = lax.axis_size("mod"), lax.axis_size("sub")
    rows, queries = train.shape[0] // (mods * subs), block.shape[1]
    dealt = pl.pallas_call(
        functools.partial(whole_kernel, mods, subs),
        out_shape=[pltpu.VMEM((mods * rows, queries), bf16 if step else f32) for step in range(subs)],
        in_specs=[in_vmem] * 2,
        out_specs=[in_vmem] * subs,
        scratch_shapes=[pltpu.VMEM((train.shape[0], queries), f32)],
        compiler_params=params(),
        cost_estimate=cost(1),
    )(keep_near(train), keep_near(block))
    terms = [to_peer(piece, 0, step) if step else piece for step, piece in enumerate(dealt)]
    added = pl.pallas_call(
        functools.partial(add_kernel, subs),
        out_shape=[pltpu.VMEM((rows, queries), f32)] * mods,
        in_specs=[in_vmem] * subs,
        out_specs=[in_vmem] * mods,
        compiler_params=params(),
        cost_estimate=cost(0.1),
    )(*map(keep_near, terms))
    return added, dealt


def held(value, first, after):
    def kernel(value_ref, *refs):
        refs[-1][...] = value_ref[first:, :]

    return pl.pallas_call(
        kernel,
        out_shape=pltpu.VMEM((value.shape[0] - first, value.shape[1]), value.dtype),
        in_specs=[in_vmem] + [pl.BlockSpec(memory_space=pl.ANY)] * len(after),
        out_specs=in_vmem,
        compiler_params=params(),
        cost_estimate=cost(0.1),
    )(keep_near(value), *after)


def sign_of(value):
    def kernel(value_ref, output):
        output[...] = value_ref[:16, :]

    return pl.pallas_call(
        kernel,
        out_shape=pltpu.VMEM((16, value.shape[1]), value.dtype),
        in_specs=[in_vmem],
        out_specs=in_vmem,
        compiler_params=params(),
        cost_estimate=cost(0.1),
    )(keep_near(value))


def scored(train, plans, arrays, dests=0, after=(), micros=0.1):
    queries = arrays[0].shape[1]
    whole_shape = (train.shape[0], queries)
    sums = [pltpu.VMEM(whole_shape, f32)] * len(plans)
    part_shape = (len(plans) * train.shape[0] // max(dests, 1), queries)
    outputs = [pltpu.VMEM(part_shape, bf16 if dest else f32) for dest in range(dests)] or sums
    return pl.pallas_call(
        functools.partial(score_kernel, plans, dests),
        out_shape=outputs,
        in_specs=[in_vmem] * (1 + len(arrays)) + [pl.BlockSpec(memory_space=pl.ANY)] * len(after),
        out_specs=[in_vmem] * len(outputs),
        scratch_shapes=sums if dests else [],
        compiler_params=params(),
        cost_estimate=cost(micros),
    )(*map(keep_near, (train, *arrays)), *after)


def settled(terms):
    def kernel(*refs):
        total = None
        for ref in refs[:-1]:
            term = ref[...].astype(f32)
            total = term if total is None else total + term
        refs[-1][...] = total

    return pl.pallas_call(
        kernel,
        out_shape=pltpu.VMEM(terms[0].shape, f32),
        in_specs=[in_vmem] * len(terms),
        out_specs=in_vmem,
        compiler_params=params(),
        cost_estimate=cost(0.1),
    )(*map(keep_near, terms))


def sum_kernel(places, counts, *refs):
    output = refs[-1]
    rows = output.shape[1]
    at = 0
    for blocks, count in zip(places, counts):
        for block, place in enumerate(blocks):
            total = None
            for ref in refs[at : at + count]:
                term = ref[block * rows : (block + 1) * rows, :].astype(f32)
                total = term if total is None else total + term
            output[place] = total
        at += count


def local(query_grads, train_grads, in_inverse, out_inverse, module_map):
    half_width = query_grads.shape[2]
    mods, subs = lax.axis_size("mod"), lax.axis_size("sub")
    parts, part = lax.axis_size("groups"), lax.axis_index("groups")
    reach = min(WINDOW_HALF, (lax.axis_size("ex") - 1) // 2)
    precon = preconditioned(query_grads, in_inverse, out_inverse, module_map)

    share = 5 * half_width // (8 * parts) // 128 * 128
    shared = share * parts
    train = train_grads.reshape(train_grads.shape[0], half_width)

    offsets = [sign * far for far in range(1, reach + 1) for sign in (-1, 1)]
    mine = lax.dynamic_slice_in_dim(precon, part * share, share, 0)
    added, dealt = whole(train, precon)
    own = settled([to_peer(piece, step, 0) if step else piece for step, piece in enumerate(added)])
    rest = held(precon, shared, added[:1])
    carried = {offset: shifted(mine, "ex", -offset) for offset in offsets}
    *others, last = offsets
    common = {offset: shifted(rest, "ex", -offset) for offset in others}
    common[last] = shifted(held(precon, shared, [sign_of(carried[offset]) for offset in offsets[:1]]), "ex", -last)
    plans = [[0, "rest"] for offset in others] + [[0]]
    arrays = [piece for offset in others for piece in (carried[offset], common[offset])] + [carried[last]]
    totals = scored(train, plans, arrays)
    plans = [["total", *range(1, parts)] for offset in offsets]
    arrays = []
    for offset, total in zip(offsets, totals):
        mine = held(carried[offset], 0, [own]) if offset == offsets[0] else carried[offset]
        arrays += [total, *[shifted(mine, "groups", step) for step in range(1, parts)]]
    totals = scored(train, plans, arrays, micros=8)
    plans = [["total"] for offset in others] + [["total", "rest"]]
    partial = scored(train, plans, [*totals, common[last]], mods * subs)
    terms = [to_peer(rows, *divmod(dest, subs)) if dest else rows for dest, rows in reversed(list(enumerate(partial)))]
    terms.append(own)
    rows = train.shape[0] // (mods * subs)
    summed = pl.pallas_call(
        functools.partial(sum_kernel, [[offset + reach for offset in offsets], [reach]], [mods * subs, 1]),
        out_shape=jax.ShapeDtypeStruct((2 * reach + 1, rows, query_grads.shape[0]), f32),
        in_specs=[in_vmem] * len(terms),
        out_specs=in_vmem,
        compiler_params=params(),
        cost_estimate=cost(1),
    )(*[keep_near(term) for term in terms])
    return summed.transpose(1, 0, 2)


def solution(mesh):
    placed = (P("ex", "mod", "sub"), P(("groups", "ex"), "mod", "sub"), P(), P(), P("mod"))
    return jax.shard_map(
        local,
        mesh=mesh,
        in_specs=placed,
        out_specs=P(("groups", "ex", "mod", "sub"), None, None),
        check_vma=False,
    )
```

```python
import functools

import jax
import jax.numpy as jnp
from jax import lax
from jax.experimental import pallas as pl
from jax.experimental.pallas import tpu as pltpu
from jax.sharding import PartitionSpec as P

WINDOW_HALF = 2
PAD = 8
VMEM_LIMIT = 32 * 1024 * 1024

f32, bf16 = jnp.float32, jnp.bfloat16
in_vmem = pl.BlockSpec(memory_space=pltpu.VMEM)


def keep_near(value):
    return pltpu.with_memory_space_constraint(value, pltpu.VMEM)


def params():
    return pltpu.CompilerParams(vmem_limit_bytes=VMEM_LIMIT)


def shifted(value, axis, steps):
    count = lax.axis_size(axis)
    pairs = [(source, (source + steps) % count) for source in range(count)]
    return lax.ppermute(value, axis, pairs)


def to_peer(value, mod_step, sub_step):
    mods, subs = lax.axis_size("mod"), lax.axis_size("sub")
    pairs = []
    for mod in range(mods):
        for sub in range(subs):
            target = ((mod + mod_step) % mods) * subs + (sub + sub_step) % subs
            pairs.append((mod * subs + sub, target))
    return lax.ppermute(value, ("mod", "sub"), pairs)


def split(value):
    high = value.astype(bf16)
    return high, (value - high.astype(f32)).astype(bf16)


def nt_dot(lhs, rhs):
    return lax.dot_general(lhs, rhs, (((1,), (1,)), ((), ())), preferred_element_type=f32)


def right_rows(pair, raw, right_ref):
    width = pair.shape[1]
    queries = raw.shape[0]
    for first in range(0, raw.shape[1], 2 * width):
        pieces = [raw[:, at : at + width] for at in (first, first + width)]
        both = nt_dot(pair, jnp.concatenate(pieces, axis=0))
        both = both[:width] + both[width:]
        half = width // 2
        for index, lanes in enumerate((slice(0, queries), slice(queries, 2 * queries))):
            for row in range(2):
                at = (first // half + 2 * index + row) * (half + PAD)
                right_ref[at : at + half, :] = both[row * half : (row + 1) * half, lanes]


def first_kernel(
    map_ref, in_ref, out_ref, raw_ref, right_ref, pair_ref, left_ref, inverse_ref, rows_ref, own_ref, sems
):
    own_rows = rows_ref.shape[0]
    sub = lax.axis_index("sub")
    module = map_ref[0]
    mine = out_ref.at[module, pl.ds(pl.multiple_of(sub * own_rows, own_rows), own_rows), :]
    copies = [
        pltpu.make_async_copy(in_ref.at[module], inverse_ref, sems.at[0]),
        pltpu.make_async_copy(mine, rows_ref, sems.at[1]),
        pltpu.make_async_copy(raw_ref, own_ref, sems.at[2]),
    ]
    for copy in copies:
        copy.start()
    copies[0].wait()
    high, low = split(inverse_ref[...].T)
    high, low = high.astype(f32), low.astype(f32)
    zero = jnp.zeros_like(high)
    pair = jnp.concatenate(
        [jnp.concatenate(row, axis=1) for row in ([high, zero], [zero, high], [low, zero], [zero, low])], axis=0
    ).astype(bf16)
    pair_ref[...] = pair
    copies[1].wait()
    rows = rows_ref[...]
    swapped = jnp.concatenate([rows[:, own_rows:], rows[:, :own_rows]], axis=1)
    rows = jnp.where(sub == 0, rows, swapped)
    high, low = split(rows)
    high, low = high.astype(f32), low.astype(f32)
    left_ref[...] = jnp.concatenate(
        [jnp.concatenate(row, axis=1) for row in ([high, high], [low, jnp.zeros_like(low)])], axis=0
    ).astype(bf16)
    copies[2].wait()
    right_rows(pair, own_ref, right_ref)


def second_kernel(pair_ref, left_ref, own_ref, raw_ref, result_ref, right_ref, done_ref):
    own_rows = left_ref.shape[0] // 2
    rank_in = result_ref.shape[0] // own_rows
    step = rank_in + PAD
    right_rows(pair_ref[...], raw_ref, right_ref)
    left = left_ref[...]
    for first in range(0, rank_in, 2):
        wide = jnp.concatenate(
            [
                jnp.concatenate(
                    [
                        own_ref[pl.ds(column, own_rows, stride=step), :],
                        right_ref[pl.ds(column, own_rows, stride=step), :],
                    ],
                    axis=0,
                )
                for column in (first, first + 1)
            ],
            axis=1,
        )
        high, low = split(wide)
        both = jnp.dot(left, jnp.concatenate([high, low], axis=0), preferred_element_type=f32)
        both = both[:own_rows] + both[own_rows:]
        queries = both.shape[1] // 2
        done_ref[pl.ds(first, own_rows, stride=step), :] = both[:, :queries]
        done_ref[pl.ds(first + 1, own_rows, stride=step), :] = both[:, queries:]
    for row in range(own_rows):
        result_ref[row * rank_in : (row + 1) * rank_in, :] = done_ref[row * step : row * step + rank_in, :].astype(bf16)


def preconditioned(query_grads, in_inverse, out_inverse, module_map):
    block_rows, _, half_width = query_grads.shape
    rank_in, rank_out = in_inverse.shape[1], out_inverse.shape[1]
    own_rows = half_width // rank_in
    raw = query_grads.reshape(block_rows, half_width)
    other = shifted(raw, "sub", 1)
    anywhere = pl.BlockSpec(memory_space=pl.ANY)
    right, pair, left = pl.pallas_call(
        first_kernel,
        out_shape=(
            pltpu.VMEM((own_rows * (rank_in + PAD), block_rows), f32),
            pltpu.VMEM((4 * rank_in, 2 * rank_in), bf16),
            pltpu.VMEM((2 * own_rows, 2 * rank_out), bf16),
        ),
        in_specs=[pl.BlockSpec(memory_space=pltpu.SMEM), anywhere, anywhere, anywhere],
        out_specs=[in_vmem, in_vmem, in_vmem],
        scratch_shapes=[
            pltpu.VMEM((rank_in, rank_in), f32),
            pltpu.VMEM((own_rows, rank_out), f32),
            pltpu.VMEM((block_rows, half_width), bf16),
            pltpu.SemaphoreType.DMA((3,)),
        ],
        compiler_params=params(),
        cost_estimate=cost(2),
    )(module_map, *[pltpu.with_memory_space_constraint(x, pltpu.HBM) for x in (in_inverse, out_inverse, raw)])
    return pl.pallas_call(
        second_kernel,
        out_shape=pltpu.VMEM((half_width, block_rows), bf16),
        in_specs=[in_vmem] * 4,
        out_specs=in_vmem,
        scratch_shapes=[pltpu.VMEM((own_rows * (rank_in + PAD), block_rows), f32)] * 2,
        compiler_params=params(),
        cost_estimate=cost(2),
    )(keep_near(pair), keep_near(left), keep_near(right), keep_near(other))


def part_dot(train_ref, ref, first):
    train = train_ref[:, pl.ds(first, ref.shape[0])]
    return jnp.dot(train, ref[...], preferred_element_type=f32)


def whole_kernel(mods, subs, train_ref, block_ref, *refs):
    outputs, sum_ref = refs[:-1], refs[-1]
    sum_ref[...] = part_dot(train_ref, block_ref, 0)
    rows = sum_ref.shape[0] // (mods * subs)
    for sub_step, output in enumerate(outputs):
        for mod_step in range(mods):
            output[mod_step * rows : (mod_step + 1) * rows, :] = sum_ref[peer_rows(mod_step, sub_step, mods, subs, rows), :].astype(output.dtype)


def peer_rows(mod_step, sub_step, mods, subs, rows):
    target = lax.rem(lax.axis_index("mod") + mod_step, mods) * subs
    target = target + lax.rem(lax.axis_index("sub") + sub_step, subs)
    return pl.ds(pl.multiple_of(target * rows, rows), rows)


def score_kernel(plans, dests, train_ref, *refs):
    count = sum(len(plan) for plan in plans)
    inputs, outputs, sums = list(refs[:count]), (), refs[-len(plans) :]
    if dests:
        outputs = refs[-len(plans) - dests : -len(plans)]
    parts = lax.axis_size("groups")
    for plan, sum_ref in zip(plans, sums):
        total = None
        for kind in plan:
            ref = inputs.pop(0)
            if kind == "total":
                term = ref[...]
            elif kind == "rest":
                term = part_dot(train_ref, ref, train_ref.shape[1] - ref.shape[0])
            else:
                share = ref.shape[0]
                source = lax.rem(lax.axis_index("groups") + parts - kind, parts)
                term = part_dot(train_ref, ref, pl.multiple_of(source * share, 128))
            total = term if total is None else total + term
        sum_ref[...] = total
    mods, subs = lax.axis_size("mod"), lax.axis_size("sub")
    rows = sums[0].shape[0] // (mods * subs)
    for dest, output in enumerate(outputs):
        place = peer_rows(*divmod(dest, subs), mods, subs, rows)
        for block, sum_ref in enumerate(sums):
            output[block * rows : (block + 1) * rows, :] = sum_ref[place, :].astype(output.dtype)


def cost(micros):
    return pl.CostEstimate(flops=int(micros * 1.15e9), bytes_accessed=0, transcendentals=0)


def add_kernel(count, *refs):
    inputs, outputs = refs[:count], refs[count:]
    rows = outputs[0].shape[0]
    for step, output in enumerate(outputs):
        total = None
        for ref in inputs:
            term = ref[step * rows : (step + 1) * rows, :].astype(f32)
            total = term if total is None else total + term
        output[...] = total.astype(output.dtype)


def whole(train, block):
    mods, subs = lax.axis_size("mod"), lax.axis_size("sub")
    rows, queries = train.shape[0] // (mods * subs), block.shape[1]
    dealt = pl.pallas_call(
        functools.partial(whole_kernel, mods, subs),
        out_shape=[pltpu.VMEM((mods * rows, queries), bf16 if step else f32) for step in range(subs)],
        in_specs=[in_vmem] * 2,
        out_specs=[in_vmem] * subs,
        scratch_shapes=[pltpu.VMEM((train.shape[0], queries), f32)],
        compiler_params=params(),
        cost_estimate=cost(1),
    )(keep_near(train), keep_near(block))
    terms = [to_peer(piece, 0, step) if step else piece for step, piece in enumerate(dealt)]
    added = pl.pallas_call(
        functools.partial(add_kernel, subs),
        out_shape=[pltpu.VMEM((rows, queries), f32)] * mods,
        in_specs=[in_vmem] * subs,
        out_specs=[in_vmem] * mods,
        compiler_params=params(),
        cost_estimate=cost(0.1),
    )(*map(keep_near, terms))
    return added, dealt


def held(value, first, after):
    def kernel(value_ref, *refs):
        refs[-1][...] = value_ref[first:, :]

    return pl.pallas_call(
        kernel,
        out_shape=pltpu.VMEM((value.shape[0] - first, value.shape[1]), value.dtype),
        in_specs=[in_vmem] + [pl.BlockSpec(memory_space=pl.ANY)] * len(after),
        out_specs=in_vmem,
        compiler_params=params(),
        cost_estimate=cost(0.1),
    )(keep_near(value), *after)


def scored(train, plans, arrays, dests=0, after=()):
    queries = arrays[0].shape[1]
    whole_shape = (train.shape[0], queries)
    sums = [pltpu.VMEM(whole_shape, f32)] * len(plans)
    part_shape = (len(plans) * train.shape[0] // max(dests, 1), queries)
    outputs = [pltpu.VMEM(part_shape, bf16 if dest else f32) for dest in range(dests)] or sums
    return pl.pallas_call(
        functools.partial(score_kernel, plans, dests),
        out_shape=outputs,
        in_specs=[in_vmem] * (1 + len(arrays)) + [pl.BlockSpec(memory_space=pl.ANY)] * len(after),
        out_specs=[in_vmem] * len(outputs),
        scratch_shapes=sums if dests else [],
        compiler_params=params(),
        cost_estimate=cost(0.1),
    )(*map(keep_near, (train, *arrays)), *after)


def settled(terms):
    def kernel(*refs):
        total = None
        for ref in refs[:-1]:
            term = ref[...].astype(f32)
            total = term if total is None else total + term
        refs[-1][...] = total

    return pl.pallas_call(
        kernel,
        out_shape=pltpu.VMEM(terms[0].shape, f32),
        in_specs=[in_vmem] * len(terms),
        out_specs=in_vmem,
        compiler_params=params(),
        cost_estimate=cost(0.1),
    )(*map(keep_near, terms))


def sum_kernel(places, counts, *refs):
    output = refs[-1]
    rows = output.shape[1]
    at = 0
    for blocks, count in zip(places, counts):
        for block, place in enumerate(blocks):
            total = None
            for ref in refs[at : at + count]:
                term = ref[block * rows : (block + 1) * rows, :].astype(f32)
                total = term if total is None else total + term
            output[place] = total
        at += count


def local(query_grads, train_grads, in_inverse, out_inverse, module_map):
    half_width = query_grads.shape[2]
    mods, subs = lax.axis_size("mod"), lax.axis_size("sub")
    parts, part = lax.axis_size("groups"), lax.axis_index("groups")
    reach = min(WINDOW_HALF, (lax.axis_size("ex") - 1) // 2)
    precon = preconditioned(query_grads, in_inverse, out_inverse, module_map)

    share = 5 * half_width // (8 * parts) // 128 * 128
    shared = share * parts
    train = train_grads.reshape(train_grads.shape[0], half_width)

    offsets = [sign * far for far in range(1, reach + 1) for sign in (-1, 1)]
    mine = lax.dynamic_slice_in_dim(precon, part * share, share, 0)
    added, dealt = whole(train, precon)
    rests = {offset: held(precon, shared, dealt[:1] if offset < 0 else added[:1]) for offset in offsets}
    carried = {offset: shifted(mine, "ex", -offset) for offset in offsets}
    common = {offset: shifted(rests[offset], "ex", -offset) for offset in offsets}
    *others, last = offsets
    plans = [[0, "rest"] for offset in others] + [[0]]
    arrays = [piece for offset in others for piece in (carried[offset], common[offset])] + [carried[last]]
    own = settled([to_peer(piece, step, 0) if step else piece for step, piece in enumerate(added)])
    totals = scored(train, plans, arrays, after=[own])
    plans = [["total", *range(1, parts)] for offset in offsets]
    arrays = []
    for offset, total in zip(offsets, totals):
        arrays += [total, *[shifted(carried[offset], "groups", step) for step in range(1, parts)]]
    totals = scored(train, plans, arrays)
    plans = [["total"] for offset in others] + [["total", "rest"]]
    partial = scored(train, plans, [*totals, common[last]], mods * subs)
    terms = [to_peer(rows, *divmod(dest, subs)) if dest else rows for dest, rows in reversed(list(enumerate(partial)))]
    terms.append(own)
    rows = train.shape[0] // (mods * subs)
    summed = pl.pallas_call(
        functools.partial(sum_kernel, [[offset + reach for offset in offsets], [reach]], [mods * subs, 1]),
        out_shape=jax.ShapeDtypeStruct((2 * reach + 1, rows, query_grads.shape[0]), f32),
        in_specs=[in_vmem] * len(terms),
        out_specs=in_vmem,
        compiler_params=params(),
        cost_estimate=cost(1),
    )(*[keep_near(term) for term in terms])
    return summed.transpose(1, 0, 2)


def solution(mesh):
    placed = (P("ex", "mod", "sub"), P(("groups", "ex"), "mod", "sub"), P(), P(), P("mod"))
    return jax.shard_map(
        local,
        mesh=mesh,
        in_specs=placed,
        out_specs=P(("groups", "ex", "mod", "sub"), None, None),
        check_vma=False,
    )
```

```python
import functools

import jax
import jax.numpy as jnp
from jax import lax
from jax.experimental import pallas as pl
from jax.experimental.pallas import tpu as pltpu
from jax.sharding import PartitionSpec as P

WINDOW_HALF = 2
PAD = 8
COLUMNS, PIECES = 4, 4
VMEM_LIMIT = 32 * 1024 * 1024

f32, bf16 = jnp.float32, jnp.bfloat16
in_vmem = pl.BlockSpec(memory_space=pltpu.VMEM)


def keep_near(value):
    return pltpu.with_memory_space_constraint(value, pltpu.VMEM)


def params():
    return pltpu.CompilerParams(vmem_limit_bytes=VMEM_LIMIT)


def shifted(value, axis, steps):
    count = lax.axis_size(axis)
    pairs = [(source, (source + steps) % count) for source in range(count)]
    return lax.ppermute(value, axis, pairs)


def to_peer(value, mod_step, sub_step):
    mods, subs = lax.axis_size("mod"), lax.axis_size("sub")
    pairs = []
    for mod in range(mods):
        for sub in range(subs):
            target = ((mod + mod_step) % mods) * subs + (sub + sub_step) % subs
            pairs.append((mod * subs + sub, target))
    return lax.ppermute(value, ("mod", "sub"), pairs)


def split(value):
    high = value.astype(bf16)
    return high, (value - high.astype(f32)).astype(bf16)


def nt_dot(lhs, rhs):
    return lax.dot_general(lhs, rhs, (((1,), (1,)), ((), ())), preferred_element_type=f32)


def right_rows(pair, raw, right_ref):
    width = pair.shape[1]
    queries = raw.shape[0]
    for first in range(0, raw.shape[1], PIECES * width):
        pieces = [raw[:, first + at * width : first + (at + 1) * width] for at in range(PIECES)]
        both = nt_dot(pair, jnp.concatenate(pieces, axis=0))
        both = both[:width] + both[width:]
        half = width // 2
        for index in range(PIECES):
            lanes = slice(index * queries, (index + 1) * queries)
            for row in range(2):
                at = (first // half + 2 * index + row) * (half + PAD)
                right_ref[at : at + half, :] = both[row * half : (row + 1) * half, lanes]


def first_kernel(
    map_ref, in_ref, out_ref, raw_ref, right_ref, pair_ref, left_ref, inverse_ref, rows_ref, own_ref, sems
):
    own_rows = rows_ref.shape[0]
    sub = lax.axis_index("sub")
    module = map_ref[0]
    mine = out_ref.at[module, pl.ds(pl.multiple_of(sub * own_rows, own_rows), own_rows), :]
    copies = [
        pltpu.make_async_copy(in_ref.at[module], inverse_ref, sems.at[0]),
        pltpu.make_async_copy(mine, rows_ref, sems.at[1]),
        pltpu.make_async_copy(raw_ref, own_ref, sems.at[2]),
    ]
    for copy in copies:
        copy.start()
    copies[0].wait()
    high, low = split(inverse_ref[...].T)
    high, low = high.astype(f32), low.astype(f32)
    zero = jnp.zeros_like(high)
    pair = jnp.concatenate(
        [jnp.concatenate(row, axis=1) for row in ([high, zero], [zero, high], [low, zero], [zero, low])], axis=0
    ).astype(bf16)
    pair_ref[...] = pair
    copies[1].wait()
    rows = rows_ref[...]
    swapped = jnp.concatenate([rows[:, own_rows:], rows[:, :own_rows]], axis=1)
    rows = jnp.where(sub == 0, rows, swapped)
    high, low = split(rows)
    high, low = high.astype(f32), low.astype(f32)
    left_ref[...] = jnp.concatenate(
        [jnp.concatenate(row, axis=1) for row in ([high, high], [low, jnp.zeros_like(low)])], axis=0
    ).astype(bf16)
    copies[2].wait()
    right_rows(pair, own_ref, right_ref)


def second_kernel(pair_ref, left_ref, own_ref, raw_ref, result_ref, right_ref, done_ref):
    own_rows = left_ref.shape[0] // 2
    rank_in = result_ref.shape[0] // own_rows
    step = rank_in + PAD
    right_rows(pair_ref[...], raw_ref, right_ref)
    left = left_ref[...]
    for first in range(0, rank_in, COLUMNS):
        wide = jnp.concatenate(
            [
                jnp.concatenate(
                    [
                        own_ref[pl.ds(column, own_rows, stride=step), :],
                        right_ref[pl.ds(column, own_rows, stride=step), :],
                    ],
                    axis=0,
                )
                for column in range(first, first + COLUMNS)
            ],
            axis=1,
        )
        high, low = split(wide)
        both = jnp.dot(left, jnp.concatenate([high, low], axis=0), preferred_element_type=f32)
        both = both[:own_rows] + both[own_rows:]
        queries = both.shape[1] // COLUMNS
        for index in range(COLUMNS):
            lanes = slice(index * queries, (index + 1) * queries)
            done_ref[pl.ds(first + index, own_rows, stride=step), :] = both[:, lanes]
    for row in range(own_rows):
        result_ref[row * rank_in : (row + 1) * rank_in, :] = done_ref[row * step : row * step + rank_in, :].astype(bf16)


def preconditioned(query_grads, in_inverse, out_inverse, module_map):
    block_rows, _, half_width = query_grads.shape
    rank_in, rank_out = in_inverse.shape[1], out_inverse.shape[1]
    own_rows = half_width // rank_in
    raw = query_grads.reshape(block_rows, half_width)
    other = shifted(raw, "sub", 1)
    anywhere = pl.BlockSpec(memory_space=pl.ANY)
    right, pair, left = pl.pallas_call(
        first_kernel,
        out_shape=(
            pltpu.VMEM((own_rows * (rank_in + PAD), block_rows), f32),
            pltpu.VMEM((4 * rank_in, 2 * rank_in), bf16),
            pltpu.VMEM((2 * own_rows, 2 * rank_out), bf16),
        ),
        in_specs=[pl.BlockSpec(memory_space=pltpu.SMEM), anywhere, anywhere, anywhere],
        out_specs=[in_vmem, in_vmem, in_vmem],
        scratch_shapes=[
            pltpu.VMEM((rank_in, rank_in), f32),
            pltpu.VMEM((own_rows, rank_out), f32),
            pltpu.VMEM((block_rows, half_width), bf16),
            pltpu.SemaphoreType.DMA((3,)),
        ],
        compiler_params=params(),
        cost_estimate=cost(2),
    )(module_map, *[pltpu.with_memory_space_constraint(x, pltpu.HBM) for x in (in_inverse, out_inverse, raw)])
    return pl.pallas_call(
        second_kernel,
        out_shape=pltpu.VMEM((half_width, block_rows), bf16),
        in_specs=[in_vmem] * 4,
        out_specs=in_vmem,
        scratch_shapes=[pltpu.VMEM((own_rows * (rank_in + PAD), block_rows), f32)] * 2,
        compiler_params=params(),
        cost_estimate=cost(2),
    )(keep_near(pair), keep_near(left), keep_near(right), keep_near(other))


def part_dot(train_ref, ref, first):
    train = train_ref[:, pl.ds(first, ref.shape[0])]
    return jnp.dot(train, ref[...], preferred_element_type=f32)


def whole_kernel(mods, subs, train_ref, block_ref, *refs):
    outputs, sum_ref = refs[:-1], refs[-1]
    sum_ref[...] = part_dot(train_ref, block_ref, 0)
    rows = sum_ref.shape[0] // (mods * subs)
    for sub_step, output in enumerate(outputs):
        for mod_step in range(mods):
            output[mod_step * rows : (mod_step + 1) * rows, :] = sum_ref[peer_rows(mod_step, sub_step, mods, subs, rows), :].astype(output.dtype)


def peer_rows(mod_step, sub_step, mods, subs, rows):
    target = lax.rem(lax.axis_index("mod") + mod_step, mods) * subs
    target = target + lax.rem(lax.axis_index("sub") + sub_step, subs)
    return pl.ds(pl.multiple_of(target * rows, rows), rows)


def score_kernel(plans, dests, train_ref, *refs):
    count = sum(len(plan) for plan in plans)
    inputs, outputs, sums = list(refs[:count]), (), refs[-len(plans) :]
    if dests:
        outputs = refs[-len(plans) - dests : -len(plans)]
    parts = lax.axis_size("groups")
    for plan, sum_ref in zip(plans, sums):
        total = None
        for kind in plan:
            ref = inputs.pop(0)
            if kind == "total":
                term = ref[...]
            elif kind == "rest":
                term = part_dot(train_ref, ref, train_ref.shape[1] - ref.shape[0])
            else:
                share = ref.shape[0]
                source = lax.rem(lax.axis_index("groups") + parts - kind, parts)
                term = part_dot(train_ref, ref, pl.multiple_of(source * share, 128))
            total = term if total is None else total + term
        sum_ref[...] = total
    mods, subs = lax.axis_size("mod"), lax.axis_size("sub")
    rows = sums[0].shape[0] // (mods * subs)
    for dest, output in enumerate(outputs):
        place = peer_rows(*divmod(dest, subs), mods, subs, rows)
        for block, sum_ref in enumerate(sums):
            output[block * rows : (block + 1) * rows, :] = sum_ref[place, :].astype(output.dtype)


def cost(micros):
    return pl.CostEstimate(flops=int(micros * 1.15e9), bytes_accessed=0, transcendentals=0)


def add_kernel(count, *refs):
    inputs, outputs = refs[:count], refs[count:]
    rows = outputs[0].shape[0]
    for step, output in enumerate(outputs):
        total = None
        for ref in inputs:
            term = ref[step * rows : (step + 1) * rows, :].astype(f32)
            total = term if total is None else total + term
        output[...] = total.astype(output.dtype)


def whole(train, block):
    mods, subs = lax.axis_size("mod"), lax.axis_size("sub")
    rows, queries = train.shape[0] // (mods * subs), block.shape[1]
    dealt = pl.pallas_call(
        functools.partial(whole_kernel, mods, subs),
        out_shape=[pltpu.VMEM((mods * rows, queries), bf16 if step else f32) for step in range(subs)],
        in_specs=[in_vmem] * 2,
        out_specs=[in_vmem] * subs,
        scratch_shapes=[pltpu.VMEM((train.shape[0], queries), f32)],
        compiler_params=params(),
        cost_estimate=cost(1),
    )(keep_near(train), keep_near(block))
    terms = [to_peer(piece, 0, step) if step else piece for step, piece in enumerate(dealt)]
    added = pl.pallas_call(
        functools.partial(add_kernel, subs),
        out_shape=[pltpu.VMEM((rows, queries), f32)] * mods,
        in_specs=[in_vmem] * subs,
        out_specs=[in_vmem] * mods,
        compiler_params=params(),
        cost_estimate=cost(0.1),
    )(*map(keep_near, terms))
    return added, dealt


def held(value, first, after):
    def kernel(value_ref, *refs):
        refs[-1][...] = value_ref[first:, :]

    return pl.pallas_call(
        kernel,
        out_shape=pltpu.VMEM((value.shape[0] - first, value.shape[1]), value.dtype),
        in_specs=[in_vmem] + [pl.BlockSpec(memory_space=pl.ANY)] * len(after),
        out_specs=in_vmem,
        compiler_params=params(),
        cost_estimate=cost(0.1),
    )(keep_near(value), *after)


def scored(train, plans, arrays, dests=0, after=()):
    queries = arrays[0].shape[1]
    whole_shape = (train.shape[0], queries)
    sums = [pltpu.VMEM(whole_shape, f32)] * len(plans)
    part_shape = (len(plans) * train.shape[0] // max(dests, 1), queries)
    outputs = [pltpu.VMEM(part_shape, bf16 if dest else f32) for dest in range(dests)] or sums
    return pl.pallas_call(
        functools.partial(score_kernel, plans, dests),
        out_shape=outputs,
        in_specs=[in_vmem] * (1 + len(arrays)) + [pl.BlockSpec(memory_space=pl.ANY)] * len(after),
        out_specs=[in_vmem] * len(outputs),
        scratch_shapes=sums if dests else [],
        compiler_params=params(),
        cost_estimate=cost(0.1),
    )(*map(keep_near, (train, *arrays)), *after)


def settled(terms):
    def kernel(*refs):
        total = None
        for ref in refs[:-1]:
            term = ref[...].astype(f32)
            total = term if total is None else total + term
        refs[-1][...] = total

    return pl.pallas_call(
        kernel,
        out_shape=pltpu.VMEM(terms[0].shape, f32),
        in_specs=[in_vmem] * len(terms),
        out_specs=in_vmem,
        compiler_params=params(),
        cost_estimate=cost(0.1),
    )(*map(keep_near, terms))


def sum_kernel(places, counts, *refs):
    output = refs[-1]
    rows = output.shape[1]
    at = 0
    for blocks, count in zip(places, counts):
        for block, place in enumerate(blocks):
            total = None
            for ref in refs[at : at + count]:
                term = ref[block * rows : (block + 1) * rows, :].astype(f32)
                total = term if total is None else total + term
            output[place] = total
        at += count


def local(query_grads, train_grads, in_inverse, out_inverse, module_map):
    half_width = query_grads.shape[2]
    mods, subs = lax.axis_size("mod"), lax.axis_size("sub")
    parts, part = lax.axis_size("groups"), lax.axis_index("groups")
    reach = min(WINDOW_HALF, (lax.axis_size("ex") - 1) // 2)
    precon = preconditioned(query_grads, in_inverse, out_inverse, module_map)

    share = 5 * half_width // (8 * parts) // 128 * 128
    shared = share * parts
    train = train_grads.reshape(train_grads.shape[0], half_width)

    offsets = [sign * far for far in range(1, reach + 1) for sign in (-1, 1)]
    mine = lax.dynamic_slice_in_dim(precon, part * share, share, 0)
    added, dealt = whole(train, precon)
    rest = held(precon, shared, added[:1])
    carried = {offset: shifted(mine, "ex", -offset) for offset in offsets}
    common = {offset: shifted(rest, "ex", -offset) for offset in offsets}
    *others, last = offsets
    plans = [[0, "rest"] for offset in others] + [[0]]
    arrays = [piece for offset in others for piece in (carried[offset], common[offset])] + [carried[last]]
    own = settled([to_peer(piece, step, 0) if step else piece for step, piece in enumerate(added)])
    totals = scored(train, plans, arrays, after=[own])
    plans = [["total", *range(1, parts)] for offset in offsets]
    arrays = []
    for offset, total in zip(offsets, totals):
        arrays += [total, *[shifted(carried[offset], "groups", step) for step in range(1, parts)]]
    totals = scored(train, plans, arrays)
    plans = [["total"] for offset in others] + [["total", "rest"]]
    partial = scored(train, plans, [*totals, common[last]], mods * subs)
    terms = [to_peer(rows, *divmod(dest, subs)) if dest else rows for dest, rows in reversed(list(enumerate(partial)))]
    terms.append(own)
    rows = train.shape[0] // (mods * subs)
    summed = pl.pallas_call(
        functools.partial(sum_kernel, [[offset + reach for offset in offsets], [reach]], [mods * subs, 1]),
        out_shape=jax.ShapeDtypeStruct((2 * reach + 1, rows, query_grads.shape[0]), f32),
        in_specs=[in_vmem] * len(terms),
        out_specs=in_vmem,
        compiler_params=params(),
        cost_estimate=cost(1),
    )(*[keep_near(term) for term in terms])
    return summed.transpose(1, 0, 2)


def solution(mesh):
    placed = (P("ex", "mod", "sub"), P(("groups", "ex"), "mod", "sub"), P(), P(), P("mod"))
    return jax.shard_map(
        local,
        mesh=mesh,
        in_specs=placed,
        out_specs=P(("groups", "ex", "mod", "sub"), None, None),
        check_vma=False,
    )
```

```python
import functools

import jax
import jax.numpy as jnp
from jax import lax
from jax.experimental import pallas as pl
from jax.experimental.pallas import tpu as pltpu
from jax.sharding import PartitionSpec as P

WINDOW_HALF = 2
PAD = 8
VMEM_LIMIT = 32 * 1024 * 1024

f32, bf16 = jnp.float32, jnp.bfloat16
in_vmem = pl.BlockSpec(memory_space=pltpu.VMEM)


def keep_near(value):
    return pltpu.with_memory_space_constraint(value, pltpu.VMEM)


def params():
    return pltpu.CompilerParams(vmem_limit_bytes=VMEM_LIMIT)


def shifted(value, axis, steps):
    count = lax.axis_size(axis)
    pairs = [(source, (source + steps) % count) for source in range(count)]
    return lax.ppermute(value, axis, pairs)


def to_peer(value, mod_step, sub_step):
    mods, subs = lax.axis_size("mod"), lax.axis_size("sub")
    pairs = []
    for mod in range(mods):
        for sub in range(subs):
            target = ((mod + mod_step) % mods) * subs + (sub + sub_step) % subs
            pairs.append((mod * subs + sub, target))
    return lax.ppermute(value, ("mod", "sub"), pairs)


def split(value):
    high = value.astype(bf16)
    return high, (value - high.astype(f32)).astype(bf16)


def nt_dot(lhs, rhs):
    return lax.dot_general(lhs, rhs, (((1,), (1,)), ((), ())), preferred_element_type=f32)


def right_rows(pair, raw, right_ref):
    width = pair.shape[1]
    queries = raw.shape[0]
    for first in range(0, raw.shape[1], 2 * width):
        pieces = [raw[:, at : at + width] for at in (first, first + width)]
        both = nt_dot(pair, jnp.concatenate(pieces, axis=0))
        both = both[:width] + both[width:]
        half = width // 2
        for index, lanes in enumerate((slice(0, queries), slice(queries, 2 * queries))):
            for row in range(2):
                at = (first // half + 2 * index + row) * (half + PAD)
                right_ref[at : at + half, :] = both[row * half : (row + 1) * half, lanes]


def first_kernel(
    map_ref, in_ref, out_ref, raw_ref, right_ref, pair_ref, left_ref, inverse_ref, rows_ref, own_ref, sems
):
    own_rows = rows_ref.shape[0]
    sub = lax.axis_index("sub")
    module = map_ref[0]
    mine = out_ref.at[module, pl.ds(pl.multiple_of(sub * own_rows, own_rows), own_rows), :]
    copies = [
        pltpu.make_async_copy(in_ref.at[module], inverse_ref, sems.at[0]),
        pltpu.make_async_copy(mine, rows_ref, sems.at[1]),
        pltpu.make_async_copy(raw_ref, own_ref, sems.at[2]),
    ]
    for copy in copies:
        copy.start()
    copies[0].wait()
    high, low = split(inverse_ref[...].T)
    high, low = high.astype(f32), low.astype(f32)
    zero = jnp.zeros_like(high)
    pair = jnp.concatenate(
        [jnp.concatenate(row, axis=1) for row in ([high, zero], [zero, high], [low, zero], [zero, low])], axis=0
    ).astype(bf16)
    pair_ref[...] = pair
    copies[1].wait()
    rows = rows_ref[...]
    swapped = jnp.concatenate([rows[:, own_rows:], rows[:, :own_rows]], axis=1)
    rows = jnp.where(sub == 0, rows, swapped)
    high, low = split(rows)
    high, low = high.astype(f32), low.astype(f32)
    left_ref[...] = jnp.concatenate(
        [jnp.concatenate(row, axis=1) for row in ([high, high], [low, jnp.zeros_like(low)])], axis=0
    ).astype(bf16)
    copies[2].wait()
    right_rows(pair, own_ref, right_ref)


def second_kernel(pair_ref, left_ref, own_ref, raw_ref, result_ref, right_ref, done_ref):
    own_rows = left_ref.shape[0] // 2
    rank_in = result_ref.shape[0] // own_rows
    step = rank_in + PAD
    right_rows(pair_ref[...], raw_ref, right_ref)
    left = left_ref[...]
    for first in range(0, rank_in, 2):
        wide = jnp.concatenate(
            [
                jnp.concatenate(
                    [
                        own_ref[pl.ds(column, own_rows, stride=step), :],
                        right_ref[pl.ds(column, own_rows, stride=step), :],
                    ],
                    axis=0,
                )
                for column in (first, first + 1)
            ],
            axis=1,
        )
        high, low = split(wide)
        both = jnp.dot(left, jnp.concatenate([high, low], axis=0), preferred_element_type=f32)
        both = both[:own_rows] + both[own_rows:]
        queries = both.shape[1] // 2
        done_ref[pl.ds(first, own_rows, stride=step), :] = both[:, :queries]
        done_ref[pl.ds(first + 1, own_rows, stride=step), :] = both[:, queries:]
    for row in range(own_rows):
        result_ref[row * rank_in : (row + 1) * rank_in, :] = done_ref[row * step : row * step + rank_in, :].astype(bf16)


def preconditioned(query_grads, in_inverse, out_inverse, module_map):
    block_rows, _, half_width = query_grads.shape
    rank_in, rank_out = in_inverse.shape[1], out_inverse.shape[1]
    own_rows = half_width // rank_in
    raw = query_grads.reshape(block_rows, half_width)
    other = shifted(raw, "sub", 1)
    anywhere = pl.BlockSpec(memory_space=pl.ANY)
    right, pair, left = pl.pallas_call(
        first_kernel,
        out_shape=(
            pltpu.VMEM((own_rows * (rank_in + PAD), block_rows), f32),
            pltpu.VMEM((4 * rank_in, 2 * rank_in), bf16),
            pltpu.VMEM((2 * own_rows, 2 * rank_out), bf16),
        ),
        in_specs=[pl.BlockSpec(memory_space=pltpu.SMEM), anywhere, anywhere, anywhere],
        out_specs=[in_vmem, in_vmem, in_vmem],
        scratch_shapes=[
            pltpu.VMEM((rank_in, rank_in), f32),
            pltpu.VMEM((own_rows, rank_out), f32),
            pltpu.VMEM((block_rows, half_width), bf16),
            pltpu.SemaphoreType.DMA((3,)),
        ],
        compiler_params=params(),
        cost_estimate=cost(2),
    )(module_map, *[pltpu.with_memory_space_constraint(x, pltpu.HBM) for x in (in_inverse, out_inverse, raw)])
    return pl.pallas_call(
        second_kernel,
        out_shape=pltpu.VMEM((half_width, block_rows), bf16),
        in_specs=[in_vmem] * 4,
        out_specs=in_vmem,
        scratch_shapes=[pltpu.VMEM((own_rows * (rank_in + PAD), block_rows), f32)] * 2,
        compiler_params=params(),
        cost_estimate=cost(2),
    )(keep_near(pair), keep_near(left), keep_near(right), keep_near(other))


def part_dot(train_ref, ref, first):
    train = train_ref[:, pl.ds(first, ref.shape[0])]
    return jnp.dot(train, ref[...], preferred_element_type=f32)


def whole_kernel(mods, subs, train_ref, block_ref, *refs):
    outputs, sum_ref = refs[:-1], refs[-1]
    sum_ref[...] = part_dot(train_ref, block_ref, 0)
    rows = sum_ref.shape[0] // (mods * subs)
    for sub_step, output in enumerate(outputs):
        for mod_step in range(mods):
            output[mod_step * rows : (mod_step + 1) * rows, :] = sum_ref[peer_rows(mod_step, sub_step, mods, subs, rows), :].astype(output.dtype)


def peer_rows(mod_step, sub_step, mods, subs, rows):
    target = lax.rem(lax.axis_index("mod") + mod_step, mods) * subs
    target = target + lax.rem(lax.axis_index("sub") + sub_step, subs)
    return pl.ds(pl.multiple_of(target * rows, rows), rows)


def score_kernel(plans, dests, train_ref, *refs):
    count = sum(len(plan) for plan in plans)
    inputs, outputs, sums = list(refs[:count]), (), refs[-len(plans) :]
    if dests:
        outputs = refs[-len(plans) - dests : -len(plans)]
    parts = lax.axis_size("groups")
    for plan, sum_ref in zip(plans, sums):
        total = None
        for kind in plan:
            ref = inputs.pop(0)
            if kind == "total":
                term = ref[...]
            elif kind == "rest":
                term = part_dot(train_ref, ref, train_ref.shape[1] - ref.shape[0])
            else:
                share = ref.shape[0]
                source = lax.rem(lax.axis_index("groups") + parts - kind, parts)
                term = part_dot(train_ref, ref, pl.multiple_of(source * share, 128))
            total = term if total is None else total + term
        sum_ref[...] = total
    mods, subs = lax.axis_size("mod"), lax.axis_size("sub")
    rows = sums[0].shape[0] // (mods * subs)
    for dest, output in enumerate(outputs):
        place = peer_rows(*divmod(dest, subs), mods, subs, rows)
        for block, sum_ref in enumerate(sums):
            output[block * rows : (block + 1) * rows, :] = sum_ref[place, :].astype(output.dtype)


def cost(micros):
    return pl.CostEstimate(flops=int(micros * 1.15e9), bytes_accessed=0, transcendentals=0)


def add_kernel(count, *refs):
    inputs, outputs = refs[:count], refs[count:]
    rows = outputs[0].shape[0]
    for step, output in enumerate(outputs):
        total = None
        for ref in inputs:
            term = ref[step * rows : (step + 1) * rows, :].astype(f32)
            total = term if total is None else total + term
        output[...] = total.astype(output.dtype)


def whole(train, block):
    mods, subs = lax.axis_size("mod"), lax.axis_size("sub")
    rows, queries = train.shape[0] // (mods * subs), block.shape[1]
    dealt = pl.pallas_call(
        functools.partial(whole_kernel, mods, subs),
        out_shape=[pltpu.VMEM((mods * rows, queries), bf16 if step else f32) for step in range(subs)],
        in_specs=[in_vmem] * 2,
        out_specs=[in_vmem] * subs,
        scratch_shapes=[pltpu.VMEM((train.shape[0], queries), f32)],
        compiler_params=params(),
        cost_estimate=cost(1),
    )(keep_near(train), keep_near(block))
    terms = [to_peer(piece, 0, step) if step else piece for step, piece in enumerate(dealt)]
    added = pl.pallas_call(
        functools.partial(add_kernel, subs),
        out_shape=[pltpu.VMEM((rows, queries), f32)] * mods,
        in_specs=[in_vmem] * subs,
        out_specs=[in_vmem] * mods,
        compiler_params=params(),
        cost_estimate=cost(0.1),
    )(*map(keep_near, terms))
    return added, dealt


def held(value, first, after):
    def kernel(value_ref, *refs):
        refs[-1][...] = value_ref[first:, :]

    return pl.pallas_call(
        kernel,
        out_shape=pltpu.VMEM((value.shape[0] - first, value.shape[1]), value.dtype),
        in_specs=[in_vmem] + [pl.BlockSpec(memory_space=pl.ANY)] * len(after),
        out_specs=in_vmem,
        compiler_params=params(),
        cost_estimate=cost(0.1),
    )(keep_near(value), *after)


def scored(train, plans, arrays, dests=0, after=(), micros=0.1):
    queries = arrays[0].shape[1]
    whole_shape = (train.shape[0], queries)
    sums = [pltpu.VMEM(whole_shape, f32)] * len(plans)
    part_shape = (len(plans) * train.shape[0] // max(dests, 1), queries)
    outputs = [pltpu.VMEM(part_shape, bf16 if dest else f32) for dest in range(dests)] or sums
    return pl.pallas_call(
        functools.partial(score_kernel, plans, dests),
        out_shape=outputs,
        in_specs=[in_vmem] * (1 + len(arrays)) + [pl.BlockSpec(memory_space=pl.ANY)] * len(after),
        out_specs=[in_vmem] * len(outputs),
        scratch_shapes=sums if dests else [],
        compiler_params=params(),
        cost_estimate=cost(micros),
    )(*map(keep_near, (train, *arrays)), *after)


def settled(terms):
    def kernel(*refs):
        total = None
        for ref in refs[:-1]:
            term = ref[...].astype(f32)
            total = term if total is None else total + term
        refs[-1][...] = total

    return pl.pallas_call(
        kernel,
        out_shape=pltpu.VMEM(terms[0].shape, f32),
        in_specs=[in_vmem] * len(terms),
        out_specs=in_vmem,
        compiler_params=params(),
        cost_estimate=cost(0.1),
    )(*map(keep_near, terms))


def sum_kernel(places, counts, *refs):
    output = refs[-1]
    rows = output.shape[1]
    at = 0
    for blocks, count in zip(places, counts):
        for block, place in enumerate(blocks):
            total = None
            for ref in refs[at : at + count]:
                term = ref[block * rows : (block + 1) * rows, :].astype(f32)
                total = term if total is None else total + term
            output[place] = total
        at += count


def local(query_grads, train_grads, in_inverse, out_inverse, module_map):
    half_width = query_grads.shape[2]
    mods, subs = lax.axis_size("mod"), lax.axis_size("sub")
    parts, part = lax.axis_size("groups"), lax.axis_index("groups")
    reach = min(WINDOW_HALF, (lax.axis_size("ex") - 1) // 2)
    precon = preconditioned(query_grads, in_inverse, out_inverse, module_map)

    share = 5 * half_width // (8 * parts) // 128 * 128
    shared = share * parts
    train = train_grads.reshape(train_grads.shape[0], half_width)

    offsets = [sign * far for far in range(1, reach + 1) for sign in (-1, 1)]
    mine = lax.dynamic_slice_in_dim(precon, part * share, share, 0)
    added, dealt = whole(train, precon)
    rests = {offset: held(precon, shared, dealt[:1] if offset < 0 else added[:1]) for offset in offsets}
    carried = {offset: shifted(mine, "ex", -offset) for offset in offsets}
    common = {offset: shifted(rests[offset], "ex", -offset) for offset in offsets}
    *others, last = offsets
    plans = [[0, "rest"] for offset in others] + [[0]]
    arrays = [piece for offset in others for piece in (carried[offset], common[offset])] + [carried[last]]
    own = settled([to_peer(piece, step, 0) if step else piece for step, piece in enumerate(added)])
    totals = scored(train, plans, arrays, after=[own], micros=1)
    plans = [["total", *range(1, parts)] for offset in offsets]
    arrays = []
    for offset, total in zip(offsets, totals):
        arrays += [total, *[shifted(carried[offset], "groups", step) for step in range(1, parts)]]
    totals = scored(train, plans, arrays)
    plans = [["total"] for offset in others] + [["total", "rest"]]
    partial = scored(train, plans, [*totals, common[last]], mods * subs)
    terms = [to_peer(rows, *divmod(dest, subs)) if dest else rows for dest, rows in reversed(list(enumerate(partial)))]
    terms.append(own)
    rows = train.shape[0] // (mods * subs)
    summed = pl.pallas_call(
        functools.partial(sum_kernel, [[offset + reach for offset in offsets], [reach]], [mods * subs, 1]),
        out_shape=jax.ShapeDtypeStruct((2 * reach + 1, rows, query_grads.shape[0]), f32),
        in_specs=[in_vmem] * len(terms),
        out_specs=in_vmem,
        compiler_params=params(),
        cost_estimate=cost(1),
    )(*[keep_near(term) for term in terms])
    return summed.transpose(1, 0, 2)


def solution(mesh):
    placed = (P("ex", "mod", "sub"), P(("groups", "ex"), "mod", "sub"), P(), P(), P("mod"))
    return jax.shard_map(
        local,
        mesh=mesh,
        in_specs=placed,
        out_specs=P(("groups", "ex", "mod", "sub"), None, None),
        check_vma=False,
    )
```

```python
import functools

import jax
import jax.numpy as jnp
from jax import lax
from jax.experimental import pallas as pl
from jax.experimental.pallas import tpu as pltpu
from jax.sharding import PartitionSpec as P

WINDOW_HALF = 2
PAD = 8
VMEM_LIMIT = 32 * 1024 * 1024

f32, bf16 = jnp.float32, jnp.bfloat16
in_vmem = pl.BlockSpec(memory_space=pltpu.VMEM)


def keep_near(value):
    return pltpu.with_memory_space_constraint(value, pltpu.VMEM)


def params():
    return pltpu.CompilerParams(vmem_limit_bytes=VMEM_LIMIT)


def shifted(value, axis, steps):
    count = lax.axis_size(axis)
    pairs = [(source, (source + steps) % count) for source in range(count)]
    return lax.ppermute(value, axis, pairs)


def to_peer(value, mod_step, sub_step):
    mods, subs = lax.axis_size("mod"), lax.axis_size("sub")
    pairs = []
    for mod in range(mods):
        for sub in range(subs):
            target = ((mod + mod_step) % mods) * subs + (sub + sub_step) % subs
            pairs.append((mod * subs + sub, target))
    return lax.ppermute(value, ("mod", "sub"), pairs)


def split(value):
    high = value.astype(bf16)
    return high, (value - high.astype(f32)).astype(bf16)


def nt_dot(lhs, rhs):
    return lax.dot_general(lhs, rhs, (((1,), (1,)), ((), ())), preferred_element_type=f32)


def right_rows(pair, raw, right_ref):
    width = pair.shape[1]
    queries = raw.shape[0]
    for first in range(0, raw.shape[1], 2 * width):
        pieces = [raw[:, at : at + width] for at in (first, first + width)]
        both = nt_dot(pair, jnp.concatenate(pieces, axis=0))
        both = both[:width] + both[width:]
        half = width // 2
        for index, lanes in enumerate((slice(0, queries), slice(queries, 2 * queries))):
            for row in range(2):
                at = (first // half + 2 * index + row) * (half + PAD)
                right_ref[at : at + half, :] = both[row * half : (row + 1) * half, lanes]


def first_kernel(
    map_ref, in_ref, out_ref, raw_ref, right_ref, pair_ref, left_ref, inverse_ref, rows_ref, own_ref, sems
):
    own_rows = rows_ref.shape[0]
    sub = lax.axis_index("sub")
    module = map_ref[0]
    mine = out_ref.at[module, pl.ds(pl.multiple_of(sub * own_rows, own_rows), own_rows), :]
    copies = [
        pltpu.make_async_copy(in_ref.at[module], inverse_ref, sems.at[0]),
        pltpu.make_async_copy(mine, rows_ref, sems.at[1]),
        pltpu.make_async_copy(raw_ref, own_ref, sems.at[2]),
    ]
    for copy in copies:
        copy.start()
    copies[0].wait()
    high, low = split(inverse_ref[...].T)
    high, low = high.astype(f32), low.astype(f32)
    zero = jnp.zeros_like(high)
    pair = jnp.concatenate(
        [jnp.concatenate(row, axis=1) for row in ([high, zero], [zero, high], [low, zero], [zero, low])], axis=0
    ).astype(bf16)
    pair_ref[...] = pair
    copies[1].wait()
    rows = rows_ref[...]
    swapped = jnp.concatenate([rows[:, own_rows:], rows[:, :own_rows]], axis=1)
    rows = jnp.where(sub == 0, rows, swapped)
    high, low = split(rows)
    high, low = high.astype(f32), low.astype(f32)
    left_ref[...] = jnp.concatenate(
        [jnp.concatenate(row, axis=1) for row in ([high, high], [low, jnp.zeros_like(low)])], axis=0
    ).astype(bf16)
    copies[2].wait()
    right_rows(pair, own_ref, right_ref)


def second_kernel(pair_ref, left_ref, own_ref, raw_ref, result_ref, right_ref, done_ref):
    own_rows = left_ref.shape[0] // 2
    rank_in = result_ref.shape[0] // own_rows
    step = rank_in + PAD
    right_rows(pair_ref[...], raw_ref, right_ref)
    left = left_ref[...]
    for first in range(0, rank_in, 2):
        wide = jnp.concatenate(
            [
                jnp.concatenate(
                    [
                        own_ref[pl.ds(column, own_rows, stride=step), :],
                        right_ref[pl.ds(column, own_rows, stride=step), :],
                    ],
                    axis=0,
                )
                for column in (first, first + 1)
            ],
            axis=1,
        )
        high, low = split(wide)
        both = jnp.dot(left, jnp.concatenate([high, low], axis=0), preferred_element_type=f32)
        both = both[:own_rows] + both[own_rows:]
        queries = both.shape[1] // 2
        done_ref[pl.ds(first, own_rows, stride=step), :] = both[:, :queries]
        done_ref[pl.ds(first + 1, own_rows, stride=step), :] = both[:, queries:]
    for row in range(own_rows):
        result_ref[row * rank_in : (row + 1) * rank_in, :] = done_ref[row * step : row * step + rank_in, :].astype(bf16)


def preconditioned(query_grads, in_inverse, out_inverse, module_map):
    block_rows, _, half_width = query_grads.shape
    rank_in, rank_out = in_inverse.shape[1], out_inverse.shape[1]
    own_rows = half_width // rank_in
    raw = query_grads.reshape(block_rows, half_width)
    other = shifted(raw, "sub", 1)
    anywhere = pl.BlockSpec(memory_space=pl.ANY)
    right, pair, left = pl.pallas_call(
        first_kernel,
        out_shape=(
            pltpu.VMEM((own_rows * (rank_in + PAD), block_rows), f32),
            pltpu.VMEM((4 * rank_in, 2 * rank_in), bf16),
            pltpu.VMEM((2 * own_rows, 2 * rank_out), bf16),
        ),
        in_specs=[pl.BlockSpec(memory_space=pltpu.SMEM), anywhere, anywhere, anywhere],
        out_specs=[in_vmem, in_vmem, in_vmem],
        scratch_shapes=[
            pltpu.VMEM((rank_in, rank_in), f32),
            pltpu.VMEM((own_rows, rank_out), f32),
            pltpu.VMEM((block_rows, half_width), bf16),
            pltpu.SemaphoreType.DMA((3,)),
        ],
        compiler_params=params(),
        cost_estimate=cost(2),
    )(module_map, *[pltpu.with_memory_space_constraint(x, pltpu.HBM) for x in (in_inverse, out_inverse, raw)])
    return pl.pallas_call(
        second_kernel,
        out_shape=pltpu.VMEM((half_width, block_rows), bf16),
        in_specs=[in_vmem] * 4,
        out_specs=in_vmem,
        scratch_shapes=[pltpu.VMEM((own_rows * (rank_in + PAD), block_rows), f32)] * 2,
        compiler_params=params(),
        cost_estimate=cost(2),
    )(keep_near(pair), keep_near(left), keep_near(right), keep_near(other))


def part_dot(train_ref, ref, first):
    train = train_ref[:, pl.ds(first, ref.shape[0])]
    return jnp.dot(train, ref[...], preferred_element_type=f32)


def whole_kernel(mods, subs, train_ref, block_ref, *refs):
    outputs, sum_ref = refs[:-1], refs[-1]
    sum_ref[...] = part_dot(train_ref, block_ref, 0)
    rows = sum_ref.shape[0] // (mods * subs)
    for sub_step, output in enumerate(outputs):
        for mod_step in range(mods):
            output[mod_step * rows : (mod_step + 1) * rows, :] = sum_ref[peer_rows(mod_step, sub_step, mods, subs, rows), :].astype(output.dtype)


def peer_rows(mod_step, sub_step, mods, subs, rows):
    target = lax.rem(lax.axis_index("mod") + mod_step, mods) * subs
    target = target + lax.rem(lax.axis_index("sub") + sub_step, subs)
    return pl.ds(pl.multiple_of(target * rows, rows), rows)


def score_kernel(plans, dests, train_ref, *refs):
    count = sum(len(plan) for plan in plans)
    inputs, outputs, sums = list(refs[:count]), (), refs[-len(plans) :]
    if dests:
        outputs = refs[-len(plans) - dests : -len(plans)]
    parts = lax.axis_size("groups")
    for plan, sum_ref in zip(plans, sums):
        total = None
        for kind in plan:
            ref = inputs.pop(0)
            if kind == "total":
                term = ref[...]
            elif kind == "rest":
                term = part_dot(train_ref, ref, train_ref.shape[1] - ref.shape[0])
            else:
                share = ref.shape[0]
                source = lax.rem(lax.axis_index("groups") + parts - kind, parts)
                term = part_dot(train_ref, ref, pl.multiple_of(source * share, 128))
            total = term if total is None else total + term
        sum_ref[...] = total
    mods, subs = lax.axis_size("mod"), lax.axis_size("sub")
    rows = sums[0].shape[0] // (mods * subs)
    for dest, output in enumerate(outputs):
        place = peer_rows(*divmod(dest, subs), mods, subs, rows)
        for block, sum_ref in enumerate(sums):
            output[block * rows : (block + 1) * rows, :] = sum_ref[place, :].astype(output.dtype)


def cost(micros):
    return pl.CostEstimate(flops=int(micros * 1.15e9), bytes_accessed=0, transcendentals=0)


def add_kernel(count, *refs):
    inputs, outputs = refs[:count], refs[count:]
    rows = outputs[0].shape[0]
    for step, output in enumerate(outputs):
        total = None
        for ref in inputs:
            term = ref[step * rows : (step + 1) * rows, :].astype(f32)
            total = term if total is None else total + term
        output[...] = total.astype(output.dtype)


def whole(train, block):
    mods, subs = lax.axis_size("mod"), lax.axis_size("sub")
    rows, queries = train.shape[0] // (mods * subs), block.shape[1]
    dealt = pl.pallas_call(
        functools.partial(whole_kernel, mods, subs),
        out_shape=[pltpu.VMEM((mods * rows, queries), bf16 if step else f32) for step in range(subs)],
        in_specs=[in_vmem] * 2,
        out_specs=[in_vmem] * subs,
        scratch_shapes=[pltpu.VMEM((train.shape[0], queries), f32)],
        compiler_params=params(),
        cost_estimate=cost(0.01),
    )(keep_near(train), keep_near(block))
    terms = [to_peer(piece, 0, step) if step else piece for step, piece in enumerate(dealt)]
    added = pl.pallas_call(
        functools.partial(add_kernel, subs),
        out_shape=[pltpu.VMEM((rows, queries), f32)] * mods,
        in_specs=[in_vmem] * subs,
        out_specs=[in_vmem] * mods,
        compiler_params=params(),
        cost_estimate=cost(0.1),
    )(*map(keep_near, terms))
    return added, dealt


def held(value, first, after, micros=0.1):
    def kernel(value_ref, *refs):
        refs[-1][...] = value_ref[first:, :]

    return pl.pallas_call(
        kernel,
        out_shape=pltpu.VMEM((value.shape[0] - first, value.shape[1]), value.dtype),
        in_specs=[in_vmem] + [pl.BlockSpec(memory_space=pl.ANY)] * len(after),
        out_specs=in_vmem,
        compiler_params=params(),
        cost_estimate=cost(micros),
    )(keep_near(value), *after)


def scored(train, plans, arrays, dests=0, after=()):
    queries = arrays[0].shape[1]
    whole_shape = (train.shape[0], queries)
    sums = [pltpu.VMEM(whole_shape, f32)] * len(plans)
    part_shape = (len(plans) * train.shape[0] // max(dests, 1), queries)
    outputs = [pltpu.VMEM(part_shape, bf16 if dest else f32) for dest in range(dests)] or sums
    return pl.pallas_call(
        functools.partial(score_kernel, plans, dests),
        out_shape=outputs,
        in_specs=[in_vmem] * (1 + len(arrays)) + [pl.BlockSpec(memory_space=pl.ANY)] * len(after),
        out_specs=[in_vmem] * len(outputs),
        scratch_shapes=sums if dests else [],
        compiler_params=params(),
        cost_estimate=cost(0.1),
    )(*map(keep_near, (train, *arrays)), *after)


def settled(terms):
    def kernel(*refs):
        total = None
        for ref in refs[:-1]:
            term = ref[...].astype(f32)
            total = term if total is None else total + term
        refs[-1][...] = total

    return pl.pallas_call(
        kernel,
        out_shape=pltpu.VMEM(terms[0].shape, f32),
        in_specs=[in_vmem] * len(terms),
        out_specs=in_vmem,
        compiler_params=params(),
        cost_estimate=cost(0.1),
    )(*map(keep_near, terms))


def sum_kernel(places, counts, *refs):
    output = refs[-1]
    rows = output.shape[1]
    at = 0
    for blocks, count in zip(places, counts):
        for block, place in enumerate(blocks):
            total = None
            for ref in refs[at : at + count]:
                term = ref[block * rows : (block + 1) * rows, :].astype(f32)
                total = term if total is None else total + term
            output[place] = total
        at += count


def local(query_grads, train_grads, in_inverse, out_inverse, module_map):
    half_width = query_grads.shape[2]
    mods, subs = lax.axis_size("mod"), lax.axis_size("sub")
    parts, part = lax.axis_size("groups"), lax.axis_index("groups")
    reach = min(WINDOW_HALF, (lax.axis_size("ex") - 1) // 2)
    precon = preconditioned(query_grads, in_inverse, out_inverse, module_map)

    share = 5 * half_width // (8 * parts) // 128 * 128
    shared = share * parts
    train = train_grads.reshape(train_grads.shape[0], half_width)

    offsets = [sign * far for far in range(1, reach + 1) for sign in (-1, 1)]
    mine = lax.dynamic_slice_in_dim(precon, part * share, share, 0)
    added, dealt = whole(train, precon)
    later = held(mine, 0, added[:1])
    rest = held(precon, shared, [later])
    carried = {offset: shifted(mine if offset < 0 else later, "ex", -offset) for offset in offsets}
    common = {offset: shifted(rest, "ex", -offset) for offset in offsets}
    *others, last = offsets
    plans = [[0, "rest"] for offset in others] + [[0]]
    arrays = [piece for offset in others for piece in (carried[offset], common[offset])] + [carried[last]]
    own = settled([to_peer(piece, step, 0) if step else piece for step, piece in enumerate(added)])
    totals = scored(train, plans, arrays, after=[own])
    plans = [["total", *range(1, parts)] for offset in offsets]
    arrays = []
    for offset, total in zip(offsets, totals):
        swap = held(carried[offset], 0, [], 3) if offset < 0 else carried[offset]
        arrays += [total, *[shifted(swap, "groups", step) for step in range(1, parts)]]
    totals = scored(train, plans, arrays)
    plans = [["total"] for offset in others] + [["total", "rest"]]
    partial = scored(train, plans, [*totals, common[last]], mods * subs)
    terms = [to_peer(rows, *divmod(dest, subs)) if dest else rows for dest, rows in reversed(list(enumerate(partial)))]
    terms.append(own)
    rows = train.shape[0] // (mods * subs)
    summed = pl.pallas_call(
        functools.partial(sum_kernel, [[offset + reach for offset in offsets], [reach]], [mods * subs, 1]),
        out_shape=jax.ShapeDtypeStruct((2 * reach + 1, rows, query_grads.shape[0]), f32),
        in_specs=[in_vmem] * len(terms),
        out_specs=in_vmem,
        compiler_params=params(),
        cost_estimate=cost(1),
    )(*[keep_near(term) for term in terms])
    return summed.transpose(1, 0, 2)


def solution(mesh):
    placed = (P("ex", "mod", "sub"), P(("groups", "ex"), "mod", "sub"), P(), P(), P("mod"))
    return jax.shard_map(
        local,
        mesh=mesh,
        in_specs=placed,
        out_specs=P(("groups", "ex", "mod", "sub"), None, None),
        check_vma=False,
    )
```

```python
import functools

import jax
import jax.numpy as jnp
from jax import lax
from jax.experimental import pallas as pl
from jax.experimental.pallas import tpu as pltpu
from jax.sharding import PartitionSpec as P

WINDOW_HALF = 2
PAD = 8
VMEM_LIMIT = 32 * 1024 * 1024

f32, bf16 = jnp.float32, jnp.bfloat16
in_vmem = pl.BlockSpec(memory_space=pltpu.VMEM)


def keep_near(value):
    return pltpu.with_memory_space_constraint(value, pltpu.VMEM)


def params():
    return pltpu.CompilerParams(vmem_limit_bytes=VMEM_LIMIT)


def shifted(value, axis, steps):
    count = lax.axis_size(axis)
    pairs = [(source, (source + steps) % count) for source in range(count)]
    return lax.ppermute(value, axis, pairs)


def to_peer(value, mod_step, sub_step):
    mods, subs = lax.axis_size("mod"), lax.axis_size("sub")
    pairs = []
    for mod in range(mods):
        for sub in range(subs):
            target = ((mod + mod_step) % mods) * subs + (sub + sub_step) % subs
            pairs.append((mod * subs + sub, target))
    return lax.ppermute(value, ("mod", "sub"), pairs)


def split(value):
    high = value.astype(bf16)
    return high, (value - high.astype(f32)).astype(bf16)


def nt_dot(lhs, rhs):
    return lax.dot_general(lhs, rhs, (((1,), (1,)), ((), ())), preferred_element_type=f32)


def right_rows(pair, raw, right_ref):
    width = pair.shape[1]
    queries = raw.shape[0]
    for first in range(0, raw.shape[1], 2 * width):
        pieces = [raw[:, at : at + width] for at in (first, first + width)]
        both = nt_dot(pair, jnp.concatenate(pieces, axis=0))
        both = both[:width] + both[width:]
        half = width // 2
        for index, lanes in enumerate((slice(0, queries), slice(queries, 2 * queries))):
            for row in range(2):
                at = (first // half + 2 * index + row) * (half + PAD)
                right_ref[at : at + half, :] = both[row * half : (row + 1) * half, lanes]


def first_kernel(
    map_ref, in_ref, out_ref, raw_ref, right_ref, pair_ref, left_ref, inverse_ref, rows_ref, own_ref, sems
):
    own_rows = rows_ref.shape[0]
    sub = lax.axis_index("sub")
    module = map_ref[0]
    mine = out_ref.at[module, pl.ds(pl.multiple_of(sub * own_rows, own_rows), own_rows), :]
    copies = [
        pltpu.make_async_copy(in_ref.at[module], inverse_ref, sems.at[0]),
        pltpu.make_async_copy(mine, rows_ref, sems.at[1]),
        pltpu.make_async_copy(raw_ref, own_ref, sems.at[2]),
    ]
    for copy in (copies[2], copies[0], copies[1]):
        copy.start()
    copies[0].wait()
    high, low = split(inverse_ref[...].T)
    high, low = high.astype(f32), low.astype(f32)
    zero = jnp.zeros_like(high)
    pair = jnp.concatenate(
        [jnp.concatenate(row, axis=1) for row in ([high, zero], [zero, high], [low, zero], [zero, low])], axis=0
    ).astype(bf16)
    pair_ref[...] = pair
    copies[1].wait()
    rows = rows_ref[...]
    swapped = jnp.concatenate([rows[:, own_rows:], rows[:, :own_rows]], axis=1)
    rows = jnp.where(sub == 0, rows, swapped)
    high, low = split(rows)
    high, low = high.astype(f32), low.astype(f32)
    left_ref[...] = jnp.concatenate(
        [jnp.concatenate(row, axis=1) for row in ([high, high], [low, jnp.zeros_like(low)])], axis=0
    ).astype(bf16)
    copies[2].wait()
    right_rows(pair, own_ref, right_ref)


def second_kernel(pair_ref, left_ref, own_ref, raw_ref, result_ref, right_ref, done_ref):
    own_rows = left_ref.shape[0] // 2
    rank_in = result_ref.shape[0] // own_rows
    step = rank_in + PAD
    right_rows(pair_ref[...], raw_ref, right_ref)
    left = left_ref[...]
    for first in range(0, rank_in, 2):
        wide = jnp.concatenate(
            [
                jnp.concatenate(
                    [
                        own_ref[pl.ds(column, own_rows, stride=step), :],
                        right_ref[pl.ds(column, own_rows, stride=step), :],
                    ],
                    axis=0,
                )
                for column in (first, first + 1)
            ],
            axis=1,
        )
        high, low = split(wide)
        both = jnp.dot(left, jnp.concatenate([high, low], axis=0), preferred_element_type=f32)
        both = both[:own_rows] + both[own_rows:]
        queries = both.shape[1] // 2
        done_ref[pl.ds(first, own_rows, stride=step), :] = both[:, :queries]
        done_ref[pl.ds(first + 1, own_rows, stride=step), :] = both[:, queries:]
    for row in range(own_rows):
        result_ref[row * rank_in : (row + 1) * rank_in, :] = done_ref[row * step : row * step + rank_in, :].astype(bf16)


def preconditioned(query_grads, in_inverse, out_inverse, module_map):
    block_rows, _, half_width = query_grads.shape
    rank_in, rank_out = in_inverse.shape[1], out_inverse.shape[1]
    own_rows = half_width // rank_in
    raw = query_grads.reshape(block_rows, half_width)
    other = shifted(raw, "sub", 1)
    anywhere = pl.BlockSpec(memory_space=pl.ANY)
    right, pair, left = pl.pallas_call(
        first_kernel,
        out_shape=(
            pltpu.VMEM((own_rows * (rank_in + PAD), block_rows), f32),
            pltpu.VMEM((4 * rank_in, 2 * rank_in), bf16),
            pltpu.VMEM((2 * own_rows, 2 * rank_out), bf16),
        ),
        in_specs=[pl.BlockSpec(memory_space=pltpu.SMEM), anywhere, anywhere, anywhere],
        out_specs=[in_vmem, in_vmem, in_vmem],
        scratch_shapes=[
            pltpu.VMEM((rank_in, rank_in), f32),
            pltpu.VMEM((own_rows, rank_out), f32),
            pltpu.VMEM((block_rows, half_width), bf16),
            pltpu.SemaphoreType.DMA((3,)),
        ],
        compiler_params=params(),
        cost_estimate=cost(2),
    )(module_map, *[pltpu.with_memory_space_constraint(x, pltpu.HBM) for x in (in_inverse, out_inverse, raw)])
    return pl.pallas_call(
        second_kernel,
        out_shape=pltpu.VMEM((half_width, block_rows), bf16),
        in_specs=[in_vmem] * 4,
        out_specs=in_vmem,
        scratch_shapes=[pltpu.VMEM((own_rows * (rank_in + PAD), block_rows), f32)] * 2,
        compiler_params=params(),
        cost_estimate=cost(2),
    )(keep_near(pair), keep_near(left), keep_near(right), keep_near(other))


def part_dot(train_ref, ref, first):
    train = train_ref[:, pl.ds(first, ref.shape[0])]
    return jnp.dot(train, ref[...], preferred_element_type=f32)


def whole_kernel(mods, subs, train_ref, block_ref, *refs):
    outputs, sum_ref = refs[:-1], refs[-1]
    sum_ref[...] = part_dot(train_ref, block_ref, 0)
    rows = sum_ref.shape[0] // (mods * subs)
    for sub_step, output in enumerate(outputs):
        for mod_step in range(mods):
            output[mod_step * rows : (mod_step + 1) * rows, :] = sum_ref[peer_rows(mod_step, sub_step, mods, subs, rows), :].astype(output.dtype)


def peer_rows(mod_step, sub_step, mods, subs, rows):
    target = lax.rem(lax.axis_index("mod") + mod_step, mods) * subs
    target = target + lax.rem(lax.axis_index("sub") + sub_step, subs)
    return pl.ds(pl.multiple_of(target * rows, rows), rows)


def score_kernel(plans, dests, train_ref, *refs):
    count = sum(len(plan) for plan in plans)
    inputs, outputs, sums = list(refs[:count]), (), refs[-len(plans) :]
    if dests:
        outputs = refs[-len(plans) - dests : -len(plans)]
    parts = lax.axis_size("groups")
    blocks = []
    for plan, sum_ref in zip(plans, sums):
        if plan == ["total"]:
            blocks.append(inputs.pop(0))
            continue
        blocks.append(sum_ref)
        total = None
        for kind in plan:
            ref = inputs.pop(0)
            if kind == "total":
                term = ref[...]
            elif kind == "rest":
                term = part_dot(train_ref, ref, train_ref.shape[1] - ref.shape[0])
            else:
                share = ref.shape[0]
                source = lax.rem(lax.axis_index("groups") + parts - kind, parts)
                term = part_dot(train_ref, ref, pl.multiple_of(source * share, 128))
            total = term if total is None else total + term
        sum_ref[...] = total
    mods, subs = lax.axis_size("mod"), lax.axis_size("sub")
    rows = sums[0].shape[0] // (mods * subs)
    for dest, output in enumerate(outputs):
        place = peer_rows(*divmod(dest, subs), mods, subs, rows)
        for block, block_ref in enumerate(blocks):
            output[block * rows : (block + 1) * rows, :] = block_ref[place, :].astype(output.dtype)


def cost(micros):
    return pl.CostEstimate(flops=int(micros * 1.15e9), bytes_accessed=0, transcendentals=0)


def add_kernel(count, *refs):
    inputs, outputs = refs[:count], refs[count:]
    rows = outputs[0].shape[0]
    for step, output in enumerate(outputs):
        total = None
        for ref in inputs:
            term = ref[step * rows : (step + 1) * rows, :].astype(f32)
            total = term if total is None else total + term
        output[...] = total.astype(output.dtype)


def whole(train, block):
    mods, subs = lax.axis_size("mod"), lax.axis_size("sub")
    rows, queries = train.shape[0] // (mods * subs), block.shape[1]
    dealt = pl.pallas_call(
        functools.partial(whole_kernel, mods, subs),
        out_shape=[pltpu.VMEM((mods * rows, queries), bf16 if step else f32) for step in range(subs)],
        in_specs=[in_vmem] * 2,
        out_specs=[in_vmem] * subs,
        scratch_shapes=[pltpu.VMEM((train.shape[0], queries), f32)],
        compiler_params=params(),
        cost_estimate=cost(1),
    )(keep_near(train), keep_near(block))
    terms = [to_peer(piece, 0, step) if step else piece for step, piece in enumerate(dealt)]
    added = pl.pallas_call(
        functools.partial(add_kernel, subs),
        out_shape=[pltpu.VMEM((rows, queries), f32)] * mods,
        in_specs=[in_vmem] * subs,
        out_specs=[in_vmem] * mods,
        compiler_params=params(),
        cost_estimate=cost(0.1),
    )(*map(keep_near, terms))
    return added, dealt


def held(value, first, after):
    def kernel(value_ref, *refs):
        refs[-1][...] = value_ref[first:, :]

    return pl.pallas_call(
        kernel,
        out_shape=pltpu.VMEM((value.shape[0] - first, value.shape[1]), value.dtype),
        in_specs=[in_vmem] + [pl.BlockSpec(memory_space=pl.ANY)] * len(after),
        out_specs=in_vmem,
        compiler_params=params(),
        cost_estimate=cost(0.1),
    )(keep_near(value), *after)


def scored(train, plans, arrays, dests=0, after=()):
    queries = arrays[0].shape[1]
    whole_shape = (train.shape[0], queries)
    sums = [pltpu.VMEM(whole_shape, f32)] * len(plans)
    part_shape = (len(plans) * train.shape[0] // max(dests, 1), queries)
    outputs = [pltpu.VMEM(part_shape, bf16 if dest else f32) for dest in range(dests)] or sums
    return pl.pallas_call(
        functools.partial(score_kernel, plans, dests),
        out_shape=outputs,
        in_specs=[in_vmem] * (1 + len(arrays)) + [pl.BlockSpec(memory_space=pl.ANY)] * len(after),
        out_specs=[in_vmem] * len(outputs),
        scratch_shapes=sums if dests else [],
        compiler_params=params(),
        cost_estimate=cost(0.1),
    )(*map(keep_near, (train, *arrays)), *after)


def settled(terms):
    def kernel(*refs):
        total = None
        for ref in refs[:-1]:
            term = ref[...].astype(f32)
            total = term if total is None else total + term
        refs[-1][...] = total

    return pl.pallas_call(
        kernel,
        out_shape=pltpu.VMEM(terms[0].shape, f32),
        in_specs=[in_vmem] * len(terms),
        out_specs=in_vmem,
        compiler_params=params(),
        cost_estimate=cost(0.1),
    )(*map(keep_near, terms))


def sum_kernel(places, counts, *refs):
    output = refs[-1]
    rows = output.shape[1]
    at = 0
    for blocks, count in zip(places, counts):
        for block, place in enumerate(blocks):
            total = None
            for ref in refs[at : at + count]:
                term = ref[block * rows : (block + 1) * rows, :].astype(f32)
                total = term if total is None else total + term
            output[place] = total
        at += count


def local(query_grads, train_grads, in_inverse, out_inverse, module_map):
    half_width = query_grads.shape[2]
    mods, subs = lax.axis_size("mod"), lax.axis_size("sub")
    parts, part = lax.axis_size("groups"), lax.axis_index("groups")
    reach = min(WINDOW_HALF, (lax.axis_size("ex") - 1) // 2)
    precon = preconditioned(query_grads, in_inverse, out_inverse, module_map)

    share = 5 * half_width // (8 * parts) // 128 * 128
    shared = share * parts
    train = train_grads.reshape(train_grads.shape[0], half_width)

    offsets = [sign * far for far in range(1, reach + 1) for sign in (-1, 1)]
    mine = lax.dynamic_slice_in_dim(precon, part * share, share, 0)
    added, dealt = whole(train, precon)
    rests = {offset: held(precon, shared, dealt[:1] if offset < 0 else added[:1]) for offset in offsets}
    carried = {offset: shifted(mine, "ex", -offset) for offset in offsets}
    common = {offset: shifted(rests[offset], "ex", -offset) for offset in offsets}
    *others, last = offsets
    plans = [[0, "rest"] for offset in others] + [[0]]
    arrays = [piece for offset in others for piece in (carried[offset], common[offset])] + [carried[last]]
    own = settled([to_peer(piece, step, 0) if step else piece for step, piece in enumerate(added)])
    totals = scored(train, plans, arrays, after=[own])
    plans = [["total", *range(1, parts)] for offset in offsets]
    arrays = []
    for offset, total in zip(offsets, totals):
        arrays += [total, *[shifted(carried[offset], "groups", step) for step in range(1, parts)]]
    totals = scored(train, plans, arrays)
    plans = [["total"] for offset in others] + [["total", "rest"]]
    partial = scored(train, plans, [*totals, common[last]], mods * subs)
    terms = [to_peer(rows, *divmod(dest, subs)) if dest else rows for dest, rows in reversed(list(enumerate(partial)))]
    terms.append(own)
    rows = train.shape[0] // (mods * subs)
    summed = pl.pallas_call(
        functools.partial(sum_kernel, [[offset + reach for offset in offsets], [reach]], [mods * subs, 1]),
        out_shape=jax.ShapeDtypeStruct((2 * reach + 1, rows, query_grads.shape[0]), f32),
        in_specs=[in_vmem] * len(terms),
        out_specs=in_vmem,
        compiler_params=params(),
        cost_estimate=cost(1),
    )(*[keep_near(term) for term in terms])
    return summed.transpose(1, 0, 2)


def solution(mesh):
    placed = (P("ex", "mod", "sub"), P(("groups", "ex"), "mod", "sub"), P(), P(), P("mod"))
    return jax.shard_map(
        local,
        mesh=mesh,
        in_specs=placed,
        out_specs=P(("groups", "ex", "mod", "sub"), None, None),
        check_vma=False,
    )
```

```python
import functools

import jax
import jax.numpy as jnp
from jax import lax
from jax.experimental import pallas as pl
from jax.experimental.pallas import tpu as pltpu
from jax.sharding import PartitionSpec as P

WINDOW_HALF = 2
PAD = 8
VMEM_LIMIT = 32 * 1024 * 1024

f32, bf16 = jnp.float32, jnp.bfloat16
in_vmem = pl.BlockSpec(memory_space=pltpu.VMEM)


def keep_near(value):
    return pltpu.with_memory_space_constraint(value, pltpu.VMEM)


def params():
    return pltpu.CompilerParams(vmem_limit_bytes=VMEM_LIMIT)


def shifted(value, axis, steps):
    count = lax.axis_size(axis)
    pairs = [(source, (source + steps) % count) for source in range(count)]
    return lax.ppermute(value, axis, pairs)


def to_peer(value, mod_step, sub_step):
    mods, subs = lax.axis_size("mod"), lax.axis_size("sub")
    pairs = []
    for mod in range(mods):
        for sub in range(subs):
            target = ((mod + mod_step) % mods) * subs + (sub + sub_step) % subs
            pairs.append((mod * subs + sub, target))
    return lax.ppermute(value, ("mod", "sub"), pairs)


def split(value):
    high = value.astype(bf16)
    return high, (value - high.astype(f32)).astype(bf16)


def nt_dot(lhs, rhs):
    return lax.dot_general(lhs, rhs, (((1,), (1,)), ((), ())), preferred_element_type=f32)


def right_rows(pair, raw, right_ref):
    width = pair.shape[1]
    queries = raw.shape[0]
    for first in range(0, raw.shape[1], 2 * width):
        pieces = [raw[:, at : at + width] for at in (first, first + width)]
        both = nt_dot(pair, jnp.concatenate(pieces, axis=0))
        both = both[:width] + both[width:]
        half = width // 2
        for index, lanes in enumerate((slice(0, queries), slice(queries, 2 * queries))):
            for row in range(2):
                at = (first // half + 2 * index + row) * (half + PAD)
                right_ref[at : at + half, :] = both[row * half : (row + 1) * half, lanes]


def first_kernel(
    map_ref, in_ref, out_ref, raw_ref, right_ref, pair_ref, left_ref, inverse_ref, rows_ref, own_ref, sems
):
    own_rows = rows_ref.shape[0]
    sub = lax.axis_index("sub")
    module = map_ref[0]
    mine = out_ref.at[module, pl.ds(pl.multiple_of(sub * own_rows, own_rows), own_rows), :]
    copies = [
        pltpu.make_async_copy(in_ref.at[module], inverse_ref, sems.at[0]),
        pltpu.make_async_copy(mine, rows_ref, sems.at[1]),
        pltpu.make_async_copy(raw_ref, own_ref, sems.at[2]),
    ]
    for copy in copies:
        copy.start()
    copies[0].wait()
    high, low = split(inverse_ref[...].T)
    high, low = high.astype(f32), low.astype(f32)
    zero = jnp.zeros_like(high)
    pair = jnp.concatenate(
        [jnp.concatenate(row, axis=1) for row in ([high, zero], [zero, high], [low, zero], [zero, low])], axis=0
    ).astype(bf16)
    pair_ref[...] = pair
    copies[1].wait()
    rows = rows_ref[...]
    swapped = jnp.concatenate([rows[:, own_rows:], rows[:, :own_rows]], axis=1)
    rows = jnp.where(sub == 0, rows, swapped)
    high, low = split(rows)
    high, low = high.astype(f32), low.astype(f32)
    left_ref[...] = jnp.concatenate(
        [jnp.concatenate(row, axis=1) for row in ([high, high], [low, jnp.zeros_like(low)])], axis=0
    ).astype(bf16)
    copies[2].wait()
    right_rows(pair, own_ref, right_ref)


def second_kernel(pair_ref, left_ref, own_ref, raw_ref, result_ref, right_ref, done_ref):
    own_rows = left_ref.shape[0] // 2
    rank_in = result_ref.shape[0] // own_rows
    step = rank_in + PAD
    right_rows(pair_ref[...], raw_ref, right_ref)
    left = left_ref[...]
    for first in range(0, rank_in, 2):
        wide = jnp.concatenate(
            [
                jnp.concatenate(
                    [
                        own_ref[pl.ds(column, own_rows, stride=step), :],
                        right_ref[pl.ds(column, own_rows, stride=step), :],
                    ],
                    axis=0,
                )
                for column in (first, first + 1)
            ],
            axis=1,
        )
        high, low = split(wide)
        both = jnp.dot(left, jnp.concatenate([high, low], axis=0), preferred_element_type=f32)
        both = both[:own_rows] + both[own_rows:]
        queries = both.shape[1] // 2
        done_ref[pl.ds(first, own_rows, stride=step), :] = both[:, :queries]
        done_ref[pl.ds(first + 1, own_rows, stride=step), :] = both[:, queries:]
    for row in range(own_rows):
        result_ref[row * rank_in : (row + 1) * rank_in, :] = done_ref[row * step : row * step + rank_in, :].astype(bf16)


def preconditioned(query_grads, in_inverse, out_inverse, module_map):
    block_rows, _, half_width = query_grads.shape
    rank_in, rank_out = in_inverse.shape[1], out_inverse.shape[1]
    own_rows = half_width // rank_in
    raw = query_grads.reshape(block_rows, half_width)
    other = shifted(raw, "sub", 1)
    anywhere = pl.BlockSpec(memory_space=pl.ANY)
    right, pair, left = pl.pallas_call(
        first_kernel,
        out_shape=(
            pltpu.VMEM((own_rows * (rank_in + PAD), block_rows), f32),
            pltpu.VMEM((4 * rank_in, 2 * rank_in), bf16),
            pltpu.VMEM((2 * own_rows, 2 * rank_out), bf16),
        ),
        in_specs=[pl.BlockSpec(memory_space=pltpu.SMEM), anywhere, anywhere, anywhere],
        out_specs=[in_vmem, in_vmem, in_vmem],
        scratch_shapes=[
            pltpu.VMEM((rank_in, rank_in), f32),
            pltpu.VMEM((own_rows, rank_out), f32),
            pltpu.VMEM((block_rows, half_width), bf16),
            pltpu.SemaphoreType.DMA((3,)),
        ],
        compiler_params=params(),
        cost_estimate=cost(2),
    )(module_map, *[pltpu.with_memory_space_constraint(x, pltpu.HBM) for x in (in_inverse, out_inverse, raw)])
    return pl.pallas_call(
        second_kernel,
        out_shape=pltpu.VMEM((half_width, block_rows), bf16),
        in_specs=[in_vmem] * 4,
        out_specs=in_vmem,
        scratch_shapes=[pltpu.VMEM((own_rows * (rank_in + PAD), block_rows), f32)] * 2,
        compiler_params=params(),
        cost_estimate=cost(2),
    )(keep_near(pair), keep_near(left), keep_near(right), keep_near(other))


def part_dot(train_ref, ref, first):
    train = train_ref[:, pl.ds(first, ref.shape[0])]
    return jnp.dot(train, ref[...], preferred_element_type=f32)


def whole_kernel(mods, subs, train_ref, block_ref, *refs):
    outputs, sum_ref = refs[:-1], refs[-1]
    sum_ref[...] = part_dot(train_ref, block_ref, 0)
    rows = sum_ref.shape[0] // (mods * subs)
    for sub_step, output in enumerate(outputs):
        for mod_step in range(mods):
            output[mod_step * rows : (mod_step + 1) * rows, :] = sum_ref[peer_rows(mod_step, sub_step, mods, subs, rows), :].astype(output.dtype)


def peer_rows(mod_step, sub_step, mods, subs, rows):
    target = lax.rem(lax.axis_index("mod") + mod_step, mods) * subs
    target = target + lax.rem(lax.axis_index("sub") + sub_step, subs)
    return pl.ds(pl.multiple_of(target * rows, rows), rows)


def score_kernel(plans, dests, train_ref, *refs):
    count = sum(len(plan) for plan in plans)
    inputs, outputs, sums = list(refs[:count]), (), refs[-len(plans) :]
    if dests:
        outputs = refs[-len(plans) - dests : -len(plans)]
    parts = lax.axis_size("groups")
    for plan, sum_ref in zip(plans, sums):
        total = None
        for kind in plan:
            ref = inputs.pop(0)
            if kind == "total":
                term = ref[...]
            elif kind == "rest":
                term = part_dot(train_ref, ref, train_ref.shape[1] - ref.shape[0])
            else:
                share = ref.shape[0]
                source = lax.rem(lax.axis_index("groups") + parts - kind, parts)
                term = part_dot(train_ref, ref, pl.multiple_of(source * share, 128))
            total = term if total is None else total + term
        sum_ref[...] = total
    mods, subs = lax.axis_size("mod"), lax.axis_size("sub")
    rows = sums[0].shape[0] // (mods * subs)
    for dest, output in enumerate(outputs):
        place = peer_rows(*divmod(dest, subs), mods, subs, rows)
        for block, sum_ref in enumerate(sums):
            output[block * rows : (block + 1) * rows, :] = sum_ref[place, :].astype(output.dtype)


def cost(micros):
    return pl.CostEstimate(flops=int(micros * 1.15e9), bytes_accessed=0, transcendentals=0)


def add_kernel(count, *refs):
    inputs, outputs = refs[:count], refs[count:]
    rows = outputs[0].shape[0]
    for step, output in enumerate(outputs):
        total = None
        for ref in inputs:
            term = ref[step * rows : (step + 1) * rows, :].astype(f32)
            total = term if total is None else total + term
        output[...] = total.astype(output.dtype)


def whole(train, block):
    mods, subs = lax.axis_size("mod"), lax.axis_size("sub")
    rows, queries = train.shape[0] // (mods * subs), block.shape[1]
    dealt = pl.pallas_call(
        functools.partial(whole_kernel, mods, subs),
        out_shape=[pltpu.VMEM((mods * rows, queries), bf16 if step else f32) for step in range(subs)],
        in_specs=[in_vmem] * 2,
        out_specs=[in_vmem] * subs,
        scratch_shapes=[pltpu.VMEM((train.shape[0], queries), f32)],
        compiler_params=params(),
        cost_estimate=cost(1),
    )(keep_near(train), keep_near(block))
    terms = [to_peer(piece, 0, step) if step else piece for step, piece in enumerate(dealt)]
    added = pl.pallas_call(
        functools.partial(add_kernel, subs),
        out_shape=[pltpu.VMEM((rows, queries), f32)] * mods,
        in_specs=[in_vmem] * subs,
        out_specs=[in_vmem] * mods,
        compiler_params=params(),
        cost_estimate=cost(0.1),
    )(*map(keep_near, terms))
    return added, dealt


def held(value, first, after):
    def kernel(value_ref, *refs):
        refs[-1][...] = value_ref[first:, :]

    return pl.pallas_call(
        kernel,
        out_shape=pltpu.VMEM((value.shape[0] - first, value.shape[1]), value.dtype),
        in_specs=[in_vmem] + [pl.BlockSpec(memory_space=pl.ANY)] * len(after),
        out_specs=in_vmem,
        compiler_params=params(),
        cost_estimate=cost(0.1),
    )(keep_near(value), *after)


def scored(train, plans, arrays, dests=0, after=()):
    queries = arrays[0].shape[1]
    whole_shape = (train.shape[0], queries)
    sums = [pltpu.VMEM(whole_shape, f32)] * len(plans)
    part_shape = (len(plans) * train.shape[0] // max(dests, 1), queries)
    outputs = [pltpu.VMEM(part_shape, bf16 if dest else f32) for dest in range(dests)] or sums
    return pl.pallas_call(
        functools.partial(score_kernel, plans, dests),
        out_shape=outputs,
        in_specs=[in_vmem] * (1 + len(arrays)) + [pl.BlockSpec(memory_space=pl.ANY)] * len(after),
        out_specs=[in_vmem] * len(outputs),
        scratch_shapes=sums if dests else [],
        compiler_params=params(),
        cost_estimate=cost(0.1),
    )(*map(keep_near, (train, *arrays)), *after)


def settled(terms):
    def kernel(*refs):
        total = None
        for ref in refs[:-1]:
            term = ref[...].astype(f32)
            total = term if total is None else total + term
        refs[-1][...] = total

    return pl.pallas_call(
        kernel,
        out_shape=pltpu.VMEM(terms[0].shape, f32),
        in_specs=[in_vmem] * len(terms),
        out_specs=in_vmem,
        compiler_params=params(),
        cost_estimate=cost(0.1),
    )(*map(keep_near, terms))


def sum_kernel(places, counts, *refs):
    output = refs[-1]
    rows = output.shape[1]
    at = 0
    for blocks, count in zip(places, counts):
        for block, place in enumerate(blocks):
            total = None
            for ref in refs[at : at + count]:
                term = ref[block * rows : (block + 1) * rows, :].astype(f32)
                total = term if total is None else total + term
            output[place] = total
        at += count


def local(query_grads, train_grads, in_inverse, out_inverse, module_map):
    half_width = query_grads.shape[2]
    mods, subs = lax.axis_size("mod"), lax.axis_size("sub")
    parts, part = lax.axis_size("groups"), lax.axis_index("groups")
    reach = min(WINDOW_HALF, (lax.axis_size("ex") - 1) // 2)
    precon = preconditioned(query_grads, in_inverse, out_inverse, module_map)

    share = 5 * half_width // (8 * parts) // 128 * 128
    shared = share * parts
    train = train_grads.reshape(train_grads.shape[0], half_width)

    offsets = [sign * far for far in range(1, reach + 1) for sign in (-1, 1)]
    mine = lax.dynamic_slice_in_dim(precon, part * share, share, 0)
    added, dealt = whole(train, precon)
    rest = held(precon, shared, added[:1])
    carried = {offset: shifted(mine, "ex", -offset) for offset in offsets}
    common = {offset: shifted(rest, "ex", -offset) for offset in offsets}
    *others, last = offsets
    plans = [[0, "rest"] for offset in others] + [[0]]
    arrays = [piece for offset in others for piece in (carried[offset], common[offset])] + [carried[last]]
    own = settled([to_peer(piece, step, 0) if step else piece for step, piece in enumerate(added)])
    totals = scored(train, plans, arrays)
    plans = [["total", *range(1, parts)] for offset in offsets]
    arrays = []
    for offset, total in zip(offsets, totals):
        arrays += [total, *[shifted(carried[offset], "groups", step) for step in range(1, parts)]]
    totals = scored(train, plans, arrays, after=[own])
    plans = [["total"] for offset in others] + [["total", "rest"]]
    partial = scored(train, plans, [*totals, common[last]], mods * subs)
    terms = [to_peer(rows, *divmod(dest, subs)) if dest else rows for dest, rows in reversed(list(enumerate(partial)))]
    terms.append(own)
    rows = train.shape[0] // (mods * subs)
    summed = pl.pallas_call(
        functools.partial(sum_kernel, [[offset + reach for offset in offsets], [reach]], [mods * subs, 1]),
        out_shape=jax.ShapeDtypeStruct((2 * reach + 1, rows, query_grads.shape[0]), f32),
        in_specs=[in_vmem] * len(terms),
        out_specs=in_vmem,
        compiler_params=params(),
        cost_estimate=cost(1),
    )(*[keep_near(term) for term in terms])
    return summed.transpose(1, 0, 2)


def solution(mesh):
    placed = (P("ex", "mod", "sub"), P(("groups", "ex"), "mod", "sub"), P(), P(), P("mod"))
    return jax.shard_map(
        local,
        mesh=mesh,
        in_specs=placed,
        out_specs=P(("groups", "ex", "mod", "sub"), None, None),
        check_vma=False,
    )
```

```python
import functools

import jax
import jax.numpy as jnp
from jax import lax
from jax.experimental import pallas as pl
from jax.experimental.pallas import tpu as pltpu
from jax.sharding import PartitionSpec as P

WINDOW_HALF = 2
PAD = 8
VMEM_LIMIT = 32 * 1024 * 1024

f32, bf16 = jnp.float32, jnp.bfloat16
in_vmem = pl.BlockSpec(memory_space=pltpu.VMEM)


def keep_near(value):
    return pltpu.with_memory_space_constraint(value, pltpu.VMEM)


def params():
    return pltpu.CompilerParams(vmem_limit_bytes=VMEM_LIMIT)


def shifted(value, axis, steps):
    count = lax.axis_size(axis)
    pairs = [(source, (source + steps) % count) for source in range(count)]
    return lax.ppermute(value, axis, pairs)


def to_peer(value, mod_step, sub_step):
    mods, subs = lax.axis_size("mod"), lax.axis_size("sub")
    pairs = []
    for mod in range(mods):
        for sub in range(subs):
            target = ((mod + mod_step) % mods) * subs + (sub + sub_step) % subs
            pairs.append((mod * subs + sub, target))
    return lax.ppermute(value, ("mod", "sub"), pairs)


def split(value):
    high = value.astype(bf16)
    return high, (value - high.astype(f32)).astype(bf16)


def nt_dot(lhs, rhs):
    return lax.dot_general(lhs, rhs, (((1,), (1,)), ((), ())), preferred_element_type=f32)


def right_rows(pair, raw, right_ref):
    width = pair.shape[1]
    queries = raw.shape[0]
    for first in range(0, raw.shape[1], 2 * width):
        pieces = [raw[:, at : at + width] for at in (first, first + width)]
        both = nt_dot(pair, jnp.concatenate(pieces, axis=0))
        both = both[:width] + both[width:]
        half = width // 2
        for index, lanes in enumerate((slice(0, queries), slice(queries, 2 * queries))):
            for row in range(2):
                at = (first // half + 2 * index + row) * (half + PAD)
                right_ref[at : at + half, :] = both[row * half : (row + 1) * half, lanes]


def first_kernel(
    map_ref, in_ref, out_ref, raw_ref, right_ref, pair_ref, left_ref, inverse_ref, rows_ref, own_ref, sems
):
    own_rows = rows_ref.shape[0]
    sub = lax.axis_index("sub")
    module = map_ref[0]
    mine = out_ref.at[module, pl.ds(pl.multiple_of(sub * own_rows, own_rows), own_rows), :]
    copies = [
        pltpu.make_async_copy(in_ref.at[module], inverse_ref, sems.at[0]),
        pltpu.make_async_copy(mine, rows_ref, sems.at[1]),
        pltpu.make_async_copy(raw_ref, own_ref, sems.at[2]),
    ]
    for copy in copies:
        copy.start()
    copies[0].wait()
    high, low = split(inverse_ref[...].T)
    high, low = high.astype(f32), low.astype(f32)
    zero = jnp.zeros_like(high)
    pair = jnp.concatenate(
        [jnp.concatenate(row, axis=1) for row in ([high, zero], [zero, high], [low, zero], [zero, low])], axis=0
    ).astype(bf16)
    pair_ref[...] = pair
    copies[1].wait()
    rows = rows_ref[...]
    swapped = jnp.concatenate([rows[:, own_rows:], rows[:, :own_rows]], axis=1)
    rows = jnp.where(sub == 0, rows, swapped)
    high, low = split(rows)
    high, low = high.astype(f32), low.astype(f32)
    left_ref[...] = jnp.concatenate(
        [jnp.concatenate(row, axis=1) for row in ([high, high], [low, jnp.zeros_like(low)])], axis=0
    ).astype(bf16)
    copies[2].wait()
    right_rows(pair, own_ref, right_ref)


def second_kernel(pair_ref, left_ref, own_ref, raw_ref, result_ref, right_ref, done_ref):
    own_rows = left_ref.shape[0] // 2
    rank_in = result_ref.shape[0] // own_rows
    step = rank_in + PAD
    right_rows(pair_ref[...], raw_ref, right_ref)
    left = left_ref[...]
    for first in range(0, rank_in, 2):
        wide = jnp.concatenate(
            [
                jnp.concatenate(
                    [
                        own_ref[pl.ds(column, own_rows, stride=step), :],
                        right_ref[pl.ds(column, own_rows, stride=step), :],
                    ],
                    axis=0,
                )
                for column in (first, first + 1)
            ],
            axis=1,
        )
        high, low = split(wide)
        both = jnp.dot(left, jnp.concatenate([high, low], axis=0), preferred_element_type=f32)
        both = both[:own_rows] + both[own_rows:]
        queries = both.shape[1] // 2
        done_ref[pl.ds(first, own_rows, stride=step), :] = both[:, :queries]
        done_ref[pl.ds(first + 1, own_rows, stride=step), :] = both[:, queries:]
    for row in range(own_rows):
        result_ref[row * rank_in : (row + 1) * rank_in, :] = done_ref[row * step : row * step + rank_in, :].astype(bf16)


def preconditioned(query_grads, in_inverse, out_inverse, module_map):
    block_rows, _, half_width = query_grads.shape
    rank_in, rank_out = in_inverse.shape[1], out_inverse.shape[1]
    own_rows = half_width // rank_in
    raw = query_grads.reshape(block_rows, half_width)
    other = shifted(raw, "sub", 1)
    anywhere = pl.BlockSpec(memory_space=pl.ANY)
    right, pair, left = pl.pallas_call(
        first_kernel,
        out_shape=(
            pltpu.VMEM((own_rows * (rank_in + PAD), block_rows), f32),
            pltpu.VMEM((4 * rank_in, 2 * rank_in), bf16),
            pltpu.VMEM((2 * own_rows, 2 * rank_out), bf16),
        ),
        in_specs=[pl.BlockSpec(memory_space=pltpu.SMEM), anywhere, anywhere, anywhere],
        out_specs=[in_vmem, in_vmem, in_vmem],
        scratch_shapes=[
            pltpu.VMEM((rank_in, rank_in), f32),
            pltpu.VMEM((own_rows, rank_out), f32),
            pltpu.VMEM((block_rows, half_width), bf16),
            pltpu.SemaphoreType.DMA((3,)),
        ],
        compiler_params=params(),
        cost_estimate=cost(2),
    )(module_map, *[pltpu.with_memory_space_constraint(x, pltpu.HBM) for x in (in_inverse, out_inverse, raw)])
    return pl.pallas_call(
        second_kernel,
        out_shape=pltpu.VMEM((half_width, block_rows), bf16),
        in_specs=[in_vmem] * 4,
        out_specs=in_vmem,
        scratch_shapes=[pltpu.VMEM((own_rows * (rank_in + PAD), block_rows), f32)] * 2,
        compiler_params=params(),
        cost_estimate=cost(2),
    )(keep_near(pair), keep_near(left), keep_near(right), keep_near(other))


def part_dot(train_ref, ref, first):
    train = train_ref[:, pl.ds(first, ref.shape[0])]
    return jnp.dot(train, ref[...], preferred_element_type=f32)


def whole_kernel(mods, subs, train_ref, block_ref, *refs):
    outputs, sum_ref = refs[:-1], refs[-1]
    sum_ref[...] = part_dot(train_ref, block_ref, 0)
    rows = sum_ref.shape[0] // (mods * subs)
    for sub_step, output in enumerate(outputs):
        for mod_step in range(mods):
            output[mod_step * rows : (mod_step + 1) * rows, :] = sum_ref[peer_rows(mod_step, sub_step, mods, subs, rows), :].astype(output.dtype)


def peer_rows(mod_step, sub_step, mods, subs, rows):
    target = lax.rem(lax.axis_index("mod") + mod_step, mods) * subs
    target = target + lax.rem(lax.axis_index("sub") + sub_step, subs)
    return pl.ds(pl.multiple_of(target * rows, rows), rows)


def score_kernel(plans, dests, train_ref, *refs):
    count = sum(len(plan) for plan in plans)
    inputs, outputs, sums = list(refs[:count]), (), refs[-len(plans) :]
    if dests:
        outputs = refs[-len(plans) - dests : -len(plans)]
    parts = lax.axis_size("groups")
    for plan, sum_ref in zip(plans, sums):
        total = None
        for kind in plan:
            ref = inputs.pop(0)
            if kind == "total":
                term = ref[...]
            elif kind == "rest":
                term = part_dot(train_ref, ref, train_ref.shape[1] - ref.shape[0])
            else:
                share = ref.shape[0]
                source = lax.rem(lax.axis_index("groups") + parts - kind, parts)
                term = part_dot(train_ref, ref, pl.multiple_of(source * share, 128))
            total = term if total is None else total + term
        sum_ref[...] = total
    mods, subs = lax.axis_size("mod"), lax.axis_size("sub")
    rows = sums[0].shape[0] // (mods * subs)
    for dest, output in enumerate(outputs):
        place = peer_rows(*divmod(dest, subs), mods, subs, rows)
        for block, sum_ref in enumerate(sums):
            output[block * rows : (block + 1) * rows, :] = sum_ref[place, :].astype(output.dtype)


def cost(micros):
    return pl.CostEstimate(flops=int(micros * 1.15e9), bytes_accessed=0, transcendentals=0)


def add_kernel(count, *refs):
    inputs, outputs = refs[:count], refs[count:]
    rows = outputs[0].shape[0]
    for step, output in enumerate(outputs):
        total = None
        for ref in inputs:
            term = ref[step * rows : (step + 1) * rows, :].astype(f32)
            total = term if total is None else total + term
        output[...] = total.astype(output.dtype)


def whole(train, block):
    mods, subs = lax.axis_size("mod"), lax.axis_size("sub")
    rows, queries = train.shape[0] // (mods * subs), block.shape[1]
    dealt = pl.pallas_call(
        functools.partial(whole_kernel, mods, subs),
        out_shape=[pltpu.VMEM((mods * rows, queries), bf16 if step else f32) for step in range(subs)],
        in_specs=[in_vmem] * 2,
        out_specs=[in_vmem] * subs,
        scratch_shapes=[pltpu.VMEM((train.shape[0], queries), f32)],
        compiler_params=params(),
        cost_estimate=cost(1),
    )(keep_near(train), keep_near(block))
    terms = [to_peer(piece, 0, step) if step else piece for step, piece in enumerate(dealt)]
    added = pl.pallas_call(
        functools.partial(add_kernel, subs),
        out_shape=[pltpu.VMEM((rows, queries), f32)] * mods,
        in_specs=[in_vmem] * subs,
        out_specs=[in_vmem] * mods,
        compiler_params=params(),
        cost_estimate=cost(0.1),
    )(*map(keep_near, terms))
    return added, dealt


def held(value, first, after):
    def kernel(value_ref, *refs):
        refs[-1][...] = value_ref[first:, :]

    return pl.pallas_call(
        kernel,
        out_shape=pltpu.VMEM((value.shape[0] - first, value.shape[1]), value.dtype),
        in_specs=[in_vmem] + [pl.BlockSpec(memory_space=pl.ANY)] * len(after),
        out_specs=in_vmem,
        compiler_params=params(),
        cost_estimate=cost(0.1),
    )(keep_near(value), *after)


def scored(train, plans, arrays, dests=0, after=()):
    queries = arrays[0].shape[1]
    whole_shape = (train.shape[0], queries)
    sums = [pltpu.VMEM(whole_shape, f32)] * len(plans)
    part_shape = (len(plans) * train.shape[0] // max(dests, 1), queries)
    outputs = [pltpu.VMEM(part_shape, bf16 if dest else f32) for dest in range(dests)] or sums
    return pl.pallas_call(
        functools.partial(score_kernel, plans, dests),
        out_shape=outputs,
        in_specs=[in_vmem] * (1 + len(arrays)) + [pl.BlockSpec(memory_space=pl.ANY)] * len(after),
        out_specs=[in_vmem] * len(outputs),
        scratch_shapes=sums if dests else [],
        compiler_params=params(),
        cost_estimate=cost(0.1),
    )(*map(keep_near, (train, *arrays)), *after)


def settled(terms):
    def kernel(*refs):
        total = None
        for ref in refs[:-1]:
            term = ref[...].astype(f32)
            total = term if total is None else total + term
        refs[-1][...] = total

    return pl.pallas_call(
        kernel,
        out_shape=pltpu.VMEM(terms[0].shape, f32),
        in_specs=[in_vmem] * len(terms),
        out_specs=in_vmem,
        compiler_params=params(),
        cost_estimate=cost(0.1),
    )(*map(keep_near, terms))


def sum_kernel(places, counts, *refs):
    output = refs[-1]
    rows = output.shape[1]
    at = 0
    for blocks, count in zip(places, counts):
        for block, place in enumerate(blocks):
            total = None
            for ref in refs[at : at + count]:
                term = ref[block * rows : (block + 1) * rows, :].astype(f32)
                total = term if total is None else total + term
            output[place] = total
        at += count


def local(query_grads, train_grads, in_inverse, out_inverse, module_map):
    half_width = query_grads.shape[2]
    mods, subs = lax.axis_size("mod"), lax.axis_size("sub")
    parts, part = lax.axis_size("groups"), lax.axis_index("groups")
    reach = min(WINDOW_HALF, (lax.axis_size("ex") - 1) // 2)
    precon = preconditioned(query_grads, in_inverse, out_inverse, module_map)

    share = 5 * half_width // (8 * parts) // 128 * 128
    shared = share * parts
    train = train_grads.reshape(train_grads.shape[0], half_width)

    offsets = [sign * far for far in range(1, reach + 1) for sign in (-1, 1)]
    mine = lax.dynamic_slice_in_dim(precon, part * share, share, 0)
    added, dealt = whole(train, precon)
    rests = {offset: held(precon, shared, dealt[:1] if offset < 0 else added[:1]) for offset in offsets}
    carried = {offset: shifted(mine, "ex", -offset) for offset in offsets}
    common = {offset: shifted(rests[offset], "ex", -offset) for offset in offsets}
    *others, last = offsets
    plans = [[0, "rest"] for offset in others] + [[0]]
    arrays = [piece for offset in others for piece in (carried[offset], common[offset])] + [carried[last]]
    own = settled([to_peer(piece, step, 0) if step else piece for step, piece in enumerate(added)])
    totals = scored(train, plans, arrays)
    plans = [["total", *range(1, parts)] for offset in offsets]
    arrays = []
    for offset, total in zip(offsets, totals):
        arrays += [total, *[shifted(carried[offset], "groups", step) for step in range(1, parts)]]
    totals = scored(train, plans, arrays, after=[own])
    plans = [["total"] for offset in others] + [["total", "rest"]]
    partial = scored(train, plans, [*totals, common[last]], mods * subs)
    terms = [to_peer(rows, *divmod(dest, subs)) if dest else rows for dest, rows in reversed(list(enumerate(partial)))]
    terms.append(own)
    rows = train.shape[0] // (mods * subs)
    summed = pl.pallas_call(
        functools.partial(sum_kernel, [[offset + reach for offset in offsets], [reach]], [mods * subs, 1]),
        out_shape=jax.ShapeDtypeStruct((2 * reach + 1, rows, query_grads.shape[0]), f32),
        in_specs=[in_vmem] * len(terms),
        out_specs=in_vmem,
        compiler_params=params(),
        cost_estimate=cost(1),
    )(*[keep_near(term) for term in terms])
    return summed.transpose(1, 0, 2)


def solution(mesh):
    placed = (P("ex", "mod", "sub"), P(("groups", "ex"), "mod", "sub"), P(), P(), P("mod"))
    return jax.shard_map(
        local,
        mesh=mesh,
        in_specs=placed,
        out_specs=P(("groups", "ex", "mod", "sub"), None, None),
        check_vma=False,
    )
```
